32 devices in a mesh: replica: 2 (over x), section: 4 (over y, core), shard: 4 (over z).
Axes of the slice: x: 2, y: 2, z: 4, core: 2. Of those that a mesh axis runs over, the one named last changes fastest.
Arguments:
- inputs: bfloat16 [2, 1, 128, 1024], P('replica', None, None, 'shard'), may hold values from -17 to 17
- targets: bfloat16 [2, 1, 128, 1024], P('replica', None, None, 'shard'), may hold values from -6 to 6
- weight_a: bfloat16 [2, 4, 1024, 3072], P('replica', 'section', None, 'shard'), may hold values from -6 to 6
- weight_b: bfloat16 [2, 4, 3072, 1024], P('replica', 'section', 'shard'), may hold values from -6 to 6
- moment_a: bfloat16 [2, 4, 1024, 3072], P('replica', 'section', None, 'shard'), may hold values from -3 to 3
- moment_b: bfloat16 [2, 4, 3072, 1024], P('replica', 'section', 'shard'), may hold values from -3 to 3
- routes: int32 [1, 3, 2, 2], replicated, may hold values from 0 to 1, each once within a row
- partners: int32 [4, 2, 2, 2], replicated, may hold values from 0 to 1, as said below
Outputs:
- new_weight_a: bfloat16 [2, 4, 1024, 3072], P('replica', 'section', None, 'shard')
- new_weight_b: bfloat16 [2, 4, 3072, 1024], P('replica', 'section', 'shard')
- new_moment_a: bfloat16 [2, 4, 1024, 3072], P('replica', 'section', None, 'shard')
- new_moment_b: bfloat16 [2, 4, 3072, 1024], P('replica', 'section', 'shard')
The draws below stay inside these ranges and needn't reach their ends.
Inputs may be any that keep to these rules, and one draw needn't show every extreme that they name: Each routes[m, s, q, :] names every replica once, so each replica of section s + 1 receives exactly one block from every replica of section s. For each section s, projection t and piece k, partners[s, t, k, :] is its own inverse (the partner of the partner is the replica itself); for each s, t and replica r, partners[s, t, :, r] names every replica once, and exactly one piece pairs r with itself.
All inputs are finite; a program needn't handle non-finite values.
Results may differ from the reference program's by a relative error of at most 0.022.
Values may be sent and summed in bfloat16 or wider, within the bound.
No kernel may reach another device: no remote copies, remote signals or barrier semaphores. Data moves between devices by JAX's collectives and lax.ppermute only.
A program may use at most 128 MiB of HBM per device.

```python
import jax
import jax.numpy as jnp
from jax import lax

D = 1024
K = 3072
B = 128
M = 1
REPLICAS = 2
SECTIONS = 4
N_REPLICA = 2
N_SECTION = 4
N_SHARD = 4


def draw_inputs(key, part):
    key = jax.random.fold_in(key, 3)
    first, second, third = jax.random.split(key, 3)
    row_scale = jnp.exp(jax.random.uniform(second, (REPLICAS, M, B, 1), jnp.float32, -1.0, 1.0))
    position = jnp.arange(D, dtype=jnp.float32) / (D - 1.0) * 2.0 - 1.0
    ramp = jnp.exp(0.8 * position)
    column_scale = jnp.exp(jax.random.uniform(third, (D,), jnp.float32, -0.6, 0.6)) * ramp
    base = jnp.clip(jax.random.normal(first, (REPLICAS, M, B, D), jnp.float32), -5.0, 5.0)
    return (base * row_scale * column_scale * 0.3).astype(jnp.bfloat16)


def pairing_table(key):
    first, second = jax.random.split(key)
    labels = jax.random.permutation(first, REPLICAS).astype(jnp.int32)
    inverse = jnp.argsort(labels, stable=True).astype(jnp.int32)
    offsets = jax.random.permutation(second, REPLICAS).astype(jnp.int32)
    mixed = jnp.bitwise_xor(labels[None, :], offsets[:, None])
    return inverse[mixed].astype(jnp.int32)


def draw_partners(key, part):
    key = jax.random.fold_in(key, 7)
    keys = jax.random.split(key, SECTIONS * 2)
    tables = jax.vmap(pairing_table)(keys)
    return tables.reshape(SECTIONS, 2, REPLICAS, REPLICAS).astype(jnp.int32)


def block_scale(stream_key, extent, cuts, least, high):
    factor_of = 1.0
    for dim, blocks in cuts:
        draws = jax.random.uniform(jax.random.fold_in(jax.random.fold_in(stream_key, 6), dim), (blocks,), jnp.float32, least / len(cuts), high / len(cuts))
        factor_of = factor_of * jnp.repeat(jnp.exp(draws), extent[dim] // blocks).reshape((-1,) + (1,) * (len(extent) - 1 - dim))
    return factor_of


def gaussian(stream_key, shape, spread, limit, pieces=(), kind=jnp.bfloat16):
    loudness = block_scale(stream_key, shape, pieces, -0.22, 0.18) if pieces else 1.0
    drawn = jax.random.normal(stream_key, shape, jnp.float32) * spread * loudness
    return jnp.minimum(jnp.maximum(drawn, -limit), limit).astype(kind)


def setup_inputs(seed: int = 0) -> dict:
    key_list = jax.random.split(jax.random.key(seed), 9)
    return {
        "inputs": draw_inputs(jax.random.fold_in(key_list[8], 71), 0),
        "targets": gaussian(key_list[1], (REPLICAS, M, B, D), 1.0, 6.0, ((0, 2), (3, 4))),
        "weight_a": gaussian(key_list[2], (REPLICAS, SECTIONS, D, K), 1.0, 6.0, ((0, 2), (1, 4), (3, 4))),
        "weight_b": gaussian(key_list[3], (REPLICAS, SECTIONS, K, D), 1.0, 6.0, ((0, 2), (1, 4), (2, 4))),
        "moment_a": gaussian(key_list[4], (REPLICAS, SECTIONS, D, K), 0.5, 3.0, ((0, 2), (1, 4), (3, 4))),
        "moment_b": gaussian(key_list[5], (REPLICAS, SECTIONS, K, D), 0.5, 3.0, ((0, 2), (1, 4), (2, 4))),
        "routes": jax.vmap(lambda own: jax.random.permutation(own, REPLICAS))(jax.random.split(key_list[6], M * (SECTIONS - 1) * REPLICAS)).reshape((M, SECTIONS - 1, REPLICAS, REPLICAS)).astype(jnp.int32),
        "partners": draw_partners(jax.random.fold_in(key_list[8], 71), 0),
    }


epsilon = 1e-05
inner_rate = 0.5
momentum_decay = 0.9
outer_rate = 0.7

def rounded(value):
    return lax.optimization_barrier(value.astype(jnp.bfloat16)).astype(jnp.float32)

def block_forward(section_input, weight_in, weight_out):
    scale_in = 1.0 / D ** 0.5
    scale_out = 1.0 / K ** 0.5
    wide = section_input.astype(jnp.float32)
    inverse_rms = lax.rsqrt(lax.optimization_barrier(jnp.mean(wide * wide, axis=-1, keepdims=True)) + epsilon)
    normed = (wide * inverse_rms).astype(jnp.bfloat16)
    preact = jnp.einsum('rmbd,rdk->rmbk', normed.astype(jnp.float32), weight_in.astype(jnp.float32)) * scale_in
    hidden = jax.nn.silu(preact).astype(jnp.bfloat16)
    share = K // N_SHARD
    total = jnp.zeros(wide.shape, jnp.float32)
    for index in range(N_SHARD):
        part_hidden = hidden[..., index * share:(index + 1) * share].astype(jnp.float32)
        part_weight = weight_out[:, index * share:(index + 1) * share, :].astype(jnp.float32)
        total = total + rounded(jnp.einsum('rmbk,rkd->rmbd', part_hidden, part_weight) * scale_out)
    output = (wide + total).astype(jnp.bfloat16)
    return (output, normed, preact, hidden, inverse_rms)

def block_backward(section_input, normed, preact, hidden, inverse_rms, weight_in, weight_out, upstream):
    scale_in = 1.0 / D ** 0.5
    scale_out = 1.0 / K ** 0.5
    up_wide = upstream.astype(jnp.float32)
    grad_out = jnp.einsum('rmbk,rmbd->rkd', hidden.astype(jnp.float32), up_wide) * scale_out
    grad_hidden = jnp.einsum('rmbd,rkd->rmbk', up_wide, weight_out.astype(jnp.float32)) * scale_out
    gate = jax.nn.sigmoid(preact)
    grad_pre = (grad_hidden * gate * (1.0 + preact * (1.0 - gate))).astype(jnp.bfloat16)
    grad_in = jnp.einsum('rmbd,rmbk->rdk', normed.astype(jnp.float32), grad_pre.astype(jnp.float32)) * scale_in
    share = K // N_SHARD
    total = jnp.zeros(up_wide.shape, jnp.float32)
    for index in range(N_SHARD):
        part_grad = grad_pre[..., index * share:(index + 1) * share].astype(jnp.float32)
        part_weight = weight_in[:, :, index * share:(index + 1) * share].astype(jnp.float32)
        total = total + rounded(jnp.einsum('rmbk,rdk->rmbd', part_grad, part_weight) * scale_in)
    exact = section_input.astype(jnp.float32) * inverse_rms
    along = lax.optimization_barrier(jnp.mean(total * exact, axis=-1, keepdims=True))
    result = (up_wide + inverse_rms * (total - exact * along)).astype(jnp.bfloat16)
    return (result, grad_in, grad_out)

def target_slots(table):
    labels = jnp.arange(N_REPLICA, dtype=jnp.int32)
    match = (table[..., None, :] == labels[:, None]).astype(jnp.int32)
    return lax.optimization_barrier(jnp.sum(match * labels, axis=-1))

def route_forward(values, table):
    group_rows = B // N_REPLICA
    grouped = values.reshape(N_REPLICA, M, N_REPLICA, group_rows, D)
    slots = jnp.transpose(target_slots(table), (1, 0, 2))
    picked = jnp.take_along_axis(grouped, slots[:, :, :, None, None], axis=2)
    return jnp.transpose(picked, (2, 1, 0, 3, 4)).reshape(N_REPLICA, M, B, D)

def route_back(values, table):
    group_rows = B // N_REPLICA
    grouped = jnp.transpose(values.reshape(N_REPLICA, M, N_REPLICA, group_rows, D), (2, 1, 0, 3, 4))
    slots = jnp.transpose(table, (1, 0, 2))
    picked = jnp.take_along_axis(grouped, slots[:, :, :, None, None], axis=2)
    return picked.reshape(N_REPLICA, M, B, D)

def partner_view(array, axis, partners):
    taken = [jnp.take(jnp.take(array, index, axis=axis), partners[index], axis=0) for index in range(N_REPLICA)]
    return jnp.stack(taken, axis=axis)

def outer_update(weights, moments, grads, partners, shape, axis):
    initial = weights.shape
    deltas = (inner_rate * grads).astype(jnp.bfloat16).reshape(shape)
    weights = weights.reshape(shape)
    moments = moments.reshape(shape)
    mean_weight = (weights.astype(jnp.float32) + partner_view(weights, axis, partners).astype(jnp.float32)) * 0.5
    mean_moment = (moments.astype(jnp.float32) + partner_view(moments, axis, partners).astype(jnp.float32)) * 0.5
    mean_delta = (deltas.astype(jnp.float32) + partner_view(deltas, axis, partners).astype(jnp.float32)) * 0.5
    new_moment = momentum_decay * mean_moment + mean_delta
    new_weight = mean_weight - outer_rate * (momentum_decay * new_moment + mean_delta)
    return (new_weight.astype(jnp.bfloat16).reshape(initial), new_moment.astype(jnp.bfloat16).reshape(initial))

def reference(inputs, targets, weight_a, weight_b, moment_a, moment_b, routes, partners):
    current = inputs
    saved = []
    final = inputs
    for section in range(N_SECTION):
        results = block_forward(current, weight_a[:, section], weight_b[:, section])
        saved.append((current,) + results[1:])
        final = results[0]
        if section + 1 < N_SECTION:
            current = route_forward(final, routes[:, section])
    upstream = (final.astype(jnp.float32) - targets.astype(jnp.float32)).astype(jnp.bfloat16)
    weights_in, weights_out, moments_in, moments_out = ([], [], [], [])
    shape_in = (N_REPLICA, N_REPLICA, D // N_REPLICA, K)
    shape_out = (N_REPLICA, N_SHARD, N_REPLICA, K // (N_SHARD * N_REPLICA), D)
    for section in reversed(range(N_SECTION)):
        section_input, normed, preact, hidden, inverse_rms = saved[section]
        result, grad_in, grad_out = block_backward(section_input, normed, preact, hidden, inverse_rms, weight_a[:, section], weight_b[:, section], upstream)
        new_in, moment_in = outer_update(weight_a[:, section], moment_a[:, section], grad_in, partners[section, 0], shape_in, 1)
        new_out, moment_out = outer_update(weight_b[:, section], moment_b[:, section], grad_out, partners[section, 1], shape_out, 2)
        weights_in.insert(0, new_in)
        weights_out.insert(0, new_out)
        moments_in.insert(0, moment_in)
        moments_out.insert(0, moment_out)
        if section > 0:
            upstream = route_back(result, routes[:, section - 1])
    return (jnp.stack(weights_in, axis=1), jnp.stack(weights_out, axis=1), jnp.stack(moments_in, axis=1), jnp.stack(moments_out, axis=1))
```

```python
import math

import jax
import jax.numpy as jnp
from jax import lax
from jax.sharding import PartitionSpec as P

epsilon = 1e-05
inner_rate = 0.5
momentum_decay = 0.9
outer_rate = 0.7

axes = ("replica", "section", "shard")
contract_rows = (((0,), (0,)), ((), ()))
contract_last = (((1,), (1,)), ((), ()))


def norm_scale(rows):
    wide = rows.astype(jnp.float32)
    return lax.rsqrt(jnp.mean(wide * wide, axis=1, keepdims=True) + epsilon)


def dot(left, right, dims=(((1,), (0,)), ((), ()))):
    return lax.dot_general(left, right, dims, preferred_element_type=jnp.float32)


def outer_mix(weight, moment, delta):
    new_moment = momentum_decay * moment + delta
    new_weight = weight - outer_rate * (momentum_decay * new_moment + delta)
    return new_weight.astype(jnp.bfloat16), new_moment.astype(jnp.bfloat16)


def per_device(inputs, targets, weight_a, weight_b, moment_a, moment_b, routes, partners):
    replicas = lax.axis_size("replica")
    sections = lax.axis_size("section")
    shards = lax.axis_size("shard")
    replica_id = lax.axis_index("replica")
    section_id = lax.axis_index("section")
    shard_id = lax.axis_index("shard")
    row_count = inputs.shape[2]
    features = inputs.shape[3]
    width = weight_a.shape[2]
    local_hidden = weight_a.shape[3]
    assert inputs.shape[1] == 1 and shards & (shards - 1) == 0
    scale_in = 1.0 / math.sqrt(width)
    scale_out = 1.0 / math.sqrt(local_hidden * shards)
    weight_in = weight_a[0, 0]
    weight_out = weight_b[0, 0]
    piece_rows = row_count // (replicas * shards)
    own_rows = replicas * piece_rows

    def flat(replica, section, shard):
        return (replica * sections + section) * shards + shard

    def across_shards(array, offset, active):
        pairs = [
            (flat(r, s, j), flat(r, s, j ^ offset))
            for r in range(replicas)
            for s in active
            for j in range(shards)
        ]
        return lax.ppermute(array, axes, pairs)

    def across_replicas(array, offset, active, step=0):
        pairs = [
            (flat(r, s, j), flat((r + offset) % replicas, s + step, j))
            for r in range(replicas)
            for s in active
            for j in range(shards)
        ]
        return lax.ppermute(array, axes, pairs)

    def gather_rows(own, active):
        parts = [own] + [across_shards(own, d, active) for d in range(1, shards)]
        return jnp.concatenate(parts, axis=0)

    def scatter_rows(term, active):
        term = term.astype(jnp.bfloat16).reshape(shards, own_rows, width)
        total = term[0].astype(jnp.float32)
        for d in range(1, shards):
            total = total + across_shards(term[d], d, active).astype(jnp.float32)
        return total

    def in_feature_order(parts):
        stacked = jnp.stack(parts)
        order = shard_id ^ jnp.arange(shards, dtype=jnp.int32)
        return jnp.concatenate(
            [lax.dynamic_index_in_dim(stacked, order[c], 0, keepdims=False) for c in range(shards)],
            axis=1,
        )

    def split_rows(array):
        blocks = array.reshape(replicas, shards, piece_rows, array.shape[1])
        places = (replica_id - jnp.arange(replicas, dtype=jnp.int32)) % replicas
        return jnp.take(blocks, places, axis=0)

    def shard_rows(split, d):
        rows = lax.dynamic_index_in_dim(split, shard_id ^ d, 1, keepdims=False)
        return rows.reshape(own_rows, split.shape[3])

    every = range(sections)
    others = range(1, replicas)

    tables = lax.dynamic_index_in_dim(partners, section_id, 0, keepdims=False)

    def piece_of(table, offset):
        wanted = (replica_id + offset) % replicas
        return jnp.argmax(table[:, replica_id] == wanted).astype(jnp.int32)

    pieces_in = [piece_of(tables[0], e) for e in range(replicas)]
    pieces_out = [piece_of(tables[1], e) for e in range(replicas)]
    size_in = width // replicas
    size_out = local_hidden // replicas

    def piece(array, index, size, axis=0):
        return lax.dynamic_slice_in_dim(array, index * size, size, axis)

    def exchange(array, pieces, size, axis=0, active=every):
        return [
            across_replicas(piece(array, pieces[e], size, axis), e, active) for e in others
        ]

    input_parts = [inputs[0, 0]] + [across_shards(inputs[0, 0], d, [0]) for d in range(1, shards)]
    first = split_rows(in_feature_order(input_parts))
    goal_split = split_rows(targets[0, 0])
    goal_parts = [shard_rows(goal_split, 0)] + [
        across_shards(shard_rows(goal_split, d), d, [sections - 1]) for d in range(1, shards)
    ]
    goal = in_feature_order(goal_parts)

    far_weight_in = exchange(weight_in, pieces_in, size_in)
    far_moment_in = exchange(moment_a[0, 0], pieces_in, size_in)
    far_weight_out = exchange(weight_out, pieces_out, size_out)
    far_moment_out = exchange(moment_b[0, 0], pieces_out, size_out)

    def slots(link):
        table = routes[0, link, replica_id]
        labels = jnp.arange(replicas, dtype=jnp.int32)
        return jnp.sum(
            labels[None, :] * (table[None, :] == labels[:, None]).astype(jnp.int32), axis=1
        )

    rows = jnp.concatenate([shard_rows(first, d) for d in range(shards)], axis=0)
    for step in range(sections):
        if step > 0:
            rows = jnp.where(section_id == step, gather_rows(incoming, [step]), rows)
        own = rows[:own_rows]
        inverse_rms = norm_scale(rows)
        normed = (rows.astype(jnp.float32) * inverse_rms).astype(jnp.bfloat16)
        preact = dot(normed, weight_in) * scale_in
        hidden = jax.nn.silu(preact).astype(jnp.bfloat16)
        total = scatter_rows(dot(hidden, weight_out) * scale_out, [step])
        output = (own.astype(jnp.float32) + total).astype(jnp.bfloat16)
        if step + 1 < sections:
            blocks = output.reshape(replicas, piece_rows, width)
            order = slots(step)
            received = []
            for e in range(replicas):
                block = order[(replica_id + e) % replicas]
                place = (replica_id - block) % replicas
                chosen = lax.dynamic_index_in_dim(blocks, place, 0, keepdims=False)
                received.append(across_replicas(chosen, e, [step], 1))
            incoming = jnp.concatenate(received, axis=0)

    far_normed = exchange(normed, pieces_in, size_in, 1)
    far_hidden = exchange(hidden, pieces_out, size_out, 1)

    gate = jax.nn.sigmoid(preact)
    slope = gate * (1.0 + preact * (1.0 - gate))
    own_scale = inverse_rms[:own_rows]
    exact = own.astype(jnp.float32) * own_scale
    incoming = (output.astype(jnp.float32) - goal.astype(jnp.float32)).astype(jnp.bfloat16)
    upstream = jnp.zeros((row_count, width), jnp.bfloat16)
    far_up = [jnp.zeros((row_count, width), jnp.bfloat16) for _ in others]
    far_pre = [jnp.zeros((row_count, local_hidden), jnp.bfloat16) for _ in others]
    for step in reversed(range(sections)):
        here = section_id == step
        upstream = jnp.where(here, gather_rows(incoming, [step]), upstream)
        far_up = [
            jnp.where(here, across_replicas(upstream, e, [step]), far_up[e - 1]) for e in others
        ]
        grad_hidden = dot(upstream, weight_out, contract_last) * scale_out
        grad_pre = (grad_hidden * slope).astype(jnp.bfloat16)
        far_pre = [
            jnp.where(here, across_replicas(grad_pre, e, [step]), far_pre[e - 1]) for e in others
        ]
        if step > 0:
            total = scatter_rows(dot(grad_pre, weight_in, contract_last) * scale_in, [step])
            along = jnp.mean(total * exact, axis=1, keepdims=True)
            result = (
                upstream[:own_rows].astype(jnp.float32) + own_scale * (total - exact * along)
            ).astype(jnp.bfloat16)
            blocks = result.reshape(replicas, piece_rows, width)
            received = jnp.stack(
                [across_replicas(blocks[e], -e, [step], -1) for e in range(replicas)]
            )
            table = routes[0, step - 1, replica_id]
            placed = []
            for e in range(replicas):
                sender = table[(replica_id - e) % replicas]
                placed.append(
                    lax.dynamic_index_in_dim(
                        received, (sender - replica_id) % replicas, 0, keepdims=False
                    )
                )
            incoming = jnp.concatenate(placed, axis=0)

    def as_delta(left, right, scale):
        return (inner_rate * (dot(left, right, contract_rows) * scale)).astype(jnp.bfloat16)

    def finish(weight, moment, left, right, far_weights, far_moments, far_left, far_right, scale,
               pieces, size):
        new_weight, new_moment = outer_mix(
            weight.astype(jnp.float32),
            moment.astype(jnp.float32),
            as_delta(left, right, scale).astype(jnp.float32),
        )
        for e in others:
            back = replicas - e

            def mean(own_array, far_array):
                return 0.5 * (own_array.astype(jnp.float32) + far_array.astype(jnp.float32))

            index = pieces[back]
            own_left = piece(left, index, size, 1)
            part_weight, part_moment = outer_mix(
                mean(piece(weight, index, size), far_weights[e - 1]),
                mean(piece(moment, index, size), far_moments[e - 1]),
                mean(
                    as_delta(own_left, right, scale),
                    as_delta(far_left[e - 1], far_right[e - 1], scale),
                ),
            )
            new_weight = lax.dynamic_update_slice_in_dim(new_weight, part_weight, index * size, 0)
            new_moment = lax.dynamic_update_slice_in_dim(new_moment, part_moment, index * size, 0)
        return new_weight[None, None], new_moment[None, None]

    new_weight_b, new_moment_b = finish(
        weight_out, moment_b[0, 0], hidden, upstream, far_weight_out, far_moment_out,
        far_hidden, far_up, scale_out, pieces_out, size_out,
    )
    new_weight_a, new_moment_a = finish(
        weight_in, moment_a[0, 0], normed, grad_pre, far_weight_in, far_moment_in,
        far_normed, far_pre, scale_in, pieces_in, size_in,
    )
    return (new_weight_a, new_weight_b, new_moment_a, new_moment_b)


def solution(mesh):
    placed = (
        P("replica", None, None, "shard"),
        P("replica", None, None, "shard"),
        P("replica", "section", None, "shard"),
        P("replica", "section", "shard", None),
        P("replica", "section", None, "shard"),
        P("replica", "section", "shard", None),
        P(),
        P(),
    )
    return jax.shard_map(
        per_device,
        mesh=mesh,
        in_specs=placed,
        out_specs=(
            P("replica", "section", None, "shard"),
            P("replica", "section", "shard", None),
            P("replica", "section", None, "shard"),
            P("replica", "section", "shard", None),
        ),
        check_vma=False,
    )
```

```python
import math

import jax
import jax.numpy as jnp
from jax import lax
from jax.sharding import PartitionSpec as P

epsilon = 1e-05
inner_rate = 0.5
momentum_decay = 0.9
outer_rate = 0.7

axes = ("replica", "section", "shard")
contract_rows = (((0,), (0,)), ((), ()))
contract_last = (((1,), (1,)), ((), ()))


def norm_scale(rows):
    wide = rows.astype(jnp.float32)
    return lax.rsqrt(jnp.mean(wide * wide, axis=1, keepdims=True) + epsilon)


def dot(left, right, dims=(((1,), (0,)), ((), ()))):
    return lax.dot_general(left, right, dims, preferred_element_type=jnp.float32)


def outer_mix(weight, moment, delta):
    new_moment = momentum_decay * moment + delta
    new_weight = weight - outer_rate * (momentum_decay * new_moment + delta)
    return new_weight.astype(jnp.bfloat16), new_moment.astype(jnp.bfloat16)


def per_device(inputs, targets, weight_a, weight_b, moment_a, moment_b, routes, partners):
    replicas = lax.axis_size("replica")
    sections = lax.axis_size("section")
    shards = lax.axis_size("shard")
    replica_id = lax.axis_index("replica")
    section_id = lax.axis_index("section")
    shard_id = lax.axis_index("shard")
    row_count = inputs.shape[2]
    features = inputs.shape[3]
    width = weight_a.shape[2]
    local_hidden = weight_a.shape[3]
    assert inputs.shape[1] == 1 and shards & (shards - 1) == 0
    scale_in = 1.0 / math.sqrt(width)
    scale_out = 1.0 / math.sqrt(local_hidden * shards)
    weight_in = weight_a[0, 0]
    weight_out = weight_b[0, 0]
    block_rows = row_count // replicas
    half = shards // 2

    def flat(replica, section, shard):
        return (replica * sections + section) * shards + shard

    def holder(section):
        return half - 1 + ((section ^ (section >> 1)) & 1)

    def move(array, sources, target):
        pairs = [
            (flat(r, s, j), flat(*target(r, s, j)))
            for r in range(replicas)
            for s, j in sources
        ]
        return lax.ppermute(array, axes, pairs)

    def to_holder(array, offset, active):
        return move(array, [(s, holder(s) ^ offset) for s in active], lambda r, s, j: (r, s, j ^ offset))

    def from_holder(array, offset, active):
        return move(array, [(s, holder(s)) for s in active], lambda r, s, j: (r, s, j ^ offset))

    def between_holders(array, offset, section, step):
        return move(
            array,
            [(section, holder(section))],
            lambda r, s, j: ((r + offset) % replicas, s + step, holder(s + step)),
        )

    def across_replicas(array, offset, active):
        return move(
            array,
            [(s, j) for s in active for j in range(shards)],
            lambda r, s, j: ((r + offset) % replicas, s, j),
        )

    def gather_features(array, section):
        parts = [array] + [to_holder(array, d, [section]) for d in range(1, shards)]
        return jnp.concatenate([parts[c ^ holder(section)] for c in range(shards)], axis=1)

    def by_offset(array):
        places = (replica_id - jnp.arange(replicas, dtype=jnp.int32)) % replicas
        blocks = array.reshape(replicas, block_rows, array.shape[1])
        return jnp.take(blocks, places, axis=0).reshape(array.shape)

    every = range(sections)
    others = range(1, replicas)
    is_holder = shard_id == half - 1 + ((section_id ^ (section_id >> 1)) & 1)

    def broadcast(array, active):
        total = from_holder(array, 1, active)
        for d in range(2, shards):
            total = total + from_holder(array, d, active)
        return jnp.where(is_holder, array, total)

    tables = lax.dynamic_index_in_dim(partners, section_id, 0, keepdims=False)

    def piece_of(table, offset):
        wanted = (replica_id + offset) % replicas
        return jnp.argmax(table[:, replica_id] == wanted).astype(jnp.int32)

    pieces_in = [piece_of(tables[0], e) for e in range(replicas)]
    pieces_out = [piece_of(tables[1], e) for e in range(replicas)]
    size_in = width // replicas
    size_out = local_hidden // replicas

    def piece(array, index, size, axis=0):
        return lax.dynamic_slice_in_dim(array, index * size, size, axis)

    def exchange_state(weight, moment, pieces, size):
        return [
            across_replicas(
                jnp.concatenate([piece(weight, pieces[e], size), piece(moment, pieces[e], size)]),
                e,
                every,
            )
            for e in others
        ]

    def exchange_factor(array, pieces, size):
        return [across_replicas(piece(array, pieces[e], size, 1), e, every) for e in others]

    parts_in = [weight_in] + [to_holder(weight_in, d, every) for d in range(1, shards)]
    parts_out = [weight_out] + [to_holder(weight_out, d, every) for d in range(1, shards)]
    far_state_in = exchange_state(weight_in, moment_a[0, 0], pieces_in, size_in)
    far_state_out = exchange_state(weight_out, moment_b[0, 0], pieces_out, size_out)
    rows = by_offset(gather_features(inputs[0, 0], 0))
    goal = by_offset(gather_features(targets[0, 0], sections - 1))
    rows, goal, far_state_in, far_state_out = lax.optimization_barrier(
        (rows, goal, far_state_in, far_state_out)
    )

    def slots(link):
        table = routes[0, link, replica_id]
        labels = jnp.arange(replicas, dtype=jnp.int32)
        return jnp.sum(
            labels[None, :] * (table[None, :] == labels[:, None]).astype(jnp.int32), axis=1
        )

    def normalise(rows):
        inverse_rms = norm_scale(rows)
        return inverse_rms, (rows.astype(jnp.float32) * inverse_rms).astype(jnp.bfloat16)

    def slope_of(preact):
        gate = jax.nn.sigmoid(preact)
        return gate * (1.0 + preact * (1.0 - gate))

    for step in range(sections):
        if step > 0:
            rows = jnp.where(section_id == step, incoming, rows)
        inverse_rms, normed = normalise(rows)
        preacts = [dot(normed, part) * scale_in for part in parts_in]
        output = rows.astype(jnp.float32)
        for preact, part in zip(preacts, parts_out):
            hidden = jax.nn.silu(preact).astype(jnp.bfloat16)
            term = (dot(hidden, part) * scale_out).astype(jnp.bfloat16)
            output = output + term.astype(jnp.float32)
        output = output.astype(jnp.bfloat16)
        if step + 1 < sections:
            blocks = output.reshape(replicas, block_rows, width)
            order = slots(step)
            received = []
            for e in range(replicas):
                block = order[(replica_id + e) % replicas]
                place = (replica_id - block) % replicas
                chosen = lax.dynamic_index_in_dim(blocks, place, 0, keepdims=False)
                received.append(between_holders(chosen, e, step, 1))
            incoming = jnp.concatenate(received, axis=0)

    slopes = [slope_of(preact) for preact in preacts]
    exact = rows.astype(jnp.float32) * inverse_rms
    own_rows = broadcast(rows, every)
    normed = normalise(own_rows)[1]
    preact = dot(normed, weight_in) * scale_in
    hidden = jax.nn.silu(preact).astype(jnp.bfloat16)
    slope = slope_of(preact)
    far_normed = exchange_factor(normed, pieces_in, size_in)
    far_hidden = exchange_factor(hidden, pieces_out, size_out)

    incoming = (output.astype(jnp.float32) - goal.astype(jnp.float32)).astype(jnp.bfloat16)
    upstream = jnp.zeros((row_count, width), jnp.bfloat16)
    for step in reversed(range(sections)):
        upstream = jnp.where(section_id == step, incoming, upstream)
        if step > 0:
            total = jnp.zeros((row_count, width), jnp.float32)
            for local_slope, part_in, part_out in zip(slopes, parts_in, parts_out):
                grad_hidden = dot(upstream, part_out, contract_last) * scale_out
                grad_pre = (grad_hidden * local_slope).astype(jnp.bfloat16)
                term = (dot(grad_pre, part_in, contract_last) * scale_in).astype(jnp.bfloat16)
                total = total + term.astype(jnp.float32)
            along = jnp.mean(total * exact, axis=1, keepdims=True)
            result = (
                upstream.astype(jnp.float32) + inverse_rms * (total - exact * along)
            ).astype(jnp.bfloat16)
            blocks = result.reshape(replicas, block_rows, width)
            received = jnp.stack(
                [between_holders(blocks[e], -e, step, -1) for e in range(replicas)]
            )
            table = routes[0, step - 1, replica_id]
            placed = []
            for e in range(replicas):
                sender = table[(replica_id - e) % replicas]
                placed.append(
                    lax.dynamic_index_in_dim(
                        received, (sender - replica_id) % replicas, 0, keepdims=False
                    )
                )
            incoming = jnp.concatenate(placed, axis=0)
            if step == 2:
                incoming, normed, hidden, slope, far_normed, far_hidden = lax.optimization_barrier(
                    (incoming, normed, hidden, slope, far_normed, far_hidden)
                )

    upstream = broadcast(upstream, every)
    far_up = [across_replicas(upstream, e, every) for e in others]
    grad_hidden = dot(upstream, weight_out, contract_last) * scale_out
    grad_pre = (grad_hidden * slope).astype(jnp.bfloat16)
    far_pre = [across_replicas(grad_pre, e, every) for e in others]

    def as_delta(left, right, scale):
        return (inner_rate * (dot(left, right, contract_rows) * scale)).astype(jnp.bfloat16)

    def finish(weight, moment, left, right, far_state, far_left, far_right, scale, pieces, size):
        new_weight, new_moment = outer_mix(
            weight.astype(jnp.float32),
            moment.astype(jnp.float32),
            as_delta(left, right, scale).astype(jnp.float32),
        )
        for e in others:
            back = replicas - e

            def mean(own_array, far_array):
                return 0.5 * (own_array.astype(jnp.float32) + far_array.astype(jnp.float32))

            index = pieces[back]
            own_left = piece(left, index, size, 1)
            part_weight, part_moment = outer_mix(
                mean(piece(weight, index, size), far_state[e - 1][:size]),
                mean(piece(moment, index, size), far_state[e - 1][size:]),
                mean(
                    as_delta(own_left, right, scale),
                    as_delta(far_left[e - 1], far_right[e - 1], scale),
                ),
            )
            new_weight = lax.dynamic_update_slice_in_dim(new_weight, part_weight, index * size, 0)
            new_moment = lax.dynamic_update_slice_in_dim(new_moment, part_moment, index * size, 0)
        return new_weight[None, None], new_moment[None, None]

    new_weight_b, new_moment_b = finish(
        weight_out, moment_b[0, 0], hidden, upstream, far_state_out, far_hidden, far_up,
        scale_out, pieces_out, size_out,
    )
    new_weight_a, new_moment_a = finish(
        weight_in, moment_a[0, 0], normed, grad_pre, far_state_in, far_normed, far_pre,
        scale_in, pieces_in, size_in,
    )
    return (new_weight_a, new_weight_b, new_moment_a, new_moment_b)


def solution(mesh):
    placed = (
        P("replica", None, None, "shard"),
        P("replica", None, None, "shard"),
        P("replica", "section", None, "shard"),
        P("replica", "section", "shard", None),
        P("replica", "section", None, "shard"),
        P("replica", "section", "shard", None),
        P(),
        P(),
    )
    return jax.shard_map(
        per_device,
        mesh=mesh,
        in_specs=placed,
        out_specs=(
            P("replica", "section", None, "shard"),
            P("replica", "section", "shard", None),
            P("replica", "section", None, "shard"),
            P("replica", "section", "shard", None),
        ),
        check_vma=False,
    )
```

```python
import functools
import math

import jax
import jax.numpy as jnp
from jax import lax
from jax.experimental import pallas as pl
from jax.experimental.pallas import tpu as pltpu
from jax.sharding import PartitionSpec as P

epsilon = 1e-05
inner_rate = 0.5
momentum_decay = 0.9
outer_rate = 0.7

axes = ("replica", "section", "shard")
contract_rows = (((0,), (0,)), ((), ()))
contract_last = (((1,), (1,)), ((), ()))


def norm_scale(rows):
    wide = rows.astype(jnp.float32)
    return lax.rsqrt(jnp.mean(wide * wide, axis=1, keepdims=True) + epsilon)


def dot(left, right, dims=(((1,), (0,)), ((), ()))):
    return lax.dot_general(left, right, dims, preferred_element_type=jnp.float32)


def outer_mix(weight, moment, delta):
    new_moment = momentum_decay * moment + delta
    new_weight = weight - outer_rate * (momentum_decay * new_moment + delta)
    return new_weight.astype(jnp.bfloat16), new_moment.astype(jnp.bfloat16)


def slope_of(preact):
    gate = jax.nn.sigmoid(preact)
    return gate * (1.0 + preact * (1.0 - gate))


def from_panels(array, rows):
    count = array.shape[0] // rows
    return jnp.concatenate([array[i * rows : (i + 1) * rows] for i in range(count)], axis=1)


def pack_kernel(heights, panel, starts, *refs):
    sources, packed, sems = refs[:-2], refs[-2], refs[-1]
    copies = []
    place = 0
    for i, (source, height) in enumerate(zip(sources, heights)):
        rows = pl.ds(pl.multiple_of(starts[0, i], height), height)
        for column in range(0, source.shape[1], panel):
            copies.append(
                pltpu.make_async_copy(
                    source.at[rows, pl.ds(column, panel)],
                    packed.at[pl.ds(place, height)],
                    sems.at[len(copies)],
                )
            )
            place += height
    for copy in copies:
        copy.start()
    for copy in copies:
        copy.wait()


def pack(arrays, heights, starts, panel):
    counts = [array.shape[1] // panel for array in arrays]
    total = sum(count * height for count, height in zip(counts, heights))
    anywhere = pl.BlockSpec(memory_space=pl.ANY)
    return pl.pallas_call(
        functools.partial(pack_kernel, heights, panel),
        out_shape=jax.ShapeDtypeStruct((total, panel), arrays[0].dtype),
        in_specs=[pl.BlockSpec(memory_space=pltpu.SMEM)] + [anywhere] * len(arrays),
        out_specs=anywhere,
        scratch_shapes=[pltpu.SemaphoreType.DMA((sum(counts),))],
        cost_estimate=pl.CostEstimate(
            flops=0, bytes_accessed=4 * total * panel, transcendentals=0
        ),
    )(starts, *arrays)


class Sizes:
    def __init__(self, shards, sections, row_count, width, local_hidden, panel, blocks):
        self.shards, self.sections, self.row_count = shards, sections, row_count
        self.width, self.local_hidden, self.panel = width, local_hidden, panel
        self.blocks = blocks
        self.block_rows = row_count // blocks
        self.panels_in = local_hidden // panel
        self.panels_out = width // panel
        self.half = width * self.panels_in
        self.scale_in = 1.0 / math.sqrt(width)
        self.scale_out = 1.0 / math.sqrt(local_hidden * shards)


def chain_kernel(sz, step, forward, backward, holder, *refs):
    refs = list(refs)
    table = refs.pop(0)
    first = forward and step == 0
    received = [] if first else [refs.pop(0) for _ in range(sz.blocks)]
    payloads = [refs.pop(0) for _ in range(sz.shards)]
    del refs[: 2 + (not backward or not forward)]
    if forward and not backward:
        state_in = None
    sends = [refs.pop(0) for _ in range(sz.blocks)]
    rows_hbm = refs.pop(0)
    second_hbm = refs.pop(0)
    slope_hbm = refs.pop(0) if not (forward and backward) else None
    weights, rows, up, out, slope, weight_sems, edge_sems, block_sems, state_sems = refs
    panel, width, hidden_size = sz.panel, sz.width, sz.local_hidden

    def weight_copy(d, which):
        return pltpu.make_async_copy(
            payloads[d].at[pl.ds(which * sz.half, sz.half)],
            weights.at[d, which],
            weight_sems.at[d, which],
        )

    def edge_copy(target, d):
        column = (holder ^ d) * panel
        return pltpu.make_async_copy(
            payloads[d].at[pl.ds(2 * sz.half, sz.row_count)],
            target.at[:, pl.ds(column, panel)],
            edge_sems.at[d],
        )

    def place(line, e):
        return pl.ds(pl.multiple_of(table[line, e], sz.block_rows), sz.block_rows)

    links = sz.sections - 1

    @pl.when(table[links + 1, step] == 1)
    def _():
        arrive = links if forward else step
        leave = links if backward else step
        block_copies = [
            pltpu.make_async_copy(
                received[e], (rows if forward else up).at[place(arrive, e)], block_sems.at[e]
            )
            for e in range(len(received))
        ]
        edge_copies = []
        if first:
            edge_copies = [edge_copy(rows, d) for d in range(sz.shards)]
        elif forward and backward:
            edge_copies = [edge_copy(out, d) for d in range(sz.shards)]
        state_copies = []
        if backward and not forward:
            state_copies = [
                pltpu.make_async_copy(rows_hbm, rows, state_sems.at[0]),
                pltpu.make_async_copy(slope_hbm, slope, state_sems.at[1]),
            ]
        for copy in block_copies + edge_copies + state_copies:
            copy.start()
        order = (0, 1) if forward else (1, 0)
        for d in range(sz.shards):
            for which in order:
                weight_copy(d, which).start()
        for copy in block_copies + edge_copies + state_copies:
            copy.wait()

        wide = rows[...].astype(jnp.float32)
        inverse_rms = lax.rsqrt(jnp.mean(wide * wide, axis=1, keepdims=True) + epsilon)
        store_copies = []
        if forward:
            store_copies.append(pltpu.make_async_copy(rows, rows_hbm, state_sems.at[0]))
            store_copies[-1].start()
            normed = (wide * inverse_rms).astype(jnp.bfloat16)
            total = [jnp.zeros((sz.row_count, panel), jnp.float32) for _ in range(sz.panels_out)]
            for d in range(sz.shards):
                weight_copy(d, 0).wait()
                hidden = []
                for p in range(sz.panels_in):
                    weight = weights[d, 0, p * width : (p + 1) * width, :]
                    preact = dot(normed, weight) * sz.scale_in
                    gate = jax.nn.sigmoid(preact)
                    hidden.append((preact * gate).astype(jnp.bfloat16))
                    column = d * hidden_size + p * panel
                    slope[:, column : column + panel] = gate * (1.0 + preact * (1.0 - gate))
                hidden = jnp.concatenate(hidden, axis=1)
                weight_copy(d, 1).wait()
                for n in range(sz.panels_out):
                    weight = weights[d, 1, n * hidden_size : (n + 1) * hidden_size, :]
                    term = (dot(hidden, weight) * sz.scale_out).astype(jnp.bfloat16)
                    total[n] = total[n] + term.astype(jnp.float32)
            output = (wide + jnp.concatenate(total, axis=1)).astype(jnp.bfloat16)
            if not backward:
                out[...] = output
                store_copies.append(pltpu.make_async_copy(slope, slope_hbm, state_sems.at[1]))
            else:
                goal = out[...].astype(jnp.float32)
                up[...] = (output.astype(jnp.float32) - goal).astype(jnp.bfloat16)
        if backward:
            second = state_sems.at[2]
            store_copies.append(pltpu.make_async_copy(up, second_hbm, second))
            store_copies[-1].start()
            total = jnp.zeros((sz.row_count, width), jnp.float32)
            for d in range(sz.shards):
                if not forward:
                    weight_copy(d, 1).wait()
                grad_hidden = jnp.zeros((sz.row_count, hidden_size), jnp.float32)
                for n in range(sz.panels_out):
                    weight = weights[d, 1, n * hidden_size : (n + 1) * hidden_size, :]
                    piece = up[:, n * panel : (n + 1) * panel]
                    grad_hidden = grad_hidden + dot(piece, weight, contract_last)
                local_slope = slope[:, d * hidden_size : (d + 1) * hidden_size]
                grad_pre = (grad_hidden * sz.scale_out * local_slope).astype(jnp.bfloat16)
                if not forward:
                    weight_copy(d, 0).wait()
                term = jnp.zeros((sz.row_count, width), jnp.float32)
                for p in range(sz.panels_in):
                    weight = weights[d, 0, p * width : (p + 1) * width, :]
                    piece = grad_pre[:, p * panel : (p + 1) * panel]
                    term = term + dot(piece, weight, contract_last)
                total = total + (term * sz.scale_in).astype(jnp.bfloat16).astype(jnp.float32)
            exact = rows[...].astype(jnp.float32) * inverse_rms
            along = jnp.mean(total * exact, axis=1, keepdims=True)
            up_wide = up[...].astype(jnp.float32)
            out[...] = (up_wide + inverse_rms * (total - exact * along)).astype(jnp.bfloat16)
        send_copies = [
            pltpu.make_async_copy(out.at[place(leave, e)], sends[e], block_sems.at[e])
            for e in range(sz.blocks)
        ]
        for copy in send_copies:
            copy.start()
        if forward and not backward:
            store_copies[-1].start()
        for copy in send_copies + store_copies:
            copy.wait()


def chain_step(sz, step, forward, backward, holder, table, received, payloads, states):
    both = forward and backward
    kept = states[:2] if both else states
    anywhere = pl.BlockSpec(memory_space=pl.ANY)
    operands = [table, *received, *payloads, *kept]
    block = jax.ShapeDtypeStruct((sz.block_rows, sz.width), jnp.bfloat16)
    shapes = [block] * sz.blocks + [jax.ShapeDtypeStruct(s.shape, s.dtype) for s in kept]
    base = len(operands) - len(kept)
    passes = (2 if forward else 0) + (2 if backward else 0)
    results = pl.pallas_call(
        functools.partial(chain_kernel, sz, step, forward, backward, holder),
        out_shape=shapes,
        in_specs=[pl.BlockSpec(memory_space=pltpu.SMEM)] + [anywhere] * (len(operands) - 1),
        out_specs=[anywhere] * len(shapes),
        input_output_aliases={base + i: sz.blocks + i for i in range(len(kept))},
        scratch_shapes=[
            pltpu.VMEM((sz.shards, 2, sz.half, sz.panel), jnp.bfloat16),
            pltpu.VMEM((sz.row_count, sz.width), jnp.bfloat16),
            pltpu.VMEM((sz.row_count, sz.width), jnp.bfloat16),
            pltpu.VMEM((sz.row_count, sz.width), jnp.bfloat16),
            pltpu.VMEM((sz.row_count, sz.shards * sz.local_hidden), jnp.float32),
            pltpu.SemaphoreType.DMA((sz.shards, 2)),
            pltpu.SemaphoreType.DMA((sz.shards,)),
            pltpu.SemaphoreType.DMA((sz.blocks,)),
            pltpu.SemaphoreType.DMA((3,)),
        ],
        compiler_params=pltpu.CompilerParams(vmem_limit_bytes=40 * 1024 * 1024),
        cost_estimate=pl.CostEstimate(
            flops=passes * 2 * sz.row_count * sz.width * sz.local_hidden * sz.shards,
            bytes_accessed=4 * sz.half * sz.panel * sz.shards,
            transcendentals=0,
        ),
    )(*operands)
    sends, kept = list(results[: sz.blocks]), list(results[sz.blocks :])
    return sends, kept + list(states[2:]) if both else kept


def per_device(inputs, targets, weight_a, weight_b, moment_a, moment_b, routes, partners):
    replicas = lax.axis_size("replica")
    sections = lax.axis_size("section")
    shards = lax.axis_size("shard")
    replica_id = lax.axis_index("replica")
    section_id = lax.axis_index("section")
    shard_id = lax.axis_index("shard")
    row_count = inputs.shape[2]
    panel = inputs.shape[3]
    width = weight_a.shape[2]
    local_hidden = weight_a.shape[3]
    assert inputs.shape[1] == 1 and shards & (shards - 1) == 0
    assert local_hidden % panel == 0 and sections > 1
    scale_in = 1.0 / math.sqrt(width)
    scale_out = 1.0 / math.sqrt(local_hidden * shards)
    weight_in = weight_a[0, 0]
    weight_out = weight_b[0, 0]
    block_rows = row_count // replicas
    links = sections - 1
    in_kernel = block_rows % 16 == 0
    sz = Sizes(
        shards, sections, row_count, width, local_hidden, panel, replicas if in_kernel else 1
    )

    def flat(replica, section, shard):
        return (replica * sections + section) * shards + shard

    def holder(section):
        return shards // 2 - 1 + ((section ^ (section >> 1)) & 1)

    def move(array, sources, target):
        pairs = [
            (flat(r, s, j), flat(*target(r, s, j)))
            for r in range(replicas)
            for s, j in sources
        ]
        return lax.ppermute(array, axes, pairs)

    def to_holder(array, offset, active):
        return move(
            array, [(s, holder(s) ^ offset) for s in active], lambda r, s, j: (r, s, j ^ offset)
        )

    def from_holder(array, offset, active):
        return move(array, [(s, holder(s)) for s in active], lambda r, s, j: (r, s, j ^ offset))

    def between_holders(array, offset, section, step):
        return move(
            array,
            [(section, holder(section))],
            lambda r, s, j: ((r + offset) % replicas, s + step, holder(s + step)),
        )

    def across_replicas(array, offset, active):
        return move(
            array,
            [(s, j) for s in active for j in range(shards)],
            lambda r, s, j: ((r + offset) % replicas, s, j),
        )

    every = range(sections)
    others = range(1, replicas)
    is_holder = shard_id == shards // 2 - 1 + ((section_id ^ (section_id >> 1)) & 1)

    def broadcast(array, active):
        total = from_holder(array, 1, active)
        for d in range(2, shards):
            total = total + from_holder(array, d, active)
        return jnp.where(is_holder, array, total)

    edge = jnp.where(section_id == 0, inputs[0, 0], targets[0, 0])
    payload = pack(
        [weight_in, weight_out, edge],
        [width, local_hidden, row_count],
        jnp.zeros((1, 3), jnp.int32),
        panel,
    )
    payloads = [payload] + [to_holder(payload, d, every) for d in range(1, shards)]

    tables = lax.dynamic_index_in_dim(partners, section_id, 0, keepdims=False)

    def piece_of(table, offset):
        wanted = (replica_id + offset) % replicas
        return jnp.argmax(table[:, replica_id] == wanted).astype(jnp.int32)

    pieces_in = [piece_of(tables[0], e) for e in range(replicas)]
    pieces_out = [piece_of(tables[1], e) for e in range(replicas)]
    size_in = width // replicas
    size_out = local_hidden // replicas

    def piece(array, index, size, axis=0):
        return lax.dynamic_slice_in_dim(array, index * size, size, axis)

    def state_pieces(e):
        four = [weight_in, moment_a[0, 0], weight_out, moment_b[0, 0]]
        heights = [size_in, size_in, size_out, size_out]
        first_in, first_out = pieces_in[e] * size_in, pieces_out[e] * size_out
        starts = jnp.stack([first_in, first_in, first_out, first_out])[None]
        return pack(four, heights, starts, panel)

    far_states = [across_replicas(state_pieces(e), e, every) for e in others]

    def exchange_factor(array, pieces, size):
        return [across_replicas(piece(array, pieces[e], size, 1), e, every) for e in others]

    offsets = jnp.arange(replicas, dtype=jnp.int32)
    there = (replica_id + offsets) % replicas
    back = (replica_id - offsets) % replicas
    own_routes = routes[0, :, replica_id, :]
    slots = jnp.sum(
        (own_routes[:, None, :] == there[None, :, None]).astype(jnp.int32)
        * offsets[None, None, :],
        axis=2,
    )
    columns = max(replicas, sections)
    ours = (is_holder & (section_id == jnp.arange(sections))).astype(jnp.int32)

    def line(values):
        return jnp.pad(values, ((0, 0), (0, columns - values.shape[1])))

    starts = jnp.concatenate([slots, back[None]]) * block_rows
    if not in_kernel:
        starts = jnp.zeros_like(starts)
    table = jnp.concatenate([line(starts), line(ours[None])]).astype(jnp.int32)

    def send_blocks(sends, arrived, left, section, step, sign):
        if in_kernel:
            return [
                between_holders(sends[e], sign * e, section, step) for e in range(replicas)
            ]
        blocks = sends[0].reshape(replicas, block_rows, width)
        moved = jnp.zeros_like(blocks)
        for e in range(replicas):
            chosen = lax.dynamic_index_in_dim(blocks, left[e], 0, keepdims=False)
            got = between_holders(chosen, sign * e, section, step)
            moved = lax.dynamic_update_index_in_dim(moved, got, arrived[e], 0)
        return [moved.reshape(row_count, width)]

    states = [
        jnp.zeros((row_count, width), jnp.bfloat16),
        jnp.zeros((row_count, width), jnp.bfloat16),
        jnp.zeros((row_count, shards * local_hidden), jnp.float32),
    ]
    received = []
    for step in range(sections):
        last = step + 1 == sections
        sends, states = chain_step(
            sz, step, True, last, holder(step), table, received, payloads, states
        )
        if not last:
            received = send_blocks(sends, back, slots[step], step, 1, 1)

    own_rows = broadcast(states[0], every)
    inverse_rms = norm_scale(own_rows)
    normed = (own_rows.astype(jnp.float32) * inverse_rms).astype(jnp.bfloat16)
    preact = dot(normed, weight_in) * scale_in
    hidden = jax.nn.silu(preact).astype(jnp.bfloat16)
    slope = slope_of(preact)
    far_normed = exchange_factor(normed, pieces_in, size_in)
    far_hidden = exchange_factor(hidden, pieces_out, size_out)

    for step in reversed(range(1, sections)):
        if step < links:
            sends, states = chain_step(
                sz, step, False, True, holder(step), table, received, payloads, states
            )
        received = send_blocks(sends, slots[step - 1], back, step, -1, -1)
        if step == min(2, links):
            received, normed, hidden, slope, far_normed, far_hidden, far_states = (
                lax.optimization_barrier(
                    (received, normed, hidden, slope, far_normed, far_hidden, far_states)
                )
            )
    upstream = states[1]
    first_up = received[0]
    if in_kernel:
        first_up = jnp.zeros((row_count, width), jnp.bfloat16)
        for e in range(replicas):
            first_up = lax.dynamic_update_slice_in_dim(
                first_up, received[e], slots[0, e] * block_rows, 0
            )
    upstream = jnp.where(section_id == 0, first_up, upstream)
    upstream = broadcast(upstream, every)
    far_up = [across_replicas(upstream, e, every) for e in others]
    grad_hidden = dot(upstream, weight_out, contract_last) * scale_out
    grad_pre = (grad_hidden * slope).astype(jnp.bfloat16)
    far_pre = [across_replicas(grad_pre, e, every) for e in others]

    def far_part(e, which):
        sizes = [size_in, size_in, size_out, size_out]
        lengths = [size_in * local_hidden // panel] * 2 + [size_out * width // panel] * 2
        begin = sum(lengths[:which])
        return from_panels(far_states[e - 1][begin : begin + lengths[which]], sizes[which])

    def as_delta(left, right, scale):
        return (inner_rate * (dot(left, right, contract_rows) * scale)).astype(jnp.bfloat16)

    def finish(weight, moment, left, right, which, far_left, far_right, scale, pieces, size):
        new_weight, new_moment = outer_mix(
            weight.astype(jnp.float32),
            moment.astype(jnp.float32),
            as_delta(left, right, scale).astype(jnp.float32),
        )
        for e in others:
            back = replicas - e

            def mean(own_array, far_array):
                return 0.5 * (own_array.astype(jnp.float32) + far_array.astype(jnp.float32))

            index = pieces[back]
            own_left = piece(left, index, size, 1)
            part_weight, part_moment = outer_mix(
                mean(piece(weight, index, size), far_part(e, which)),
                mean(piece(moment, index, size), far_part(e, which + 1)),
                mean(
                    as_delta(own_left, right, scale),
                    as_delta(far_left[e - 1], far_right[e - 1], scale),
                ),
            )
            new_weight = lax.dynamic_update_slice_in_dim(new_weight, part_weight, index * size, 0)
            new_moment = lax.dynamic_update_slice_in_dim(new_moment, part_moment, index * size, 0)
        return new_weight[None, None], new_moment[None, None]

    new_weight_b, new_moment_b = finish(
        weight_out, moment_b[0, 0], hidden, upstream, 2, far_hidden, far_up,
        scale_out, pieces_out, size_out,
    )
    new_weight_a, new_moment_a = finish(
        weight_in, moment_a[0, 0], normed, grad_pre, 0, far_normed, far_pre,
        scale_in, pieces_in, size_in,
    )
    return (new_weight_a, new_weight_b, new_moment_a, new_moment_b)


def solution(mesh):
    placed = (
        P("replica", None, None, "shard"),
        P("replica", None, None, "shard"),
        P("replica", "section", None, "shard"),
        P("replica", "section", "shard", None),
        P("replica", "section", None, "shard"),
        P("replica", "section", "shard", None),
        P(),
        P(),
    )
    return jax.shard_map(
        per_device,
        mesh=mesh,
        in_specs=placed,
        out_specs=(
            P("replica", "section", None, "shard"),
            P("replica", "section", "shard", None),
            P("replica", "section", None, "shard"),
            P("replica", "section", "shard", None),
        ),
        check_vma=False,
    )
```

```python
import functools
import math

import jax
import jax.numpy as jnp
from jax import lax
from jax.experimental import pallas as pl
from jax.experimental.pallas import tpu as pltpu
from jax.sharding import PartitionSpec as P

epsilon = 1e-05
inner_rate = 0.5
momentum_decay = 0.9
outer_rate = 0.7

axes = ("replica", "section", "shard")
contract_rows = (((0,), (0,)), ((), ()))
contract_last = (((1,), (1,)), ((), ()))


def norm_scale(rows):
    wide = rows.astype(jnp.float32)
    return lax.rsqrt(jnp.mean(wide * wide, axis=1, keepdims=True) + epsilon)


def dot(left, right, dims=(((1,), (0,)), ((), ()))):
    return lax.dot_general(left, right, dims, preferred_element_type=jnp.float32)


def outer_mix(weight, moment, delta):
    new_moment = momentum_decay * moment + delta
    new_weight = weight - outer_rate * (momentum_decay * new_moment + delta)
    return new_weight.astype(jnp.bfloat16), new_moment.astype(jnp.bfloat16)


def slope_of(preact):
    gate = jax.nn.sigmoid(preact)
    return gate * (1.0 + preact * (1.0 - gate))


def from_panels(array, rows):
    count = array.shape[0] // rows
    return jnp.concatenate([array[i * rows : (i + 1) * rows] for i in range(count)], axis=1)


def pack_kernel(heights, panel, starts, *refs):
    sources, (packed, buffer, read_sems, write_sems) = refs[:-4], refs[-4:]
    reads, writes = [], []
    place = 0
    for i, (source, height) in enumerate(zip(sources, heights)):
        rows = pl.ds(pl.multiple_of(starts[0, i], height), height)
        for column in range(0, source.shape[1], panel):
            k = len(reads)
            there = pl.ds(place, height)
            reads.append(
                pltpu.make_async_copy(
                    source.at[rows, pl.ds(column, panel)], buffer.at[there], read_sems.at[k]
                )
            )
            writes.append(
                pltpu.make_async_copy(buffer.at[there], packed.at[there], write_sems.at[k])
            )
            place += height
    for copy in reads:
        copy.start()
    for read, write in zip(reads, writes):
        read.wait()
        write.start()
    for copy in writes:
        copy.wait()


def pack(arrays, heights, starts, panel):
    counts = [array.shape[1] // panel for array in arrays]
    total = sum(count * height for count, height in zip(counts, heights))
    anywhere = pl.BlockSpec(memory_space=pl.ANY)
    return pl.pallas_call(
        functools.partial(pack_kernel, heights, panel),
        out_shape=jax.ShapeDtypeStruct((total, panel), arrays[0].dtype),
        in_specs=[pl.BlockSpec(memory_space=pltpu.SMEM)] + [anywhere] * len(arrays),
        out_specs=anywhere,
        scratch_shapes=[
            pltpu.VMEM((total, panel), arrays[0].dtype),
            pltpu.SemaphoreType.DMA((sum(counts),)),
            pltpu.SemaphoreType.DMA((sum(counts),)),
        ],
        compiler_params=pltpu.CompilerParams(vmem_limit_bytes=16 * 1024 * 1024),
        cost_estimate=pl.CostEstimate(
            flops=0, bytes_accessed=4 * total * panel, transcendentals=0
        ),
    )(starts, *arrays)


class Sizes:
    def __init__(self, shards, sections, row_count, width, local_hidden, panel, blocks):
        self.shards, self.sections, self.row_count = shards, sections, row_count
        self.width, self.local_hidden, self.panel = width, local_hidden, panel
        self.blocks = blocks
        self.block_rows = row_count // blocks
        self.panels_in = local_hidden // panel
        self.panels_out = width // panel
        self.half = width * self.panels_in
        self.scale_in = 1.0 / math.sqrt(width)
        self.scale_out = 1.0 / math.sqrt(local_hidden * shards)


def chain_kernel(sz, step, forward, backward, holder, *refs):
    refs = list(refs)
    table = refs.pop(0)
    first = forward and step == 0
    received = [] if first else [refs.pop(0) for _ in range(sz.blocks)]
    payloads = [refs.pop(0) for _ in range(sz.shards)]
    del refs[: 2 + (not backward or not forward)]
    if forward and not backward:
        state_in = None
    sends = [refs.pop(0) for _ in range(sz.blocks)]
    rows_hbm = refs.pop(0)
    second_hbm = refs.pop(0)
    slope_hbm = refs.pop(0) if not (forward and backward) else None
    weights, rows, up, out, slope, weight_sems, edge_sems, block_sems, state_sems = refs
    panel, width, hidden_size = sz.panel, sz.width, sz.local_hidden

    def weight_copy(d, which):
        return pltpu.make_async_copy(
            payloads[d].at[pl.ds(which * sz.half, sz.half)],
            weights.at[d, which],
            weight_sems.at[d, which],
        )

    def edge_copy(target, d):
        column = (holder ^ d) * panel
        return pltpu.make_async_copy(
            payloads[d].at[pl.ds(2 * sz.half, sz.row_count)],
            target.at[:, pl.ds(column, panel)],
            edge_sems.at[d],
        )

    def place(line, e):
        return pl.ds(pl.multiple_of(table[line, e], sz.block_rows), sz.block_rows)

    links = sz.sections - 1

    @pl.when(table[links + 1, step] == 1)
    def _():
        arrive = links if forward else step
        leave = links if backward else step
        block_copies = [
            pltpu.make_async_copy(
                received[e], (rows if forward else up).at[place(arrive, e)], block_sems.at[e]
            )
            for e in range(len(received))
        ]
        edge_copies = []
        if first:
            edge_copies = [edge_copy(rows, d) for d in range(sz.shards)]
        elif forward and backward:
            edge_copies = [edge_copy(out, d) for d in range(sz.shards)]
        state_copies = []
        if backward and not forward:
            state_copies = [
                pltpu.make_async_copy(rows_hbm, rows, state_sems.at[0]),
                pltpu.make_async_copy(slope_hbm, slope, state_sems.at[1]),
            ]
        for copy in block_copies + edge_copies + state_copies:
            copy.start()
        order = (0, 1) if forward else (1, 0)
        for d in range(sz.shards):
            for which in order:
                weight_copy(d, which).start()
        for copy in block_copies + edge_copies + state_copies:
            copy.wait()

        wide = rows[...].astype(jnp.float32)
        inverse_rms = lax.rsqrt(jnp.mean(wide * wide, axis=1, keepdims=True) + epsilon)
        store_copies = []
        if forward:
            store_copies.append(pltpu.make_async_copy(rows, rows_hbm, state_sems.at[0]))
            store_copies[-1].start()
            normed = (wide * inverse_rms).astype(jnp.bfloat16)
            total = [jnp.zeros((sz.row_count, panel), jnp.float32) for _ in range(sz.panels_out)]
            for d in range(sz.shards):
                weight_copy(d, 0).wait()
                hidden = []
                for p in range(sz.panels_in):
                    weight = weights[d, 0, p * width : (p + 1) * width, :]
                    preact = dot(normed, weight) * sz.scale_in
                    gate = jax.nn.sigmoid(preact)
                    hidden.append((preact * gate).astype(jnp.bfloat16))
                    column = d * hidden_size + p * panel
                    slope[:, column : column + panel] = gate * (1.0 + preact * (1.0 - gate))
                hidden = jnp.concatenate(hidden, axis=1)
                weight_copy(d, 1).wait()
                for n in range(sz.panels_out):
                    weight = weights[d, 1, n * hidden_size : (n + 1) * hidden_size, :]
                    term = (dot(hidden, weight) * sz.scale_out).astype(jnp.bfloat16)
                    total[n] = total[n] + term.astype(jnp.float32)
            output = (wide + jnp.concatenate(total, axis=1)).astype(jnp.bfloat16)
            if not backward:
                out[...] = output
                store_copies.append(pltpu.make_async_copy(slope, slope_hbm, state_sems.at[1]))
            else:
                goal = out[...].astype(jnp.float32)
                up[...] = (output.astype(jnp.float32) - goal).astype(jnp.bfloat16)
        if backward:
            second = state_sems.at[2]
            store_copies.append(pltpu.make_async_copy(up, second_hbm, second))
            store_copies[-1].start()
            up_turned = up[...].T
            total = jnp.zeros((width, sz.row_count), jnp.float32)
            for d in range(sz.shards):
                if not forward:
                    weight_copy(d, 1).wait()
                grad_hidden = jnp.zeros((hidden_size, sz.row_count), jnp.float32)
                for n in range(sz.panels_out):
                    weight = weights[d, 1, n * hidden_size : (n + 1) * hidden_size, :]
                    piece = up_turned[n * panel : (n + 1) * panel, :]
                    grad_hidden = grad_hidden + dot(weight, piece)
                local_slope = slope[:, d * hidden_size : (d + 1) * hidden_size].T
                grad_pre = (grad_hidden * sz.scale_out * local_slope).astype(jnp.bfloat16)
                if not forward:
                    weight_copy(d, 0).wait()
                term = jnp.zeros((width, sz.row_count), jnp.float32)
                for p in range(sz.panels_in):
                    weight = weights[d, 0, p * width : (p + 1) * width, :]
                    piece = grad_pre[p * panel : (p + 1) * panel, :]
                    term = term + dot(weight, piece)
                total = total + (term * sz.scale_in).astype(jnp.bfloat16).astype(jnp.float32)
            total = total.T
            exact = rows[...].astype(jnp.float32) * inverse_rms
            along = jnp.mean(total * exact, axis=1, keepdims=True)
            up_wide = up[...].astype(jnp.float32)
            out[...] = (up_wide + inverse_rms * (total - exact * along)).astype(jnp.bfloat16)
        send_copies = [
            pltpu.make_async_copy(out.at[place(leave, e)], sends[e], block_sems.at[e])
            for e in range(sz.blocks)
        ]
        for copy in send_copies:
            copy.start()
        if forward and not backward:
            store_copies[-1].start()
        for copy in send_copies + store_copies:
            copy.wait()


def chain_step(sz, step, forward, backward, holder, table, received, payloads, states):
    both = forward and backward
    kept = states[:2] if both else states
    anywhere = pl.BlockSpec(memory_space=pl.ANY)
    operands = [table, *received, *payloads, *kept]
    block = jax.ShapeDtypeStruct((sz.block_rows, sz.width), jnp.bfloat16)
    shapes = [block] * sz.blocks + [jax.ShapeDtypeStruct(s.shape, s.dtype) for s in kept]
    base = len(operands) - len(kept)
    passes = (2 if forward else 0) + (2 if backward else 0)
    results = pl.pallas_call(
        functools.partial(chain_kernel, sz, step, forward, backward, holder),
        out_shape=shapes,
        in_specs=[pl.BlockSpec(memory_space=pltpu.SMEM)] + [anywhere] * (len(operands) - 1),
        out_specs=[anywhere] * len(shapes),
        input_output_aliases={base + i: sz.blocks + i for i in range(len(kept))},
        scratch_shapes=[
            pltpu.VMEM((sz.shards, 2, sz.half, sz.panel), jnp.bfloat16),
            pltpu.VMEM((sz.row_count, sz.width), jnp.bfloat16),
            pltpu.VMEM((sz.row_count, sz.width), jnp.bfloat16),
            pltpu.VMEM((sz.row_count, sz.width), jnp.bfloat16),
            pltpu.VMEM((sz.row_count, sz.shards * sz.local_hidden), jnp.float32),
            pltpu.SemaphoreType.DMA((sz.shards, 2)),
            pltpu.SemaphoreType.DMA((sz.shards,)),
            pltpu.SemaphoreType.DMA((sz.blocks,)),
            pltpu.SemaphoreType.DMA((3,)),
        ],
        compiler_params=pltpu.CompilerParams(vmem_limit_bytes=40 * 1024 * 1024),
        cost_estimate=pl.CostEstimate(
            flops=passes * 2 * sz.row_count * sz.width * sz.local_hidden * sz.shards,
            bytes_accessed=4 * sz.half * sz.panel * sz.shards,
            transcendentals=0,
        ),
    )(*operands)
    sends, kept = list(results[: sz.blocks]), list(results[sz.blocks :])
    return sends, kept + list(states[2:]) if both else kept


def per_device(inputs, targets, weight_a, weight_b, moment_a, moment_b, routes, partners):
    replicas = lax.axis_size("replica")
    sections = lax.axis_size("section")
    shards = lax.axis_size("shard")
    replica_id = lax.axis_index("replica")
    section_id = lax.axis_index("section")
    shard_id = lax.axis_index("shard")
    row_count = inputs.shape[2]
    panel = inputs.shape[3]
    width = weight_a.shape[2]
    local_hidden = weight_a.shape[3]
    assert inputs.shape[1] == 1 and shards & (shards - 1) == 0
    assert local_hidden % panel == 0 and sections > 1
    scale_in = 1.0 / math.sqrt(width)
    scale_out = 1.0 / math.sqrt(local_hidden * shards)
    weight_in = weight_a[0, 0]
    weight_out = weight_b[0, 0]
    block_rows = row_count // replicas
    links = sections - 1
    in_kernel = block_rows % 16 == 0
    sz = Sizes(
        shards, sections, row_count, width, local_hidden, panel, replicas if in_kernel else 1
    )

    def flat(replica, section, shard):
        return (replica * sections + section) * shards + shard

    def holder(section):
        return shards // 2 - 1 + ((section ^ (section >> 1)) & 1)

    def move(array, sources, target):
        pairs = [
            (flat(r, s, j), flat(*target(r, s, j)))
            for r in range(replicas)
            for s, j in sources
        ]
        return lax.ppermute(array, axes, pairs)

    def to_holder(array, offset, active):
        return move(
            array, [(s, holder(s) ^ offset) for s in active], lambda r, s, j: (r, s, j ^ offset)
        )

    def from_holder(array, offset, active):
        return move(array, [(s, holder(s)) for s in active], lambda r, s, j: (r, s, j ^ offset))

    def between_holders(array, offset, section, step):
        return move(
            array,
            [(section, holder(section))],
            lambda r, s, j: ((r + offset) % replicas, s + step, holder(s + step)),
        )

    def across_replicas(array, offset, active):
        return move(
            array,
            [(s, j) for s in active for j in range(shards)],
            lambda r, s, j: ((r + offset) % replicas, s, j),
        )

    every = range(sections)
    others = range(1, replicas)
    is_holder = shard_id == shards // 2 - 1 + ((section_id ^ (section_id >> 1)) & 1)

    def broadcast(array, active):
        total = from_holder(array, 1, active)
        for d in range(2, shards):
            total = total + from_holder(array, d, active)
        return jnp.where(is_holder, array, total)

    edge = jnp.where(section_id == 0, inputs[0, 0], targets[0, 0])
    payload = pack(
        [weight_in, weight_out, edge],
        [width, local_hidden, row_count],
        jnp.zeros((1, 3), jnp.int32),
        panel,
    )
    payloads = [payload] + [to_holder(payload, d, every) for d in range(1, shards)]

    tables = lax.dynamic_index_in_dim(partners, section_id, 0, keepdims=False)

    def piece_of(table, offset):
        wanted = (replica_id + offset) % replicas
        return jnp.argmax(table[:, replica_id] == wanted).astype(jnp.int32)

    pieces_in = [piece_of(tables[0], e) for e in range(replicas)]
    pieces_out = [piece_of(tables[1], e) for e in range(replicas)]
    size_in = width // replicas
    size_out = local_hidden // replicas

    def piece(array, index, size, axis=0):
        return lax.dynamic_slice_in_dim(array, index * size, size, axis)

    def state_pieces(e):
        four = [weight_in, moment_a[0, 0], weight_out, moment_b[0, 0]]
        heights = [size_in, size_in, size_out, size_out]
        first_in, first_out = pieces_in[e] * size_in, pieces_out[e] * size_out
        starts = jnp.stack([first_in, first_in, first_out, first_out])[None]
        return pack(four, heights, starts, panel)

    far_states = [across_replicas(state_pieces(e), e, every) for e in others]

    def exchange_factor(array, pieces, size):
        return [across_replicas(piece(array, pieces[e], size, 1), e, every) for e in others]

    offsets = jnp.arange(replicas, dtype=jnp.int32)
    there = (replica_id + offsets) % replicas
    back = (replica_id - offsets) % replicas
    own_routes = routes[0, :, replica_id, :]
    slots = jnp.sum(
        (own_routes[:, None, :] == there[None, :, None]).astype(jnp.int32)
        * offsets[None, None, :],
        axis=2,
    )
    columns = max(replicas, sections)
    ours = (is_holder & (section_id == jnp.arange(sections))).astype(jnp.int32)

    def line(values):
        return jnp.pad(values, ((0, 0), (0, columns - values.shape[1])))

    starts = jnp.concatenate([slots, back[None]]) * block_rows
    if not in_kernel:
        starts = jnp.zeros_like(starts)
    table = jnp.concatenate([line(starts), line(ours[None])]).astype(jnp.int32)

    def send_blocks(sends, arrived, left, section, step, sign):
        if in_kernel:
            return [
                between_holders(sends[e], sign * e, section, step) for e in range(replicas)
            ]
        blocks = sends[0].reshape(replicas, block_rows, width)
        moved = jnp.zeros_like(blocks)
        for e in range(replicas):
            chosen = lax.dynamic_index_in_dim(blocks, left[e], 0, keepdims=False)
            got = between_holders(chosen, sign * e, section, step)
            moved = lax.dynamic_update_index_in_dim(moved, got, arrived[e], 0)
        return [moved.reshape(row_count, width)]

    states = [
        jnp.zeros((row_count, width), jnp.bfloat16),
        jnp.zeros((row_count, width), jnp.bfloat16),
        jnp.zeros((row_count, shards * local_hidden), jnp.float32),
    ]
    received = []
    for step in range(sections):
        last = step + 1 == sections
        sends, states = chain_step(
            sz, step, True, last, holder(step), table, received, payloads, states
        )
        if not last:
            received = send_blocks(sends, back, slots[step], step, 1, 1)

    own_rows = broadcast(states[0], every)
    inverse_rms = norm_scale(own_rows)
    normed = (own_rows.astype(jnp.float32) * inverse_rms).astype(jnp.bfloat16)
    preact = dot(normed, weight_in) * scale_in
    hidden = jax.nn.silu(preact).astype(jnp.bfloat16)
    slope = slope_of(preact)
    far_normed = exchange_factor(normed, pieces_in, size_in)
    far_hidden = exchange_factor(hidden, pieces_out, size_out)

    for step in reversed(range(1, sections)):
        if step < links:
            sends, states = chain_step(
                sz, step, False, True, holder(step), table, received, payloads, states
            )
        received = send_blocks(sends, slots[step - 1], back, step, -1, -1)
        if step == min(2, links):
            received, normed, hidden, slope, far_normed, far_hidden, far_states = (
                lax.optimization_barrier(
                    (received, normed, hidden, slope, far_normed, far_hidden, far_states)
                )
            )
    upstream = states[1]
    first_up = received[0]
    if in_kernel:
        first_up = jnp.zeros((row_count, width), jnp.bfloat16)
        for e in range(replicas):
            first_up = lax.dynamic_update_slice_in_dim(
                first_up, received[e], slots[0, e] * block_rows, 0
            )
    upstream = jnp.where(section_id == 0, first_up, upstream)
    upstream = broadcast(upstream, every)
    far_up = [across_replicas(upstream, e, every) for e in others]
    grad_hidden = dot(upstream, weight_out, contract_last) * scale_out
    grad_pre = (grad_hidden * slope).astype(jnp.bfloat16)
    far_pre = [across_replicas(grad_pre, e, every) for e in others]

    def far_part(e, which):
        sizes = [size_in, size_in, size_out, size_out]
        lengths = [size_in * local_hidden // panel] * 2 + [size_out * width // panel] * 2
        begin = sum(lengths[:which])
        return from_panels(far_states[e - 1][begin : begin + lengths[which]], sizes[which])

    def as_delta(left, right, scale):
        return (inner_rate * (dot(left, right, contract_rows) * scale)).astype(jnp.bfloat16)

    def finish(weight, moment, left, right, which, far_left, far_right, scale, pieces, size):
        new_weight, new_moment = outer_mix(
            weight.astype(jnp.float32),
            moment.astype(jnp.float32),
            as_delta(left, right, scale).astype(jnp.float32),
        )
        for e in others:
            back = replicas - e

            def mean(own_array, far_array):
                return 0.5 * (own_array.astype(jnp.float32) + far_array.astype(jnp.float32))

            index = pieces[back]
            own_left = piece(left, index, size, 1)
            part_weight, part_moment = outer_mix(
                mean(piece(weight, index, size), far_part(e, which)),
                mean(piece(moment, index, size), far_part(e, which + 1)),
                mean(
                    as_delta(own_left, right, scale),
                    as_delta(far_left[e - 1], far_right[e - 1], scale),
                ),
            )
            new_weight = lax.dynamic_update_slice_in_dim(new_weight, part_weight, index * size, 0)
            new_moment = lax.dynamic_update_slice_in_dim(new_moment, part_moment, index * size, 0)
        return new_weight[None, None], new_moment[None, None]

    new_weight_b, new_moment_b = finish(
        weight_out, moment_b[0, 0], hidden, upstream, 2, far_hidden, far_up,
        scale_out, pieces_out, size_out,
    )
    new_weight_a, new_moment_a = finish(
        weight_in, moment_a[0, 0], normed, grad_pre, 0, far_normed, far_pre,
        scale_in, pieces_in, size_in,
    )
    return (new_weight_a, new_weight_b, new_moment_a, new_moment_b)


def solution(mesh):
    placed = (
        P("replica", None, None, "shard"),
        P("replica", None, None, "shard"),
        P("replica", "section", None, "shard"),
        P("replica", "section", "shard", None),
        P("replica", "section", None, "shard"),
        P("replica", "section", "shard", None),
        P(),
        P(),
    )
    return jax.shard_map(
        per_device,
        mesh=mesh,
        in_specs=placed,
        out_specs=(
            P("replica", "section", None, "shard"),
            P("replica", "section", "shard", None),
            P("replica", "section", None, "shard"),
            P("replica", "section", "shard", None),
        ),
        check_vma=False,
    )
```

```python
import functools
import math

import jax
import jax.numpy as jnp
from jax import lax
from jax.experimental import pallas as pl
from jax.experimental.pallas import tpu as pltpu
from jax.sharding import PartitionSpec as P

epsilon = 1e-05
inner_rate = 0.5
momentum_decay = 0.9
outer_rate = 0.7

axes = ("replica", "section", "shard")
contract_rows = (((0,), (0,)), ((), ()))
contract_last = (((1,), (1,)), ((), ()))


def norm_scale(rows):
    wide = rows.astype(jnp.float32)
    return lax.rsqrt(jnp.mean(wide * wide, axis=1, keepdims=True) + epsilon)


def dot(left, right, dims=(((1,), (0,)), ((), ()))):
    return lax.dot_general(left, right, dims, preferred_element_type=jnp.float32)


def outer_mix(weight, moment, delta):
    new_moment = momentum_decay * moment + delta
    new_weight = weight - outer_rate * (momentum_decay * new_moment + delta)
    return new_weight.astype(jnp.bfloat16), new_moment.astype(jnp.bfloat16)


def slope_of(preact):
    gate = jax.nn.sigmoid(preact)
    return gate * (1.0 + preact * (1.0 - gate))


def from_panels(array, rows):
    count = array.shape[0] // rows
    return jnp.concatenate([array[i * rows : (i + 1) * rows] for i in range(count)], axis=1)


def pack_kernel(heights, panel, starts, *refs):
    sources, (packed, buffer, read_sems, write_sems) = refs[:-4], refs[-4:]
    reads, writes = [], []
    place = 0
    for i, (source, height) in enumerate(zip(sources, heights)):
        rows = pl.ds(pl.multiple_of(starts[0, i], height), height)
        for column in range(0, source.shape[1], panel):
            k = len(reads)
            there = pl.ds(place, height)
            reads.append(
                pltpu.make_async_copy(
                    source.at[rows, pl.ds(column, panel)], buffer.at[there], read_sems.at[k]
                )
            )
            writes.append(
                pltpu.make_async_copy(buffer.at[there], packed.at[there], write_sems.at[k])
            )
            place += height
    for copy in reads:
        copy.start()
    for read, write in zip(reads, writes):
        read.wait()
        write.start()
    for copy in writes:
        copy.wait()


def pack(arrays, heights, starts, panel):
    counts = [array.shape[1] // panel for array in arrays]
    total = sum(count * height for count, height in zip(counts, heights))
    anywhere = pl.BlockSpec(memory_space=pl.ANY)
    return pl.pallas_call(
        functools.partial(pack_kernel, heights, panel),
        out_shape=jax.ShapeDtypeStruct((total, panel), arrays[0].dtype),
        in_specs=[pl.BlockSpec(memory_space=pltpu.SMEM)] + [anywhere] * len(arrays),
        out_specs=anywhere,
        scratch_shapes=[
            pltpu.VMEM((total, panel), arrays[0].dtype),
            pltpu.SemaphoreType.DMA((sum(counts),)),
            pltpu.SemaphoreType.DMA((sum(counts),)),
        ],
        compiler_params=pltpu.CompilerParams(vmem_limit_bytes=16 * 1024 * 1024),
        cost_estimate=pl.CostEstimate(
            flops=0, bytes_accessed=4 * total * panel, transcendentals=0
        ),
    )(starts, *arrays)


class Sizes:
    def __init__(self, sections, row_count, width, local_hidden, panel, hidden_total, blocks):
        self.sections, self.row_count = sections, row_count
        self.width, self.local_hidden, self.panel = width, local_hidden, panel
        self.blocks = blocks
        self.block_rows = row_count // blocks
        self.panels_in = local_hidden // panel
        self.panels_out = width // panel
        self.half = width * self.panels_in
        self.scale_in = 1.0 / math.sqrt(width)
        self.scale_out = 1.0 / math.sqrt(hidden_total)


def chain_kernel(sz, step, forward, counts, *refs):
    refs = list(refs)

    def take(count):
        taken = refs[:count]
        del refs[:count]
        return taken

    (table,) = take(1)
    received, edges, payloads = take(counts[0]), take(counts[1]), take(2)
    take(3)
    sends = take(counts[2])
    rows_hbm, up_hbm, slope_hbm = take(3)
    weights, landing, rows, up, out, slope = take(6)
    weight_sems, block_sems, edge_sems, send_sems, state_sems = take(5)
    panel, width, hidden_size = sz.panel, sz.width, sz.local_hidden
    links = sz.sections - 1
    whole = pl.ds(0, sz.row_count)

    def weight_copy(d, which):
        return pltpu.make_async_copy(
            payloads[d].at[pl.ds(which * sz.half, sz.half)],
            weights.at[d, which],
            weight_sems.at[d, which],
        )

    def place(line, e):
        return pl.ds(pl.multiple_of(table[line, e], sz.block_rows), sz.block_rows)

    @pl.when(table[links + 1, step] == 1)
    def _():
        sequence = [(d, which if forward else 1 - which) for d in range(2) for which in range(2)]
        arrive = links if forward else step
        first_copies = []
        for i, source in enumerate(received):
            e, a = divmod(i, 2)
            rows_there = whole if len(received) == 2 else place(arrive, e)
            first_copies.append(
                pltpu.make_async_copy(source, landing.at[a, rows_there], block_sems.at[i])
            )
        if edges:
            edge_refs = [payload.at[pl.ds(2 * sz.half, sz.row_count)] for payload in payloads]
            for d, source in enumerate(edge_refs + edges):
                column = pl.ds(pl.multiple_of(table[links + 2, d], panel), panel)
                first_copies.append(
                    pltpu.make_async_copy(source, out.at[:, column], edge_sems.at[d])
                )
        if not forward:
            first_copies.append(pltpu.make_async_copy(rows_hbm, rows, state_sems.at[0]))
            first_copies.append(pltpu.make_async_copy(slope_hbm, slope, state_sems.at[1]))
        for copy in first_copies:
            copy.start()
        for item in sequence[:2]:
            weight_copy(*item).start()

        def arrived(item):
            weight_copy(*item).wait()
            later = sequence.index(item) + 2
            if later < len(sequence):
                weight_copy(*sequence[later]).start()

        for copy in first_copies:
            copy.wait()
        if received:
            total = landing[0].astype(jnp.float32) + landing[1].astype(jnp.float32)
            total = total.astype(jnp.bfloat16)
        if forward:
            rows[...] = total if received else out[...]
        elif edges:
            goal = out[...].astype(jnp.float32)
            up[...] = (total.astype(jnp.float32) - goal).astype(jnp.bfloat16)
        else:
            up[...] = total
        fresh, fresh_hbm = (rows, rows_hbm) if forward else (up, up_hbm)
        store_copies = [pltpu.make_async_copy(fresh, fresh_hbm, state_sems.at[2])]
        store_copies[0].start()

        wide = rows[...].astype(jnp.float32)
        inverse_rms = lax.rsqrt(jnp.mean(wide * wide, axis=1, keepdims=True) + epsilon)
        leads = table[links + 2, 2] > table[links + 2, 0]
        if forward:
            normed = (wide * inverse_rms).astype(jnp.bfloat16)
            total = [jnp.zeros((sz.row_count, panel), jnp.float32) for _ in range(sz.panels_out)]
            for d in range(2):
                arrived((d, 0))
                hidden = []
                for p in range(sz.panels_in):
                    weight = weights[d, 0, p * width : (p + 1) * width, :]
                    preact = dot(normed, weight) * sz.scale_in
                    gate = jax.nn.sigmoid(preact)
                    hidden.append((preact * gate).astype(jnp.bfloat16))
                    column = d * hidden_size + p * panel
                    slope[:, column : column + panel] = gate * (1.0 + preact * (1.0 - gate))
                hidden = jnp.concatenate(hidden, axis=1)
                arrived((d, 1))
                for n in range(sz.panels_out):
                    weight = weights[d, 1, n * hidden_size : (n + 1) * hidden_size, :]
                    total[n] = total[n] + dot(hidden, weight)
            total = jnp.concatenate(total, axis=1) * sz.scale_out
            out[...] = (total + jnp.where(leads, wide, 0.0)).astype(jnp.bfloat16)
            store_copies.append(pltpu.make_async_copy(slope, slope_hbm, state_sems.at[1]))
        else:
            up_turned = up[...].T
            total = jnp.zeros((width, sz.row_count), jnp.float32)
            for d in range(2):
                arrived((d, 1))
                grad_hidden = jnp.zeros((hidden_size, sz.row_count), jnp.float32)
                for n in range(sz.panels_out):
                    weight = weights[d, 1, n * hidden_size : (n + 1) * hidden_size, :]
                    piece = up_turned[n * panel : (n + 1) * panel, :]
                    grad_hidden = grad_hidden + dot(weight, piece)
                local_slope = slope[:, d * hidden_size : (d + 1) * hidden_size].T
                grad_pre = (grad_hidden * sz.scale_out * local_slope).astype(jnp.bfloat16)
                arrived((d, 0))
                for p in range(sz.panels_in):
                    weight = weights[d, 0, p * width : (p + 1) * width, :]
                    piece = grad_pre[p * panel : (p + 1) * panel, :]
                    total = total + dot(weight, piece)
            total = total.T * sz.scale_in
            exact = wide * inverse_rms
            along = jnp.mean(total * exact, axis=1, keepdims=True)
            own = jnp.where(leads, up[...].astype(jnp.float32), 0.0)
            out[...] = (own + inverse_rms * (total - exact * along)).astype(jnp.bfloat16)
        leave = step if forward else links
        send_copies = []
        for e, target in enumerate(sends):
            rows_here = whole if len(sends) == 1 else place(leave, e)
            send_copies.append(
                pltpu.make_async_copy(out.at[rows_here], target, send_sems.at[e])
            )
        for copy in send_copies + store_copies[1:]:
            copy.start()
        for copy in send_copies + store_copies:
            copy.wait()


def chain_step(sz, step, forward, table, received, edges, payloads, states):
    last = step + 1 == sz.sections
    count = 1 if forward and last else sz.blocks
    anywhere = pl.BlockSpec(memory_space=pl.ANY)
    operands = [table, *received, *edges, *payloads, *states]
    block = jax.ShapeDtypeStruct((sz.row_count // count, sz.width), jnp.bfloat16)
    shapes = [block] * count + [jax.ShapeDtypeStruct(s.shape, s.dtype) for s in states]
    base = len(operands) - len(states)
    whole = (sz.row_count, sz.width)
    results = pl.pallas_call(
        functools.partial(
            chain_kernel, sz, step, forward, (len(received), len(edges), count)
        ),
        out_shape=shapes,
        in_specs=[pl.BlockSpec(memory_space=pltpu.SMEM)] + [anywhere] * (len(operands) - 1),
        out_specs=[anywhere] * len(shapes),
        input_output_aliases={base + i: count + i for i in range(len(states))},
        scratch_shapes=[
            pltpu.VMEM((2, 2, sz.half, sz.panel), jnp.bfloat16),
            pltpu.VMEM((2,) + whole, jnp.bfloat16),
            pltpu.VMEM(whole, jnp.bfloat16),
            pltpu.VMEM(whole, jnp.bfloat16),
            pltpu.VMEM(whole, jnp.bfloat16),
            pltpu.VMEM((sz.row_count, 2 * sz.local_hidden), jnp.float32),
            pltpu.SemaphoreType.DMA((2, 2)),
            pltpu.SemaphoreType.DMA((max(1, len(received)),)),
            pltpu.SemaphoreType.DMA((4,)),
            pltpu.SemaphoreType.DMA((count,)),
            pltpu.SemaphoreType.DMA((3,)),
        ],
        compiler_params=pltpu.CompilerParams(vmem_limit_bytes=32 * 1024 * 1024),
        cost_estimate=pl.CostEstimate(
            flops=8 * sz.row_count * sz.width * sz.local_hidden,
            bytes_accessed=8 * sz.half * sz.panel,
            transcendentals=0,
        ),
    )(*operands)
    return list(results[:count]), list(results[count:])


def per_device(inputs, targets, weight_a, weight_b, moment_a, moment_b, routes, partners):
    replicas = lax.axis_size("replica")
    sections = lax.axis_size("section")
    shards = lax.axis_size("shard")
    replica_id = lax.axis_index("replica")
    section_id = lax.axis_index("section")
    shard_id = lax.axis_index("shard")
    row_count = inputs.shape[2]
    panel = inputs.shape[3]
    width = weight_a.shape[2]
    local_hidden = weight_a.shape[3]
    assert inputs.shape[1] == 1 and shards == 4
    assert local_hidden % panel == 0 and sections > 2
    hidden_total = local_hidden * shards
    scale_in = 1.0 / math.sqrt(width)
    scale_out = 1.0 / math.sqrt(hidden_total)
    weight_in = weight_a[0, 0]
    weight_out = weight_b[0, 0]
    block_rows = row_count // replicas
    links = sections - 1
    in_kernel = block_rows % 16 == 0
    blocks = replicas if in_kernel else 1
    sz = Sizes(sections, row_count, width, local_hidden, panel, hidden_total, blocks)

    def flat(replica, section, shard):
        return (replica * sections + section) * shards + shard

    def turn(section):
        return (section ^ (section >> 1)) & 1

    def holders(section):
        return [j for j in range(shards) if (j & 1) != turn(section)]

    def move(array, sources, target):
        pairs = [
            (flat(r, s, j), flat(*target(r, s, j)))
            for r in range(replicas)
            for s, j in sources
        ]
        return lax.ppermute(array, axes, pairs)

    def holder_sources(active):
        return [(s, j) for s in active for j in holders(s)]

    def to_holders(array, offset, active):
        sources = [(s, j ^ offset) for s, j in holder_sources(active)]
        return move(array, sources, lambda r, s, j: (r, s, j ^ offset))

    def from_holders(array, offset, active):
        return move(array, holder_sources(active), lambda r, s, j: (r, s, j ^ offset))

    def between_holders(array, offset, other_half, section, step):
        shift = turn(section) ^ turn(section + step) ^ (2 * other_half)
        return move(
            array,
            holder_sources([section]),
            lambda r, s, j: ((r + offset) % replicas, s + step, j ^ shift),
        )

    def across_replicas(array, offset, active):
        return move(
            array,
            [(s, j) for s in active for j in range(shards)],
            lambda r, s, j: ((r + offset) % replicas, s, j),
        )

    every = range(sections)
    others = range(1, replicas)
    is_holder = (shard_id & 1) != turn(section_id)

    edge = jnp.where(section_id == 0, inputs[0, 0], targets[0, 0])
    edges = [to_holders(edge, d, [0, links]) for d in (2, 3)]
    payload = pack(
        [weight_in, weight_out, edge],
        [width, local_hidden, row_count],
        jnp.zeros((1, 3), jnp.int32),
        panel,
    )
    payloads = [payload, to_holders(payload, 1, every)]

    tables = lax.dynamic_index_in_dim(partners, section_id, 0, keepdims=False)

    def piece_of(table, offset):
        wanted = (replica_id + offset) % replicas
        return jnp.argmax(table[:, replica_id] == wanted).astype(jnp.int32)

    pieces_in = [piece_of(tables[0], e) for e in range(replicas)]
    pieces_out = [piece_of(tables[1], e) for e in range(replicas)]
    size_in = width // replicas
    size_out = local_hidden // replicas

    def piece(array, index, size, axis=0):
        return lax.dynamic_slice_in_dim(array, index * size, size, axis)

    def state_pieces(weight, moment, index, size):
        starts = jnp.broadcast_to(index * size, (1, 2))
        return pack([weight, moment], [size, size], starts, panel)

    def exchange(arrays, active):
        return [across_replicas(array, e, active) for e, array in zip(others, arrays)]

    packed_in = [state_pieces(weight_in, moment_a[0, 0], pieces_in[e], size_in) for e in others]
    packed_out = [
        state_pieces(weight_out, moment_b[0, 0], pieces_out[e], size_out) for e in others
    ]
    early = range(sections // 2, sections)
    late = range(sections // 2)
    far_states_in = exchange(packed_in, every)
    far_states_out = exchange(packed_out, early)

    offsets = jnp.arange(replicas, dtype=jnp.int32)
    there = (replica_id + offsets) % replicas
    back = (replica_id - offsets) % replicas
    own_routes = routes[0, :, replica_id, :]
    slots = jnp.sum(
        (own_routes[:, None, :] == there[None, :, None]).astype(jnp.int32)
        * offsets[None, None, :],
        axis=2,
    )
    columns = max(replicas, sections, shards)
    ours = (is_holder & (section_id == jnp.arange(sections))).astype(jnp.int32)
    features = (shard_id ^ jnp.arange(shards, dtype=jnp.int32)) * panel

    def line(values):
        return jnp.pad(values, ((0, 0), (0, columns - values.shape[1])))

    starts = jnp.concatenate([slots, back[None]]) * block_rows
    if not in_kernel:
        starts = jnp.zeros_like(starts)
    table = jnp.concatenate([line(starts), line(ours[None]), line(features[None])])
    table = table.astype(jnp.int32)

    def send_blocks(sends, arrived, left, section, step):
        sign = step
        if in_kernel:
            return [
                between_holders(sends[e], sign * e, a, section, step)
                for e in range(replicas)
                for a in range(2)
            ]
        parts = sends[0].reshape(replicas, block_rows, width)
        moved = [jnp.zeros_like(parts), jnp.zeros_like(parts)]
        for e in range(replicas):
            chosen = lax.dynamic_index_in_dim(parts, left[e], 0, keepdims=False)
            for a in range(2):
                got = between_holders(chosen, sign * e, a, section, step)
                moved[a] = lax.dynamic_update_index_in_dim(moved[a], got, arrived[e], 0)
        return [one.reshape(row_count, width) for one in moved]

    states = [
        jnp.zeros((row_count, width), jnp.bfloat16),
        jnp.zeros((row_count, width), jnp.bfloat16),
        jnp.zeros((row_count, 2 * local_hidden), jnp.float32),
    ]
    received = []
    for step in every:
        sends, states = chain_step(
            sz, step, True, table, received, edges if step == 0 else [], payloads, states
        )
        if step < links:
            received = send_blocks(sends, back, slots[step], step, 1)
        else:
            received = [sends[0], from_holders(sends[0], 2, [links])]
        if step == len(late) - 1:
            received, packed_out = lax.optimization_barrier((received, packed_out))
            far_late = exchange(packed_out, late)

    for step in reversed(range(1, sections)):
        sends, states = chain_step(
            sz, step, False, table, received, edges if step == links else [], payloads, states
        )
        received = send_blocks(sends, slots[step - 1], back, step, -1)

    known, sends = lax.optimization_barrier((jnp.concatenate(states[:2]), sends))
    known = jnp.where(is_holder, known, from_holders(known, 1, every))
    own_rows, upstream = known[:row_count], known[row_count:]
    inverse_rms = norm_scale(own_rows)
    normed = (own_rows.astype(jnp.float32) * inverse_rms).astype(jnp.bfloat16)
    preact = dot(normed, weight_in) * scale_in
    hidden = jax.nn.silu(preact).astype(jnp.bfloat16)
    slope = slope_of(preact)

    def before_slope(upstream):
        grad_hidden = dot(upstream, weight_out, contract_last) * scale_out
        return (grad_hidden * slope).astype(jnp.bfloat16)

    grad_pre = before_slope(upstream)
    far_normed = exchange([piece(normed, pieces_in[e], size_in, 1) for e in others], every)
    far_hidden = exchange([piece(hidden, pieces_out[e], size_out, 1) for e in others], every)
    rest = range(1, sections)
    far_up = exchange([upstream] * len(others), rest)
    far_pre = exchange([grad_pre] * len(others), rest)

    halves = []
    for a in range(2):
        half = received[a]
        if in_kernel:
            half = jnp.zeros((row_count, width), jnp.bfloat16)
            for e in range(replicas):
                half = lax.dynamic_update_slice_in_dim(
                    half, received[2 * e + a], slots[0, e] * block_rows, 0
                )
        halves.append(half.astype(jnp.float32))
    first_up = (halves[0] + halves[1]).astype(jnp.bfloat16)
    first_up = jnp.where(is_holder, first_up, from_holders(first_up, 1, [0]))
    first_pre = before_slope(first_up)
    here = section_id == 0

    def merge(first, other):
        return jnp.where(here, first, other)

    far_up = [
        merge(one, two) for one, two in zip(exchange([first_up] * len(others), [0]), far_up)
    ]
    far_pre = [
        merge(one, two) for one, two in zip(exchange([first_pre] * len(others), [0]), far_pre)
    ]
    upstream = merge(first_up, upstream)
    grad_pre = merge(first_pre, grad_pre)
    far_states_out = [
        jnp.where(section_id < len(late), one, two)
        for one, two in zip(far_late, far_states_out)
    ]
    far_states = {0: far_states_in, 2: far_states_out}

    def far_part(e, which):
        size = size_out if which & 2 else size_in
        both = from_panels(far_states[which & 2][e - 1], size)
        half = both.shape[1] // 2
        return both[:, half:] if which & 1 else both[:, :half]

    def as_delta(left, right, scale):
        return (inner_rate * (dot(left, right, contract_rows) * scale)).astype(jnp.bfloat16)

    def finish(weight, moment, left, right, which, far_left, far_right, scale, pieces, size):
        new_weight, new_moment = outer_mix(
            weight.astype(jnp.float32),
            moment.astype(jnp.float32),
            as_delta(left, right, scale).astype(jnp.float32),
        )
        for e in others:
            back = replicas - e

            def mean(own_array, far_array):
                return 0.5 * (own_array.astype(jnp.float32) + far_array.astype(jnp.float32))

            index = pieces[back]
            own_left = piece(left, index, size, 1)
            part_weight, part_moment = outer_mix(
                mean(piece(weight, index, size), far_part(e, which)),
                mean(piece(moment, index, size), far_part(e, which + 1)),
                mean(
                    as_delta(own_left, right, scale),
                    as_delta(far_left[e - 1], far_right[e - 1], scale),
                ),
            )
            new_weight = lax.dynamic_update_slice_in_dim(new_weight, part_weight, index * size, 0)
            new_moment = lax.dynamic_update_slice_in_dim(new_moment, part_moment, index * size, 0)
        return new_weight[None, None], new_moment[None, None]

    new_weight_b, new_moment_b = finish(
        weight_out, moment_b[0, 0], hidden, upstream, 2, far_hidden, far_up,
        scale_out, pieces_out, size_out,
    )
    new_weight_a, new_moment_a = finish(
        weight_in, moment_a[0, 0], normed, grad_pre, 0, far_normed, far_pre,
        scale_in, pieces_in, size_in,
    )
    return (new_weight_a, new_weight_b, new_moment_a, new_moment_b)


def solution(mesh):
    placed = (
        P("replica", None, None, "shard"),
        P("replica", None, None, "shard"),
        P("replica", "section", None, "shard"),
        P("replica", "section", "shard", None),
        P("replica", "section", None, "shard"),
        P("replica", "section", "shard", None),
        P(),
        P(),
    )
    return jax.shard_map(
        per_device,
        mesh=mesh,
        in_specs=placed,
        out_specs=(
            P("replica", "section", None, "shard"),
            P("replica", "section", "shard", None),
            P("replica", "section", None, "shard"),
            P("replica", "section", "shard", None),
        ),
        check_vma=False,
    )
```

```python
import functools
import math

import jax
import jax.numpy as jnp
from jax import lax
from jax.experimental import pallas as pl
from jax.experimental.pallas import tpu as pltpu
from jax.sharding import PartitionSpec as P

epsilon = 1e-05
inner_rate = 0.5
momentum_decay = 0.9
outer_rate = 0.7

axes = ("replica", "section", "shard")
contract_rows = (((0,), (0,)), ((), ()))
contract_last = (((1,), (1,)), ((), ()))


def norm_scale(rows):
    wide = rows.astype(jnp.float32)
    return lax.rsqrt(jnp.mean(wide * wide, axis=1, keepdims=True) + epsilon)


def dot(left, right, dims=(((1,), (0,)), ((), ()))):
    return lax.dot_general(left, right, dims, preferred_element_type=jnp.float32)


def outer_mix(weight, moment, delta):
    new_moment = momentum_decay * moment + delta
    new_weight = weight - outer_rate * (momentum_decay * new_moment + delta)
    return new_weight.astype(jnp.bfloat16), new_moment.astype(jnp.bfloat16)


def slope_of(preact):
    gate = jax.nn.sigmoid(preact)
    return gate * (1.0 + preact * (1.0 - gate))


def from_panels(array, rows):
    count = array.shape[0] // rows
    return jnp.concatenate([array[i * rows : (i + 1) * rows] for i in range(count)], axis=1)


def pack_kernel(heights, panel, starts, *refs):
    sources, (packed, buffer, read_sems, write_sems) = refs[:-4], refs[-4:]
    reads, writes = [], []
    place = 0
    for i, (source, height) in enumerate(zip(sources, heights)):
        rows = pl.ds(pl.multiple_of(starts[0, i], height), height)
        for column in range(0, source.shape[1], panel):
            k = len(reads)
            there = pl.ds(place, height)
            reads.append(
                pltpu.make_async_copy(
                    source.at[rows, pl.ds(column, panel)], buffer.at[there], read_sems.at[k]
                )
            )
            writes.append(
                pltpu.make_async_copy(buffer.at[there], packed.at[there], write_sems.at[k])
            )
            place += height
    for copy in reads:
        copy.start()
    for read, write in zip(reads, writes):
        read.wait()
        write.start()
    for copy in writes:
        copy.wait()


def pack(arrays, heights, starts, panel):
    counts = [array.shape[1] // panel for array in arrays]
    total = sum(count * height for count, height in zip(counts, heights))
    anywhere = pl.BlockSpec(memory_space=pl.ANY)
    return pl.pallas_call(
        functools.partial(pack_kernel, heights, panel),
        out_shape=jax.ShapeDtypeStruct((total, panel), arrays[0].dtype),
        in_specs=[pl.BlockSpec(memory_space=pltpu.SMEM)] + [anywhere] * len(arrays),
        out_specs=anywhere,
        scratch_shapes=[
            pltpu.VMEM((total, panel), arrays[0].dtype),
            pltpu.SemaphoreType.DMA((sum(counts),)),
            pltpu.SemaphoreType.DMA((sum(counts),)),
        ],
        compiler_params=pltpu.CompilerParams(vmem_limit_bytes=16 * 1024 * 1024),
        cost_estimate=pl.CostEstimate(
            flops=0, bytes_accessed=4 * total * panel, transcendentals=0
        ),
    )(starts, *arrays)


class Sizes:
    def __init__(self, sections, row_count, width, local_hidden, panel, hidden_total, blocks):
        self.sections, self.row_count = sections, row_count
        self.width, self.local_hidden, self.panel = width, local_hidden, panel
        self.blocks = blocks
        self.block_rows = row_count // blocks
        self.panels_in = local_hidden // panel
        self.panels_out = width // panel
        self.half = width * self.panels_in
        self.scale_in = 1.0 / math.sqrt(width)
        self.scale_out = 1.0 / math.sqrt(hidden_total)


def chain_kernel(sz, step, forward, counts, *refs):
    refs = list(refs)

    def take(count):
        taken = refs[:count]
        del refs[:count]
        return taken

    (table,) = take(1)
    received, edges, payloads = take(counts[0]), take(counts[1]), take(2)
    take(1)
    sends = take(counts[2])
    (state,) = take(1)
    weights, landing, rows, up, out, slope, wide_store = take(7)
    weight_sems, block_sems, edge_sems, send_sems, state_sems = take(5)
    panel, width, hidden_size = sz.panel, sz.width, sz.local_hidden
    links = sz.sections - 1
    whole = pl.ds(0, sz.row_count)

    def weight_copy(d, which):
        return pltpu.make_async_copy(
            payloads[d].at[pl.ds(which * sz.half, sz.half)],
            weights.at[d, which],
            weight_sems.at[d, which],
        )

    def place(line, e):
        return pl.ds(pl.multiple_of(table[line, e], sz.block_rows), sz.block_rows)

    def state_part(k, columns):
        return state.at[pl.ds(k * sz.row_count, sz.row_count), pl.ds(0, columns)]

    rows_hbm, up_hbm = state_part(0, width), state_part(1, width)
    slope_hbm = state_part(2, 2 * hidden_size)

    @pl.when(table[links + 1, step] == 1)
    def _():
        sequence = [(d, which if forward else 1 - which) for d in range(2) for which in range(2)]
        arrive = links if forward else step
        first_copies = []
        for i, source in enumerate(received):
            e, a = divmod(i, 2)
            rows_there = whole if len(received) == 2 else place(arrive, e)
            first_copies.append(
                pltpu.make_async_copy(source, landing.at[a, rows_there], block_sems.at[i])
            )
        if edges:
            edge_refs = [payload.at[pl.ds(2 * sz.half, sz.row_count)] for payload in payloads]
            for d, source in enumerate(edge_refs + edges):
                column = pl.ds(pl.multiple_of(table[links + 2, d], panel), panel)
                first_copies.append(
                    pltpu.make_async_copy(source, out.at[:, column], edge_sems.at[d])
                )
        if not forward:
            first_copies.append(pltpu.make_async_copy(rows_hbm, wide_store, state_sems.at[0]))
            first_copies.append(pltpu.make_async_copy(slope_hbm, slope, state_sems.at[1]))
        for copy in first_copies:
            copy.start()
        for item in sequence[:2]:
            weight_copy(*item).start()

        def arrived(item):
            weight_copy(*item).wait()
            later = sequence.index(item) + 2
            if later < len(sequence):
                weight_copy(*sequence[later]).start()

        for copy in first_copies:
            copy.wait()
        if received:
            total = landing[0].astype(jnp.float32) + landing[1].astype(jnp.float32)
            total = total.astype(jnp.bfloat16)
        if forward:
            rows[...] = total if received else out[...]
        elif edges:
            goal = out[...].astype(jnp.float32)
            up[...] = (total.astype(jnp.float32) - goal).astype(jnp.bfloat16)
        else:
            up[...] = total
        if forward:
            wide = rows[...].astype(jnp.float32)
            wide_store[...] = wide
            store_copies = [pltpu.make_async_copy(wide_store, rows_hbm, state_sems.at[2])]
        else:
            wide = wide_store[...]
            up_store = slope.at[:, pl.ds(0, width)]
            store_copies = [pltpu.make_async_copy(up_store, up_hbm, state_sems.at[2])]
        inverse_rms = lax.rsqrt(jnp.mean(wide * wide, axis=1, keepdims=True) + epsilon)
        leads = table[links + 2, 2] > table[links + 2, 0]
        if forward:
            normed = (wide * inverse_rms).astype(jnp.bfloat16)
            total = [jnp.zeros((sz.row_count, panel), jnp.float32) for _ in range(sz.panels_out)]
            for d in range(2):
                arrived((d, 0))
                hidden = []
                for p in range(sz.panels_in):
                    weight = weights[d, 0, p * width : (p + 1) * width, :]
                    preact = dot(normed, weight) * sz.scale_in
                    gate = jax.nn.sigmoid(preact)
                    hidden.append((preact * gate).astype(jnp.bfloat16))
                    column = d * hidden_size + p * panel
                    slope[:, column : column + panel] = gate * (1.0 + preact * (1.0 - gate))
                hidden = jnp.concatenate(hidden, axis=1)
                arrived((d, 1))
                for n in range(sz.panels_out):
                    weight = weights[d, 1, n * hidden_size : (n + 1) * hidden_size, :]
                    total[n] = total[n] + dot(hidden, weight)
            total = jnp.concatenate(total, axis=1) * sz.scale_out
            out[...] = (total + jnp.where(leads, wide, 0.0)).astype(jnp.bfloat16)
            store_copies.append(pltpu.make_async_copy(slope, slope_hbm, state_sems.at[1]))
        else:
            up_turned = up[...].T
            total = jnp.zeros((width, sz.row_count), jnp.float32)
            for d in range(2):
                arrived((d, 1))
                grad_hidden = jnp.zeros((hidden_size, sz.row_count), jnp.float32)
                for n in range(sz.panels_out):
                    weight = weights[d, 1, n * hidden_size : (n + 1) * hidden_size, :]
                    piece = up_turned[n * panel : (n + 1) * panel, :]
                    grad_hidden = grad_hidden + dot(weight, piece)
                local_slope = slope[:, d * hidden_size : (d + 1) * hidden_size].T
                grad_pre = (grad_hidden * sz.scale_out * local_slope).astype(jnp.bfloat16)
                arrived((d, 0))
                for p in range(sz.panels_in):
                    weight = weights[d, 0, p * width : (p + 1) * width, :]
                    piece = grad_pre[p * panel : (p + 1) * panel, :]
                    total = total + dot(weight, piece)
            total = total.T * sz.scale_in
            exact = wide * inverse_rms
            along = jnp.mean(total * exact, axis=1, keepdims=True)
            own = up[...].astype(jnp.float32)
            slope[:, :width] = own
            own = jnp.where(leads, own, 0.0)
            out[...] = (own + inverse_rms * (total - exact * along)).astype(jnp.bfloat16)
        leave = step if forward else links
        send_copies = []
        for e, target in enumerate(sends):
            rows_here = whole if len(sends) == 1 else place(leave, e)
            send_copies.append(
                pltpu.make_async_copy(out.at[rows_here], target, send_sems.at[e])
            )
        for copy in send_copies + store_copies:
            copy.start()
        for copy in send_copies + store_copies:
            copy.wait()


def chain_step(sz, step, forward, table, received, edges, payloads, state):
    last = step + 1 == sz.sections
    count = 1 if forward and last else sz.blocks
    anywhere = pl.BlockSpec(memory_space=pl.ANY)
    operands = [table, *received, *edges, *payloads, state]
    block = jax.ShapeDtypeStruct((sz.row_count // count, sz.width), jnp.bfloat16)
    shapes = [block] * count + [jax.ShapeDtypeStruct(state.shape, state.dtype)]
    whole = (sz.row_count, sz.width)
    results = pl.pallas_call(
        functools.partial(
            chain_kernel, sz, step, forward, (len(received), len(edges), count)
        ),
        out_shape=shapes,
        in_specs=[pl.BlockSpec(memory_space=pltpu.SMEM)] + [anywhere] * (len(operands) - 1),
        out_specs=[anywhere] * len(shapes),
        input_output_aliases={len(operands) - 1: count},
        scratch_shapes=[
            pltpu.VMEM((2, 2, sz.half, sz.panel), jnp.bfloat16),
            pltpu.VMEM((2,) + whole, jnp.bfloat16),
            pltpu.VMEM(whole, jnp.bfloat16),
            pltpu.VMEM(whole, jnp.bfloat16),
            pltpu.VMEM(whole, jnp.bfloat16),
            pltpu.VMEM((sz.row_count, 2 * sz.local_hidden), jnp.float32),
            pltpu.VMEM(whole, jnp.float32),
            pltpu.SemaphoreType.DMA((2, 2)),
            pltpu.SemaphoreType.DMA((max(1, len(received)),)),
            pltpu.SemaphoreType.DMA((4,)),
            pltpu.SemaphoreType.DMA((count,)),
            pltpu.SemaphoreType.DMA((3,)),
        ],
        compiler_params=pltpu.CompilerParams(vmem_limit_bytes=32 * 1024 * 1024),
        cost_estimate=pl.CostEstimate(
            flops=8 * sz.row_count * sz.width * sz.local_hidden,
            bytes_accessed=8 * sz.half * sz.panel,
            transcendentals=0,
        ),
    )(*operands)
    return list(results[:count]), results[count]


def per_device(inputs, targets, weight_a, weight_b, moment_a, moment_b, routes, partners):
    replicas = lax.axis_size("replica")
    sections = lax.axis_size("section")
    shards = lax.axis_size("shard")
    replica_id = lax.axis_index("replica")
    section_id = lax.axis_index("section")
    shard_id = lax.axis_index("shard")
    row_count = inputs.shape[2]
    panel = inputs.shape[3]
    width = weight_a.shape[2]
    local_hidden = weight_a.shape[3]
    assert inputs.shape[1] == 1 and shards == 4
    assert local_hidden % panel == 0 and sections > 2
    hidden_total = local_hidden * shards
    scale_in = 1.0 / math.sqrt(width)
    scale_out = 1.0 / math.sqrt(hidden_total)
    weight_in = weight_a[0, 0]
    weight_out = weight_b[0, 0]
    block_rows = row_count // replicas
    links = sections - 1
    in_kernel = block_rows % 16 == 0
    blocks = replicas if in_kernel else 1
    sz = Sizes(sections, row_count, width, local_hidden, panel, hidden_total, blocks)

    def flat(replica, section, shard):
        return (replica * sections + section) * shards + shard

    def turn(section):
        return (section ^ (section >> 1)) & 1

    def holders(section):
        return [j for j in range(shards) if (j & 1) != turn(section)]

    def move(array, sources, target):
        pairs = [
            (flat(r, s, j), flat(*target(r, s, j)))
            for r in range(replicas)
            for s, j in sources
        ]
        return lax.ppermute(array, axes, pairs)

    def holder_sources(active):
        return [(s, j) for s in active for j in holders(s)]

    def to_holders(array, offset, active):
        sources = [(s, j ^ offset) for s, j in holder_sources(active)]
        return move(array, sources, lambda r, s, j: (r, s, j ^ offset))

    def from_holders(array, offset, active):
        return move(array, holder_sources(active), lambda r, s, j: (r, s, j ^ offset))

    def between_holders(array, offset, other_half, section, step):
        shift = turn(section) ^ turn(section + step) ^ (2 * other_half)
        return move(
            array,
            holder_sources([section]),
            lambda r, s, j: ((r + offset) % replicas, s + step, j ^ shift),
        )

    def across_replicas(array, offset, active):
        return move(
            array,
            [(s, j) for s in active for j in range(shards)],
            lambda r, s, j: ((r + offset) % replicas, s, j),
        )

    every = range(sections)
    others = range(1, replicas)
    is_holder = (shard_id & 1) != turn(section_id)

    edge = jnp.where(section_id == 0, inputs[0, 0], targets[0, 0])
    edges = [to_holders(edge, d, [0, links]) for d in (2, 3)]
    payload = pack(
        [weight_in, weight_out, edge],
        [width, local_hidden, row_count],
        jnp.zeros((1, 3), jnp.int32),
        panel,
    )
    payloads = [payload, to_holders(payload, 1, every)]

    tables = lax.dynamic_index_in_dim(partners, section_id, 0, keepdims=False)

    def piece_of(table, offset):
        wanted = (replica_id + offset) % replicas
        return jnp.argmax(table[:, replica_id] == wanted).astype(jnp.int32)

    pieces_in = [piece_of(tables[0], e) for e in range(replicas)]
    pieces_out = [piece_of(tables[1], e) for e in range(replicas)]
    size_in = width // replicas
    size_out = local_hidden // replicas

    def piece(array, index, size, axis=0):
        return lax.dynamic_slice_in_dim(array, index * size, size, axis)

    def state_pieces(weight, moment, index, size):
        starts = jnp.broadcast_to(index * size, (1, 2))
        return pack([weight, moment], [size, size], starts, panel)

    def exchange(arrays, active):
        return [across_replicas(array, e, active) for e, array in zip(others, arrays)]

    packed_in = [state_pieces(weight_in, moment_a[0, 0], pieces_in[e], size_in) for e in others]
    packed_out = [
        state_pieces(weight_out, moment_b[0, 0], pieces_out[e], size_out) for e in others
    ]
    early = range(sections // 2, sections)
    late = range(sections // 2)
    far_states_in = exchange(packed_in, every)
    far_states_out = exchange(packed_out, early)

    offsets = jnp.arange(replicas, dtype=jnp.int32)
    there = (replica_id + offsets) % replicas
    back = (replica_id - offsets) % replicas
    own_routes = routes[0, :, replica_id, :]
    slots = jnp.sum(
        (own_routes[:, None, :] == there[None, :, None]).astype(jnp.int32)
        * offsets[None, None, :],
        axis=2,
    )
    columns = max(replicas, sections, shards)
    ours = (is_holder & (section_id == jnp.arange(sections))).astype(jnp.int32)
    features = (shard_id ^ jnp.arange(shards, dtype=jnp.int32)) * panel

    def line(values):
        return jnp.pad(values, ((0, 0), (0, columns - values.shape[1])))

    starts = jnp.concatenate([slots, back[None]]) * block_rows
    if not in_kernel:
        starts = jnp.zeros_like(starts)
    table = jnp.concatenate([line(starts), line(ours[None]), line(features[None])])
    table = table.astype(jnp.int32)

    def send_blocks(sends, arrived, left, section, step):
        sign = step
        if in_kernel:
            return [
                between_holders(sends[e], sign * e, a, section, step)
                for e in range(replicas)
                for a in range(2)
            ]
        parts = sends[0].reshape(replicas, block_rows, width)
        moved = [jnp.zeros_like(parts), jnp.zeros_like(parts)]
        for e in range(replicas):
            chosen = lax.dynamic_index_in_dim(parts, left[e], 0, keepdims=False)
            for a in range(2):
                got = between_holders(chosen, sign * e, a, section, step)
                moved[a] = lax.dynamic_update_index_in_dim(moved[a], got, arrived[e], 0)
        return [one.reshape(row_count, width) for one in moved]

    state = jnp.zeros((5 * row_count, 2 * local_hidden), jnp.float32)
    received = []
    for step in every:
        sends, state = chain_step(
            sz, step, True, table, received, edges if step == 0 else [], payloads, state
        )
        if step < links:
            received = send_blocks(sends, back, slots[step], step, 1)
        else:
            received = [sends[0], from_holders(sends[0], 2, [links])]
        if step == len(late) - 1:
            received, packed_out = lax.optimization_barrier((received, packed_out))
            far_late = exchange(packed_out, late)
        if step == len(late):
            received, far_states_in, far_states_out = lax.optimization_barrier(
                (received, far_states_in, far_states_out)
            )

    for step in reversed(range(1, sections)):
        sends, state = chain_step(
            sz, step, False, table, received, edges if step == links else [], payloads, state
        )
        received = send_blocks(sends, slots[step - 1], back, step, -1)
        if step == len(late):
            received, far_late = lax.optimization_barrier((received, far_late))

    known = state[: 2 * row_count, :width].astype(jnp.bfloat16)
    known = jnp.where(is_holder, known, from_holders(known, 1, every))
    own_rows, upstream = known[:row_count], known[row_count:]
    inverse_rms = norm_scale(own_rows)
    normed = (own_rows.astype(jnp.float32) * inverse_rms).astype(jnp.bfloat16)
    preact = dot(normed, weight_in) * scale_in
    hidden = jax.nn.silu(preact).astype(jnp.bfloat16)
    slope = slope_of(preact)

    def before_slope(upstream):
        grad_hidden = dot(upstream, weight_out, contract_last) * scale_out
        return (grad_hidden * slope).astype(jnp.bfloat16)

    grad_pre = before_slope(upstream)
    far_normed = exchange([piece(normed, pieces_in[e], size_in, 1) for e in others], every)
    far_hidden = exchange([piece(hidden, pieces_out[e], size_out, 1) for e in others], every)
    rest = range(1, sections)
    far_up = exchange([upstream] * len(others), rest)
    far_pre = exchange([grad_pre] * len(others), rest)

    halves = []
    for a in range(2):
        half = received[a]
        if in_kernel:
            half = jnp.zeros((row_count, width), jnp.bfloat16)
            for e in range(replicas):
                half = lax.dynamic_update_slice_in_dim(
                    half, received[2 * e + a], slots[0, e] * block_rows, 0
                )
        halves.append(half.astype(jnp.float32))
    first_up = (halves[0] + halves[1]).astype(jnp.bfloat16)
    first_up = jnp.where(is_holder, first_up, from_holders(first_up, 1, [0]))
    first_pre = before_slope(first_up)
    here = section_id == 0

    def merge(first, other):
        return jnp.where(here, first, other)

    far_up = [
        merge(one, two) for one, two in zip(exchange([first_up] * len(others), [0]), far_up)
    ]
    far_pre = [
        merge(one, two) for one, two in zip(exchange([first_pre] * len(others), [0]), far_pre)
    ]
    upstream = merge(first_up, upstream)
    grad_pre = merge(first_pre, grad_pre)
    far_states_out = [
        jnp.where(section_id < len(late), one, two)
        for one, two in zip(far_late, far_states_out)
    ]
    far_states = {0: far_states_in, 2: far_states_out}

    def far_part(e, which):
        size = size_out if which & 2 else size_in
        both = from_panels(far_states[which & 2][e - 1], size)
        half = both.shape[1] // 2
        return both[:, half:] if which & 1 else both[:, :half]

    def as_delta(left, right, scale):
        return (inner_rate * (dot(left, right, contract_rows) * scale)).astype(jnp.bfloat16)

    def finish(weight, moment, left, right, which, far_left, far_right, scale, pieces, size):
        new_weight, new_moment = outer_mix(
            weight.astype(jnp.float32),
            moment.astype(jnp.float32),
            as_delta(left, right, scale).astype(jnp.float32),
        )
        for e in others:
            back = replicas - e

            def mean(own_array, far_array):
                return 0.5 * (own_array.astype(jnp.float32) + far_array.astype(jnp.float32))

            index = pieces[back]
            own_left = piece(left, index, size, 1)
            part_weight, part_moment = outer_mix(
                mean(piece(weight, index, size), far_part(e, which)),
                mean(piece(moment, index, size), far_part(e, which + 1)),
                mean(
                    as_delta(own_left, right, scale),
                    as_delta(far_left[e - 1], far_right[e - 1], scale),
                ),
            )
            new_weight = lax.dynamic_update_slice_in_dim(new_weight, part_weight, index * size, 0)
            new_moment = lax.dynamic_update_slice_in_dim(new_moment, part_moment, index * size, 0)
        return new_weight[None, None], new_moment[None, None]

    new_weight_b, new_moment_b = finish(
        weight_out, moment_b[0, 0], hidden, upstream, 2, far_hidden, far_up,
        scale_out, pieces_out, size_out,
    )
    new_weight_a, new_moment_a = finish(
        weight_in, moment_a[0, 0], normed, grad_pre, 0, far_normed, far_pre,
        scale_in, pieces_in, size_in,
    )
    return (new_weight_a, new_weight_b, new_moment_a, new_moment_b)


def solution(mesh):
    placed = (
        P("replica", None, None, "shard"),
        P("replica", None, None, "shard"),
        P("replica", "section", None, "shard"),
        P("replica", "section", "shard", None),
        P("replica", "section", None, "shard"),
        P("replica", "section", "shard", None),
        P(),
        P(),
    )
    return jax.shard_map(
        per_device,
        mesh=mesh,
        in_specs=placed,
        out_specs=(
            P("replica", "section", None, "shard"),
            P("replica", "section", "shard", None),
            P("replica", "section", None, "shard"),
            P("replica", "section", "shard", None),
        ),
        check_vma=False,
    )
```

```python
import functools
import math

import jax
import jax.numpy as jnp
from jax import lax
from jax.experimental import pallas as pl
from jax.experimental.pallas import tpu as pltpu
from jax.sharding import PartitionSpec as P

epsilon = 1e-05
inner_rate = 0.5
momentum_decay = 0.9
outer_rate = 0.7

axes = ("replica", "section", "shard")
contract_rows = (((0,), (0,)), ((), ()))
contract_last = (((1,), (1,)), ((), ()))


def dot(left, right, dims=(((1,), (0,)), ((), ()))):
    return lax.dot_general(left, right, dims, preferred_element_type=jnp.float32)


def outer_mix(weight, moment, delta):
    new_moment = momentum_decay * moment + delta
    new_weight = weight - outer_rate * (momentum_decay * new_moment + delta)
    return new_weight.astype(jnp.bfloat16), new_moment.astype(jnp.bfloat16)


def from_panels(array, rows):
    count = array.shape[0] // rows
    return jnp.concatenate([array[i * rows : (i + 1) * rows] for i in range(count)], axis=1)


def pack_kernel(heights, panel, starts, *refs):
    sources, (packed, buffer, read_sems, write_sems) = refs[:-4], refs[-4:]
    reads, writes = [], []
    place = 0
    for i, (source, height) in enumerate(zip(sources, heights)):
        rows = pl.ds(pl.multiple_of(starts[0, i], height), height)
        for column in range(0, source.shape[1], panel):
            k = len(reads)
            there = pl.ds(place, height)
            reads.append(
                pltpu.make_async_copy(
                    source.at[rows, pl.ds(column, panel)], buffer.at[there], read_sems.at[k]
                )
            )
            writes.append(
                pltpu.make_async_copy(buffer.at[there], packed.at[there], write_sems.at[k])
            )
            place += height
    for copy in reads:
        copy.start()
    for read, write in zip(reads, writes):
        read.wait()
        write.start()
    for copy in writes:
        copy.wait()


def pack(arrays, heights, starts, panel):
    counts = [array.shape[1] // panel for array in arrays]
    total = sum(count * height for count, height in zip(counts, heights))
    anywhere = pl.BlockSpec(memory_space=pl.ANY)
    return pl.pallas_call(
        functools.partial(pack_kernel, heights, panel),
        out_shape=jax.ShapeDtypeStruct((total, panel), arrays[0].dtype),
        in_specs=[pl.BlockSpec(memory_space=pltpu.SMEM)] + [anywhere] * len(arrays),
        out_specs=anywhere,
        scratch_shapes=[
            pltpu.VMEM((total, panel), arrays[0].dtype),
            pltpu.SemaphoreType.DMA((sum(counts),)),
            pltpu.SemaphoreType.DMA((sum(counts),)),
        ],
        compiler_params=pltpu.CompilerParams(vmem_limit_bytes=16 * 1024 * 1024),
        cost_estimate=pl.CostEstimate(
            flops=0, bytes_accessed=4 * total * panel, transcendentals=0
        ),
    )(starts, *arrays)


class Sizes:
    def __init__(self, sections, row_count, width, local_hidden, panel, hidden_total, blocks):
        self.sections, self.row_count = sections, row_count
        self.width, self.local_hidden, self.panel = width, local_hidden, panel
        self.blocks = blocks
        self.block_rows = row_count // blocks
        self.panels_in = local_hidden // panel
        self.panels_out = width // panel
        self.half = width * self.panels_in
        self.scale_in = 1.0 / math.sqrt(width)
        self.scale_out = 1.0 / math.sqrt(hidden_total)


def chain_kernel(sz, step, forward, counts, *refs):
    refs = list(refs)

    def take(count):
        taken = refs[:count]
        del refs[:count]
        return taken

    (table,) = take(1)
    received, edges, payloads = take(counts[0]), take(counts[1]), take(2)
    take(1)
    sends = take(counts[2])
    (state,) = take(1)
    weights, landing, rows, up, out, slope, wide_store = take(7)
    weight_sems, block_sems, edge_sems, send_sems, state_sems = take(5)
    panel, width, hidden_size = sz.panel, sz.width, sz.local_hidden
    links = sz.sections - 1
    whole = pl.ds(0, sz.row_count)

    def weight_copy(d, which):
        return pltpu.make_async_copy(
            payloads[d].at[pl.ds(which * sz.half, sz.half)],
            weights.at[d, which],
            weight_sems.at[d, which],
        )

    def place(line, e):
        return pl.ds(pl.multiple_of(table[line, e], sz.block_rows), sz.block_rows)

    def state_part(k, columns):
        return state.at[pl.ds(k * sz.row_count, sz.row_count), pl.ds(0, columns)]

    rows_hbm, up_hbm = state_part(0, width), state_part(1, width)
    slope_hbm = state_part(2, 2 * hidden_size)

    @pl.when(table[links + 1, step] == 1)
    def _():
        sequence = [(d, which if forward else 1 - which) for d in range(2) for which in range(2)]
        arrive = links if forward else step
        first_copies = []
        for i, source in enumerate(received):
            e, a = divmod(i, 2)
            rows_there = whole if len(received) == 2 else place(arrive, e)
            first_copies.append(
                pltpu.make_async_copy(source, landing.at[a, rows_there], block_sems.at[i])
            )
        if edges:
            edge_refs = [payload.at[pl.ds(2 * sz.half, sz.row_count)] for payload in payloads]
            for d, source in enumerate(edge_refs + edges):
                column = pl.ds(pl.multiple_of(table[links + 2, d], panel), panel)
                first_copies.append(
                    pltpu.make_async_copy(source, out.at[:, column], edge_sems.at[d])
                )
        if not forward:
            first_copies.append(pltpu.make_async_copy(rows_hbm, wide_store, state_sems.at[0]))
            first_copies.append(pltpu.make_async_copy(slope_hbm, slope, state_sems.at[1]))
        for copy in first_copies:
            copy.start()
        for item in sequence[:2]:
            weight_copy(*item).start()

        def arrived(item):
            weight_copy(*item).wait()
            later = sequence.index(item) + 2
            if later < len(sequence):
                weight_copy(*sequence[later]).start()

        for copy in first_copies:
            copy.wait()
        if received:
            total = landing[0].astype(jnp.float32) + landing[1].astype(jnp.float32)
            total = total.astype(jnp.bfloat16)
        if forward:
            rows[...] = total if received else out[...]
        elif edges:
            goal = out[...].astype(jnp.float32)
            up[...] = (total.astype(jnp.float32) - goal).astype(jnp.bfloat16)
        else:
            up[...] = total
        if forward:
            wide = rows[...].astype(jnp.float32)
            wide_store[...] = wide
            store_copies = [pltpu.make_async_copy(wide_store, rows_hbm, state_sems.at[2])]
        else:
            wide = wide_store[...]
            up_store = slope.at[:, pl.ds(0, width)]
            store_copies = [pltpu.make_async_copy(up_store, up_hbm, state_sems.at[2])]
        inverse_rms = lax.rsqrt(jnp.mean(wide * wide, axis=1, keepdims=True) + epsilon)
        leads = table[links + 2, 2] > table[links + 2, 0]
        if forward:
            normed = (wide * inverse_rms).astype(jnp.bfloat16)
            total = [jnp.zeros((sz.row_count, panel), jnp.float32) for _ in range(sz.panels_out)]
            for d in range(2):
                arrived((d, 0))
                hidden = []
                for p in range(sz.panels_in):
                    weight = weights[d, 0, p * width : (p + 1) * width, :]
                    preact = dot(normed, weight) * sz.scale_in
                    gate = jax.nn.sigmoid(preact)
                    hidden.append((preact * gate).astype(jnp.bfloat16))
                    column = d * hidden_size + p * panel
                    slope[:, column : column + panel] = gate * (1.0 + preact * (1.0 - gate))
                hidden = jnp.concatenate(hidden, axis=1)
                arrived((d, 1))
                for n in range(sz.panels_out):
                    weight = weights[d, 1, n * hidden_size : (n + 1) * hidden_size, :]
                    total[n] = total[n] + dot(hidden, weight)
            total = jnp.concatenate(total, axis=1) * sz.scale_out
            out[...] = (total + jnp.where(leads, wide, 0.0)).astype(jnp.bfloat16)
            store_copies.append(pltpu.make_async_copy(slope, slope_hbm, state_sems.at[1]))
        else:
            up_turned = up[...].T
            total = jnp.zeros((width, sz.row_count), jnp.float32)
            for d in range(2):
                arrived((d, 1))
                grad_hidden = jnp.zeros((hidden_size, sz.row_count), jnp.float32)
                for n in range(sz.panels_out):
                    weight = weights[d, 1, n * hidden_size : (n + 1) * hidden_size, :]
                    piece = up_turned[n * panel : (n + 1) * panel, :]
                    grad_hidden = grad_hidden + dot(weight, piece)
                local_slope = slope[:, d * hidden_size : (d + 1) * hidden_size].T
                grad_pre = (grad_hidden * sz.scale_out * local_slope).astype(jnp.bfloat16)
                arrived((d, 0))
                for p in range(sz.panels_in):
                    weight = weights[d, 0, p * width : (p + 1) * width, :]
                    piece = grad_pre[p * panel : (p + 1) * panel, :]
                    total = total + dot(weight, piece)
            total = total.T * sz.scale_in
            exact = wide * inverse_rms
            along = jnp.mean(total * exact, axis=1, keepdims=True)
            own = up[...].astype(jnp.float32)
            slope[:, :width] = own
            own = jnp.where(leads, own, 0.0)
            out[...] = (own + inverse_rms * (total - exact * along)).astype(jnp.bfloat16)
        leave = step if forward else links
        send_copies = []
        for e, target in enumerate(sends):
            rows_here = whole if len(sends) == 1 else place(leave, e)
            send_copies.append(
                pltpu.make_async_copy(out.at[rows_here], target, send_sems.at[e])
            )
        for copy in send_copies + store_copies:
            copy.start()
        for copy in send_copies + store_copies:
            copy.wait()


def chain_step(sz, step, forward, table, received, edges, payloads, state):
    last = step + 1 == sz.sections
    count = 1 if forward and last else sz.blocks
    anywhere = pl.BlockSpec(memory_space=pl.ANY)
    operands = [table, *received, *edges, *payloads, state]
    block = jax.ShapeDtypeStruct((sz.row_count // count, sz.width), jnp.bfloat16)
    shapes = [block] * count + [jax.ShapeDtypeStruct(state.shape, state.dtype)]
    whole = (sz.row_count, sz.width)
    results = pl.pallas_call(
        functools.partial(
            chain_kernel, sz, step, forward, (len(received), len(edges), count)
        ),
        out_shape=shapes,
        in_specs=[pl.BlockSpec(memory_space=pltpu.SMEM)] + [anywhere] * (len(operands) - 1),
        out_specs=[anywhere] * len(shapes),
        input_output_aliases={len(operands) - 1: count},
        scratch_shapes=[
            pltpu.VMEM((2, 2, sz.half, sz.panel), jnp.bfloat16),
            pltpu.VMEM((2,) + whole, jnp.bfloat16),
            pltpu.VMEM(whole, jnp.bfloat16),
            pltpu.VMEM(whole, jnp.bfloat16),
            pltpu.VMEM(whole, jnp.bfloat16),
            pltpu.VMEM((sz.row_count, 2 * sz.local_hidden), jnp.float32),
            pltpu.VMEM(whole, jnp.float32),
            pltpu.SemaphoreType.DMA((2, 2)),
            pltpu.SemaphoreType.DMA((max(1, len(received)),)),
            pltpu.SemaphoreType.DMA((4,)),
            pltpu.SemaphoreType.DMA((count,)),
            pltpu.SemaphoreType.DMA((3,)),
        ],
        compiler_params=pltpu.CompilerParams(vmem_limit_bytes=32 * 1024 * 1024),
        cost_estimate=pl.CostEstimate(
            flops=8 * sz.row_count * sz.width * sz.local_hidden,
            bytes_accessed=8 * sz.half * sz.panel,
            transcendentals=0,
        ),
    )(*operands)
    return list(results[:count]), results[count]


def share_kernel(sz, whole, *refs):
    if whole:
        known, payload, normed_ref, hidden_ref, slope, weights, sem = refs
    else:
        known, slope, payload, grad_pre, weights, sem = refs
    panel, width, hidden_size = sz.panel, sz.width, sz.local_hidden
    rows_count = sz.row_count
    which = 0 if whole else 1
    copy = pltpu.make_async_copy(payload.at[pl.ds(which * sz.half, sz.half)], weights, sem)
    copy.start()
    if whole:
        wide = known[...].astype(jnp.float32)
        inverse_rms = lax.rsqrt(jnp.mean(wide * wide, axis=1, keepdims=True) + epsilon)
        normed = (wide * inverse_rms).astype(jnp.bfloat16)
        normed_ref[...] = normed
        copy.wait()
        for p in range(sz.panels_in):
            preact = dot(normed, weights[p * width : (p + 1) * width, :]) * sz.scale_in
            gate = jax.nn.sigmoid(preact)
            here = slice(p * panel, (p + 1) * panel)
            hidden_ref[:, here] = (preact * gate).astype(jnp.bfloat16)
            slope[:, here] = gate * (1.0 + preact * (1.0 - gate))
    else:
        copy.wait()
        grad_hidden = jnp.zeros((rows_count, hidden_size), jnp.float32)
        for n in range(sz.panels_out):
            piece = known[:, n * panel : (n + 1) * panel]
            weight = weights[n * hidden_size : (n + 1) * hidden_size, :]
            grad_hidden = grad_hidden + dot(piece, weight, contract_last)
        grad_pre[...] = (grad_hidden * sz.scale_out * slope[...]).astype(jnp.bfloat16)


def share_call(sz, operands, payload):
    whole = len(operands) == 1
    rows_count, hidden_size = sz.row_count, sz.local_hidden
    narrow = jax.ShapeDtypeStruct((rows_count, hidden_size), jnp.bfloat16)
    shapes = [narrow]
    if whole:
        shapes = [
            jax.ShapeDtypeStruct((rows_count, sz.width), jnp.bfloat16),
            narrow,
            jax.ShapeDtypeStruct((rows_count, hidden_size), jnp.float32),
        ]
    inside = pl.BlockSpec(memory_space=pltpu.VMEM)
    return pl.pallas_call(
        functools.partial(share_kernel, sz, whole),
        out_shape=shapes,
        in_specs=[inside] * len(operands) + [pl.BlockSpec(memory_space=pl.ANY)],
        out_specs=[inside] * len(shapes),
        scratch_shapes=[
            pltpu.VMEM((sz.half, sz.panel), jnp.bfloat16),
            pltpu.SemaphoreType.DMA,
        ],
        compiler_params=pltpu.CompilerParams(vmem_limit_bytes=24 * 1024 * 1024),
        cost_estimate=pl.CostEstimate(
            flops=2 * rows_count * sz.width * hidden_size,
            bytes_accessed=2 * sz.half * sz.panel,
            transcendentals=0,
        ),
    )(*operands, payload)


def per_device(inputs, targets, weight_a, weight_b, moment_a, moment_b, routes, partners):
    replicas = lax.axis_size("replica")
    sections = lax.axis_size("section")
    shards = lax.axis_size("shard")
    replica_id = lax.axis_index("replica")
    section_id = lax.axis_index("section")
    shard_id = lax.axis_index("shard")
    row_count = inputs.shape[2]
    panel = inputs.shape[3]
    width = weight_a.shape[2]
    local_hidden = weight_a.shape[3]
    assert inputs.shape[1] == 1 and shards == 4
    assert local_hidden % panel == 0 and sections > 2
    hidden_total = local_hidden * shards
    scale_in = 1.0 / math.sqrt(width)
    scale_out = 1.0 / math.sqrt(hidden_total)
    weight_in = weight_a[0, 0]
    weight_out = weight_b[0, 0]
    block_rows = row_count // replicas
    links = sections - 1
    in_kernel = block_rows % 16 == 0
    blocks = replicas if in_kernel else 1
    sz = Sizes(sections, row_count, width, local_hidden, panel, hidden_total, blocks)

    def flat(replica, section, shard):
        return (replica * sections + section) * shards + shard

    def turn(section):
        return (section ^ (section >> 1)) & 1

    def holders(section):
        return [j for j in range(shards) if (j & 1) != turn(section)]

    def move(array, sources, target):
        pairs = [
            (flat(r, s, j), flat(*target(r, s, j)))
            for r in range(replicas)
            for s, j in sources
        ]
        return lax.ppermute(array, axes, pairs)

    def holder_sources(active):
        return [(s, j) for s in active for j in holders(s)]

    def to_holders(array, offset, active):
        sources = [(s, j ^ offset) for s, j in holder_sources(active)]
        return move(array, sources, lambda r, s, j: (r, s, j ^ offset))

    def from_holders(array, offset, active):
        return move(array, holder_sources(active), lambda r, s, j: (r, s, j ^ offset))

    def between_holders(array, offset, other_half, section, step):
        shift = turn(section) ^ turn(section + step) ^ (2 * other_half)
        return move(
            array,
            holder_sources([section]),
            lambda r, s, j: ((r + offset) % replicas, s + step, j ^ shift),
        )

    def across_replicas(array, offset, active):
        return move(
            array,
            [(s, j) for s in active for j in range(shards)],
            lambda r, s, j: ((r + offset) % replicas, s, j),
        )

    every = range(sections)
    others = range(1, replicas)
    is_holder = (shard_id & 1) != turn(section_id)

    edge = jnp.where(section_id == 0, inputs[0, 0], targets[0, 0])
    edges = [to_holders(edge, d, [0, links]) for d in (2, 3)]
    payload = pack(
        [weight_in, weight_out, edge],
        [width, local_hidden, row_count],
        jnp.zeros((1, 3), jnp.int32),
        panel,
    )
    payloads = [payload, to_holders(payload, 1, every)]

    tables = lax.dynamic_index_in_dim(partners, section_id, 0, keepdims=False)

    def piece_of(table, offset):
        wanted = (replica_id + offset) % replicas
        return jnp.argmax(table[:, replica_id] == wanted).astype(jnp.int32)

    pieces_in = [piece_of(tables[0], e) for e in range(replicas)]
    pieces_out = [piece_of(tables[1], e) for e in range(replicas)]
    size_in = width // replicas
    size_out = local_hidden // replicas

    def piece(array, index, size, axis=0):
        return lax.dynamic_slice_in_dim(array, index * size, size, axis)

    def state_pieces(weight, moment, index, size):
        starts = jnp.broadcast_to(index * size, (1, 2))
        return pack([weight, moment], [size, size], starts, panel)

    def exchange(arrays, active):
        return [across_replicas(array, e, active) for e, array in zip(others, arrays)]

    packed_in = [state_pieces(weight_in, moment_a[0, 0], pieces_in[e], size_in) for e in others]
    packed_out = [
        state_pieces(weight_out, moment_b[0, 0], pieces_out[e], size_out) for e in others
    ]
    early = range(sections // 2, sections)
    late = range(sections // 2)
    far_states_in = exchange(packed_in, every)
    payloads, edges, far_states_in, packed_out = lax.optimization_barrier(
        (payloads, edges, far_states_in, packed_out)
    )
    far_states_out = exchange(packed_out, early)

    offsets = jnp.arange(replicas, dtype=jnp.int32)
    there = (replica_id + offsets) % replicas
    back = (replica_id - offsets) % replicas
    own_routes = routes[0, :, replica_id, :]
    slots = jnp.sum(
        (own_routes[:, None, :] == there[None, :, None]).astype(jnp.int32)
        * offsets[None, None, :],
        axis=2,
    )
    columns = max(replicas, sections, shards)
    ours = (is_holder & (section_id == jnp.arange(sections))).astype(jnp.int32)
    features = (shard_id ^ jnp.arange(shards, dtype=jnp.int32)) * panel

    def line(values):
        return jnp.pad(values, ((0, 0), (0, columns - values.shape[1])))

    starts = jnp.concatenate([slots, back[None]]) * block_rows
    if not in_kernel:
        starts = jnp.zeros_like(starts)
    table = jnp.concatenate([line(starts), line(ours[None]), line(features[None])])
    table = table.astype(jnp.int32)

    def send_blocks(sends, arrived, left, section, step):
        sign = step
        if in_kernel:
            return [
                between_holders(sends[e], sign * e, a, section, step)
                for e in range(replicas)
                for a in range(2)
            ]
        parts = sends[0].reshape(replicas, block_rows, width)
        moved = [jnp.zeros_like(parts), jnp.zeros_like(parts)]
        for e in range(replicas):
            chosen = lax.dynamic_index_in_dim(parts, left[e], 0, keepdims=False)
            for a in range(2):
                got = between_holders(chosen, sign * e, a, section, step)
                moved[a] = lax.dynamic_update_index_in_dim(moved[a], got, arrived[e], 0)
        return [one.reshape(row_count, width) for one in moved]

    state = jnp.zeros((5 * row_count, 2 * local_hidden), jnp.float32)

    def part_of(state, k):
        return state[k * row_count : (k + 1) * row_count, :width].astype(jnp.bfloat16)

    row_parts = []

    def spread_rows(received, state, active):
        received, rows, row_parts[:] = lax.optimization_barrier(
            (received, part_of(state, 0), row_parts)
        )
        row_parts.append(from_holders(rows, 1, active))
        return received

    received = []
    for step in every:
        sends, state = chain_step(
            sz, step, True, table, received, edges if step == 0 else [], payloads, state
        )
        if step < links:
            received = send_blocks(sends, back, slots[step], step, 1)
        else:
            received = [sends[0], from_holders(sends[0], 2, [links])]
        if len(late) - 1 <= step < links:
            received = spread_rows(received, state, late if step < len(late) else [step])
        if step == len(late) - 1:
            received, packed_out = lax.optimization_barrier((received, packed_out))
            far_late = exchange(packed_out, late)
        if step == len(late):
            received, far_states_out = lax.optimization_barrier((received, far_states_out))

    for step in reversed(range(1, sections)):
        sends, state = chain_step(
            sz, step, False, table, received, edges if step == links else [], payloads, state
        )
        received = send_blocks(sends, slots[step - 1], back, step, -1)
        if step == links:
            received = spread_rows(received, state, [links])
        if step == len(late):
            received, far_late, row_parts = lax.optimization_barrier(
                (received, far_late, row_parts)
            )

    own_rows = jnp.where(is_holder, part_of(state, 0), sum(row_parts[1:], row_parts[0]))
    normed, hidden, slope = share_call(sz, [own_rows], payload)

    def bundle(e):
        first, second = normed, hidden
        first = piece(first, pieces_in[e], size_in, 1)
        return jnp.concatenate([first, piece(second, pieces_out[e], size_out, 1)], axis=1)

    bundles = exchange([bundle(e) for e in others], every)
    received, bundles = lax.optimization_barrier((received, bundles))
    far_normed = [one[:, :size_in] for one in bundles]
    far_hidden = [one[:, size_in:] for one in bundles]

    halves = []
    for a in range(2):
        half = received[a]
        if in_kernel:
            half = jnp.zeros((row_count, width), jnp.bfloat16)
            for e in range(replicas):
                half = lax.dynamic_update_slice_in_dim(
                    half, received[2 * e + a], slots[0, e] * block_rows, 0
                )
        halves.append(half.astype(jnp.float32))
    first_up = (halves[0] + halves[1]).astype(jnp.bfloat16)
    upstream = jnp.where(section_id == 0, first_up, part_of(state, 1))
    upstream = jnp.where(is_holder, upstream, from_holders(upstream, 1, every))
    far_up = exchange([upstream] * len(others), every)
    (grad_pre,) = share_call(sz, [upstream, slope], payload)
    far_pre = exchange([grad_pre] * len(others), every)
    far_states_out = [
        jnp.where(section_id < len(late), one, two)
        for one, two in zip(far_late, far_states_out)
    ]
    far_states = {0: far_states_in, 2: far_states_out}

    def far_part(e, which):
        size = size_out if which & 2 else size_in
        both = from_panels(far_states[which & 2][e - 1], size)
        half = both.shape[1] // 2
        return both[:, half:] if which & 1 else both[:, :half]

    def as_delta(left, right, scale):
        return (inner_rate * (dot(left, right, contract_rows) * scale)).astype(jnp.bfloat16)

    def finish(weight, moment, left, right, which, far_left, far_right, scale, pieces, size):
        new_weight, new_moment = outer_mix(
            weight.astype(jnp.float32),
            moment.astype(jnp.float32),
            as_delta(left, right, scale).astype(jnp.float32),
        )
        for e in others:
            back = replicas - e

            def mean(own_array, far_array):
                return 0.5 * (own_array.astype(jnp.float32) + far_array.astype(jnp.float32))

            index = pieces[back]
            own_left = piece(left, index, size, 1)
            part_weight, part_moment = outer_mix(
                mean(piece(weight, index, size), far_part(e, which)),
                mean(piece(moment, index, size), far_part(e, which + 1)),
                mean(
                    as_delta(own_left, right, scale),
                    as_delta(far_left[e - 1], far_right[e - 1], scale),
                ),
            )
            new_weight = lax.dynamic_update_slice_in_dim(new_weight, part_weight, index * size, 0)
            new_moment = lax.dynamic_update_slice_in_dim(new_moment, part_moment, index * size, 0)
        return new_weight[None, None], new_moment[None, None]

    new_weight_b, new_moment_b = finish(
        weight_out, moment_b[0, 0], hidden, upstream, 2, far_hidden, far_up,
        scale_out, pieces_out, size_out,
    )
    new_weight_a, new_moment_a = finish(
        weight_in, moment_a[0, 0], normed, grad_pre, 0, far_normed, far_pre,
        scale_in, pieces_in, size_in,
    )
    return (new_weight_a, new_weight_b, new_moment_a, new_moment_b)


def solution(mesh):
    placed = (
        P("replica", None, None, "shard"),
        P("replica", None, None, "shard"),
        P("replica", "section", None, "shard"),
        P("replica", "section", "shard", None),
        P("replica", "section", None, "shard"),
        P("replica", "section", "shard", None),
        P(),
        P(),
    )
    return jax.shard_map(
        per_device,
        mesh=mesh,
        in_specs=placed,
        out_specs=(
            P("replica", "section", None, "shard"),
            P("replica", "section", "shard", None),
            P("replica", "section", None, "shard"),
            P("replica", "section", "shard", None),
        ),
        check_vma=False,
    )
```

```python
import functools
import math

import jax
import jax.numpy as jnp
from jax import lax
from jax.experimental import pallas as pl
from jax.experimental.pallas import tpu as pltpu
from jax.sharding import PartitionSpec as P

epsilon = 1e-05
inner_rate = 0.5
momentum_decay = 0.9
outer_rate = 0.7

axes = ("replica", "section", "shard")
contract_rows = (((0,), (0,)), ((), ()))
contract_last = (((1,), (1,)), ((), ()))


def dot(left, right, dims=(((1,), (0,)), ((), ()))):
    return lax.dot_general(left, right, dims, preferred_element_type=jnp.float32)


def outer_mix(weight, moment, delta):
    new_moment = momentum_decay * moment + delta
    new_weight = weight - outer_rate * (momentum_decay * new_moment + delta)
    return new_weight.astype(jnp.bfloat16), new_moment.astype(jnp.bfloat16)


def pack_kernel(size, starts, *refs):
    sources, (packed, buffer, read_sems, write_sems) = refs[:-4], refs[-4:]
    rows = pl.ds(pl.multiple_of(starts[0], size), size)
    reads, writes = [], []
    for k, source in enumerate(sources):
        there = pl.ds(k * size, size)
        reads.append(
            pltpu.make_async_copy(source.at[rows], buffer.at[there], read_sems.at[k])
        )
        writes.append(
            pltpu.make_async_copy(buffer.at[there], packed.at[there], write_sems.at[k])
        )
    for copy in reads:
        copy.start()
    for read, write in zip(reads, writes):
        read.wait()
        write.start()
    for copy in writes:
        copy.wait()


def pack(arrays, start, size):
    shape = (len(arrays) * size, arrays[0].shape[1])
    anywhere = pl.BlockSpec(memory_space=pl.ANY)
    return pl.pallas_call(
        functools.partial(pack_kernel, size),
        out_shape=jax.ShapeDtypeStruct(shape, arrays[0].dtype),
        in_specs=[pl.BlockSpec(memory_space=pltpu.SMEM)] + [anywhere] * len(arrays),
        out_specs=anywhere,
        scratch_shapes=[
            pltpu.VMEM(shape, arrays[0].dtype),
            pltpu.SemaphoreType.DMA((len(arrays),)),
            pltpu.SemaphoreType.DMA((len(arrays),)),
        ],
        compiler_params=pltpu.CompilerParams(vmem_limit_bytes=16 * 1024 * 1024),
        cost_estimate=pl.CostEstimate(
            flops=0, bytes_accessed=4 * shape[0] * shape[1], transcendentals=0
        ),
    )(start.reshape(1), *arrays)


class Sizes:
    def __init__(self, sections, row_count, width, local_hidden, panel, hidden_total, blocks):
        self.sections, self.row_count = sections, row_count
        self.width, self.local_hidden, self.panel = width, local_hidden, panel
        self.blocks = blocks
        self.block_rows = row_count // blocks
        self.panels_in = local_hidden // panel
        self.panels_out = width // panel
        self.scale_in = 1.0 / math.sqrt(width)
        self.scale_out = 1.0 / math.sqrt(hidden_total)


def chain_kernel(sz, step, forward, counts, *refs):
    refs = list(refs)

    def take(count):
        taken = refs[:count]
        del refs[:count]
        return taken

    first = forward and step == 0
    parts = 1 if first else 2
    (table,) = take(1)
    received, edges, sources = take(counts[0]), take(counts[1]), take(2 * parts)
    take(0 if first else 1)
    sends = take(counts[2])
    (state,) = take(1)
    weights_in, weights_out, landing, rows, up, out, slope, wide_store = take(8)
    weight_sems, block_sems, edge_sems, send_sems, state_sems = take(5)
    panel, width, hidden_size = sz.panel, sz.width, sz.local_hidden
    links = sz.sections - 1
    whole = pl.ds(0, sz.row_count)

    def weight_copy(d, which):
        weights = (weights_in, weights_out)[which]
        return pltpu.make_async_copy(
            sources[2 * d + which], weights.at[d], weight_sems.at[d, which]
        )

    def place(line, e):
        return pl.ds(pl.multiple_of(table[line, e], sz.block_rows), sz.block_rows)

    def state_part(k, columns):
        return state.at[pl.ds(k * sz.row_count, sz.row_count), pl.ds(0, columns)]

    rows_hbm, up_hbm = state_part(0, width), state_part(1, width)
    slope_hbm = state_part(2, 2 * hidden_size)

    @pl.when(table[links + 1, step] == 1)
    def _():
        sequence = [
            (d, which if forward else 1 - which) for d in range(parts) for which in range(2)
        ]
        arrive = links if forward else step
        first_copies = []
        for i, source in enumerate(received):
            e, a = divmod(i, 2)
            rows_there = whole if len(received) == 2 else place(arrive, e)
            first_copies.append(
                pltpu.make_async_copy(source, landing.at[a, rows_there], block_sems.at[i])
            )
        for d, source in enumerate(edges):
            column = pl.ds(pl.multiple_of(table[links + 2, d], panel), panel)
            first_copies.append(
                pltpu.make_async_copy(source, out.at[:, column], edge_sems.at[d])
            )
        if not forward:
            first_copies.append(pltpu.make_async_copy(rows_hbm, wide_store, state_sems.at[0]))
            first_copies.append(pltpu.make_async_copy(slope_hbm, slope, state_sems.at[1]))
        for copy in first_copies:
            copy.start()
        for item in sequence[:2]:
            weight_copy(*item).start()

        def arrived(item):
            weight_copy(*item).wait()
            later = sequence.index(item) + 2
            if later < len(sequence):
                weight_copy(*sequence[later]).start()

        for copy in first_copies:
            copy.wait()
        if received:
            total = landing[0].astype(jnp.float32) + landing[1].astype(jnp.float32)
            total = total.astype(jnp.bfloat16)
        if forward:
            rows[...] = total if received else out[...]
        elif edges:
            goal = out[...].astype(jnp.float32)
            up[...] = (total.astype(jnp.float32) - goal).astype(jnp.bfloat16)
        else:
            up[...] = total
        if forward:
            wide = rows[...].astype(jnp.float32)
            wide_store[...] = wide
            store_copies = [pltpu.make_async_copy(wide_store, rows_hbm, state_sems.at[2])]
        else:
            wide = wide_store[...]
            up_store = slope.at[:, pl.ds(0, width)]
            store_copies = [pltpu.make_async_copy(up_store, up_hbm, state_sems.at[2])]
        inverse_rms = lax.rsqrt(jnp.mean(wide * wide, axis=1, keepdims=True) + epsilon)
        leads = table[links + 2, 4] == 1
        if forward:
            normed = (wide * inverse_rms).astype(jnp.bfloat16)
            total = [jnp.zeros((sz.row_count, panel), jnp.float32) for _ in range(sz.panels_out)]
            for d in range(parts):
                arrived((d, 0))
                hidden = []
                for p in range(sz.panels_in):
                    weight = weights_in[d, :, p * panel : (p + 1) * panel]
                    preact = dot(normed, weight) * sz.scale_in
                    gate = jax.nn.sigmoid(preact)
                    hidden.append((preact * gate).astype(jnp.bfloat16))
                    column = d * hidden_size + p * panel
                    slope[:, column : column + panel] = gate * (1.0 + preact * (1.0 - gate))
                hidden = jnp.concatenate(hidden, axis=1)
                arrived((d, 1))
                for n in range(sz.panels_out):
                    weight = weights_out[d, :, n * panel : (n + 1) * panel]
                    total[n] = total[n] + dot(hidden, weight)
            total = jnp.concatenate(total, axis=1) * sz.scale_out
            out[...] = (total + jnp.where(leads, wide, 0.0)).astype(jnp.bfloat16)
            store_copies.append(pltpu.make_async_copy(slope, slope_hbm, state_sems.at[1]))
        else:
            up_turned = up[...].T
            total = jnp.zeros((width, sz.row_count), jnp.float32)
            for d in range(parts):
                arrived((d, 1))
                grad_hidden = dot(weights_out[d], up_turned)
                local_slope = slope[:, d * hidden_size : (d + 1) * hidden_size].T
                grad_pre = (grad_hidden * sz.scale_out * local_slope).astype(jnp.bfloat16)
                arrived((d, 0))
                total = total + dot(weights_in[d], grad_pre)
            total = total.T * sz.scale_in
            exact = wide * inverse_rms
            along = jnp.mean(total * exact, axis=1, keepdims=True)
            own = up[...].astype(jnp.float32)
            slope[:, :width] = own
            own = jnp.where(leads, own, 0.0)
            out[...] = (own + inverse_rms * (total - exact * along)).astype(jnp.bfloat16)
        leave = step if forward else links
        send_copies = []
        for e, target in enumerate(sends):
            rows_here = whole if len(sends) == 1 else place(leave, e)
            send_copies.append(
                pltpu.make_async_copy(out.at[rows_here], target, send_sems.at[e])
            )
        for copy in send_copies + store_copies:
            copy.start()
        for copy in send_copies + store_copies:
            copy.wait()


def chain_step(sz, step, forward, table, received, edges, weights, state):
    first = forward and step == 0
    count = 1 if forward and step in (0, sz.sections - 1) else sz.blocks
    anywhere = pl.BlockSpec(memory_space=pl.ANY)
    operands = [table, *received, *edges, *(weights[:2] if first else [*weights, state])]
    block = jax.ShapeDtypeStruct((sz.row_count // count, sz.width), jnp.bfloat16)
    kept = jax.ShapeDtypeStruct((12 * sz.row_count, 2 * sz.local_hidden), jnp.float32)
    shapes = [block] * count + [kept]
    whole = (sz.row_count, sz.width)
    results = pl.pallas_call(
        functools.partial(
            chain_kernel, sz, step, forward, (len(received), len(edges), count)
        ),
        out_shape=shapes,
        in_specs=[pl.BlockSpec(memory_space=pltpu.SMEM)] + [anywhere] * (len(operands) - 1),
        out_specs=[anywhere] * len(shapes),
        input_output_aliases={} if first else {len(operands) - 1: count},
        scratch_shapes=[
            pltpu.VMEM((2, sz.width, sz.local_hidden), jnp.bfloat16),
            pltpu.VMEM((2, sz.local_hidden, sz.width), jnp.bfloat16),
            pltpu.VMEM((2,) + whole, jnp.bfloat16),
            pltpu.VMEM(whole, jnp.bfloat16),
            pltpu.VMEM(whole, jnp.bfloat16),
            pltpu.VMEM(whole, jnp.bfloat16),
            pltpu.VMEM((sz.row_count, 2 * sz.local_hidden), jnp.float32),
            pltpu.VMEM(whole, jnp.float32),
            pltpu.SemaphoreType.DMA((2, 2)),
            pltpu.SemaphoreType.DMA((max(1, len(received)),)),
            pltpu.SemaphoreType.DMA((4,)),
            pltpu.SemaphoreType.DMA((count,)),
            pltpu.SemaphoreType.DMA((3,)),
        ],
        compiler_params=pltpu.CompilerParams(vmem_limit_bytes=32 * 1024 * 1024),
        cost_estimate=pl.CostEstimate(
            flops=8 * sz.row_count * sz.width * sz.local_hidden,
            bytes_accessed=8 * sz.width * sz.local_hidden,
            transcendentals=0,
        ),
    )(*operands)
    return list(results[:count]), results[count]


def share_kernel(sz, whole, *refs):
    if whole:
        known, source, normed_ref, hidden_ref, slope, weights, sem = refs
    else:
        known, slope, source, grad_pre, weights, sem = refs
    panel = sz.panel
    copy = pltpu.make_async_copy(source, weights, sem)
    copy.start()
    if whole:
        wide = known[...].astype(jnp.float32)
        inverse_rms = lax.rsqrt(jnp.mean(wide * wide, axis=1, keepdims=True) + epsilon)
        normed = (wide * inverse_rms).astype(jnp.bfloat16)
        normed_ref[...] = normed
        copy.wait()
        for p in range(sz.panels_in):
            here = slice(p * panel, (p + 1) * panel)
            preact = dot(normed, weights[:, here]) * sz.scale_in
            gate = jax.nn.sigmoid(preact)
            hidden_ref[:, here] = (preact * gate).astype(jnp.bfloat16)
            slope[:, here] = gate * (1.0 + preact * (1.0 - gate))
    else:
        copy.wait()
        grad_hidden = dot(known[...], weights[...], contract_last)
        grad_pre[...] = (grad_hidden * sz.scale_out * slope[...]).astype(jnp.bfloat16)


def share_call(sz, operands, weight):
    whole = len(operands) == 1
    rows_count, hidden_size = sz.row_count, sz.local_hidden
    narrow = jax.ShapeDtypeStruct((rows_count, hidden_size), jnp.bfloat16)
    shapes = [narrow]
    if whole:
        shapes = [
            jax.ShapeDtypeStruct((rows_count, sz.width), jnp.bfloat16),
            narrow,
            jax.ShapeDtypeStruct((rows_count, hidden_size), jnp.float32),
        ]
    inside = pl.BlockSpec(memory_space=pltpu.VMEM)
    return pl.pallas_call(
        functools.partial(share_kernel, sz, whole),
        out_shape=shapes,
        in_specs=[inside] * len(operands) + [pl.BlockSpec(memory_space=pl.ANY)],
        out_specs=[inside] * len(shapes),
        scratch_shapes=[
            pltpu.VMEM(weight.shape, jnp.bfloat16),
            pltpu.SemaphoreType.DMA,
        ],
        compiler_params=pltpu.CompilerParams(vmem_limit_bytes=24 * 1024 * 1024),
        cost_estimate=pl.CostEstimate(
            flops=2 * rows_count * sz.width * hidden_size,
            bytes_accessed=2 * sz.width * hidden_size,
            transcendentals=0,
        ),
    )(*operands, weight)


def per_device(inputs, targets, weight_a, weight_b, moment_a, moment_b, routes, partners):
    replicas = lax.axis_size("replica")
    sections = lax.axis_size("section")
    shards = lax.axis_size("shard")
    replica_id = lax.axis_index("replica")
    section_id = lax.axis_index("section")
    shard_id = lax.axis_index("shard")
    row_count = inputs.shape[2]
    panel = inputs.shape[3]
    width = weight_a.shape[2]
    local_hidden = weight_a.shape[3]
    assert inputs.shape[1] == 1 and shards == 4
    assert local_hidden % panel == 0 and sections > 2
    hidden_total = local_hidden * shards
    scale_in = 1.0 / math.sqrt(width)
    scale_out = 1.0 / math.sqrt(hidden_total)
    weight_in = weight_a[0, 0]
    weight_out = weight_b[0, 0]
    block_rows = row_count // replicas
    links = sections - 1
    in_kernel = block_rows % 16 == 0
    blocks = replicas if in_kernel else 1
    sz = Sizes(sections, row_count, width, local_hidden, panel, hidden_total, blocks)

    def flat(replica, section, shard):
        return (replica * sections + section) * shards + shard

    def turn(section):
        return (section ^ (section >> 1)) & 1

    def holders(section):
        return [j for j in range(shards) if (j & 1) != turn(section)]

    def move(array, sources, target):
        pairs = [
            (flat(r, s, j), flat(*target(r, s, j)))
            for r in range(replicas)
            for s, j in sources
        ]
        return lax.ppermute(array, axes, pairs)

    def holder_sources(active):
        return [(s, j) for s in active for j in holders(s)]

    def to_holders(array, offset, active):
        sources = [(s, j ^ offset) for s, j in holder_sources(active)]
        return move(array, sources, lambda r, s, j: (r, s, j ^ offset))

    def from_holders(array, offset, active):
        return move(array, holder_sources(active), lambda r, s, j: (r, s, j ^ offset))

    def between_holders(array, offset, other_half, section, step):
        shift = turn(section) ^ turn(section + step) ^ (2 * other_half)
        return move(
            array,
            holder_sources([section]),
            lambda r, s, j: ((r + offset) % replicas, s + step, j ^ shift),
        )

    def across_replicas(array, offset, active):
        return move(
            array,
            [(s, j) for s in active for j in range(shards)],
            lambda r, s, j: ((r + offset) % replicas, s, j),
        )

    every = range(sections)
    others = range(1, replicas)
    is_holder = (shard_id & 1) != turn(section_id)

    edge = jnp.where(section_id == 0, inputs[0, 0], targets[0, 0])
    ends = [(s, j) for s in (0, links) for j in range(shards)]
    edges = [edge] + [
        move(edge, ends, lambda r, s, j, d=d: (r, s, j ^ d)) for d in range(1, shards)
    ]
    rest = range(1, sections)
    near = [to_holders(weight_in, 1, rest), to_holders(weight_out, 1, rest)]

    tables = lax.dynamic_index_in_dim(partners, section_id, 0, keepdims=False)

    def piece_of(table, offset):
        wanted = (replica_id + offset) % replicas
        return jnp.argmax(table[:, replica_id] == wanted).astype(jnp.int32)

    pieces_in = [piece_of(tables[0], e) for e in range(replicas)]
    pieces_out = [piece_of(tables[1], e) for e in range(replicas)]
    size_in = width // replicas
    size_out = local_hidden // replicas

    def piece(array, index, size, axis=0):
        return lax.dynamic_slice_in_dim(array, index * size, size, axis)

    def exchange(arrays, active):
        return [across_replicas(array, e, active) for e, array in zip(others, arrays)]

    packed_in = [
        pack([weight_in, moment_a[0, 0]], pieces_in[e] * size_in, size_in) for e in others
    ]
    packed_out = [
        pack([weight_out, moment_b[0, 0]], pieces_out[e] * size_out, size_out) for e in others
    ]
    early = range(sections // 2, sections)
    late = range(sections // 2)
    far_states_in = exchange(packed_in, every)

    offsets = jnp.arange(replicas, dtype=jnp.int32)
    there = (replica_id + offsets) % replicas
    back = (replica_id - offsets) % replicas
    own_routes = routes[0, :, replica_id, :]
    slots = jnp.sum(
        (own_routes[:, None, :] == there[None, :, None]).astype(jnp.int32)
        * offsets[None, None, :],
        axis=2,
    )
    columns = max(replicas, sections, shards + 1)
    steps = jnp.arange(sections)
    ours = ((is_holder | (steps == 0)) & (section_id == steps)).astype(jnp.int32)
    features = (shard_id ^ jnp.arange(shards, dtype=jnp.int32)) * panel
    leads = (is_holder & ((shard_id & 2) == 0)).astype(jnp.int32)
    features = jnp.append(features, leads)

    def line(values):
        return jnp.pad(values, ((0, 0), (0, columns - values.shape[1])))

    starts = jnp.concatenate([slots, back[None]]) * block_rows
    if not in_kernel:
        starts = jnp.zeros_like(starts)
    table = jnp.concatenate([line(starts), line(ours[None]), line(features[None])])
    table = table.astype(jnp.int32)

    def send_blocks(sends, arrived, left, section, step):
        sign = step
        if in_kernel:
            return [
                between_holders(sends[e], sign * e, a, section, step)
                for e in range(replicas)
                for a in range(2)
            ]
        parts = sends[0].reshape(replicas, block_rows, width)
        moved = [jnp.zeros_like(parts), jnp.zeros_like(parts)]
        for e in range(replicas):
            chosen = lax.dynamic_index_in_dim(parts, left[e], 0, keepdims=False)
            for a in range(2):
                got = between_holders(chosen, sign * e, a, section, step)
                moved[a] = lax.dynamic_update_index_in_dim(moved[a], got, arrived[e], 0)
        return [one.reshape(row_count, width) for one in moved]

    def part_of(state, k):
        return state[k * row_count : (k + 1) * row_count, :width].astype(jnp.bfloat16)

    row_parts = []

    def spread_rows(received, state, active):
        received, rows, row_parts[:] = lax.optimization_barrier(
            (received, part_of(state, 0), row_parts)
        )
        row_parts.append(from_holders(rows, 1, active))
        return received

    weights = [weight_in, weight_out, *near]
    received, state = [], None
    for step in every:
        sends, state = chain_step(
            sz, step, True, table, received, edges if step == 0 else [], weights, state
        )
        if step == 0:
            total = sends[0].astype(jnp.float32)
            total = total + to_holders(sends[0], 1, [0]).astype(jnp.float32)
            sends = [total.astype(jnp.bfloat16)]
            if in_kernel:
                sends = [piece(sends[0], slots[0, e], block_rows) for e in range(replicas)]
        if step < links:
            received = send_blocks(sends, back, slots[step], step, 1)
            if step == 0:
                received, far_states_in, packed_out = lax.optimization_barrier(
                    (received, far_states_in, packed_out)
                )
                far_states_out = exchange(packed_out, early)
        else:
            received = [sends[0], from_holders(sends[0], 2, [links])]
        if len(late) - 1 <= step < links:
            received = spread_rows(received, state, late if step < len(late) else [step])
        if step == len(late) - 1:
            received, packed_out = lax.optimization_barrier((received, packed_out))
            far_late = exchange(packed_out, late)
        if step == len(late):
            received, far_states_out = lax.optimization_barrier((received, far_states_out))

    for step in reversed(range(1, sections)):
        sends, state = chain_step(
            sz, step, False, table, received, edges if step == links else [], weights, state
        )
        received = send_blocks(sends, slots[step - 1], back, step, -1)
        if step == links:
            received = spread_rows(received, state, [links])
        if step == len(late):
            received, far_late, row_parts = lax.optimization_barrier(
                (received, far_late, row_parts)
            )

    own_rows = jnp.where(is_holder, part_of(state, 0), sum(row_parts[1:], row_parts[0]))
    normed, hidden, slope = share_call(sz, [own_rows], weight_in)

    def bundle(e):
        first, second = normed, hidden
        first = piece(first, pieces_in[e], size_in, 1)
        return jnp.concatenate([first, piece(second, pieces_out[e], size_out, 1)], axis=1)

    bundles = exchange([bundle(e) for e in others], every)
    received, bundles = lax.optimization_barrier((received, bundles))
    far_normed = [one[:, :size_in] for one in bundles]
    far_hidden = [one[:, size_in:] for one in bundles]

    halves = []
    for a in range(2):
        half = received[a]
        if in_kernel:
            half = jnp.zeros((row_count, width), jnp.bfloat16)
            for e in range(replicas):
                half = lax.dynamic_update_slice_in_dim(
                    half, received[2 * e + a], slots[0, e] * block_rows, 0
                )
        halves.append(half.astype(jnp.float32))
    first_up = (halves[0] + halves[1]).astype(jnp.bfloat16)
    upstream = jnp.where(section_id == 0, first_up, part_of(state, 1))
    upstream = jnp.where(is_holder, upstream, from_holders(upstream, 1, every))
    far_up = exchange([upstream] * len(others), every)
    (grad_pre,) = share_call(sz, [upstream, slope], weight_out)
    far_pre = exchange([grad_pre] * len(others), every)
    far_states_out = [
        jnp.where(section_id < len(late), one, two)
        for one, two in zip(far_late, far_states_out)
    ]
    far_states = {0: far_states_in, 2: far_states_out}

    def far_part(e, which):
        size = size_out if which & 2 else size_in
        both = far_states[which & 2][e - 1]
        return both[size:] if which & 1 else both[:size]

    def as_delta(left, right, scale):
        return (inner_rate * (dot(left, right, contract_rows) * scale)).astype(jnp.bfloat16)

    def finish(weight, moment, left, right, which, far_left, far_right, scale, pieces, size):
        new_weight, new_moment = outer_mix(
            weight.astype(jnp.float32),
            moment.astype(jnp.float32),
            as_delta(left, right, scale).astype(jnp.float32),
        )
        for e in others:
            back = replicas - e

            def mean(own_array, far_array):
                return 0.5 * (own_array.astype(jnp.float32) + far_array.astype(jnp.float32))

            index = pieces[back]
            own_left = piece(left, index, size, 1)
            part_weight, part_moment = outer_mix(
                mean(piece(weight, index, size), far_part(e, which)),
                mean(piece(moment, index, size), far_part(e, which + 1)),
                mean(
                    as_delta(own_left, right, scale),
                    as_delta(far_left[e - 1], far_right[e - 1], scale),
                ),
            )
            new_weight = lax.dynamic_update_slice_in_dim(new_weight, part_weight, index * size, 0)
            new_moment = lax.dynamic_update_slice_in_dim(new_moment, part_moment, index * size, 0)
        return new_weight[None, None], new_moment[None, None]

    new_weight_b, new_moment_b = finish(
        weight_out, moment_b[0, 0], hidden, upstream, 2, far_hidden, far_up,
        scale_out, pieces_out, size_out,
    )
    new_weight_a, new_moment_a = finish(
        weight_in, moment_a[0, 0], normed, grad_pre, 0, far_normed, far_pre,
        scale_in, pieces_in, size_in,
    )
    return (new_weight_a, new_weight_b, new_moment_a, new_moment_b)


def solution(mesh):
    placed = (
        P("replica", None, None, "shard"),
        P("replica", None, None, "shard"),
        P("replica", "section", None, "shard"),
        P("replica", "section", "shard", None),
        P("replica", "section", None, "shard"),
        P("replica", "section", "shard", None),
        P(),
        P(),
    )
    return jax.shard_map(
        per_device,
        mesh=mesh,
        in_specs=placed,
        out_specs=(
            P("replica", "section", None, "shard"),
            P("replica", "section", "shard", None),
            P("replica", "section", None, "shard"),
            P("replica", "section", "shard", None),
        ),
        check_vma=False,
    )
```

```python
import functools
import math

import jax
import jax.numpy as jnp
from jax import lax
from jax.experimental import pallas as pl
from jax.experimental.pallas import tpu as pltpu
from jax.sharding import PartitionSpec as P

epsilon = 1e-05
inner_rate = 0.5
momentum_decay = 0.9
outer_rate = 0.7

axes = ("replica", "section", "shard")
contract_rows = (((0,), (0,)), ((), ()))
contract_last = (((1,), (1,)), ((), ()))


def dot(left, right, dims=(((1,), (0,)), ((), ()))):
    return lax.dot_general(left, right, dims, preferred_element_type=jnp.float32)


def outer_mix(weight, moment, delta):
    new_moment = momentum_decay * moment + delta
    new_weight = weight - outer_rate * (momentum_decay * new_moment + delta)
    return new_weight.astype(jnp.bfloat16), new_moment.astype(jnp.bfloat16)


def pack_kernel(size, starts, *refs):
    sources, (packed, buffer, read_sems, write_sems) = refs[:-4], refs[-4:]
    rows = pl.ds(pl.multiple_of(starts[0], size), size)
    reads, writes = [], []
    for k, source in enumerate(sources):
        there = pl.ds(k * size, size)
        reads.append(
            pltpu.make_async_copy(source.at[rows], buffer.at[there], read_sems.at[k])
        )
        writes.append(
            pltpu.make_async_copy(buffer.at[there], packed.at[there], write_sems.at[k])
        )
    for copy in reads:
        copy.start()
    for read, write in zip(reads, writes):
        read.wait()
        write.start()
    for copy in writes:
        copy.wait()


def pack(arrays, start, size):
    shape = (len(arrays) * size, arrays[0].shape[1])
    anywhere = pl.BlockSpec(memory_space=pl.ANY)
    return pl.pallas_call(
        functools.partial(pack_kernel, size),
        out_shape=jax.ShapeDtypeStruct(shape, arrays[0].dtype),
        in_specs=[pl.BlockSpec(memory_space=pltpu.SMEM)] + [anywhere] * len(arrays),
        out_specs=anywhere,
        scratch_shapes=[
            pltpu.VMEM(shape, arrays[0].dtype),
            pltpu.SemaphoreType.DMA((len(arrays),)),
            pltpu.SemaphoreType.DMA((len(arrays),)),
        ],
        compiler_params=pltpu.CompilerParams(vmem_limit_bytes=16 * 1024 * 1024),
        cost_estimate=pl.CostEstimate(
            flops=0, bytes_accessed=4 * shape[0] * shape[1], transcendentals=0
        ),
    )(start.reshape(1), *arrays)


class Sizes:
    def __init__(self, sections, row_count, width, local_hidden, panel, hidden_total, blocks):
        self.sections, self.row_count = sections, row_count
        self.width, self.local_hidden, self.panel = width, local_hidden, panel
        self.blocks = blocks
        self.block_rows = row_count // blocks
        self.panels_in = local_hidden // panel
        self.panels_out = width // panel
        self.scale_in = 1.0 / math.sqrt(width)
        self.scale_out = 1.0 / math.sqrt(hidden_total)


def chain_kernel(sz, step, forward, counts, *refs):
    refs = list(refs)

    def take(count):
        taken = refs[:count]
        del refs[:count]
        return taken

    first = forward and step == 0
    parts = 1 if first else 2
    (table,) = take(1)
    received, edges, sources = take(counts[0]), take(counts[1]), take(2 * parts)
    take(0 if first else 1)
    sends = take(counts[2])
    fresh_hbm, state = take(2)
    weights_in, weights_out, landing, rows, up, out, slope, wide_store = take(8)
    weight_sems, block_sems, edge_sems, send_sems, state_sems = take(5)
    panel, width, hidden_size = sz.panel, sz.width, sz.local_hidden
    links = sz.sections - 1
    whole = pl.ds(0, sz.row_count)

    def weight_copy(d, which):
        weights = (weights_in, weights_out)[which]
        return pltpu.make_async_copy(
            sources[2 * d + which], weights.at[d], weight_sems.at[d, which]
        )

    def place(line, e):
        return pl.ds(pl.multiple_of(table[line, e], sz.block_rows), sz.block_rows)

    def state_part(k, columns):
        return state.at[pl.ds(k * sz.row_count, sz.row_count), pl.ds(0, columns)]

    rows_hbm, slope_hbm = state_part(0, width), state_part(1, 2 * hidden_size)

    @pl.when(table[links + 1, step] == 1)
    def _():
        sequence = [
            (d, which if forward else 1 - which) for d in range(parts) for which in range(2)
        ]
        arrive = links if forward else step
        first_copies = []
        for i, source in enumerate(received):
            e, a = divmod(i, 2)
            rows_there = whole if len(received) == 2 else place(arrive, e)
            first_copies.append(
                pltpu.make_async_copy(source, landing.at[a, rows_there], block_sems.at[i])
            )
        for d, source in enumerate(edges):
            column = pl.ds(pl.multiple_of(table[links + 2, d], panel), panel)
            first_copies.append(
                pltpu.make_async_copy(source, out.at[:, column], edge_sems.at[d])
            )
        if not forward:
            first_copies.append(pltpu.make_async_copy(rows_hbm, wide_store, state_sems.at[0]))
            first_copies.append(pltpu.make_async_copy(slope_hbm, slope, state_sems.at[1]))
        for copy in first_copies:
            copy.start()
        for item in sequence[:2]:
            weight_copy(*item).start()

        def arrived(item):
            weight_copy(*item).wait()
            later = sequence.index(item) + 2
            if later < len(sequence):
                weight_copy(*sequence[later]).start()

        for copy in first_copies:
            copy.wait()
        if received:
            total = landing[0].astype(jnp.float32) + landing[1].astype(jnp.float32)
            total = total.astype(jnp.bfloat16)
        if forward:
            rows[...] = total if received else out[...]
        elif edges:
            goal = out[...].astype(jnp.float32)
            up[...] = (total.astype(jnp.float32) - goal).astype(jnp.bfloat16)
        else:
            up[...] = total
        fresh = rows if forward else up
        store_copies = [pltpu.make_async_copy(fresh, fresh_hbm, state_sems.at[2])]
        if forward:
            wide = rows[...].astype(jnp.float32)
            wide_store[...] = wide
            store_copies.append(pltpu.make_async_copy(wide_store, rows_hbm, state_sems.at[0]))
        else:
            wide = wide_store[...]
        inverse_rms = lax.rsqrt(jnp.mean(wide * wide, axis=1, keepdims=True) + epsilon)
        leads = table[links + 2, 4] == 1
        if forward:
            normed = (wide * inverse_rms).astype(jnp.bfloat16)
            total = [jnp.zeros((sz.row_count, panel), jnp.float32) for _ in range(sz.panels_out)]
            for d in range(parts):
                arrived((d, 0))
                hidden = []
                for p in range(sz.panels_in):
                    weight = weights_in[d, :, p * panel : (p + 1) * panel]
                    preact = dot(normed, weight) * sz.scale_in
                    gate = jax.nn.sigmoid(preact)
                    hidden.append((preact * gate).astype(jnp.bfloat16))
                    column = d * hidden_size + p * panel
                    slope[:, column : column + panel] = gate * (1.0 + preact * (1.0 - gate))
                hidden = jnp.concatenate(hidden, axis=1)
                arrived((d, 1))
                for n in range(sz.panels_out):
                    weight = weights_out[d, :, n * panel : (n + 1) * panel]
                    total[n] = total[n] + dot(hidden, weight)
            total = jnp.concatenate(total, axis=1) * sz.scale_out
            out[...] = (total + jnp.where(leads, wide, 0.0)).astype(jnp.bfloat16)
            store_copies.append(pltpu.make_async_copy(slope, slope_hbm, state_sems.at[1]))
        else:
            up_turned = up[...].T
            total = jnp.zeros((width, sz.row_count), jnp.float32)
            for d in range(parts):
                arrived((d, 1))
                grad_hidden = dot(weights_out[d], up_turned)
                local_slope = slope[:, d * hidden_size : (d + 1) * hidden_size].T
                grad_pre = (grad_hidden * sz.scale_out * local_slope).astype(jnp.bfloat16)
                arrived((d, 0))
                total = total + dot(weights_in[d], grad_pre)
            total = total.T * sz.scale_in
            exact = wide * inverse_rms
            along = jnp.mean(total * exact, axis=1, keepdims=True)
            own = jnp.where(leads, up[...].astype(jnp.float32), 0.0)
            out[...] = (own + inverse_rms * (total - exact * along)).astype(jnp.bfloat16)
        leave = step if forward else links
        send_copies = []
        for e, target in enumerate(sends):
            rows_here = whole if len(sends) == 1 else place(leave, e)
            send_copies.append(
                pltpu.make_async_copy(out.at[rows_here], target, send_sems.at[e])
            )
        for copy in send_copies + store_copies:
            copy.start()
        for copy in send_copies + store_copies:
            copy.wait()


def chain_step(sz, step, forward, table, received, edges, weights, state):
    first = forward and step == 0
    count = 1 if forward and step in (0, sz.sections - 1) else sz.blocks
    anywhere = pl.BlockSpec(memory_space=pl.ANY)
    operands = [table, *received, *edges, *(weights[:2] if first else [*weights, state])]
    block = jax.ShapeDtypeStruct((sz.row_count // count, sz.width), jnp.bfloat16)
    kept = jax.ShapeDtypeStruct((2 * sz.row_count, 2 * sz.local_hidden), jnp.float32)
    fresh = jax.ShapeDtypeStruct((sz.row_count, sz.width), jnp.bfloat16)
    shapes = [block] * count + [fresh, kept]
    in_hbm = pl.BlockSpec(memory_space=pltpu.HBM)
    in_specs = [pl.BlockSpec(memory_space=pltpu.SMEM)] + [anywhere] * (len(operands) - 1)
    if not first:
        in_specs[-1] = in_hbm
    whole = (sz.row_count, sz.width)
    results = pl.pallas_call(
        functools.partial(
            chain_kernel, sz, step, forward, (len(received), len(edges), count)
        ),
        out_shape=shapes,
        in_specs=in_specs,
        out_specs=[anywhere] * (count + 1) + [in_hbm],
        input_output_aliases={} if first else {len(operands) - 1: count + 1},
        scratch_shapes=[
            pltpu.VMEM((2, sz.width, sz.local_hidden), jnp.bfloat16),
            pltpu.VMEM((2, sz.local_hidden, sz.width), jnp.bfloat16),
            pltpu.VMEM((2,) + whole, jnp.bfloat16),
            pltpu.VMEM(whole, jnp.bfloat16),
            pltpu.VMEM(whole, jnp.bfloat16),
            pltpu.VMEM(whole, jnp.bfloat16),
            pltpu.VMEM((sz.row_count, 2 * sz.local_hidden), jnp.float32),
            pltpu.VMEM(whole, jnp.float32),
            pltpu.SemaphoreType.DMA((2, 2)),
            pltpu.SemaphoreType.DMA((max(1, len(received)),)),
            pltpu.SemaphoreType.DMA((4,)),
            pltpu.SemaphoreType.DMA((count,)),
            pltpu.SemaphoreType.DMA((3,)),
        ],
        compiler_params=pltpu.CompilerParams(vmem_limit_bytes=32 * 1024 * 1024),
        cost_estimate=pl.CostEstimate(
            flops=8 * sz.row_count * sz.width * sz.local_hidden,
            bytes_accessed=8 * sz.width * sz.local_hidden,
            transcendentals=0,
        ),
    )(*operands)
    return list(results[:count]), results[count], results[count + 1]


def share_kernel(sz, whole, *refs):
    if whole:
        known, source, normed_ref, hidden_ref, slope, weights, sem = refs
    else:
        known, slope, source, grad_pre, weights, sem = refs
    panel = sz.panel
    copy = pltpu.make_async_copy(source, weights, sem)
    copy.start()
    if whole:
        wide = known[...].astype(jnp.float32)
        inverse_rms = lax.rsqrt(jnp.mean(wide * wide, axis=1, keepdims=True) + epsilon)
        normed = (wide * inverse_rms).astype(jnp.bfloat16)
        normed_ref[...] = normed
        copy.wait()
        for p in range(sz.panels_in):
            here = slice(p * panel, (p + 1) * panel)
            preact = dot(normed, weights[:, here]) * sz.scale_in
            gate = jax.nn.sigmoid(preact)
            hidden_ref[:, here] = (preact * gate).astype(jnp.bfloat16)
            slope[:, here] = gate * (1.0 + preact * (1.0 - gate))
    else:
        copy.wait()
        grad_hidden = dot(known[...], weights[...], contract_last)
        grad_pre[...] = (grad_hidden * sz.scale_out * slope[...]).astype(jnp.bfloat16)


def share_call(sz, operands, weight):
    whole = len(operands) == 1
    rows_count, hidden_size = sz.row_count, sz.local_hidden
    narrow = jax.ShapeDtypeStruct((rows_count, hidden_size), jnp.bfloat16)
    shapes = [narrow]
    if whole:
        shapes = [
            jax.ShapeDtypeStruct((rows_count, sz.width), jnp.bfloat16),
            narrow,
            jax.ShapeDtypeStruct((rows_count, hidden_size), jnp.float32),
        ]
    inside = pl.BlockSpec(memory_space=pltpu.VMEM)
    return pl.pallas_call(
        functools.partial(share_kernel, sz, whole),
        out_shape=shapes,
        in_specs=[inside] * len(operands) + [pl.BlockSpec(memory_space=pl.ANY)],
        out_specs=[inside] * len(shapes),
        scratch_shapes=[
            pltpu.VMEM(weight.shape, jnp.bfloat16),
            pltpu.SemaphoreType.DMA,
        ],
        compiler_params=pltpu.CompilerParams(vmem_limit_bytes=24 * 1024 * 1024),
        cost_estimate=pl.CostEstimate(
            flops=2 * rows_count * sz.width * hidden_size,
            bytes_accessed=2 * sz.width * hidden_size,
            transcendentals=0,
        ),
    )(*operands, weight)


def per_device(inputs, targets, weight_a, weight_b, moment_a, moment_b, routes, partners):
    replicas = lax.axis_size("replica")
    sections = lax.axis_size("section")
    shards = lax.axis_size("shard")
    replica_id = lax.axis_index("replica")
    section_id = lax.axis_index("section")
    shard_id = lax.axis_index("shard")
    row_count = inputs.shape[2]
    panel = inputs.shape[3]
    width = weight_a.shape[2]
    local_hidden = weight_a.shape[3]
    assert inputs.shape[1] == 1 and shards == 4
    assert local_hidden % panel == 0 and sections > 2
    hidden_total = local_hidden * shards
    scale_in = 1.0 / math.sqrt(width)
    scale_out = 1.0 / math.sqrt(hidden_total)
    weight_in = weight_a[0, 0]
    weight_out = weight_b[0, 0]
    block_rows = row_count // replicas
    links = sections - 1
    in_kernel = block_rows % 16 == 0
    blocks = replicas if in_kernel else 1
    sz = Sizes(sections, row_count, width, local_hidden, panel, hidden_total, blocks)

    def flat(replica, section, shard):
        return (replica * sections + section) * shards + shard

    def turn(section):
        return (section ^ (section >> 1)) & 1

    def holders(section):
        return [j for j in range(shards) if (j & 1) != turn(section)]

    def move(array, sources, target):
        pairs = [
            (flat(r, s, j), flat(*target(r, s, j)))
            for r in range(replicas)
            for s, j in sources
        ]
        return lax.ppermute(array, axes, pairs)

    def holder_sources(active):
        return [(s, j) for s in active for j in holders(s)]

    def to_holders(array, offset, active):
        sources = [(s, j ^ offset) for s, j in holder_sources(active)]
        return move(array, sources, lambda r, s, j: (r, s, j ^ offset))

    def from_holders(array, offset, active):
        return move(array, holder_sources(active), lambda r, s, j: (r, s, j ^ offset))

    def between_holders(array, offset, other_half, section, step):
        shift = turn(section) ^ turn(section + step) ^ (2 * other_half)
        return move(
            array,
            holder_sources([section]),
            lambda r, s, j: ((r + offset) % replicas, s + step, j ^ shift),
        )

    def across_replicas(array, offset, active):
        return move(
            array,
            [(s, j) for s in active for j in range(shards)],
            lambda r, s, j: ((r + offset) % replicas, s, j),
        )

    every = range(sections)
    others = range(1, replicas)
    is_holder = (shard_id & 1) != turn(section_id)

    edge = jnp.where(section_id == 0, inputs[0, 0], targets[0, 0])
    ends = [(s, j) for s in (0, links) for j in range(shards)]
    edges = [edge] + [
        move(edge, ends, lambda r, s, j, d=d: (r, s, j ^ d)) for d in range(1, shards)
    ]
    rest = range(1, sections)
    near = [to_holders(weight_in, 1, rest), to_holders(weight_out, 1, rest)]

    tables = lax.dynamic_index_in_dim(partners, section_id, 0, keepdims=False)

    def piece_of(table, offset):
        wanted = (replica_id + offset) % replicas
        return jnp.argmax(table[:, replica_id] == wanted).astype(jnp.int32)

    pieces_in = [piece_of(tables[0], e) for e in range(replicas)]
    pieces_out = [piece_of(tables[1], e) for e in range(replicas)]
    size_in = width // replicas
    size_out = local_hidden // replicas

    def piece(array, index, size, axis=0):
        return lax.dynamic_slice_in_dim(array, index * size, size, axis)

    def exchange(arrays, active):
        return [across_replicas(array, e, active) for e, array in zip(others, arrays)]

    packed_in = [
        pack([weight_in, moment_a[0, 0]], pieces_in[e] * size_in, size_in) for e in others
    ]
    packed_out = [
        pack([weight_out, moment_b[0, 0]], pieces_out[e] * size_out, size_out) for e in others
    ]
    early = range(sections // 2, sections)
    late = range(sections // 2)
    far_states_in = exchange(packed_in, every)

    offsets = jnp.arange(replicas, dtype=jnp.int32)
    there = (replica_id + offsets) % replicas
    back = (replica_id - offsets) % replicas
    own_routes = routes[0, :, replica_id, :]
    slots = jnp.sum(
        (own_routes[:, None, :] == there[None, :, None]).astype(jnp.int32)
        * offsets[None, None, :],
        axis=2,
    )
    columns = max(replicas, sections, shards + 1)
    steps = jnp.arange(sections)
    ours = ((is_holder | (steps == 0)) & (section_id == steps)).astype(jnp.int32)
    features = (shard_id ^ jnp.arange(shards, dtype=jnp.int32)) * panel
    leads = (is_holder & ((shard_id & 2) == 0)).astype(jnp.int32)
    features = jnp.append(features, leads)

    def line(values):
        return jnp.pad(values, ((0, 0), (0, columns - values.shape[1])))

    starts = jnp.concatenate([slots, back[None]]) * block_rows
    if not in_kernel:
        starts = jnp.zeros_like(starts)
    table = jnp.concatenate([line(starts), line(ours[None]), line(features[None])])
    table = table.astype(jnp.int32)

    def send_blocks(sends, arrived, left, section, step):
        sign = step
        if in_kernel:
            return [
                between_holders(sends[e], sign * e, a, section, step)
                for e in range(replicas)
                for a in range(2)
            ]
        parts = sends[0].reshape(replicas, block_rows, width)
        moved = [jnp.zeros_like(parts), jnp.zeros_like(parts)]
        for e in range(replicas):
            chosen = lax.dynamic_index_in_dim(parts, left[e], 0, keepdims=False)
            for a in range(2):
                got = between_holders(chosen, sign * e, a, section, step)
                moved[a] = lax.dynamic_update_index_in_dim(moved[a], got, arrived[e], 0)
        return [one.reshape(row_count, width) for one in moved]

    row_parts = []

    def spread_rows(received, rows, active):
        received, rows, row_parts[:] = lax.optimization_barrier(
            (received, rows, row_parts)
        )
        row_parts.append(from_holders(rows, 1, active))
        return received

    weights = [weight_in, weight_out, *near]
    received, state = [], None
    for step in every:
        sends, fresh, state = chain_step(
            sz, step, True, table, received, edges if step == 0 else [], weights, state
        )
        rows = fresh if step == 0 else jnp.where(section_id == step, fresh, rows)
        if step == 0:
            total = sends[0].astype(jnp.float32)
            total = total + to_holders(sends[0], 1, [0]).astype(jnp.float32)
            sends = [total.astype(jnp.bfloat16)]
            if in_kernel:
                sends = [piece(sends[0], slots[0, e], block_rows) for e in range(replicas)]
        if step < links:
            received = send_blocks(sends, back, slots[step], step, 1)
            if step == 0:
                received, far_states_in, packed_out = lax.optimization_barrier(
                    (received, far_states_in, packed_out)
                )
                far_states_out = exchange(packed_out, early)
        else:
            received = [sends[0], from_holders(sends[0], 2, [links])]
        if len(late) - 1 <= step < links:
            received = spread_rows(received, rows, late if step < len(late) else [step])
        if step == len(late) - 1:
            received, packed_out = lax.optimization_barrier((received, packed_out))
            far_late = exchange(packed_out, late)
        if step == len(late):
            received, far_states_out = lax.optimization_barrier((received, far_states_out))

    for step in reversed(range(1, sections)):
        sends, fresh, state = chain_step(
            sz, step, False, table, received, edges if step == links else [], weights, state
        )
        upstream = fresh if step == links else jnp.where(section_id == step, fresh, upstream)
        received = send_blocks(sends, slots[step - 1], back, step, -1)
        if step == links:
            received = spread_rows(received, rows, [links])
        if step == len(late):
            received, far_late, row_parts = lax.optimization_barrier(
                (received, far_late, row_parts)
            )

    own_rows = jnp.where(is_holder, rows, sum(row_parts[1:], row_parts[0]))
    normed, hidden, slope = share_call(sz, [own_rows], weight_in)

    def bundle(e):
        first, second = normed, hidden
        first = piece(first, pieces_in[e], size_in, 1)
        return jnp.concatenate([first, piece(second, pieces_out[e], size_out, 1)], axis=1)

    bundles = exchange([bundle(e) for e in others], every)
    received, bundles = lax.optimization_barrier((received, bundles))
    far_normed = [one[:, :size_in] for one in bundles]
    far_hidden = [one[:, size_in:] for one in bundles]

    halves = []
    for a in range(2):
        half = received[a]
        if in_kernel:
            half = jnp.zeros((row_count, width), jnp.bfloat16)
            for e in range(replicas):
                half = lax.dynamic_update_slice_in_dim(
                    half, received[2 * e + a], slots[0, e] * block_rows, 0
                )
        halves.append(half.astype(jnp.float32))
    first_up = (halves[0] + halves[1]).astype(jnp.bfloat16)
    upstream = jnp.where(section_id == 0, first_up, upstream)
    upstream = jnp.where(is_holder, upstream, from_holders(upstream, 1, every))
    far_up = exchange([upstream] * len(others), every)
    (grad_pre,) = share_call(sz, [upstream, slope], weight_out)
    far_pre = exchange([grad_pre] * len(others), every)
    far_states_out = [
        jnp.where(section_id < len(late), one, two)
        for one, two in zip(far_late, far_states_out)
    ]
    far_states = {0: far_states_in, 2: far_states_out}

    def far_part(e, which):
        size = size_out if which & 2 else size_in
        both = far_states[which & 2][e - 1]
        return both[size:] if which & 1 else both[:size]

    def as_delta(left, right, scale):
        return (inner_rate * (dot(left, right, contract_rows) * scale)).astype(jnp.bfloat16)

    def finish(weight, moment, left, right, which, far_left, far_right, scale, pieces, size):
        new_weight, new_moment = outer_mix(
            weight.astype(jnp.float32),
            moment.astype(jnp.float32),
            as_delta(left, right, scale).astype(jnp.float32),
        )
        for e in others:
            back = replicas - e

            def mean(own_array, far_array):
                return 0.5 * (own_array.astype(jnp.float32) + far_array.astype(jnp.float32))

            index = pieces[back]
            own_left = piece(left, index, size, 1)
            part_weight, part_moment = outer_mix(
                mean(piece(weight, index, size), far_part(e, which)),
                mean(piece(moment, index, size), far_part(e, which + 1)),
                mean(
                    as_delta(own_left, right, scale),
                    as_delta(far_left[e - 1], far_right[e - 1], scale),
                ),
            )
            new_weight = lax.dynamic_update_slice_in_dim(new_weight, part_weight, index * size, 0)
            new_moment = lax.dynamic_update_slice_in_dim(new_moment, part_moment, index * size, 0)
        return new_weight[None, None], new_moment[None, None]

    new_weight_b, new_moment_b = finish(
        weight_out, moment_b[0, 0], hidden, upstream, 2, far_hidden, far_up,
        scale_out, pieces_out, size_out,
    )
    new_weight_a, new_moment_a = finish(
        weight_in, moment_a[0, 0], normed, grad_pre, 0, far_normed, far_pre,
        scale_in, pieces_in, size_in,
    )
    return (new_weight_a, new_weight_b, new_moment_a, new_moment_b)


def solution(mesh):
    placed = (
        P("replica", None, None, "shard"),
        P("replica", None, None, "shard"),
        P("replica", "section", None, "shard"),
        P("replica", "section", "shard", None),
        P("replica", "section", None, "shard"),
        P("replica", "section", "shard", None),
        P(),
        P(),
    )
    return jax.shard_map(
        per_device,
        mesh=mesh,
        in_specs=placed,
        out_specs=(
            P("replica", "section", None, "shard"),
            P("replica", "section", "shard", None),
            P("replica", "section", None, "shard"),
            P("replica", "section", "shard", None),
        ),
        check_vma=False,
    )
```

```python
import functools
import math

import jax
import jax.numpy as jnp
from jax import lax
from jax.experimental import pallas as pl
from jax.experimental.pallas import tpu as pltpu
from jax.sharding import PartitionSpec as P

epsilon = 1e-05
inner_rate = 0.5
momentum_decay = 0.9
outer_rate = 0.7

axes = ("replica", "section", "shard")
contract_rows = (((0,), (0,)), ((), ()))
contract_last = (((1,), (1,)), ((), ()))


def dot(left, right, dims=(((1,), (0,)), ((), ()))):
    return lax.dot_general(left, right, dims, preferred_element_type=jnp.float32)


def outer_mix(weight, moment, delta):
    new_moment = momentum_decay * moment + delta
    new_weight = weight - outer_rate * (momentum_decay * new_moment + delta)
    return new_weight.astype(jnp.bfloat16), new_moment.astype(jnp.bfloat16)


def pack_kernel(size, starts, *refs):
    sources, (packed, buffer, read_sems, write_sems) = refs[:-4], refs[-4:]
    rows = pl.ds(pl.multiple_of(starts[0], size), size)
    reads, writes = [], []
    for k, source in enumerate(sources):
        there = pl.ds(k * size, size)
        reads.append(
            pltpu.make_async_copy(source.at[rows], buffer.at[there], read_sems.at[k])
        )
        writes.append(
            pltpu.make_async_copy(buffer.at[there], packed.at[there], write_sems.at[k])
        )
    for copy in reads:
        copy.start()
    for read, write in zip(reads, writes):
        read.wait()
        write.start()
    for copy in writes:
        copy.wait()


def pack(arrays, start, size):
    shape = (len(arrays) * size, arrays[0].shape[1])
    anywhere = pl.BlockSpec(memory_space=pl.ANY)
    return pl.pallas_call(
        functools.partial(pack_kernel, size),
        out_shape=jax.ShapeDtypeStruct(shape, arrays[0].dtype),
        in_specs=[pl.BlockSpec(memory_space=pltpu.SMEM)] + [anywhere] * len(arrays),
        out_specs=anywhere,
        scratch_shapes=[
            pltpu.VMEM(shape, arrays[0].dtype),
            pltpu.SemaphoreType.DMA((len(arrays),)),
            pltpu.SemaphoreType.DMA((len(arrays),)),
        ],
        compiler_params=pltpu.CompilerParams(vmem_limit_bytes=62 * 1024 * 1024),
        cost_estimate=pl.CostEstimate(
            flops=0, bytes_accessed=4 * shape[0] * shape[1], transcendentals=0
        ),
    )(start.reshape(1), *arrays)


class Sizes:
    def __init__(self, sections, row_count, width, local_hidden, panel, hidden_total, blocks):
        self.sections, self.row_count = sections, row_count
        self.width, self.local_hidden, self.panel = width, local_hidden, panel
        self.blocks = blocks
        self.block_rows = row_count // blocks
        self.panels_in = local_hidden // panel
        self.panels_out = width // panel
        self.scale_in = 1.0 / math.sqrt(width)
        self.scale_out = 1.0 / math.sqrt(hidden_total)


def chain_kernel(sz, step, forward, counts, *refs):
    refs = list(refs)

    def take(count):
        taken = refs[:count]
        del refs[:count]
        return taken

    first = forward and step == 0
    parts = 1 if first else 2
    (table,) = take(1)
    received, edges, sources = take(counts[0]), take(counts[1]), take(2 * parts)
    take(0 if first else 1)
    sends = take(counts[2])
    fresh_hbm, state = take(2)
    weights_in, weights_out, landing, rows, up, out, slope, wide_store = take(8)
    weight_sems, block_sems, edge_sems, send_sems, state_sems = take(5)
    panel, width, hidden_size = sz.panel, sz.width, sz.local_hidden
    links = sz.sections - 1
    whole = pl.ds(0, sz.row_count)

    def weight_copy(d, which):
        weights = (weights_in, weights_out)[which]
        return pltpu.make_async_copy(
            sources[2 * d + which], weights.at[d], weight_sems.at[d, which]
        )

    def place(line, e):
        return pl.ds(pl.multiple_of(table[line, e], sz.block_rows), sz.block_rows)

    def state_part(k, columns):
        return state.at[pl.ds(k * sz.row_count, sz.row_count), pl.ds(0, columns)]

    rows_hbm, slope_hbm = state_part(0, width), state_part(1, 2 * hidden_size)

    @pl.when(table[links + 1, step] == 1)
    def _():
        sequence = [
            (d, which if forward else 1 - which) for d in range(parts) for which in range(2)
        ]
        arrive = links if forward else step
        first_copies = []
        for i, source in enumerate(received):
            e, a = divmod(i, 2)
            rows_there = whole if len(received) == 2 else place(arrive, e)
            first_copies.append(
                pltpu.make_async_copy(source, landing.at[a, rows_there], block_sems.at[i])
            )
        for d, source in enumerate(edges):
            column = pl.ds(pl.multiple_of(table[links + 2, d], panel), panel)
            first_copies.append(
                pltpu.make_async_copy(source, out.at[:, column], edge_sems.at[d])
            )
        if not forward:
            first_copies.append(pltpu.make_async_copy(rows_hbm, wide_store, state_sems.at[0]))
            first_copies.append(pltpu.make_async_copy(slope_hbm, slope, state_sems.at[1]))
        for copy in first_copies:
            copy.start()
        for item in sequence[:2]:
            weight_copy(*item).start()

        def arrived(item):
            weight_copy(*item).wait()
            later = sequence.index(item) + 2
            if later < len(sequence):
                weight_copy(*sequence[later]).start()

        for copy in first_copies:
            copy.wait()
        if received:
            total = landing[0].astype(jnp.float32) + landing[1].astype(jnp.float32)
            total = total.astype(jnp.bfloat16)
        if forward:
            rows[...] = total if received else out[...]
        elif edges:
            goal = out[...].astype(jnp.float32)
            up[...] = (total.astype(jnp.float32) - goal).astype(jnp.bfloat16)
        else:
            up[...] = total
        fresh = rows if forward else up
        store_copies = [pltpu.make_async_copy(fresh, fresh_hbm, state_sems.at[2])]
        if forward:
            wide = rows[...].astype(jnp.float32)
            wide_store[...] = wide
            store_copies.append(pltpu.make_async_copy(wide_store, rows_hbm, state_sems.at[0]))
        else:
            wide = wide_store[...]
        inverse_rms = lax.rsqrt(jnp.mean(wide * wide, axis=1, keepdims=True) + epsilon)
        leads = table[links + 2, 4] == 1
        if forward:
            normed = (wide * inverse_rms).astype(jnp.bfloat16)
            total = [jnp.zeros((sz.row_count, panel), jnp.float32) for _ in range(sz.panels_out)]
            for d in range(parts):
                arrived((d, 0))
                hidden = []
                for p in range(sz.panels_in):
                    weight = weights_in[d, :, p * panel : (p + 1) * panel]
                    preact = dot(normed, weight) * sz.scale_in
                    gate = jax.nn.sigmoid(preact)
                    hidden.append((preact * gate).astype(jnp.bfloat16))
                    column = d * hidden_size + p * panel
                    slope[:, column : column + panel] = gate * (1.0 + preact * (1.0 - gate))
                hidden = jnp.concatenate(hidden, axis=1)
                arrived((d, 1))
                for n in range(sz.panels_out):
                    weight = weights_out[d, :, n * panel : (n + 1) * panel]
                    total[n] = total[n] + dot(hidden, weight)
            total = jnp.concatenate(total, axis=1) * sz.scale_out
            out[...] = (total + jnp.where(leads, wide, 0.0)).astype(jnp.bfloat16)
            store_copies.append(pltpu.make_async_copy(slope, slope_hbm, state_sems.at[1]))
        else:
            up_turned = up[...].T
            total = jnp.zeros((width, sz.row_count), jnp.float32)
            for d in range(parts):
                arrived((d, 1))
                grad_hidden = dot(weights_out[d], up_turned)
                local_slope = slope[:, d * hidden_size : (d + 1) * hidden_size].T
                grad_pre = (grad_hidden * sz.scale_out * local_slope).astype(jnp.bfloat16)
                arrived((d, 0))
                total = total + dot(weights_in[d], grad_pre)
            total = total.T * sz.scale_in
            exact = wide * inverse_rms
            along = jnp.mean(total * exact, axis=1, keepdims=True)
            own = jnp.where(leads, up[...].astype(jnp.float32), 0.0)
            out[...] = (own + inverse_rms * (total - exact * along)).astype(jnp.bfloat16)
        leave = step if forward else links
        send_copies = []
        for e, target in enumerate(sends):
            rows_here = whole if len(sends) == 1 else place(leave, e)
            send_copies.append(
                pltpu.make_async_copy(out.at[rows_here], target, send_sems.at[e])
            )
        for copy in send_copies + store_copies:
            copy.start()
        for copy in send_copies + store_copies:
            copy.wait()


def chain_step(sz, step, forward, table, received, edges, weights, state):
    first = forward and step == 0
    count = 1 if forward and step in (0, sz.sections - 1) else sz.blocks
    anywhere = pl.BlockSpec(memory_space=pl.ANY)
    operands = [table, *received, *edges, *(weights[:2] if first else [*weights, state])]
    block = jax.ShapeDtypeStruct((sz.row_count // count, sz.width), jnp.bfloat16)
    kept = jax.ShapeDtypeStruct((4 * sz.row_count, 2 * sz.local_hidden), jnp.float32)
    fresh = jax.ShapeDtypeStruct((sz.row_count, sz.width), jnp.bfloat16)
    shapes = [block] * count + [fresh, kept]
    in_hbm = pl.BlockSpec(memory_space=pltpu.HBM)
    in_specs = [pl.BlockSpec(memory_space=pltpu.SMEM)] + [anywhere] * (len(operands) - 1)
    if not first:
        in_specs[-1] = in_hbm
    whole = (sz.row_count, sz.width)
    results = pl.pallas_call(
        functools.partial(
            chain_kernel, sz, step, forward, (len(received), len(edges), count)
        ),
        out_shape=shapes,
        in_specs=in_specs,
        out_specs=[anywhere] * (count + 1) + [in_hbm],
        input_output_aliases={} if first else {len(operands) - 1: count + 1},
        scratch_shapes=[
            pltpu.VMEM((2, sz.width, sz.local_hidden), jnp.bfloat16),
            pltpu.VMEM((2, sz.local_hidden, sz.width), jnp.bfloat16),
            pltpu.VMEM((2,) + whole, jnp.bfloat16),
            pltpu.VMEM(whole, jnp.bfloat16),
            pltpu.VMEM(whole, jnp.bfloat16),
            pltpu.VMEM(whole, jnp.bfloat16),
            pltpu.VMEM((sz.row_count, 2 * sz.local_hidden), jnp.float32),
            pltpu.VMEM(whole, jnp.float32),
            pltpu.SemaphoreType.DMA((2, 2)),
            pltpu.SemaphoreType.DMA((max(1, len(received)),)),
            pltpu.SemaphoreType.DMA((4,)),
            pltpu.SemaphoreType.DMA((count,)),
            pltpu.SemaphoreType.DMA((3,)),
        ],
        compiler_params=pltpu.CompilerParams(vmem_limit_bytes=62 * 1024 * 1024),
        cost_estimate=pl.CostEstimate(
            flops=8 * sz.row_count * sz.width * sz.local_hidden,
            bytes_accessed=8 * sz.width * sz.local_hidden,
            transcendentals=0,
        ),
    )(*operands)
    return list(results[:count]), results[count], results[count + 1]


def share_kernel(sz, whole, *refs):
    if whole:
        known, source, normed_ref, hidden_ref, slope, weights, sem = refs
    else:
        known, slope, source, grad_pre, weights, sem = refs
    panel = sz.panel
    copy = pltpu.make_async_copy(source, weights, sem)
    copy.start()
    if whole:
        wide = known[...].astype(jnp.float32)
        inverse_rms = lax.rsqrt(jnp.mean(wide * wide, axis=1, keepdims=True) + epsilon)
        normed = (wide * inverse_rms).astype(jnp.bfloat16)
        normed_ref[...] = normed
        copy.wait()
        for p in range(sz.panels_in):
            here = slice(p * panel, (p + 1) * panel)
            preact = dot(normed, weights[:, here]) * sz.scale_in
            gate = jax.nn.sigmoid(preact)
            hidden_ref[:, here] = (preact * gate).astype(jnp.bfloat16)
            slope[:, here] = gate * (1.0 + preact * (1.0 - gate))
    else:
        copy.wait()
        grad_hidden = dot(known[...], weights[...], contract_last)
        grad_pre[...] = (grad_hidden * sz.scale_out * slope[...]).astype(jnp.bfloat16)


def share_call(sz, operands, weight):
    whole = len(operands) == 1
    rows_count, hidden_size = sz.row_count, sz.local_hidden
    narrow = jax.ShapeDtypeStruct((rows_count, hidden_size), jnp.bfloat16)
    shapes = [narrow]
    if whole:
        shapes = [
            jax.ShapeDtypeStruct((rows_count, sz.width), jnp.bfloat16),
            narrow,
            jax.ShapeDtypeStruct((rows_count, hidden_size), jnp.float32),
        ]
    inside = pl.BlockSpec(memory_space=pltpu.VMEM)
    return pl.pallas_call(
        functools.partial(share_kernel, sz, whole),
        out_shape=shapes,
        in_specs=[inside] * len(operands) + [pl.BlockSpec(memory_space=pl.ANY)],
        out_specs=[inside] * len(shapes),
        scratch_shapes=[
            pltpu.VMEM(weight.shape, jnp.bfloat16),
            pltpu.SemaphoreType.DMA,
        ],
        compiler_params=pltpu.CompilerParams(vmem_limit_bytes=62 * 1024 * 1024),
        cost_estimate=pl.CostEstimate(
            flops=2 * rows_count * sz.width * hidden_size,
            bytes_accessed=2 * sz.width * hidden_size,
            transcendentals=0,
        ),
    )(*operands, weight)


def per_device(inputs, targets, weight_a, weight_b, moment_a, moment_b, routes, partners):
    replicas = lax.axis_size("replica")
    sections = lax.axis_size("section")
    shards = lax.axis_size("shard")
    replica_id = lax.axis_index("replica")
    section_id = lax.axis_index("section")
    shard_id = lax.axis_index("shard")
    row_count = inputs.shape[2]
    panel = inputs.shape[3]
    width = weight_a.shape[2]
    local_hidden = weight_a.shape[3]
    assert inputs.shape[1] == 1 and shards == 4
    assert local_hidden % panel == 0 and sections > 2
    hidden_total = local_hidden * shards
    scale_in = 1.0 / math.sqrt(width)
    scale_out = 1.0 / math.sqrt(hidden_total)
    weight_in = weight_a[0, 0]
    weight_out = weight_b[0, 0]
    block_rows = row_count // replicas
    links = sections - 1
    in_kernel = block_rows % 16 == 0
    blocks = replicas if in_kernel else 1
    sz = Sizes(sections, row_count, width, local_hidden, panel, hidden_total, blocks)

    def flat(replica, section, shard):
        return (replica * sections + section) * shards + shard

    def turn(section):
        return (section ^ (section >> 1)) & 1

    def holders(section):
        return [j for j in range(shards) if (j & 1) != turn(section)]

    def move(array, sources, target):
        pairs = [
            (flat(r, s, j), flat(*target(r, s, j)))
            for r in range(replicas)
            for s, j in sources
        ]
        return lax.ppermute(array, axes, pairs)

    def holder_sources(active):
        return [(s, j) for s in active for j in holders(s)]

    def to_holders(array, offset, active):
        sources = [(s, j ^ offset) for s, j in holder_sources(active)]
        return move(array, sources, lambda r, s, j: (r, s, j ^ offset))

    def from_holders(array, offset, active):
        return move(array, holder_sources(active), lambda r, s, j: (r, s, j ^ offset))

    def between_holders(array, offset, other_half, section, step):
        shift = turn(section) ^ turn(section + step) ^ (2 * other_half)
        return move(
            array,
            holder_sources([section]),
            lambda r, s, j: ((r + offset) % replicas, s + step, j ^ shift),
        )

    def across_replicas(array, offset, active):
        return move(
            array,
            [(s, j) for s in active for j in range(shards)],
            lambda r, s, j: ((r + offset) % replicas, s, j),
        )

    every = range(sections)
    others = range(1, replicas)
    is_holder = (shard_id & 1) != turn(section_id)

    edge = jnp.where(section_id == 0, inputs[0, 0], targets[0, 0])
    ends = [(s, j) for s in (0, links) for j in range(shards)]
    edges = [edge] + [
        move(edge, ends, lambda r, s, j, d=d: (r, s, j ^ d)) for d in range(1, shards)
    ]
    rest = range(1, sections)
    near = [to_holders(weight_in, 1, rest), to_holders(weight_out, 1, rest)]

    tables = lax.dynamic_index_in_dim(partners, section_id, 0, keepdims=False)

    def piece_of(table, offset):
        wanted = (replica_id + offset) % replicas
        return jnp.argmax(table[:, replica_id] == wanted).astype(jnp.int32)

    pieces_in = [piece_of(tables[0], e) for e in range(replicas)]
    pieces_out = [piece_of(tables[1], e) for e in range(replicas)]
    size_in = width // replicas
    size_out = local_hidden // replicas

    def piece(array, index, size, axis=0):
        return lax.dynamic_slice_in_dim(array, index * size, size, axis)

    def exchange(arrays, active):
        return [across_replicas(array, e, active) for e, array in zip(others, arrays)]

    packed_in = [
        pack([weight_in, moment_a[0, 0]], pieces_in[e] * size_in, size_in) for e in others
    ]
    packed_out = [
        pack([weight_out, moment_b[0, 0]], pieces_out[e] * size_out, size_out) for e in others
    ]
    early = range(sections // 2, sections)
    late = range(sections // 2)
    far_states_in = exchange(packed_in, every)

    offsets = jnp.arange(replicas, dtype=jnp.int32)
    there = (replica_id + offsets) % replicas
    back = (replica_id - offsets) % replicas
    own_routes = routes[0, :, replica_id, :]
    slots = jnp.sum(
        (own_routes[:, None, :] == there[None, :, None]).astype(jnp.int32)
        * offsets[None, None, :],
        axis=2,
    )
    columns = max(replicas, sections, shards + 1)
    steps = jnp.arange(sections)
    ours = ((is_holder | (steps == 0)) & (section_id == steps)).astype(jnp.int32)
    features = (shard_id ^ jnp.arange(shards, dtype=jnp.int32)) * panel
    leads = (is_holder & ((shard_id & 2) == 0)).astype(jnp.int32)
    features = jnp.append(features, leads)

    def line(values):
        return jnp.pad(values, ((0, 0), (0, columns - values.shape[1])))

    starts = jnp.concatenate([slots, back[None]]) * block_rows
    if not in_kernel:
        starts = jnp.zeros_like(starts)
    table = jnp.concatenate([line(starts), line(ours[None]), line(features[None])])
    table = table.astype(jnp.int32)

    def send_blocks(sends, arrived, left, section, step):
        sign = step
        if in_kernel:
            return [
                between_holders(sends[e], sign * e, a, section, step)
                for e in range(replicas)
                for a in range(2)
            ]
        parts = sends[0].reshape(replicas, block_rows, width)
        moved = [jnp.zeros_like(parts), jnp.zeros_like(parts)]
        for e in range(replicas):
            chosen = lax.dynamic_index_in_dim(parts, left[e], 0, keepdims=False)
            for a in range(2):
                got = between_holders(chosen, sign * e, a, section, step)
                moved[a] = lax.dynamic_update_index_in_dim(moved[a], got, arrived[e], 0)
        return [one.reshape(row_count, width) for one in moved]

    row_parts = []

    def spread_rows(received, rows, active):
        received, rows, row_parts[:] = lax.optimization_barrier(
            (received, rows, row_parts)
        )
        row_parts.append(from_holders(rows, 1, active))
        return received

    weights = [weight_in, weight_out, *near]
    received, state = [], None
    for step in every:
        sends, fresh, state = chain_step(
            sz, step, True, table, received, edges if step == 0 else [], weights, state
        )
        rows = fresh if step == 0 else jnp.where(section_id == step, fresh, rows)
        if step == 0:
            total = sends[0].astype(jnp.float32)
            total = total + to_holders(sends[0], 1, [0]).astype(jnp.float32)
            sends = [total.astype(jnp.bfloat16)]
            if in_kernel:
                sends = [piece(sends[0], slots[0, e], block_rows) for e in range(replicas)]
        if step < links:
            received = send_blocks(sends, back, slots[step], step, 1)
            if step == 0:
                received, far_states_in, packed_out = lax.optimization_barrier(
                    (received, far_states_in, packed_out)
                )
                far_states_out = exchange(packed_out, early)
        else:
            received = [sends[0], from_holders(sends[0], 2, [links])]
        if len(late) - 1 <= step < links:
            received = spread_rows(received, rows, late if step < len(late) else [step])
        if step == len(late) - 1:
            received, packed_out = lax.optimization_barrier((received, packed_out))
            far_late = exchange(packed_out, late)
        if step == len(late):
            received, far_states_out = lax.optimization_barrier((received, far_states_out))

    for step in reversed(range(1, sections)):
        sends, fresh, state = chain_step(
            sz, step, False, table, received, edges if step == links else [], weights, state
        )
        upstream = fresh if step == links else jnp.where(section_id == step, fresh, upstream)
        received = send_blocks(sends, slots[step - 1], back, step, -1)
        if step == links:
            received = spread_rows(received, rows, [links])
        if step == len(late):
            received, far_late, row_parts = lax.optimization_barrier(
                (received, far_late, row_parts)
            )

    own_rows = jnp.where(is_holder, rows, sum(row_parts[1:], row_parts[0]))
    normed, hidden, slope = share_call(sz, [own_rows], weight_in)

    def bundle(e):
        first, second = normed, hidden
        first = piece(first, pieces_in[e], size_in, 1)
        return jnp.concatenate([first, piece(second, pieces_out[e], size_out, 1)], axis=1)

    bundles = exchange([bundle(e) for e in others], every)
    received, bundles = lax.optimization_barrier((received, bundles))
    far_normed = [one[:, :size_in] for one in bundles]
    far_hidden = [one[:, size_in:] for one in bundles]

    halves = []
    for a in range(2):
        half = received[a]
        if in_kernel:
            half = jnp.zeros((row_count, width), jnp.bfloat16)
            for e in range(replicas):
                half = lax.dynamic_update_slice_in_dim(
                    half, received[2 * e + a], slots[0, e] * block_rows, 0
                )
        halves.append(half.astype(jnp.float32))
    first_up = (halves[0] + halves[1]).astype(jnp.bfloat16)
    upstream = jnp.where(section_id == 0, first_up, upstream)
    upstream = jnp.where(is_holder, upstream, from_holders(upstream, 1, every))
    far_up = exchange([upstream] * len(others), every)
    (grad_pre,) = share_call(sz, [upstream, slope], weight_out)
    far_pre = exchange([grad_pre] * len(others), every)
    far_states_out = [
        jnp.where(section_id < len(late), one, two)
        for one, two in zip(far_late, far_states_out)
    ]
    far_states = {0: far_states_in, 2: far_states_out}

    def far_part(e, which):
        size = size_out if which & 2 else size_in
        both = far_states[which & 2][e - 1]
        return both[size:] if which & 1 else both[:size]

    def as_delta(left, right, scale):
        return (inner_rate * (dot(left, right, contract_rows) * scale)).astype(jnp.bfloat16)

    def finish(weight, moment, left, right, which, far_left, far_right, scale, pieces, size):
        new_weight, new_moment = outer_mix(
            weight.astype(jnp.float32),
            moment.astype(jnp.float32),
            as_delta(left, right, scale).astype(jnp.float32),
        )
        for e in others:
            back = replicas - e

            def mean(own_array, far_array):
                return 0.5 * (own_array.astype(jnp.float32) + far_array.astype(jnp.float32))

            index = pieces[back]
            own_left = piece(left, index, size, 1)
            part_weight, part_moment = outer_mix(
                mean(piece(weight, index, size), far_part(e, which)),
                mean(piece(moment, index, size), far_part(e, which + 1)),
                mean(
                    as_delta(own_left, right, scale),
                    as_delta(far_left[e - 1], far_right[e - 1], scale),
                ),
            )
            new_weight = lax.dynamic_update_slice_in_dim(new_weight, part_weight, index * size, 0)
            new_moment = lax.dynamic_update_slice_in_dim(new_moment, part_moment, index * size, 0)
        return new_weight[None, None], new_moment[None, None]

    new_weight_b, new_moment_b = finish(
        weight_out, moment_b[0, 0], hidden, upstream, 2, far_hidden, far_up,
        scale_out, pieces_out, size_out,
    )
    new_weight_a, new_moment_a = finish(
        weight_in, moment_a[0, 0], normed, grad_pre, 0, far_normed, far_pre,
        scale_in, pieces_in, size_in,
    )
    return (new_weight_a, new_weight_b, new_moment_a, new_moment_b)


def solution(mesh):
    placed = (
        P("replica", None, None, "shard"),
        P("replica", None, None, "shard"),
        P("replica", "section", None, "shard"),
        P("replica", "section", "shard", None),
        P("replica", "section", None, "shard"),
        P("replica", "section", "shard", None),
        P(),
        P(),
    )
    return jax.shard_map(
        per_device,
        mesh=mesh,
        in_specs=placed,
        out_specs=(
            P("replica", "section", None, "shard"),
            P("replica", "section", "shard", None),
            P("replica", "section", None, "shard"),
            P("replica", "section", "shard", None),
        ),
        check_vma=False,
    )
```

```python
import functools
import math

import jax
import jax.numpy as jnp
from jax import lax
from jax.experimental import pallas as pl
from jax.experimental.pallas import tpu as pltpu
from jax.sharding import PartitionSpec as P

epsilon = 1e-05
inner_rate = 0.5
momentum_decay = 0.9
outer_rate = 0.7

axes = ("replica", "section", "shard")
contract_rows = (((0,), (0,)), ((), ()))
contract_last = (((1,), (1,)), ((), ()))


def dot(left, right, dims=(((1,), (0,)), ((), ()))):
    return lax.dot_general(left, right, dims, preferred_element_type=jnp.float32)


def outer_mix(weight, moment, delta):
    new_moment = momentum_decay * moment + delta
    new_weight = weight - outer_rate * (momentum_decay * new_moment + delta)
    return new_weight.astype(jnp.bfloat16), new_moment.astype(jnp.bfloat16)


def pack_kernel(size, starts, *refs):
    sources, (packed, buffer, read_sems, write_sems) = refs[:-4], refs[-4:]
    rows = pl.ds(pl.multiple_of(starts[0], size), size)
    reads, writes = [], []
    for k, source in enumerate(sources):
        there = pl.ds(k * size, size)
        reads.append(
            pltpu.make_async_copy(source.at[rows], buffer.at[there], read_sems.at[k])
        )
        writes.append(
            pltpu.make_async_copy(buffer.at[there], packed.at[there], write_sems.at[k])
        )
    for copy in reads:
        copy.start()
    for read, write in zip(reads, writes):
        read.wait()
        write.start()
    for copy in writes:
        copy.wait()


def pack(arrays, start, size):
    shape = (len(arrays) * size, arrays[0].shape[1])
    anywhere = pl.BlockSpec(memory_space=pl.ANY)
    return pl.pallas_call(
        functools.partial(pack_kernel, size),
        out_shape=jax.ShapeDtypeStruct(shape, arrays[0].dtype),
        in_specs=[pl.BlockSpec(memory_space=pltpu.SMEM)] + [anywhere] * len(arrays),
        out_specs=anywhere,
        scratch_shapes=[
            pltpu.VMEM(shape, arrays[0].dtype),
            pltpu.SemaphoreType.DMA((len(arrays),)),
            pltpu.SemaphoreType.DMA((len(arrays),)),
        ],
        compiler_params=pltpu.CompilerParams(vmem_limit_bytes=32 * 1024 * 1024),
        cost_estimate=pl.CostEstimate(
            flops=0, bytes_accessed=4 * shape[0] * shape[1], transcendentals=0
        ),
    )(start.reshape(1), *arrays)


class Sizes:
    def __init__(self, sections, row_count, width, local_hidden, panel, hidden_total, blocks):
        self.sections, self.row_count = sections, row_count
        self.width, self.local_hidden, self.panel = width, local_hidden, panel
        self.blocks = blocks
        self.block_rows = row_count // blocks
        self.panels_in = local_hidden // panel
        self.panels_out = width // panel
        self.scale_in = 1.0 / math.sqrt(width)
        self.scale_out = 1.0 / math.sqrt(hidden_total)


def chain_kernel(sz, step, forward, counts, *refs):
    refs = list(refs)

    def take(count):
        taken = refs[:count]
        del refs[:count]
        return taken

    first = forward and step == 0
    parts = 1 if first else 2
    (table,) = take(1)
    received, edges, sources = take(counts[0]), take(counts[1]), take(2 * parts)
    take(1)
    sends = take(counts[2])
    fresh_hbm, state = take(2)
    weights_in, weights_out, landing, rows, up, out, slope, wide_store = take(8)
    weight_sems, block_sems, edge_sems, send_sems, state_sems = take(5)
    panel, width, hidden_size = sz.panel, sz.width, sz.local_hidden
    links = sz.sections - 1
    whole = pl.ds(0, sz.row_count)

    def weight_copy(d, which):
        weights = (weights_in, weights_out)[which]
        return pltpu.make_async_copy(
            sources[2 * d + which], weights.at[d], weight_sems.at[d, which]
        )

    def place(line, e):
        return pl.ds(pl.multiple_of(table[line, e], sz.block_rows), sz.block_rows)

    def state_part(k, columns):
        return state.at[pl.ds(k * sz.row_count, sz.row_count), pl.ds(0, columns)]

    rows_hbm, slope_hbm = state_part(0, width), state_part(1, 2 * hidden_size)

    @pl.when(table[links + 1, step] == 1)
    def _():
        sequence = [
            (d, which if forward else 1 - which) for d in range(parts) for which in range(2)
        ]
        arrive = links if forward else step
        first_copies = []
        for i, source in enumerate(received):
            e, a = divmod(i, 2)
            rows_there = whole if len(received) == 2 else place(arrive, e)
            first_copies.append(
                pltpu.make_async_copy(source, landing.at[a, rows_there], block_sems.at[i])
            )
        for d, source in enumerate(edges):
            column = pl.ds(pl.multiple_of(table[links + 2, d], panel), panel)
            first_copies.append(
                pltpu.make_async_copy(source, out.at[:, column], edge_sems.at[d])
            )
        if not forward:
            first_copies.append(pltpu.make_async_copy(rows_hbm, wide_store, state_sems.at[0]))
            first_copies.append(pltpu.make_async_copy(slope_hbm, slope, state_sems.at[1]))
        for copy in first_copies:
            copy.start()
        for item in sequence[:2]:
            weight_copy(*item).start()

        def arrived(item):
            weight_copy(*item).wait()
            later = sequence.index(item) + 2
            if later < len(sequence):
                weight_copy(*sequence[later]).start()

        for copy in first_copies:
            copy.wait()
        if received:
            total = landing[0].astype(jnp.float32) + landing[1].astype(jnp.float32)
            total = total.astype(jnp.bfloat16)
        if forward:
            rows[...] = total if received else out[...]
        elif edges:
            goal = out[...].astype(jnp.float32)
            up[...] = (total.astype(jnp.float32) - goal).astype(jnp.bfloat16)
        else:
            up[...] = total
        fresh = rows if forward else up
        store_copies = [pltpu.make_async_copy(fresh, fresh_hbm, state_sems.at[2])]
        if forward:
            wide = rows[...].astype(jnp.float32)
            wide_store[...] = wide
            store_copies.append(pltpu.make_async_copy(wide_store, rows_hbm, state_sems.at[0]))
        else:
            wide = wide_store[...]
        inverse_rms = lax.rsqrt(jnp.mean(wide * wide, axis=1, keepdims=True) + epsilon)
        leads = table[links + 2, 4] == 1
        if forward:
            normed = (wide * inverse_rms).astype(jnp.bfloat16)
            total = [jnp.zeros((sz.row_count, panel), jnp.float32) for _ in range(sz.panels_out)]
            for d in range(parts):
                arrived((d, 0))
                hidden = []
                for p in range(sz.panels_in):
                    weight = weights_in[d, :, p * panel : (p + 1) * panel]
                    preact = dot(normed, weight) * sz.scale_in
                    gate = jax.nn.sigmoid(preact)
                    hidden.append((preact * gate).astype(jnp.bfloat16))
                    column = d * hidden_size + p * panel
                    slope[:, column : column + panel] = gate * (1.0 + preact * (1.0 - gate))
                hidden = jnp.concatenate(hidden, axis=1)
                arrived((d, 1))
                for n in range(sz.panels_out):
                    weight = weights_out[d, :, n * panel : (n + 1) * panel]
                    total[n] = total[n] + dot(hidden, weight)
            total = jnp.concatenate(total, axis=1) * sz.scale_out
            out[...] = (total + jnp.where(leads, wide, 0.0)).astype(jnp.bfloat16)
            store_copies.append(pltpu.make_async_copy(slope, slope_hbm, state_sems.at[1]))
        else:
            up_turned = up[...].T
            total = jnp.zeros((width, sz.row_count), jnp.float32)
            for d in range(parts):
                arrived((d, 1))
                grad_hidden = dot(weights_out[d], up_turned)
                local_slope = slope[:, d * hidden_size : (d + 1) * hidden_size].T
                grad_pre = (grad_hidden * sz.scale_out * local_slope).astype(jnp.bfloat16)
                arrived((d, 0))
                total = total + dot(weights_in[d], grad_pre)
            total = total.T * sz.scale_in
            exact = wide * inverse_rms
            along = jnp.mean(total * exact, axis=1, keepdims=True)
            own = jnp.where(leads, up[...].astype(jnp.float32), 0.0)
            out[...] = (own + inverse_rms * (total - exact * along)).astype(jnp.bfloat16)
        leave = step if forward else links
        send_copies = []
        for e, target in enumerate(sends):
            rows_here = whole if len(sends) == 1 else place(leave, e)
            send_copies.append(
                pltpu.make_async_copy(out.at[rows_here], target, send_sems.at[e])
            )
        for copy in send_copies + store_copies:
            copy.start()
        for copy in send_copies + store_copies:
            copy.wait()


def chain_step(sz, step, forward, table, received, edges, weights, state):
    first = forward and step == 0
    count = 1 if forward and step in (0, sz.sections - 1) else sz.blocks
    anywhere = pl.BlockSpec(memory_space=pl.ANY)
    operands = [table, *received, *edges, *(weights[:2] if first else weights), state]
    block = jax.ShapeDtypeStruct((sz.row_count // count, sz.width), jnp.bfloat16)
    kept = jax.ShapeDtypeStruct(state.shape, state.dtype)
    fresh = jax.ShapeDtypeStruct((sz.row_count, sz.width), jnp.bfloat16)
    shapes = [block] * count + [fresh, kept]
    in_specs = [pl.BlockSpec(memory_space=pltpu.SMEM)] + [anywhere] * (len(operands) - 1)
    whole = (sz.row_count, sz.width)
    results = pl.pallas_call(
        functools.partial(
            chain_kernel, sz, step, forward, (len(received), len(edges), count)
        ),
        out_shape=shapes,
        in_specs=in_specs,
        out_specs=[anywhere] * len(shapes),
        input_output_aliases={len(operands) - 1: count + 1},
        scratch_shapes=[
            pltpu.VMEM((2, sz.width, sz.local_hidden), jnp.bfloat16),
            pltpu.VMEM((2, sz.local_hidden, sz.width), jnp.bfloat16),
            pltpu.VMEM((2,) + whole, jnp.bfloat16),
            pltpu.VMEM(whole, jnp.bfloat16),
            pltpu.VMEM(whole, jnp.bfloat16),
            pltpu.VMEM(whole, jnp.bfloat16),
            pltpu.VMEM((sz.row_count, 2 * sz.local_hidden), jnp.float32),
            pltpu.VMEM(whole, jnp.float32),
            pltpu.SemaphoreType.DMA((2, 2)),
            pltpu.SemaphoreType.DMA((max(1, len(received)),)),
            pltpu.SemaphoreType.DMA((4,)),
            pltpu.SemaphoreType.DMA((count,)),
            pltpu.SemaphoreType.DMA((3,)),
        ],
        compiler_params=pltpu.CompilerParams(vmem_limit_bytes=32 * 1024 * 1024),
        cost_estimate=pl.CostEstimate(
            flops=8 * sz.row_count * sz.width * sz.local_hidden,
            bytes_accessed=8 * sz.width * sz.local_hidden,
            transcendentals=0,
        ),
    )(*operands)
    return list(results[:count]), results[count], results[count + 1]


def share_kernel(sz, whole, *refs):
    if whole:
        known, source, normed_ref, hidden_ref, slope, weights, sem = refs
    else:
        known, slope, source, grad_pre, weights, sem = refs
    panel = sz.panel
    copy = pltpu.make_async_copy(source, weights, sem)
    copy.start()
    if whole:
        wide = known[...].astype(jnp.float32)
        inverse_rms = lax.rsqrt(jnp.mean(wide * wide, axis=1, keepdims=True) + epsilon)
        normed = (wide * inverse_rms).astype(jnp.bfloat16)
        normed_ref[...] = normed
        copy.wait()
        for p in range(sz.panels_in):
            here = slice(p * panel, (p + 1) * panel)
            preact = dot(normed, weights[:, here]) * sz.scale_in
            gate = jax.nn.sigmoid(preact)
            hidden_ref[:, here] = (preact * gate).astype(jnp.bfloat16)
            slope[:, here] = gate * (1.0 + preact * (1.0 - gate))
    else:
        copy.wait()
        grad_hidden = dot(known[...], weights[...], contract_last)
        grad_pre[...] = (grad_hidden * sz.scale_out * slope[...]).astype(jnp.bfloat16)


def share_call(sz, operands, weight):
    whole = len(operands) == 1
    rows_count, hidden_size = sz.row_count, sz.local_hidden
    narrow = jax.ShapeDtypeStruct((rows_count, hidden_size), jnp.bfloat16)
    shapes = [narrow]
    if whole:
        shapes = [
            jax.ShapeDtypeStruct((rows_count, sz.width), jnp.bfloat16),
            narrow,
            jax.ShapeDtypeStruct((rows_count, hidden_size), jnp.float32),
        ]
    inside = pl.BlockSpec(memory_space=pltpu.VMEM)
    return pl.pallas_call(
        functools.partial(share_kernel, sz, whole),
        out_shape=shapes,
        in_specs=[inside] * len(operands) + [pl.BlockSpec(memory_space=pl.ANY)],
        out_specs=[inside] * len(shapes),
        scratch_shapes=[
            pltpu.VMEM(weight.shape, jnp.bfloat16),
            pltpu.SemaphoreType.DMA,
        ],
        compiler_params=pltpu.CompilerParams(vmem_limit_bytes=32 * 1024 * 1024),
        cost_estimate=pl.CostEstimate(
            flops=2 * rows_count * sz.width * hidden_size,
            bytes_accessed=2 * sz.width * hidden_size,
            transcendentals=0,
        ),
    )(*operands, weight)


def per_device(inputs, targets, weight_a, weight_b, moment_a, moment_b, routes, partners):
    replicas = lax.axis_size("replica")
    sections = lax.axis_size("section")
    shards = lax.axis_size("shard")
    replica_id = lax.axis_index("replica")
    section_id = lax.axis_index("section")
    shard_id = lax.axis_index("shard")
    row_count = inputs.shape[2]
    panel = inputs.shape[3]
    width = weight_a.shape[2]
    local_hidden = weight_a.shape[3]
    assert inputs.shape[1] == 1 and shards == 4
    assert local_hidden % panel == 0 and sections > 2
    hidden_total = local_hidden * shards
    scale_in = 1.0 / math.sqrt(width)
    scale_out = 1.0 / math.sqrt(hidden_total)
    weight_in = weight_a[0, 0]
    weight_out = weight_b[0, 0]
    block_rows = row_count // replicas
    links = sections - 1
    in_kernel = block_rows % 16 == 0
    blocks = replicas if in_kernel else 1
    sz = Sizes(sections, row_count, width, local_hidden, panel, hidden_total, blocks)

    def flat(replica, section, shard):
        return (replica * sections + section) * shards + shard

    def turn(section):
        return (section ^ (section >> 1)) & 1

    def holders(section):
        return [j for j in range(shards) if (j & 1) != turn(section)]

    def move(array, sources, target):
        pairs = [
            (flat(r, s, j), flat(*target(r, s, j)))
            for r in range(replicas)
            for s, j in sources
        ]
        return lax.ppermute(array, axes, pairs)

    def holder_sources(active):
        return [(s, j) for s in active for j in holders(s)]

    def to_holders(array, offset, active):
        sources = [(s, j ^ offset) for s, j in holder_sources(active)]
        return move(array, sources, lambda r, s, j: (r, s, j ^ offset))

    def from_holders(array, offset, active):
        return move(array, holder_sources(active), lambda r, s, j: (r, s, j ^ offset))

    def between_holders(array, offset, other_half, section, step):
        shift = turn(section) ^ turn(section + step) ^ (2 * other_half)
        return move(
            array,
            holder_sources([section]),
            lambda r, s, j: ((r + offset) % replicas, s + step, j ^ shift),
        )

    def across_replicas(array, offset, active):
        return move(
            array,
            [(s, j) for s in active for j in range(shards)],
            lambda r, s, j: ((r + offset) % replicas, s, j),
        )

    every = range(sections)
    others = range(1, replicas)
    is_holder = (shard_id & 1) != turn(section_id)

    edge = jnp.where(section_id == 0, inputs[0, 0], targets[0, 0])
    ends = [(s, j) for s in (0, links) for j in range(shards)]
    edges = [edge] + [
        move(edge, ends, lambda r, s, j, d=d: (r, s, j ^ d)) for d in range(1, shards)
    ]
    rest = range(1, sections)
    near = [to_holders(weight_in, 1, rest), to_holders(weight_out, 1, rest)]

    tables = lax.dynamic_index_in_dim(partners, section_id, 0, keepdims=False)

    def piece_of(table, offset):
        wanted = (replica_id + offset) % replicas
        return jnp.argmax(table[:, replica_id] == wanted).astype(jnp.int32)

    pieces_in = [piece_of(tables[0], e) for e in range(replicas)]
    pieces_out = [piece_of(tables[1], e) for e in range(replicas)]
    size_in = width // replicas
    size_out = local_hidden // replicas

    def piece(array, index, size, axis=0):
        return lax.dynamic_slice_in_dim(array, index * size, size, axis)

    def exchange(arrays, active):
        return [across_replicas(array, e, active) for e, array in zip(others, arrays)]

    packed_in = [
        pack([weight_in, moment_a[0, 0]], pieces_in[e] * size_in, size_in) for e in others
    ]
    packed_out = [
        pack([weight_out, moment_b[0, 0]], pieces_out[e] * size_out, size_out) for e in others
    ]
    early = range(sections // 2, sections)
    late = range(sections // 2)
    far_states_in = exchange(packed_in, every)

    offsets = jnp.arange(replicas, dtype=jnp.int32)
    there = (replica_id + offsets) % replicas
    back = (replica_id - offsets) % replicas
    own_routes = routes[0, :, replica_id, :]
    slots = jnp.sum(
        (own_routes[:, None, :] == there[None, :, None]).astype(jnp.int32)
        * offsets[None, None, :],
        axis=2,
    )
    columns = max(replicas, sections, shards + 1)
    steps = jnp.arange(sections)
    ours = ((is_holder | (steps == 0)) & (section_id == steps)).astype(jnp.int32)
    features = (shard_id ^ jnp.arange(shards, dtype=jnp.int32)) * panel
    leads = (is_holder & ((shard_id & 2) == 0)).astype(jnp.int32)
    features = jnp.append(features, leads)

    def line(values):
        return jnp.pad(values, ((0, 0), (0, columns - values.shape[1])))

    starts = jnp.concatenate([slots, back[None]]) * block_rows
    if not in_kernel:
        starts = jnp.zeros_like(starts)
    table = jnp.concatenate([line(starts), line(ours[None]), line(features[None])])
    table = table.astype(jnp.int32)

    def send_blocks(sends, arrived, left, section, step):
        sign = step
        if in_kernel:
            return [
                between_holders(sends[e], sign * e, a, section, step)
                for e in range(replicas)
                for a in range(2)
            ]
        parts = sends[0].reshape(replicas, block_rows, width)
        moved = [jnp.zeros_like(parts), jnp.zeros_like(parts)]
        for e in range(replicas):
            chosen = lax.dynamic_index_in_dim(parts, left[e], 0, keepdims=False)
            for a in range(2):
                got = between_holders(chosen, sign * e, a, section, step)
                moved[a] = lax.dynamic_update_index_in_dim(moved[a], got, arrived[e], 0)
        return [one.reshape(row_count, width) for one in moved]

    row_parts = []

    def spread_rows(received, rows, active):
        received, rows, row_parts[:] = lax.optimization_barrier(
            (received, rows, row_parts)
        )
        row_parts.append(from_holders(rows, 1, active))
        return received

    weights = [weight_in, weight_out, *near]
    state = jnp.zeros((5 * row_count, 2 * local_hidden), jnp.float32)
    received = []
    for step in every:
        sends, fresh, state = chain_step(
            sz, step, True, table, received, edges if step == 0 else [], weights, state
        )
        rows = fresh if step == 0 else jnp.where(section_id == step, fresh, rows)
        if step == 0:
            total = sends[0].astype(jnp.float32)
            total = total + to_holders(sends[0], 1, [0]).astype(jnp.float32)
            sends = [total.astype(jnp.bfloat16)]
            if in_kernel:
                sends = [piece(sends[0], slots[0, e], block_rows) for e in range(replicas)]
        if step < links:
            received = send_blocks(sends, back, slots[step], step, 1)
            if step == 0:
                received, far_states_in, packed_out = lax.optimization_barrier(
                    (received, far_states_in, packed_out)
                )
                far_states_out = exchange(packed_out, early)
        else:
            received = [sends[0], from_holders(sends[0], 2, [links])]
        if len(late) - 1 <= step < links:
            received = spread_rows(received, rows, late if step < len(late) else [step])
        if step == len(late) - 1:
            received, packed_out = lax.optimization_barrier((received, packed_out))
            far_late = exchange(packed_out, late)
        if step == len(late):
            received, far_states_out = lax.optimization_barrier((received, far_states_out))

    for step in reversed(range(1, sections)):
        sends, fresh, state = chain_step(
            sz, step, False, table, received, edges if step == links else [], weights, state
        )
        upstream = fresh if step == links else jnp.where(section_id == step, fresh, upstream)
        received = send_blocks(sends, slots[step - 1], back, step, -1)
        if step == links:
            received = spread_rows(received, rows, [links])
        if step == len(late):
            received, far_late, row_parts = lax.optimization_barrier(
                (received, far_late, row_parts)
            )

    upstream, rows, row_parts = lax.optimization_barrier((upstream, rows, row_parts))
    own_rows = jnp.where(is_holder, rows, sum(row_parts[1:], row_parts[0]))
    normed, hidden, slope = share_call(sz, [own_rows], weight_in)

    def bundle(e):
        first, second = normed, hidden
        first = piece(first, pieces_in[e], size_in, 1)
        return jnp.concatenate([first, piece(second, pieces_out[e], size_out, 1)], axis=1)

    bundles = exchange([bundle(e) for e in others], every)
    received, bundles = lax.optimization_barrier((received, bundles))
    far_normed = [one[:, :size_in] for one in bundles]
    far_hidden = [one[:, size_in:] for one in bundles]

    halves = []
    for a in range(2):
        half = received[a]
        if in_kernel:
            half = jnp.zeros((row_count, width), jnp.bfloat16)
            for e in range(replicas):
                half = lax.dynamic_update_slice_in_dim(
                    half, received[2 * e + a], slots[0, e] * block_rows, 0
                )
        halves.append(half.astype(jnp.float32))
    first_up = (halves[0] + halves[1]).astype(jnp.bfloat16)
    upstream = jnp.where(section_id == 0, first_up, upstream)
    upstream = jnp.where(is_holder, upstream, from_holders(upstream, 1, every))
    far_up = exchange([upstream] * len(others), every)
    (grad_pre,) = share_call(sz, [upstream, slope], weight_out)
    far_pre = exchange([grad_pre] * len(others), every)
    far_states_out = [
        jnp.where(section_id < len(late), one, two)
        for one, two in zip(far_late, far_states_out)
    ]
    far_states = {0: far_states_in, 2: far_states_out}

    def far_part(e, which):
        size = size_out if which & 2 else size_in
        both = far_states[which & 2][e - 1]
        return both[size:] if which & 1 else both[:size]

    def as_delta(left, right, scale):
        return (inner_rate * (dot(left, right, contract_rows) * scale)).astype(jnp.bfloat16)

    def finish(weight, moment, left, right, which, far_left, far_right, scale, pieces, size):
        new_weight, new_moment = outer_mix(
            weight.astype(jnp.float32),
            moment.astype(jnp.float32),
            as_delta(left, right, scale).astype(jnp.float32),
        )
        for e in others:
            back = replicas - e

            def mean(own_array, far_array):
                return 0.5 * (own_array.astype(jnp.float32) + far_array.astype(jnp.float32))

            index = pieces[back]
            own_left = piece(left, index, size, 1)
            part_weight, part_moment = outer_mix(
                mean(piece(weight, index, size), far_part(e, which)),
                mean(piece(moment, index, size), far_part(e, which + 1)),
                mean(
                    as_delta(own_left, right, scale),
                    as_delta(far_left[e - 1], far_right[e - 1], scale),
                ),
            )
            new_weight = lax.dynamic_update_slice_in_dim(new_weight, part_weight, index * size, 0)
            new_moment = lax.dynamic_update_slice_in_dim(new_moment, part_moment, index * size, 0)
        return new_weight[None, None], new_moment[None, None]

    new_weight_b, new_moment_b = finish(
        weight_out, moment_b[0, 0], hidden, upstream, 2, far_hidden, far_up,
        scale_out, pieces_out, size_out,
    )
    new_weight_a, new_moment_a = finish(
        weight_in, moment_a[0, 0], normed, grad_pre, 0, far_normed, far_pre,
        scale_in, pieces_in, size_in,
    )
    return (new_weight_a, new_weight_b, new_moment_a, new_moment_b)


def solution(mesh):
    placed = (
        P("replica", None, None, "shard"),
        P("replica", None, None, "shard"),
        P("replica", "section", None, "shard"),
        P("replica", "section", "shard", None),
        P("replica", "section", None, "shard"),
        P("replica", "section", "shard", None),
        P(),
        P(),
    )
    return jax.shard_map(
        per_device,
        mesh=mesh,
        in_specs=placed,
        out_specs=(
            P("replica", "section", None, "shard"),
            P("replica", "section", "shard", None),
            P("replica", "section", None, "shard"),
            P("replica", "section", "shard", None),
        ),
        check_vma=False,
    )
```

```python
import functools
import math

import jax
import jax.numpy as jnp
from jax import lax
from jax.experimental import pallas as pl
from jax.experimental.pallas import tpu as pltpu
from jax.sharding import PartitionSpec as P

epsilon = 1e-05
inner_rate = 0.5
momentum_decay = 0.9
outer_rate = 0.7

axes = ("replica", "section", "shard")
contract_rows = (((0,), (0,)), ((), ()))
contract_last = (((1,), (1,)), ((), ()))


def dot(left, right, dims=(((1,), (0,)), ((), ()))):
    return lax.dot_general(left, right, dims, preferred_element_type=jnp.float32)


def outer_mix(weight, moment, delta):
    new_moment = momentum_decay * moment + delta
    new_weight = weight - outer_rate * (momentum_decay * new_moment + delta)
    return new_weight.astype(jnp.bfloat16), new_moment.astype(jnp.bfloat16)


def pack_kernel(size, starts, *refs):
    sources, (packed, buffer, read_sems, write_sems) = refs[:-4], refs[-4:]
    rows = pl.ds(pl.multiple_of(starts[0], size), size)
    reads, writes = [], []
    for k, source in enumerate(sources):
        there = pl.ds(k * size, size)
        reads.append(
            pltpu.make_async_copy(source.at[rows], buffer.at[there], read_sems.at[k])
        )
        writes.append(
            pltpu.make_async_copy(buffer.at[there], packed.at[there], write_sems.at[k])
        )
    for copy in reads:
        copy.start()
    for read, write in zip(reads, writes):
        read.wait()
        write.start()
    for copy in writes:
        copy.wait()


def pack(arrays, start, size):
    shape = (len(arrays) * size, arrays[0].shape[1])
    anywhere = pl.BlockSpec(memory_space=pl.ANY)
    return pl.pallas_call(
        functools.partial(pack_kernel, size),
        out_shape=jax.ShapeDtypeStruct(shape, arrays[0].dtype),
        in_specs=[pl.BlockSpec(memory_space=pltpu.SMEM)] + [anywhere] * len(arrays),
        out_specs=anywhere,
        scratch_shapes=[
            pltpu.VMEM(shape, arrays[0].dtype),
            pltpu.SemaphoreType.DMA((len(arrays),)),
            pltpu.SemaphoreType.DMA((len(arrays),)),
        ],
        compiler_params=pltpu.CompilerParams(vmem_limit_bytes=58 * 1024 * 1024),
        cost_estimate=pl.CostEstimate(
            flops=0, bytes_accessed=4 * shape[0] * shape[1], transcendentals=0
        ),
    )(start.reshape(1), *arrays)


class Sizes:
    def __init__(self, sections, row_count, width, local_hidden, panel, hidden_total, blocks):
        self.sections, self.row_count = sections, row_count
        self.width, self.local_hidden, self.panel = width, local_hidden, panel
        self.blocks = blocks
        self.block_rows = row_count // blocks
        self.panels_in = local_hidden // panel
        self.panels_out = width // panel
        self.scale_in = 1.0 / math.sqrt(width)
        self.scale_out = 1.0 / math.sqrt(hidden_total)


def chain_kernel(sz, step, forward, counts, *refs):
    refs = list(refs)

    def take(count):
        taken = refs[:count]
        del refs[:count]
        return taken

    first = forward and step == 0
    parts = 1 if first else 2
    (table,) = take(1)
    received, edges, sources = take(counts[0]), take(counts[1]), take(2 * parts)
    take(0 if first else 1)
    sends = take(counts[2])
    fresh_hbm, state = take(2)
    weights_in, weights_out, landing, rows, up, out, slope, wide_store = take(8)
    weight_sems, block_sems, edge_sems, send_sems, state_sems = take(5)
    panel, width, hidden_size = sz.panel, sz.width, sz.local_hidden
    links = sz.sections - 1
    whole = pl.ds(0, sz.row_count)

    def weight_copy(d, which):
        weights = (weights_in, weights_out)[which]
        return pltpu.make_async_copy(
            sources[2 * d + which], weights.at[d], weight_sems.at[d, which]
        )

    def place(line, e):
        return pl.ds(pl.multiple_of(table[line, e], sz.block_rows), sz.block_rows)

    def state_part(k, columns):
        return state.at[pl.ds(k * sz.row_count, sz.row_count), pl.ds(0, columns)]

    rows_hbm, slope_hbm = state_part(0, width), state_part(1, 2 * hidden_size)

    @pl.when(table[links + 1, step] == 1)
    def _():
        sequence = [
            (d, which if forward else 1 - which) for d in range(parts) for which in range(2)
        ]
        arrive = links if forward else step
        first_copies = []
        for i, source in enumerate(received):
            e, a = divmod(i, 2)
            rows_there = whole if len(received) == 2 else place(arrive, e)
            first_copies.append(
                pltpu.make_async_copy(source, landing.at[a, rows_there], block_sems.at[i])
            )
        for d in range(2 * len(edges)):
            column = pl.ds(pl.multiple_of(table[links + 2, d], panel), panel)
            source = edges[d // 2].at[pl.ds((d % 2) * sz.row_count, sz.row_count)]
            first_copies.append(
                pltpu.make_async_copy(source, out.at[:, column], edge_sems.at[d])
            )
        if not forward:
            first_copies.append(pltpu.make_async_copy(rows_hbm, wide_store, state_sems.at[0]))
            first_copies.append(pltpu.make_async_copy(slope_hbm, slope, state_sems.at[1]))
        for copy in first_copies:
            copy.start()
        for item in sequence[:2]:
            weight_copy(*item).start()

        def arrived(item):
            weight_copy(*item).wait()
            later = sequence.index(item) + 2
            if later < len(sequence):
                weight_copy(*sequence[later]).start()

        for copy in first_copies:
            copy.wait()
        if received:
            total = landing[0].astype(jnp.float32) + landing[1].astype(jnp.float32)
            total = total.astype(jnp.bfloat16)
        if forward:
            rows[...] = total if received else out[...]
        elif edges:
            goal = out[...].astype(jnp.float32)
            up[...] = (total.astype(jnp.float32) - goal).astype(jnp.bfloat16)
        else:
            up[...] = total
        fresh = rows if forward else up
        store_copies = [pltpu.make_async_copy(fresh, fresh_hbm, state_sems.at[2])]
        if forward:
            wide = rows[...].astype(jnp.float32)
            wide_store[...] = wide
            store_copies.append(pltpu.make_async_copy(wide_store, rows_hbm, state_sems.at[0]))
        else:
            wide = wide_store[...]
        inverse_rms = lax.rsqrt(jnp.mean(wide * wide, axis=1, keepdims=True) + epsilon)
        leads = table[links + 2, 4] == 1
        if forward:
            normed = (wide * inverse_rms).astype(jnp.bfloat16)
            total = [jnp.zeros((sz.row_count, panel), jnp.float32) for _ in range(sz.panels_out)]
            for d in range(parts):
                arrived((d, 0))
                hidden = []
                for p in range(sz.panels_in):
                    weight = weights_in[d, :, p * panel : (p + 1) * panel]
                    preact = dot(normed, weight) * sz.scale_in
                    gate = jax.nn.sigmoid(preact)
                    hidden.append((preact * gate).astype(jnp.bfloat16))
                    column = d * hidden_size + p * panel
                    slope[:, column : column + panel] = gate * (1.0 + preact * (1.0 - gate))
                hidden = jnp.concatenate(hidden, axis=1)
                arrived((d, 1))
                for n in range(sz.panels_out):
                    weight = weights_out[d, :, n * panel : (n + 1) * panel]
                    total[n] = total[n] + dot(hidden, weight)
            total = jnp.concatenate(total, axis=1) * sz.scale_out
            out[...] = (total + jnp.where(leads, wide, 0.0)).astype(jnp.bfloat16)
            store_copies.append(pltpu.make_async_copy(slope, slope_hbm, state_sems.at[1]))
        else:
            up_turned = up[...].T
            total = jnp.zeros((width, sz.row_count), jnp.float32)
            for d in range(parts):
                arrived((d, 1))
                grad_hidden = dot(weights_out[d], up_turned)
                local_slope = slope[:, d * hidden_size : (d + 1) * hidden_size].T
                grad_pre = (grad_hidden * sz.scale_out * local_slope).astype(jnp.bfloat16)
                arrived((d, 0))
                total = total + dot(weights_in[d], grad_pre)
            total = total.T * sz.scale_in
            exact = wide * inverse_rms
            along = jnp.mean(total * exact, axis=1, keepdims=True)
            own = jnp.where(leads, up[...].astype(jnp.float32), 0.0)
            out[...] = (own + inverse_rms * (total - exact * along)).astype(jnp.bfloat16)
        leave = step if forward else links
        send_copies = []
        for e, target in enumerate(sends):
            rows_here = whole if len(sends) == 1 else place(leave, e)
            send_copies.append(
                pltpu.make_async_copy(out.at[rows_here], target, send_sems.at[e])
            )
        for copy in send_copies + store_copies:
            copy.start()
        for copy in send_copies + store_copies:
            copy.wait()


def chain_step(sz, step, forward, table, received, edges, weights, state):
    first = forward and step == 0
    count = 1 if forward and step in (0, sz.sections - 1) else sz.blocks
    anywhere = pl.BlockSpec(memory_space=pl.ANY)
    operands = [table, *received, *edges, *(weights[:2] if first else [*weights, state])]
    block = jax.ShapeDtypeStruct((sz.row_count // count, sz.width), jnp.bfloat16)
    kept = jax.ShapeDtypeStruct((24 * sz.row_count, 2 * sz.local_hidden), jnp.float32)
    fresh = jax.ShapeDtypeStruct((sz.row_count, sz.width), jnp.bfloat16)
    shapes = [block] * count + [fresh, kept]
    in_specs = [pl.BlockSpec(memory_space=pltpu.SMEM)] + [anywhere] * (len(operands) - 1)
    whole = (sz.row_count, sz.width)
    results = pl.pallas_call(
        functools.partial(
            chain_kernel, sz, step, forward, (len(received), len(edges), count)
        ),
        out_shape=shapes,
        in_specs=in_specs,
        out_specs=[anywhere] * len(shapes),
        input_output_aliases={} if first else {len(operands) - 1: count + 1},
        scratch_shapes=[
            pltpu.VMEM((2, sz.width, sz.local_hidden), jnp.bfloat16),
            pltpu.VMEM((2, sz.local_hidden, sz.width), jnp.bfloat16),
            pltpu.VMEM((2,) + whole, jnp.bfloat16),
            pltpu.VMEM(whole, jnp.bfloat16),
            pltpu.VMEM(whole, jnp.bfloat16),
            pltpu.VMEM(whole, jnp.bfloat16),
            pltpu.VMEM((sz.row_count, 2 * sz.local_hidden), jnp.float32),
            pltpu.VMEM(whole, jnp.float32),
            pltpu.SemaphoreType.DMA((2, 2)),
            pltpu.SemaphoreType.DMA((max(1, len(received)),)),
            pltpu.SemaphoreType.DMA((4,)),
            pltpu.SemaphoreType.DMA((count,)),
            pltpu.SemaphoreType.DMA((3,)),
        ],
        compiler_params=pltpu.CompilerParams(vmem_limit_bytes=58 * 1024 * 1024),
        cost_estimate=pl.CostEstimate(
            flops=8 * sz.row_count * sz.width * sz.local_hidden,
            bytes_accessed=8 * sz.width * sz.local_hidden,
            transcendentals=0,
        ),
    )(*operands)
    return list(results[:count]), results[count], results[count + 1]


def share_kernel(sz, whole, *refs):
    if whole:
        known, source, normed_ref, hidden_ref, slope, weights, sem = refs
    else:
        known, slope, source, grad_pre, weights, sem = refs
    panel = sz.panel
    copy = pltpu.make_async_copy(source, weights, sem)
    copy.start()
    if whole:
        wide = known[...].astype(jnp.float32)
        inverse_rms = lax.rsqrt(jnp.mean(wide * wide, axis=1, keepdims=True) + epsilon)
        normed = (wide * inverse_rms).astype(jnp.bfloat16)
        normed_ref[...] = normed
        copy.wait()
        for p in range(sz.panels_in):
            here = slice(p * panel, (p + 1) * panel)
            preact = dot(normed, weights[:, here]) * sz.scale_in
            gate = jax.nn.sigmoid(preact)
            hidden_ref[:, here] = (preact * gate).astype(jnp.bfloat16)
            slope[:, here] = gate * (1.0 + preact * (1.0 - gate))
    else:
        copy.wait()
        grad_hidden = dot(known[...], weights[...], contract_last)
        grad_pre[...] = (grad_hidden * sz.scale_out * slope[...]).astype(jnp.bfloat16)


def share_call(sz, operands, weight):
    whole = len(operands) == 1
    rows_count, hidden_size = sz.row_count, sz.local_hidden
    narrow = jax.ShapeDtypeStruct((rows_count, hidden_size), jnp.bfloat16)
    shapes = [narrow]
    if whole:
        shapes = [
            jax.ShapeDtypeStruct((rows_count, sz.width), jnp.bfloat16),
            narrow,
            jax.ShapeDtypeStruct((rows_count, hidden_size), jnp.float32),
        ]
    inside = pl.BlockSpec(memory_space=pltpu.VMEM)
    return pl.pallas_call(
        functools.partial(share_kernel, sz, whole),
        out_shape=shapes,
        in_specs=[inside] * len(operands) + [pl.BlockSpec(memory_space=pl.ANY)],
        out_specs=[inside] * len(shapes),
        scratch_shapes=[
            pltpu.VMEM(weight.shape, jnp.bfloat16),
            pltpu.SemaphoreType.DMA,
        ],
        compiler_params=pltpu.CompilerParams(vmem_limit_bytes=58 * 1024 * 1024),
        cost_estimate=pl.CostEstimate(
            flops=2 * rows_count * sz.width * hidden_size,
            bytes_accessed=2 * sz.width * hidden_size,
            transcendentals=0,
        ),
    )(*operands, weight)


def per_device(inputs, targets, weight_a, weight_b, moment_a, moment_b, routes, partners):
    replicas = lax.axis_size("replica")
    sections = lax.axis_size("section")
    shards = lax.axis_size("shard")
    replica_id = lax.axis_index("replica")
    section_id = lax.axis_index("section")
    shard_id = lax.axis_index("shard")
    row_count = inputs.shape[2]
    panel = inputs.shape[3]
    width = weight_a.shape[2]
    local_hidden = weight_a.shape[3]
    assert inputs.shape[1] == 1 and shards == 4
    assert local_hidden % panel == 0 and sections > 2
    hidden_total = local_hidden * shards
    scale_in = 1.0 / math.sqrt(width)
    scale_out = 1.0 / math.sqrt(hidden_total)
    weight_in = weight_a[0, 0]
    weight_out = weight_b[0, 0]
    block_rows = row_count // replicas
    links = sections - 1
    in_kernel = block_rows % 16 == 0
    blocks = replicas if in_kernel else 1
    sz = Sizes(sections, row_count, width, local_hidden, panel, hidden_total, blocks)

    def flat(replica, section, shard):
        return (replica * sections + section) * shards + shard

    def turn(section):
        return (section ^ (section >> 1)) & 1

    def holders(section):
        return [j for j in range(shards) if (j & 1) != turn(section)]

    def move(array, sources, target):
        pairs = [
            (flat(r, s, j), flat(*target(r, s, j)))
            for r in range(replicas)
            for s, j in sources
        ]
        return lax.ppermute(array, axes, pairs)

    def holder_sources(active):
        return [(s, j) for s in active for j in holders(s)]

    def to_holders(array, offset, active):
        sources = [(s, j ^ offset) for s, j in holder_sources(active)]
        return move(array, sources, lambda r, s, j: (r, s, j ^ offset))

    def from_holders(array, offset, active):
        return move(array, holder_sources(active), lambda r, s, j: (r, s, j ^ offset))

    def between_holders(array, offset, other_half, section, step):
        shift = turn(section) ^ turn(section + step) ^ (2 * other_half)
        return move(
            array,
            holder_sources([section]),
            lambda r, s, j: ((r + offset) % replicas, s + step, j ^ shift),
        )

    def across_replicas(array, offset, active):
        return move(
            array,
            [(s, j) for s in active for j in range(shards)],
            lambda r, s, j: ((r + offset) % replicas, s, j),
        )

    every = range(sections)
    others = range(1, replicas)
    is_holder = (shard_id & 1) != turn(section_id)

    edge = jnp.where(section_id == 0, inputs[0, 0], targets[0, 0])
    ends = [(s, j) for s in (0, links) for j in range(shards)]

    def at_ends(array, offset):
        return move(array, ends, lambda r, s, j: (r, s, j ^ offset))

    pair = jnp.concatenate([edge, at_ends(edge, 1)])
    edges = [pair, at_ends(pair, 2)]
    rest = range(1, sections)
    near = [to_holders(weight_in, 1, rest), to_holders(weight_out, 1, rest)]

    tables = lax.dynamic_index_in_dim(partners, section_id, 0, keepdims=False)

    def piece_of(table, offset):
        wanted = (replica_id + offset) % replicas
        return jnp.argmax(table[:, replica_id] == wanted).astype(jnp.int32)

    pieces_in = [piece_of(tables[0], e) for e in range(replicas)]
    pieces_out = [piece_of(tables[1], e) for e in range(replicas)]
    size_in = width // replicas
    size_out = local_hidden // replicas

    def piece(array, index, size, axis=0):
        return lax.dynamic_slice_in_dim(array, index * size, size, axis)

    def exchange(arrays, active):
        return [across_replicas(array, e, active) for e, array in zip(others, arrays)]

    packed_in = [
        pack([weight_in, moment_a[0, 0]], pieces_in[e] * size_in, size_in) for e in others
    ]
    packed_out = [
        pack([weight_out, moment_b[0, 0]], pieces_out[e] * size_out, size_out) for e in others
    ]
    early = range(sections // 2, sections)
    late = range(sections // 2)
    far_states_in = exchange(packed_in, every)

    offsets = jnp.arange(replicas, dtype=jnp.int32)
    there = (replica_id + offsets) % replicas
    back = (replica_id - offsets) % replicas
    own_routes = routes[0, :, replica_id, :]
    slots = jnp.sum(
        (own_routes[:, None, :] == there[None, :, None]).astype(jnp.int32)
        * offsets[None, None, :],
        axis=2,
    )
    columns = max(replicas, sections, shards + 1)
    steps = jnp.arange(sections)
    ours = ((is_holder | (steps == 0)) & (section_id == steps)).astype(jnp.int32)
    features = (shard_id ^ jnp.arange(shards, dtype=jnp.int32)) * panel
    leads = (is_holder & ((shard_id & 2) == 0)).astype(jnp.int32)
    features = jnp.append(features, leads)

    def line(values):
        return jnp.pad(values, ((0, 0), (0, columns - values.shape[1])))

    starts = jnp.concatenate([slots, back[None]]) * block_rows
    if not in_kernel:
        starts = jnp.zeros_like(starts)
    table = jnp.concatenate([line(starts), line(ours[None]), line(features[None])])
    table = table.astype(jnp.int32)

    def send_blocks(sends, arrived, left, section, step):
        sign = step
        if in_kernel:
            return [
                between_holders(sends[e], sign * e, a, section, step)
                for e in range(replicas)
                for a in range(2)
            ]
        parts = sends[0].reshape(replicas, block_rows, width)
        moved = [jnp.zeros_like(parts), jnp.zeros_like(parts)]
        for e in range(replicas):
            chosen = lax.dynamic_index_in_dim(parts, left[e], 0, keepdims=False)
            for a in range(2):
                got = between_holders(chosen, sign * e, a, section, step)
                moved[a] = lax.dynamic_update_index_in_dim(moved[a], got, arrived[e], 0)
        return [one.reshape(row_count, width) for one in moved]

    row_parts = []

    def spread_rows(received, rows, active):
        received, rows, row_parts[:] = lax.optimization_barrier(
            (received, rows, row_parts)
        )
        row_parts.append(from_holders(rows, 1, active))
        return received

    weights = [weight_in, weight_out, *near]
    received, state = [], None
    for step in every:
        sends, fresh, state = chain_step(
            sz, step, True, table, received, edges if step == 0 else [], weights, state
        )
        rows = fresh if step == 0 else jnp.where(section_id == step, fresh, rows)
        if step == 0:
            total = sends[0].astype(jnp.float32)
            total = total + at_ends(sends[0], 1).astype(jnp.float32)
            sends = [total.astype(jnp.bfloat16)]
            if in_kernel:
                sends = [piece(sends[0], slots[0, e], block_rows) for e in range(replicas)]
        if step < links:
            received = send_blocks(sends, back, slots[step], step, 1)
            if step == 0:
                received, far_states_in, packed_out = lax.optimization_barrier(
                    (received, far_states_in, packed_out)
                )
                far_states_out = exchange(packed_out, early)
        else:
            received = [sends[0], at_ends(sends[0], 2)]
        if step == len(late) - 1:
            received = spread_rows(received, rows, late)
        if step == len(late) - 1:
            received, packed_out = lax.optimization_barrier((received, packed_out))
            far_late = exchange(packed_out, late)
        if step == len(late):
            received, far_states_out = lax.optimization_barrier((received, far_states_out))

    for step in reversed(range(1, sections)):
        sends, fresh, state = chain_step(
            sz, step, False, table, received, edges if step == links else [], weights, state
        )
        upstream = fresh if step == links else jnp.where(section_id == step, fresh, upstream)
        received = send_blocks(sends, slots[step - 1], back, step, -1)
        if step == links:
            received = spread_rows(received, rows, early)
        if step == len(late):
            received, far_late, row_parts = lax.optimization_barrier(
                (received, far_late, row_parts)
            )

    upstream, rows, row_parts = lax.optimization_barrier((upstream, rows, row_parts))
    own_rows = jnp.where(is_holder, rows, sum(row_parts[1:], row_parts[0]))
    normed, hidden, slope = share_call(sz, [own_rows], weight_in)

    def bundle(e):
        first, second = normed, hidden
        first = piece(first, pieces_in[e], size_in, 1)
        return jnp.concatenate([first, piece(second, pieces_out[e], size_out, 1)], axis=1)

    bundles = exchange([bundle(e) for e in others], every)
    received, bundles = lax.optimization_barrier((received, bundles))
    far_normed = [one[:, :size_in] for one in bundles]
    far_hidden = [one[:, size_in:] for one in bundles]

    halves = []
    for a in range(2):
        half = received[a]
        if in_kernel:
            half = jnp.zeros((row_count, width), jnp.bfloat16)
            for e in range(replicas):
                half = lax.dynamic_update_slice_in_dim(
                    half, received[2 * e + a], slots[0, e] * block_rows, 0
                )
        halves.append(half.astype(jnp.float32))
    first_up = (halves[0] + halves[1]).astype(jnp.bfloat16)
    upstream = jnp.where(section_id == 0, first_up, upstream)
    upstream = jnp.where(is_holder, upstream, from_holders(upstream, 1, every))
    far_up = exchange([upstream] * len(others), every)
    (grad_pre,) = share_call(sz, [upstream, slope], weight_out)
    far_pre = exchange([grad_pre] * len(others), every)
    far_states_out = [
        jnp.where(section_id < len(late), one, two)
        for one, two in zip(far_late, far_states_out)
    ]
    far_states = {0: far_states_in, 2: far_states_out}

    def far_part(e, which):
        size = size_out if which & 2 else size_in
        both = far_states[which & 2][e - 1]
        return both[size:] if which & 1 else both[:size]

    def as_delta(left, right, scale):
        return (inner_rate * (dot(left, right, contract_rows) * scale)).astype(jnp.bfloat16)

    def finish(weight, moment, left, right, which, far_left, far_right, scale, pieces, size):
        new_weight, new_moment = outer_mix(
            weight.astype(jnp.float32),
            moment.astype(jnp.float32),
            as_delta(left, right, scale).astype(jnp.float32),
        )
        for e in others:
            back = replicas - e

            def mean(own_array, far_array):
                return 0.5 * (own_array.astype(jnp.float32) + far_array.astype(jnp.float32))

            index = pieces[back]
            own_left = piece(left, index, size, 1)
            part_weight, part_moment = outer_mix(
                mean(piece(weight, index, size), far_part(e, which)),
                mean(piece(moment, index, size), far_part(e, which + 1)),
                mean(
                    as_delta(own_left, right, scale),
                    as_delta(far_left[e - 1], far_right[e - 1], scale),
                ),
            )
            new_weight = lax.dynamic_update_slice_in_dim(new_weight, part_weight, index * size, 0)
            new_moment = lax.dynamic_update_slice_in_dim(new_moment, part_moment, index * size, 0)
        return new_weight[None, None], new_moment[None, None]

    new_weight_b, new_moment_b = finish(
        weight_out, moment_b[0, 0], hidden, upstream, 2, far_hidden, far_up,
        scale_out, pieces_out, size_out,
    )
    new_weight_a, new_moment_a = finish(
        weight_in, moment_a[0, 0], normed, grad_pre, 0, far_normed, far_pre,
        scale_in, pieces_in, size_in,
    )
    return (new_weight_a, new_weight_b, new_moment_a, new_moment_b)


def solution(mesh):
    placed = (
        P("replica", None, None, "shard"),
        P("replica", None, None, "shard"),
        P("replica", "section", None, "shard"),
        P("replica", "section", "shard", None),
        P("replica", "section", None, "shard"),
        P("replica", "section", "shard", None),
        P(),
        P(),
    )
    return jax.shard_map(
        per_device,
        mesh=mesh,
        in_specs=placed,
        out_specs=(
            P("replica", "section", None, "shard"),
            P("replica", "section", "shard", None),
            P("replica", "section", None, "shard"),
            P("replica", "section", "shard", None),
        ),
        check_vma=False,
    )
```

```python
import functools
import math

import jax
import jax.numpy as jnp
from jax import lax
from jax.experimental import pallas as pl
from jax.experimental.pallas import tpu as pltpu
from jax.sharding import PartitionSpec as P

epsilon = 1e-05
inner_rate = 0.5
momentum_decay = 0.9
outer_rate = 0.7

axes = ("replica", "section", "shard")
contract_rows = (((0,), (0,)), ((), ()))
contract_last = (((1,), (1,)), ((), ()))


def dot(left, right, dims=(((1,), (0,)), ((), ()))):
    return lax.dot_general(left, right, dims, preferred_element_type=jnp.float32)


def outer_mix(weight, moment, delta):
    new_moment = momentum_decay * moment + delta
    new_weight = weight - outer_rate * (momentum_decay * new_moment + delta)
    return new_weight.astype(jnp.bfloat16), new_moment.astype(jnp.bfloat16)


def pack_kernel(size, starts, *refs):
    sources, (packed, buffer, read_sems, write_sems) = refs[:-4], refs[-4:]
    rows = pl.ds(pl.multiple_of(starts[0], size), size)
    reads, writes = [], []
    for k, source in enumerate(sources):
        there = pl.ds(k * size, size)
        reads.append(
            pltpu.make_async_copy(source.at[rows], buffer.at[there], read_sems.at[k])
        )
        writes.append(
            pltpu.make_async_copy(buffer.at[there], packed.at[there], write_sems.at[k])
        )
    for copy in reads:
        copy.start()
    for read, write in zip(reads, writes):
        read.wait()
        write.start()
    for copy in writes:
        copy.wait()


def pack(arrays, start, size):
    shape = (len(arrays) * size, arrays[0].shape[1])
    anywhere = pl.BlockSpec(memory_space=pl.ANY)
    return pl.pallas_call(
        functools.partial(pack_kernel, size),
        out_shape=jax.ShapeDtypeStruct(shape, arrays[0].dtype),
        in_specs=[pl.BlockSpec(memory_space=pltpu.SMEM)] + [anywhere] * len(arrays),
        out_specs=anywhere,
        scratch_shapes=[
            pltpu.VMEM(shape, arrays[0].dtype),
            pltpu.SemaphoreType.DMA((len(arrays),)),
            pltpu.SemaphoreType.DMA((len(arrays),)),
        ],
        compiler_params=pltpu.CompilerParams(vmem_limit_bytes=32 * 1024 * 1024),
        cost_estimate=pl.CostEstimate(
            flops=0, bytes_accessed=4 * shape[0] * shape[1], transcendentals=0
        ),
    )(start.reshape(1), *arrays)


class Sizes:
    def __init__(self, sections, row_count, width, local_hidden, panel, hidden_total, blocks):
        self.sections, self.row_count = sections, row_count
        self.width, self.local_hidden, self.panel = width, local_hidden, panel
        self.blocks = blocks
        self.block_rows = row_count // blocks
        self.panels_in = local_hidden // panel
        self.panels_out = width // panel
        self.scale_in = 1.0 / math.sqrt(width)
        self.scale_out = 1.0 / math.sqrt(hidden_total)


def chain_kernel(sz, step, forward, counts, *refs):
    refs = list(refs)

    def take(count):
        taken = refs[:count]
        del refs[:count]
        return taken

    first = forward and step == 0
    parts = 1 if first else 2
    (table,) = take(1)
    received, edges, sources = take(counts[0]), take(counts[1]), take(2 * parts)
    take(0 if first else 1)
    sends = take(counts[2])
    fresh_hbm, state = take(2)
    weights_in, weights_out, landing, rows, up, out, slope, wide_store = take(8)
    weight_sems, block_sems, edge_sems, send_sems, state_sems = take(5)
    panel, width, hidden_size = sz.panel, sz.width, sz.local_hidden
    links = sz.sections - 1
    whole = pl.ds(0, sz.row_count)

    def weight_copy(d, which):
        weights = (weights_in, weights_out)[which]
        return pltpu.make_async_copy(
            sources[2 * d + which], weights.at[d], weight_sems.at[d, which]
        )

    def place(line, e):
        return pl.ds(pl.multiple_of(table[line, e], sz.block_rows), sz.block_rows)

    def state_part(k, columns):
        return state.at[pl.ds(k * sz.row_count, sz.row_count), pl.ds(0, columns)]

    rows_hbm, slope_hbm = state_part(0, width), state_part(1, 2 * hidden_size)

    @pl.when(table[links + 1, step] == 1)
    def _():
        sequence = [
            (d, which if forward else 1 - which) for d in range(parts) for which in range(2)
        ]
        arrive = links if forward else step
        first_copies = []
        for i, source in enumerate(received):
            e, a = divmod(i, 2)
            rows_there = whole if len(received) == 2 else place(arrive, e)
            first_copies.append(
                pltpu.make_async_copy(source, landing.at[a, rows_there], block_sems.at[i])
            )
        for d in range(2 * len(edges)):
            column = pl.ds(pl.multiple_of(table[links + 2, d], panel), panel)
            source = edges[d // 2].at[pl.ds((d % 2) * sz.row_count, sz.row_count)]
            first_copies.append(
                pltpu.make_async_copy(source, out.at[:, column], edge_sems.at[d])
            )
        if not forward:
            first_copies.append(pltpu.make_async_copy(rows_hbm, wide_store, state_sems.at[0]))
            first_copies.append(pltpu.make_async_copy(slope_hbm, slope, state_sems.at[1]))
        for copy in first_copies:
            copy.start()
        for item in sequence[:2]:
            weight_copy(*item).start()

        def arrived(item):
            weight_copy(*item).wait()
            later = sequence.index(item) + 2
            if later < len(sequence):
                weight_copy(*sequence[later]).start()

        for copy in first_copies:
            copy.wait()
        if received:
            total = landing[0].astype(jnp.float32) + landing[1].astype(jnp.float32)
            total = total.astype(jnp.bfloat16)
        if forward:
            rows[...] = total if received else out[...]
        elif edges:
            goal = out[...].astype(jnp.float32)
            up[...] = (total.astype(jnp.float32) - goal).astype(jnp.bfloat16)
        else:
            up[...] = total
        fresh = rows if forward else up
        store_copies = [pltpu.make_async_copy(fresh, fresh_hbm, state_sems.at[2])]
        if forward:
            wide = rows[...].astype(jnp.float32)
            wide_store[...] = wide
            store_copies.append(pltpu.make_async_copy(wide_store, rows_hbm, state_sems.at[0]))
        else:
            wide = wide_store[...]
        inverse_rms = lax.rsqrt(jnp.mean(wide * wide, axis=1, keepdims=True) + epsilon)
        leads = table[links + 2, 4] == 1
        if forward:
            normed = (wide * inverse_rms).astype(jnp.bfloat16)
            total = [jnp.zeros((sz.row_count, panel), jnp.float32) for _ in range(sz.panels_out)]
            for d in range(parts):
                arrived((d, 0))
                hidden = []
                for p in range(sz.panels_in):
                    weight = weights_in[d, :, p * panel : (p + 1) * panel]
                    preact = dot(normed, weight) * sz.scale_in
                    gate = jax.nn.sigmoid(preact)
                    hidden.append((preact * gate).astype(jnp.bfloat16))
                    column = d * hidden_size + p * panel
                    slope[:, column : column + panel] = gate * (1.0 + preact * (1.0 - gate))
                hidden = jnp.concatenate(hidden, axis=1)
                arrived((d, 1))
                for n in range(sz.panels_out):
                    weight = weights_out[d, :, n * panel : (n + 1) * panel]
                    total[n] = total[n] + dot(hidden, weight)
            total = jnp.concatenate(total, axis=1) * sz.scale_out
            out[...] = (total + jnp.where(leads, wide, 0.0)).astype(jnp.bfloat16)
            store_copies.append(pltpu.make_async_copy(slope, slope_hbm, state_sems.at[1]))
        else:
            up_turned = up[...].T
            total = jnp.zeros((width, sz.row_count), jnp.float32)
            for d in range(parts):
                arrived((d, 1))
                grad_hidden = dot(weights_out[d], up_turned)
                local_slope = slope[:, d * hidden_size : (d + 1) * hidden_size].T
                grad_pre = (grad_hidden * sz.scale_out * local_slope).astype(jnp.bfloat16)
                arrived((d, 0))
                total = total + dot(weights_in[d], grad_pre)
            total = total.T * sz.scale_in
            exact = wide * inverse_rms
            along = jnp.mean(total * exact, axis=1, keepdims=True)
            own = jnp.where(leads, up[...].astype(jnp.float32), 0.0)
            out[...] = (own + inverse_rms * (total - exact * along)).astype(jnp.bfloat16)
        leave = step if forward else links
        send_copies = []
        for e, target in enumerate(sends):
            rows_here = whole if len(sends) == 1 else place(leave, e)
            send_copies.append(
                pltpu.make_async_copy(out.at[rows_here], target, send_sems.at[e])
            )
        for copy in send_copies + store_copies:
            copy.start()
        for copy in send_copies + store_copies:
            copy.wait()


def chain_step(sz, step, forward, table, received, edges, weights, state):
    first = forward and step == 0
    count = 1 if forward and step in (0, sz.sections - 1) else sz.blocks
    anywhere = pl.BlockSpec(memory_space=pl.ANY)
    operands = [table, *received, *edges, *(weights[:2] if first else [*weights, state])]
    block = jax.ShapeDtypeStruct((sz.row_count // count, sz.width), jnp.bfloat16)
    kept = jax.ShapeDtypeStruct((48 * sz.row_count, 2 * sz.local_hidden), jnp.float32)
    fresh = jax.ShapeDtypeStruct((sz.row_count, sz.width), jnp.bfloat16)
    shapes = [block] * count + [fresh, kept]
    in_specs = [pl.BlockSpec(memory_space=pltpu.SMEM)] + [anywhere] * (len(operands) - 1)
    whole = (sz.row_count, sz.width)
    results = pl.pallas_call(
        functools.partial(
            chain_kernel, sz, step, forward, (len(received), len(edges), count)
        ),
        out_shape=shapes,
        in_specs=in_specs,
        out_specs=[anywhere] * len(shapes),
        input_output_aliases={} if first else {len(operands) - 1: count + 1},
        scratch_shapes=[
            pltpu.VMEM((2, sz.width, sz.local_hidden), jnp.bfloat16),
            pltpu.VMEM((2, sz.local_hidden, sz.width), jnp.bfloat16),
            pltpu.VMEM((2,) + whole, jnp.bfloat16),
            pltpu.VMEM(whole, jnp.bfloat16),
            pltpu.VMEM(whole, jnp.bfloat16),
            pltpu.VMEM(whole, jnp.bfloat16),
            pltpu.VMEM((sz.row_count, 2 * sz.local_hidden), jnp.float32),
            pltpu.VMEM(whole, jnp.float32),
            pltpu.SemaphoreType.DMA((2, 2)),
            pltpu.SemaphoreType.DMA((max(1, len(received)),)),
            pltpu.SemaphoreType.DMA((4,)),
            pltpu.SemaphoreType.DMA((count,)),
            pltpu.SemaphoreType.DMA((3,)),
        ],
        compiler_params=pltpu.CompilerParams(vmem_limit_bytes=32 * 1024 * 1024),
        cost_estimate=pl.CostEstimate(
            flops=8 * sz.row_count * sz.width * sz.local_hidden,
            bytes_accessed=8 * sz.width * sz.local_hidden,
            transcendentals=0,
        ),
    )(*operands)
    return list(results[:count]), results[count], results[count + 1]


def share_kernel(sz, whole, *refs):
    if whole:
        known, source, normed_ref, hidden_ref, slope, weights, sem = refs
    else:
        known, slope, source, grad_pre, weights, sem = refs
    panel = sz.panel
    copy = pltpu.make_async_copy(source, weights, sem)
    copy.start()
    if whole:
        wide = known[...].astype(jnp.float32)
        inverse_rms = lax.rsqrt(jnp.mean(wide * wide, axis=1, keepdims=True) + epsilon)
        normed = (wide * inverse_rms).astype(jnp.bfloat16)
        normed_ref[...] = normed
        copy.wait()
        for p in range(sz.panels_in):
            here = slice(p * panel, (p + 1) * panel)
            preact = dot(normed, weights[:, here]) * sz.scale_in
            gate = jax.nn.sigmoid(preact)
            hidden_ref[:, here] = (preact * gate).astype(jnp.bfloat16)
            slope[:, here] = gate * (1.0 + preact * (1.0 - gate))
    else:
        copy.wait()
        grad_hidden = dot(known[...], weights[...], contract_last)
        grad_pre[...] = (grad_hidden * sz.scale_out * slope[...]).astype(jnp.bfloat16)


def share_call(sz, operands, weight):
    whole = len(operands) == 1
    rows_count, hidden_size = sz.row_count, sz.local_hidden
    narrow = jax.ShapeDtypeStruct((rows_count, hidden_size), jnp.bfloat16)
    shapes = [narrow]
    if whole:
        shapes = [
            jax.ShapeDtypeStruct((rows_count, sz.width), jnp.bfloat16),
            narrow,
            jax.ShapeDtypeStruct((rows_count, hidden_size), jnp.float32),
        ]
    inside = pl.BlockSpec(memory_space=pltpu.VMEM)
    return pl.pallas_call(
        functools.partial(share_kernel, sz, whole),
        out_shape=shapes,
        in_specs=[inside] * len(operands) + [pl.BlockSpec(memory_space=pl.ANY)],
        out_specs=[inside] * len(shapes),
        scratch_shapes=[
            pltpu.VMEM(weight.shape, jnp.bfloat16),
            pltpu.SemaphoreType.DMA,
        ],
        compiler_params=pltpu.CompilerParams(vmem_limit_bytes=32 * 1024 * 1024),
        cost_estimate=pl.CostEstimate(
            flops=2 * rows_count * sz.width * hidden_size,
            bytes_accessed=2 * sz.width * hidden_size,
            transcendentals=0,
        ),
    )(*operands, weight)


def per_device(inputs, targets, weight_a, weight_b, moment_a, moment_b, routes, partners):
    replicas = lax.axis_size("replica")
    sections = lax.axis_size("section")
    shards = lax.axis_size("shard")
    replica_id = lax.axis_index("replica")
    section_id = lax.axis_index("section")
    shard_id = lax.axis_index("shard")
    row_count = inputs.shape[2]
    panel = inputs.shape[3]
    width = weight_a.shape[2]
    local_hidden = weight_a.shape[3]
    assert inputs.shape[1] == 1 and shards == 4
    assert local_hidden % panel == 0 and sections > 2
    hidden_total = local_hidden * shards
    scale_in = 1.0 / math.sqrt(width)
    scale_out = 1.0 / math.sqrt(hidden_total)
    weight_in = weight_a[0, 0]
    weight_out = weight_b[0, 0]
    block_rows = row_count // replicas
    links = sections - 1
    in_kernel = block_rows % 16 == 0
    blocks = replicas if in_kernel else 1
    sz = Sizes(sections, row_count, width, local_hidden, panel, hidden_total, blocks)

    def flat(replica, section, shard):
        return (replica * sections + section) * shards + shard

    def turn(section):
        return (section ^ (section >> 1)) & 1

    def holders(section):
        return [j for j in range(shards) if (j & 1) != turn(section)]

    def move(array, sources, target):
        pairs = [
            (flat(r, s, j), flat(*target(r, s, j)))
            for r in range(replicas)
            for s, j in sources
        ]
        return lax.ppermute(array, axes, pairs)

    def holder_sources(active):
        return [(s, j) for s in active for j in holders(s)]

    def to_holders(array, offset, active):
        sources = [(s, j ^ offset) for s, j in holder_sources(active)]
        return move(array, sources, lambda r, s, j: (r, s, j ^ offset))

    def from_holders(array, offset, active):
        return move(array, holder_sources(active), lambda r, s, j: (r, s, j ^ offset))

    def between_holders(array, offset, other_half, section, step):
        shift = turn(section) ^ turn(section + step) ^ (2 * other_half)
        return move(
            array,
            holder_sources([section]),
            lambda r, s, j: ((r + offset) % replicas, s + step, j ^ shift),
        )

    def across_replicas(array, offset, active):
        return move(
            array,
            [(s, j) for s in active for j in range(shards)],
            lambda r, s, j: ((r + offset) % replicas, s, j),
        )

    every = range(sections)
    others = range(1, replicas)
    is_holder = (shard_id & 1) != turn(section_id)

    edge = jnp.where(section_id == 0, inputs[0, 0], targets[0, 0])
    ends = [(s, j) for s in (0, links) for j in range(shards)]

    def at_ends(array, offset):
        return move(array, ends, lambda r, s, j: (r, s, j ^ offset))

    pair = jnp.concatenate([edge, at_ends(edge, 1)])
    edges = [pair, at_ends(pair, 2)]
    rest = range(1, sections)
    near = [to_holders(weight_in, 1, rest), to_holders(weight_out, 1, rest)]

    tables = lax.dynamic_index_in_dim(partners, section_id, 0, keepdims=False)

    def piece_of(table, offset):
        wanted = (replica_id + offset) % replicas
        return jnp.argmax(table[:, replica_id] == wanted).astype(jnp.int32)

    pieces_in = [piece_of(tables[0], e) for e in range(replicas)]
    pieces_out = [piece_of(tables[1], e) for e in range(replicas)]
    size_in = width // replicas
    size_out = local_hidden // replicas

    def piece(array, index, size, axis=0):
        return lax.dynamic_slice_in_dim(array, index * size, size, axis)

    def exchange(arrays, active):
        return [across_replicas(array, e, active) for e, array in zip(others, arrays)]

    packed_in = [
        pack([weight_in, moment_a[0, 0]], pieces_in[e] * size_in, size_in) for e in others
    ]
    packed_out = [
        pack([weight_out, moment_b[0, 0]], pieces_out[e] * size_out, size_out) for e in others
    ]
    early = range(sections // 2, sections)
    late = range(sections // 2)
    far_states_in = exchange(packed_in, every)

    offsets = jnp.arange(replicas, dtype=jnp.int32)
    there = (replica_id + offsets) % replicas
    back = (replica_id - offsets) % replicas
    own_routes = routes[0, :, replica_id, :]
    slots = jnp.sum(
        (own_routes[:, None, :] == there[None, :, None]).astype(jnp.int32)
        * offsets[None, None, :],
        axis=2,
    )
    columns = max(replicas, sections, shards + 1)
    steps = jnp.arange(sections)
    ours = ((is_holder | (steps == 0)) & (section_id == steps)).astype(jnp.int32)
    features = (shard_id ^ jnp.arange(shards, dtype=jnp.int32)) * panel
    leads = (is_holder & ((shard_id & 2) == 0)).astype(jnp.int32)
    features = jnp.append(features, leads)

    def line(values):
        return jnp.pad(values, ((0, 0), (0, columns - values.shape[1])))

    starts = jnp.concatenate([slots, back[None]]) * block_rows
    if not in_kernel:
        starts = jnp.zeros_like(starts)
    table = jnp.concatenate([line(starts), line(ours[None]), line(features[None])])
    table = table.astype(jnp.int32)

    def send_blocks(sends, arrived, left, section, step):
        sign = step
        if in_kernel:
            return [
                between_holders(sends[e], sign * e, a, section, step)
                for e in range(replicas)
                for a in range(2)
            ]
        parts = sends[0].reshape(replicas, block_rows, width)
        moved = [jnp.zeros_like(parts), jnp.zeros_like(parts)]
        for e in range(replicas):
            chosen = lax.dynamic_index_in_dim(parts, left[e], 0, keepdims=False)
            for a in range(2):
                got = between_holders(chosen, sign * e, a, section, step)
                moved[a] = lax.dynamic_update_index_in_dim(moved[a], got, arrived[e], 0)
        return [one.reshape(row_count, width) for one in moved]

    row_parts = []

    def spread_rows(received, rows, active):
        received, rows, row_parts[:] = lax.optimization_barrier(
            (received, rows, row_parts)
        )
        row_parts.append(from_holders(rows, 1, active))
        return received

    def bundle(normed, hidden, e):
        parts = [
            piece(normed, pieces_in[e], size_in, 1), piece(hidden, pieces_out[e], size_out, 1)
        ]
        return jnp.concatenate(parts, axis=1)

    weights = [weight_in, weight_out, *near]
    received, state = [], None
    for step in every:
        sends, fresh, state = chain_step(
            sz, step, True, table, received, edges if step == 0 else [], weights, state
        )
        rows = fresh if step == 0 else jnp.where(section_id == step, fresh, rows)
        if step == 0:
            total = sends[0].astype(jnp.float32)
            total = total + at_ends(sends[0], 1).astype(jnp.float32)
            sends = [total.astype(jnp.bfloat16)]
            if in_kernel:
                sends = [piece(sends[0], slots[0, e], block_rows) for e in range(replicas)]
        if step < links:
            received = send_blocks(sends, back, slots[step], step, 1)
            if step == 0:
                received, far_states_in, packed_out = lax.optimization_barrier(
                    (received, far_states_in, packed_out)
                )
                far_states_out = exchange(packed_out, early)
        else:
            received = [sends[0], at_ends(sends[0], 2)]
            row_parts.append(from_holders(rows, 1, early))
            own_rows = jnp.where(is_holder, rows, sum(row_parts[1:], row_parts[0]))
            received, *shares = lax.optimization_barrier(
                (received, *share_call(sz, [own_rows], weight_in))
            )
            normed, hidden, slope = shares
            bundles = exchange([bundle(normed, hidden, e) for e in others], every)
        if step == len(late) - 1:
            received = spread_rows(received, rows, late)
        if step == len(late) - 1:
            received, packed_out = lax.optimization_barrier((received, packed_out))
            far_late = exchange(packed_out, late)
        if step == len(late):
            received, far_states_out = lax.optimization_barrier((received, far_states_out))

    for step in reversed(range(1, sections)):
        sends, fresh, state = chain_step(
            sz, step, False, table, received, edges if step == links else [], weights, state
        )
        upstream = fresh if step == links else jnp.where(section_id == step, fresh, upstream)
        received = send_blocks(sends, slots[step - 1], back, step, -1)
        if step == len(late):
            received, far_late, bundles = lax.optimization_barrier(
                (received, far_late, bundles)
            )

    far_normed = [one[:, :size_in] for one in bundles]
    far_hidden = [one[:, size_in:] for one in bundles]

    halves = []
    for a in range(2):
        half = received[a]
        if in_kernel:
            half = jnp.zeros((row_count, width), jnp.bfloat16)
            for e in range(replicas):
                half = lax.dynamic_update_slice_in_dim(
                    half, received[2 * e + a], slots[0, e] * block_rows, 0
                )
        halves.append(half.astype(jnp.float32))
    first_up = (halves[0] + halves[1]).astype(jnp.bfloat16)
    upstream = jnp.where(section_id == 0, first_up, upstream)
    upstream = jnp.where(is_holder, upstream, from_holders(upstream, 1, every))
    far_up = exchange([upstream] * len(others), every)
    (grad_pre,) = share_call(sz, [upstream, slope], weight_out)
    far_pre = exchange([grad_pre] * len(others), every)
    far_states_out = [
        jnp.where(section_id < len(late), one, two)
        for one, two in zip(far_late, far_states_out)
    ]
    far_states = {0: far_states_in, 2: far_states_out}

    def far_part(e, which):
        size = size_out if which & 2 else size_in
        both = far_states[which & 2][e - 1]
        return both[size:] if which & 1 else both[:size]

    def as_delta(left, right, scale):
        return (inner_rate * (dot(left, right, contract_rows) * scale)).astype(jnp.bfloat16)

    def finish(weight, moment, left, right, which, far_left, far_right, scale, pieces, size):
        new_weight, new_moment = outer_mix(
            weight.astype(jnp.float32),
            moment.astype(jnp.float32),
            as_delta(left, right, scale).astype(jnp.float32),
        )
        for e in others:
            back = replicas - e

            def mean(own_array, far_array):
                return 0.5 * (own_array.astype(jnp.float32) + far_array.astype(jnp.float32))

            index = pieces[back]
            own_left = piece(left, index, size, 1)
            part_weight, part_moment = outer_mix(
                mean(piece(weight, index, size), far_part(e, which)),
                mean(piece(moment, index, size), far_part(e, which + 1)),
                mean(
                    as_delta(own_left, right, scale),
                    as_delta(far_left[e - 1], far_right[e - 1], scale),
                ),
            )
            new_weight = lax.dynamic_update_slice_in_dim(new_weight, part_weight, index * size, 0)
            new_moment = lax.dynamic_update_slice_in_dim(new_moment, part_moment, index * size, 0)
        return new_weight[None, None], new_moment[None, None]

    new_weight_b, new_moment_b = finish(
        weight_out, moment_b[0, 0], hidden, upstream, 2, far_hidden, far_up,
        scale_out, pieces_out, size_out,
    )
    new_weight_a, new_moment_a = finish(
        weight_in, moment_a[0, 0], normed, grad_pre, 0, far_normed, far_pre,
        scale_in, pieces_in, size_in,
    )
    return (new_weight_a, new_weight_b, new_moment_a, new_moment_b)


def solution(mesh):
    placed = (
        P("replica", None, None, "shard"),
        P("replica", None, None, "shard"),
        P("replica", "section", None, "shard"),
        P("replica", "section", "shard", None),
        P("replica", "section", None, "shard"),
        P("replica", "section", "shard", None),
        P(),
        P(),
    )
    return jax.shard_map(
        per_device,
        mesh=mesh,
        in_specs=placed,
        out_specs=(
            P("replica", "section", None, "shard"),
            P("replica", "section", "shard", None),
            P("replica", "section", None, "shard"),
            P("replica", "section", "shard", None),
        ),
        check_vma=False,
    )
```

```python
import functools
import math

import jax
import jax.numpy as jnp
from jax import lax
from jax.experimental import pallas as pl
from jax.experimental.pallas import tpu as pltpu
from jax.sharding import PartitionSpec as P

epsilon = 1e-05
inner_rate = 0.5
momentum_decay = 0.9
outer_rate = 0.7

axes = ("replica", "section", "shard")
contract_rows = (((0,), (0,)), ((), ()))
contract_last = (((1,), (1,)), ((), ()))


def dot(left, right, dims=(((1,), (0,)), ((), ()))):
    return lax.dot_general(left, right, dims, preferred_element_type=jnp.float32)


def outer_mix(weight, moment, delta):
    new_moment = momentum_decay * moment + delta
    new_weight = weight - outer_rate * (momentum_decay * new_moment + delta)
    return new_weight.astype(jnp.bfloat16), new_moment.astype(jnp.bfloat16)


def pack_kernel(size, starts, *refs):
    sources, (packed, buffer, read_sems, write_sems) = refs[:-4], refs[-4:]
    rows = pl.ds(pl.multiple_of(starts[0], size), size)
    reads, writes = [], []
    for k, source in enumerate(sources):
        there = pl.ds(k * size, size)
        reads.append(
            pltpu.make_async_copy(source.at[rows], buffer.at[there], read_sems.at[k])
        )
        writes.append(
            pltpu.make_async_copy(buffer.at[there], packed.at[there], write_sems.at[k])
        )
    for copy in reads:
        copy.start()
    for read, write in zip(reads, writes):
        read.wait()
        write.start()
    for copy in writes:
        copy.wait()


def pack(arrays, start, size):
    shape = (len(arrays) * size, arrays[0].shape[1])
    anywhere = pl.BlockSpec(memory_space=pl.ANY)
    return pl.pallas_call(
        functools.partial(pack_kernel, size),
        out_shape=jax.ShapeDtypeStruct(shape, arrays[0].dtype),
        in_specs=[pl.BlockSpec(memory_space=pltpu.SMEM)] + [anywhere] * len(arrays),
        out_specs=anywhere,
        scratch_shapes=[
            pltpu.VMEM(shape, arrays[0].dtype),
            pltpu.SemaphoreType.DMA((len(arrays),)),
            pltpu.SemaphoreType.DMA((len(arrays),)),
        ],
        compiler_params=pltpu.CompilerParams(vmem_limit_bytes=32 * 1024 * 1024),
        cost_estimate=pl.CostEstimate(
            flops=0, bytes_accessed=4 * shape[0] * shape[1], transcendentals=0
        ),
    )(start.reshape(1), *arrays)


class Sizes:
    def __init__(self, sections, row_count, width, local_hidden, panel, hidden_total, blocks):
        self.sections, self.row_count = sections, row_count
        self.width, self.local_hidden, self.panel = width, local_hidden, panel
        self.blocks = blocks
        self.block_rows = row_count // blocks
        self.panels_in = local_hidden // panel
        self.panels_out = width // panel
        self.scale_in = 1.0 / math.sqrt(width)
        self.scale_out = 1.0 / math.sqrt(hidden_total)


def kept_place(sz, step, forward):
    return (step if forward else sz.sections + step) * sz.row_count


def chain_kernel(sz, step, forward, counts, *refs):
    refs = list(refs)

    def take(count):
        taken = refs[:count]
        del refs[:count]
        return taken

    first = forward and step == 0
    parts = 1 if first else 2
    (table,) = take(1)
    received, edges, sources = take(counts[0]), take(counts[1]), take(2 * parts)
    take(0 if first else 2)
    sends = take(counts[2])
    kept, state = take(2)
    weights_in, weights_out, landing, rows, up, out, slope, wide_store = take(8)
    weight_sems, block_sems, edge_sems, send_sems, state_sems = take(5)
    panel, width, hidden_size = sz.panel, sz.width, sz.local_hidden
    links = sz.sections - 1
    whole = pl.ds(0, sz.row_count)

    def weight_copy(d, which):
        weights = (weights_in, weights_out)[which]
        return pltpu.make_async_copy(
            sources[2 * d + which], weights.at[d], weight_sems.at[d, which]
        )

    def place(line, e):
        return pl.ds(pl.multiple_of(table[line, e], sz.block_rows), sz.block_rows)

    def state_part(k, columns):
        return state.at[pl.ds(k * sz.row_count, sz.row_count), pl.ds(0, columns)]

    fresh_hbm = kept.at[pl.ds(kept_place(sz, step, forward), sz.row_count)]
    rows_hbm, slope_hbm = state_part(0, width), state_part(1, 2 * hidden_size)

    @pl.when(table[links + 1, step] == 1)
    def _():
        sequence = [
            (d, which if forward else 1 - which) for d in range(parts) for which in range(2)
        ]
        arrive = links if forward else step
        first_copies = []
        for i, source in enumerate(received):
            e, a = divmod(i, 2)
            rows_there = whole if len(received) == 2 else place(arrive, e)
            first_copies.append(
                pltpu.make_async_copy(source, landing.at[a, rows_there], block_sems.at[i])
            )
        for d in range(2 * len(edges)):
            column = pl.ds(pl.multiple_of(table[links + 2, d], panel), panel)
            source = edges[d // 2].at[pl.ds((d % 2) * sz.row_count, sz.row_count)]
            first_copies.append(
                pltpu.make_async_copy(source, out.at[:, column], edge_sems.at[d])
            )
        if not forward:
            first_copies.append(pltpu.make_async_copy(rows_hbm, wide_store, state_sems.at[0]))
            slope_copy = pltpu.make_async_copy(slope_hbm, slope, state_sems.at[1])
        for copy in first_copies:
            copy.start()
        for i, item in enumerate(sequence):
            weight_copy(*item).start()
            if i == 0 and not forward:
                slope_copy.start()

        def arrived(item):
            weight_copy(*item).wait()

        for copy in first_copies:
            copy.wait()
        if received:
            total = landing[0].astype(jnp.float32) + landing[1].astype(jnp.float32)
            total = total.astype(jnp.bfloat16)
        if forward:
            rows[...] = total if received else out[...]
        elif edges:
            goal = out[...].astype(jnp.float32)
            up[...] = (total.astype(jnp.float32) - goal).astype(jnp.bfloat16)
        else:
            up[...] = total
        fresh = rows if forward else up
        store_copies = [pltpu.make_async_copy(fresh, fresh_hbm, state_sems.at[2])]
        if forward:
            wide = rows[...].astype(jnp.float32)
            wide_store[...] = wide
            store_copies.append(pltpu.make_async_copy(wide_store, rows_hbm, state_sems.at[0]))
        else:
            wide = wide_store[...]
        inverse_rms = lax.rsqrt(jnp.mean(wide * wide, axis=1, keepdims=True) + epsilon)
        leads = table[links + 2, 4] == 1
        if forward:
            normed = (wide * inverse_rms).astype(jnp.bfloat16)
            total = [jnp.zeros((sz.row_count, panel), jnp.float32) for _ in range(sz.panels_out)]
            for d in range(parts):
                arrived((d, 0))
                hidden = []
                for p in range(sz.panels_in):
                    weight = weights_in[d, :, p * panel : (p + 1) * panel]
                    preact = dot(normed, weight) * sz.scale_in
                    gate = jax.nn.sigmoid(preact)
                    hidden.append((preact * gate).astype(jnp.bfloat16))
                    column = d * hidden_size + p * panel
                    slope[:, column : column + panel] = gate * (1.0 + preact * (1.0 - gate))
                hidden = jnp.concatenate(hidden, axis=1)
                arrived((d, 1))
                for n in range(sz.panels_out):
                    weight = weights_out[d, :, n * panel : (n + 1) * panel]
                    total[n] = total[n] + dot(hidden, weight)
            total = jnp.concatenate(total, axis=1) * sz.scale_out
            out[...] = (total + jnp.where(leads, wide, 0.0)).astype(jnp.bfloat16)
            store_copies.append(pltpu.make_async_copy(slope, slope_hbm, state_sems.at[1]))
        else:
            up_turned = up[...].T
            total = jnp.zeros((width, sz.row_count), jnp.float32)
            for d in range(parts):
                arrived((d, 1))
                grad_hidden = dot(weights_out[d], up_turned)
                if d == 0:
                    slope_copy.wait()
                local_slope = slope[:, d * hidden_size : (d + 1) * hidden_size].T
                grad_pre = (grad_hidden * sz.scale_out * local_slope).astype(jnp.bfloat16)
                arrived((d, 0))
                total = total + dot(weights_in[d], grad_pre)
            total = total.T * sz.scale_in
            exact = wide * inverse_rms
            along = jnp.mean(total * exact, axis=1, keepdims=True)
            own = jnp.where(leads, up[...].astype(jnp.float32), 0.0)
            out[...] = (own + inverse_rms * (total - exact * along)).astype(jnp.bfloat16)
        leave = step if forward else links
        send_copies = []
        for e, target in enumerate(sends):
            rows_here = whole if len(sends) == 1 else place(leave, e)
            send_copies.append(
                pltpu.make_async_copy(out.at[rows_here], target, send_sems.at[e])
            )
        for copy in send_copies + store_copies:
            copy.start()
        for copy in send_copies + store_copies:
            copy.wait()


def chain_step(sz, step, forward, table, received, edges, weights, stores):
    first = forward and step == 0
    count = 1 if forward and step in (0, sz.sections - 1) else sz.blocks
    anywhere = pl.BlockSpec(memory_space=pl.ANY)
    operands = [table, *received, *edges, *(weights[:2] if first else [*weights, *stores])]
    block = jax.ShapeDtypeStruct((sz.row_count // count, sz.width), jnp.bfloat16)
    shapes = [block] * count + [
        jax.ShapeDtypeStruct((144 * sz.row_count, sz.width), jnp.bfloat16),
        jax.ShapeDtypeStruct((48 * sz.row_count, 2 * sz.local_hidden), jnp.float32),
    ]
    in_specs = [pl.BlockSpec(memory_space=pltpu.SMEM)] + [anywhere] * (len(operands) - 1)
    whole = (sz.row_count, sz.width)
    results = pl.pallas_call(
        functools.partial(
            chain_kernel, sz, step, forward, (len(received), len(edges), count)
        ),
        out_shape=shapes,
        in_specs=in_specs,
        out_specs=[anywhere] * len(shapes),
        input_output_aliases=(
            {} if first else {len(operands) - 2: count, len(operands) - 1: count + 1}
        ),
        scratch_shapes=[
            pltpu.VMEM((2, sz.width, sz.local_hidden), jnp.bfloat16),
            pltpu.VMEM((2, sz.local_hidden, sz.width), jnp.bfloat16),
            pltpu.VMEM((2,) + whole, jnp.bfloat16),
            pltpu.VMEM(whole, jnp.bfloat16),
            pltpu.VMEM(whole, jnp.bfloat16),
            pltpu.VMEM(whole, jnp.bfloat16),
            pltpu.VMEM((sz.row_count, 2 * sz.local_hidden), jnp.float32),
            pltpu.VMEM(whole, jnp.float32),
            pltpu.SemaphoreType.DMA((2, 2)),
            pltpu.SemaphoreType.DMA((max(1, len(received)),)),
            pltpu.SemaphoreType.DMA((4,)),
            pltpu.SemaphoreType.DMA((count,)),
            pltpu.SemaphoreType.DMA((3,)),
        ],
        compiler_params=pltpu.CompilerParams(vmem_limit_bytes=32 * 1024 * 1024),
        cost_estimate=pl.CostEstimate(
            flops=8 * sz.row_count * sz.width * sz.local_hidden,
            bytes_accessed=8 * sz.width * sz.local_hidden,
            transcendentals=0,
        ),
    )(*operands)
    return list(results[:count]), list(results[count:])


def share_kernel(sz, whole, *refs):
    if whole:
        known, source, normed_ref, hidden_ref, slope, weights, sem = refs
    else:
        known, slope, source, grad_pre, weights, sem = refs
    panel = sz.panel
    copy = pltpu.make_async_copy(source, weights, sem)
    copy.start()
    if whole:
        wide = known[...].astype(jnp.float32)
        inverse_rms = lax.rsqrt(jnp.mean(wide * wide, axis=1, keepdims=True) + epsilon)
        normed = (wide * inverse_rms).astype(jnp.bfloat16)
        normed_ref[...] = normed
        copy.wait()
        for p in range(sz.panels_in):
            here = slice(p * panel, (p + 1) * panel)
            preact = dot(normed, weights[:, here]) * sz.scale_in
            gate = jax.nn.sigmoid(preact)
            hidden_ref[:, here] = (preact * gate).astype(jnp.bfloat16)
            slope[:, here] = gate * (1.0 + preact * (1.0 - gate))
    else:
        copy.wait()
        grad_hidden = dot(known[...], weights[...], contract_last)
        grad_pre[...] = (grad_hidden * sz.scale_out * slope[...]).astype(jnp.bfloat16)


def share_call(sz, operands, weight):
    whole = len(operands) == 1
    rows_count, hidden_size = sz.row_count, sz.local_hidden
    narrow = jax.ShapeDtypeStruct((rows_count, hidden_size), jnp.bfloat16)
    shapes = [narrow]
    if whole:
        shapes = [
            jax.ShapeDtypeStruct((rows_count, sz.width), jnp.bfloat16),
            narrow,
            jax.ShapeDtypeStruct((rows_count, hidden_size), jnp.float32),
        ]
    inside = pl.BlockSpec(memory_space=pltpu.VMEM)
    return pl.pallas_call(
        functools.partial(share_kernel, sz, whole),
        out_shape=shapes,
        in_specs=[inside] * len(operands) + [pl.BlockSpec(memory_space=pl.ANY)],
        out_specs=[inside] * len(shapes),
        scratch_shapes=[
            pltpu.VMEM(weight.shape, jnp.bfloat16),
            pltpu.SemaphoreType.DMA,
        ],
        compiler_params=pltpu.CompilerParams(vmem_limit_bytes=32 * 1024 * 1024),
        cost_estimate=pl.CostEstimate(
            flops=2 * rows_count * sz.width * hidden_size,
            bytes_accessed=2 * sz.width * hidden_size,
            transcendentals=0,
        ),
    )(*operands, weight)


def per_device(inputs, targets, weight_a, weight_b, moment_a, moment_b, routes, partners):
    replicas = lax.axis_size("replica")
    sections = lax.axis_size("section")
    shards = lax.axis_size("shard")
    replica_id = lax.axis_index("replica")
    section_id = lax.axis_index("section")
    shard_id = lax.axis_index("shard")
    row_count = inputs.shape[2]
    panel = inputs.shape[3]
    width = weight_a.shape[2]
    local_hidden = weight_a.shape[3]
    assert inputs.shape[1] == 1 and shards == 4
    assert local_hidden % panel == 0 and sections > 2
    hidden_total = local_hidden * shards
    scale_in = 1.0 / math.sqrt(width)
    scale_out = 1.0 / math.sqrt(hidden_total)
    weight_in = weight_a[0, 0]
    weight_out = weight_b[0, 0]
    block_rows = row_count // replicas
    links = sections - 1
    in_kernel = block_rows % 16 == 0
    blocks = replicas if in_kernel else 1
    sz = Sizes(sections, row_count, width, local_hidden, panel, hidden_total, blocks)

    def flat(replica, section, shard):
        return (replica * sections + section) * shards + shard

    def turn(section):
        return (section ^ (section >> 1)) & 1

    def holders(section):
        return [j for j in range(shards) if (j & 1) != turn(section)]

    def move(array, sources, target):
        pairs = [
            (flat(r, s, j), flat(*target(r, s, j)))
            for r in range(replicas)
            for s, j in sources
        ]
        return lax.ppermute(array, axes, pairs)

    def holder_sources(active):
        return [(s, j) for s in active for j in holders(s)]

    def to_holders(array, offset, active):
        sources = [(s, j ^ offset) for s, j in holder_sources(active)]
        return move(array, sources, lambda r, s, j: (r, s, j ^ offset))

    def from_holders(array, offset, active):
        return move(array, holder_sources(active), lambda r, s, j: (r, s, j ^ offset))

    def between_holders(array, offset, other_half, section, step):
        shift = turn(section) ^ turn(section + step) ^ (2 * other_half)
        return move(
            array,
            holder_sources([section]),
            lambda r, s, j: ((r + offset) % replicas, s + step, j ^ shift),
        )

    def across_replicas(array, offset, active):
        return move(
            array,
            [(s, j) for s in active for j in range(shards)],
            lambda r, s, j: ((r + offset) % replicas, s, j),
        )

    every = range(sections)
    others = range(1, replicas)
    is_holder = (shard_id & 1) != turn(section_id)

    edge = jnp.where(section_id == 0, inputs[0, 0], targets[0, 0])
    ends = [(s, j) for s in (0, links) for j in range(shards)]

    def at_ends(array, offset):
        return move(array, ends, lambda r, s, j: (r, s, j ^ offset))

    pair = jnp.concatenate([edge, at_ends(edge, 1)])
    edges = [pair, at_ends(pair, 2)]
    rest = range(1, sections)
    near = [to_holders(weight_in, 1, rest), to_holders(weight_out, 1, rest)]

    tables = lax.dynamic_index_in_dim(partners, section_id, 0, keepdims=False)

    def piece_of(table, offset):
        wanted = (replica_id + offset) % replicas
        return jnp.argmax(table[:, replica_id] == wanted).astype(jnp.int32)

    pieces_in = [piece_of(tables[0], e) for e in range(replicas)]
    pieces_out = [piece_of(tables[1], e) for e in range(replicas)]
    size_in = width // replicas
    size_out = local_hidden // replicas

    def piece(array, index, size, axis=0):
        return lax.dynamic_slice_in_dim(array, index * size, size, axis)

    def exchange(arrays, active):
        return [across_replicas(array, e, active) for e, array in zip(others, arrays)]

    packed_in = [
        pack([weight_in, moment_a[0, 0]], pieces_in[e] * size_in, size_in) for e in others
    ]
    packed_out = [
        pack([weight_out, moment_b[0, 0]], pieces_out[e] * size_out, size_out) for e in others
    ]
    early = range(sections // 2, sections)
    late = range(sections // 2)
    far_states_in = exchange(packed_in, every)

    offsets = jnp.arange(replicas, dtype=jnp.int32)
    there = (replica_id + offsets) % replicas
    back = (replica_id - offsets) % replicas
    own_routes = routes[0, :, replica_id, :]
    slots = jnp.sum(
        (own_routes[:, None, :] == there[None, :, None]).astype(jnp.int32)
        * offsets[None, None, :],
        axis=2,
    )
    columns = max(replicas, sections, shards + 1)
    steps = jnp.arange(sections)
    ours = ((is_holder | (steps == 0)) & (section_id == steps)).astype(jnp.int32)
    features = (shard_id ^ jnp.arange(shards, dtype=jnp.int32)) * panel
    leads = (is_holder & ((shard_id & 2) == 0)).astype(jnp.int32)
    features = jnp.append(features, leads)

    def line(values):
        return jnp.pad(values, ((0, 0), (0, columns - values.shape[1])))

    starts = jnp.concatenate([slots, back[None]]) * block_rows
    if not in_kernel:
        starts = jnp.zeros_like(starts)
    table = jnp.concatenate([line(starts), line(ours[None]), line(features[None])])
    table = table.astype(jnp.int32)

    def send_blocks(sends, arrived, left, section, step):
        sign = step
        if in_kernel:
            return [
                between_holders(sends[e], sign * e, a, section, step)
                for e in range(replicas)
                for a in range(2)
            ]
        parts = sends[0].reshape(replicas, block_rows, width)
        moved = [jnp.zeros_like(parts), jnp.zeros_like(parts)]
        for e in range(replicas):
            chosen = lax.dynamic_index_in_dim(parts, left[e], 0, keepdims=False)
            for a in range(2):
                got = between_holders(chosen, sign * e, a, section, step)
                moved[a] = lax.dynamic_update_index_in_dim(moved[a], got, arrived[e], 0)
        return [one.reshape(row_count, width) for one in moved]

    def kept_of(stores, steps, forward):
        places = [kept_place(sz, step, forward) for step in steps]
        result = stores[0][places[0] : places[0] + row_count]
        for step, place in zip(steps[1:], places[1:]):
            result = jnp.where(section_id == step, stores[0][place : place + row_count], result)
        return result

    row_parts = []

    def spread_rows(received, rows, active):
        received, rows, row_parts[:] = lax.optimization_barrier(
            (received, rows, row_parts)
        )
        row_parts.append(from_holders(rows, 1, active))
        return received

    def bundle(normed, hidden, e):
        parts = [
            piece(normed, pieces_in[e], size_in, 1), piece(hidden, pieces_out[e], size_out, 1)
        ]
        return jnp.concatenate(parts, axis=1)

    weights = [weight_in, weight_out, *near]
    received, stores = [], []
    for step in every:
        sends, stores = chain_step(
            sz, step, True, table, received, edges if step == 0 else [], weights, stores
        )
        if step in (len(late) - 1, links):
            rows = kept_of(stores, range(step + 1), True)
        if step == 0:
            total = sends[0].astype(jnp.float32)
            total = total + at_ends(sends[0], 1).astype(jnp.float32)
            sends = [total.astype(jnp.bfloat16)]
            if in_kernel:
                sends = [piece(sends[0], slots[0, e], block_rows) for e in range(replicas)]
        if step < links:
            received = send_blocks(sends, back, slots[step], step, 1)
            if step == 0:
                received, far_states_in, packed_out = lax.optimization_barrier(
                    (received, far_states_in, packed_out)
                )
                far_states_out = exchange(packed_out, early)
        else:
            received = [sends[0], at_ends(sends[0], 2)]
            row_parts.append(from_holders(rows, 1, early))
            own_rows = jnp.where(is_holder, rows, sum(row_parts[1:], row_parts[0]))
            received, *shares = lax.optimization_barrier(
                (received, *share_call(sz, [own_rows], weight_in))
            )
            normed, hidden, slope = shares
            bundles = exchange([bundle(normed, hidden, e) for e in others], every)
        if step == len(late) - 1:
            received = spread_rows(received, rows, late)
        if step == len(late) - 1:
            received, packed_out = lax.optimization_barrier((received, packed_out))
            far_late = exchange(packed_out, late)
        if step == len(late):
            received, far_states_out = lax.optimization_barrier((received, far_states_out))

    for step in reversed(range(1, sections)):
        sends, stores = chain_step(
            sz, step, False, table, received, edges if step == links else [], weights, stores
        )
        received = send_blocks(sends, slots[step - 1], back, step, -1)
        if step == len(late):
            received, far_late, bundles = lax.optimization_barrier(
                (received, far_late, bundles)
            )

    far_normed = [one[:, :size_in] for one in bundles]
    far_hidden = [one[:, size_in:] for one in bundles]

    halves = []
    for a in range(2):
        half = received[a]
        if in_kernel:
            half = jnp.zeros((row_count, width), jnp.bfloat16)
            for e in range(replicas):
                half = lax.dynamic_update_slice_in_dim(
                    half, received[2 * e + a], slots[0, e] * block_rows, 0
                )
        halves.append(half.astype(jnp.float32))
    first_up = (halves[0] + halves[1]).astype(jnp.bfloat16)
    upstream = jnp.where(section_id == 0, first_up, kept_of(stores, rest, False))
    upstream = jnp.where(is_holder, upstream, from_holders(upstream, 1, every))
    far_up = exchange([upstream] * len(others), every)
    (grad_pre,) = share_call(sz, [upstream, slope], weight_out)
    far_pre = exchange([grad_pre] * len(others), every)
    far_states_out = [
        jnp.where(section_id < len(late), one, two)
        for one, two in zip(far_late, far_states_out)
    ]
    far_states = {0: far_states_in, 2: far_states_out}

    def far_part(e, which):
        size = size_out if which & 2 else size_in
        both = far_states[which & 2][e - 1]
        return both[size:] if which & 1 else both[:size]

    def as_delta(left, right, scale):
        return (inner_rate * (dot(left, right, contract_rows) * scale)).astype(jnp.bfloat16)

    def finish(weight, moment, left, right, which, far_left, far_right, scale, pieces, size):
        new_weight, new_moment = outer_mix(
            weight.astype(jnp.float32),
            moment.astype(jnp.float32),
            as_delta(left, right, scale).astype(jnp.float32),
        )
        for e in others:
            back = replicas - e

            def mean(own_array, far_array):
                return 0.5 * (own_array.astype(jnp.float32) + far_array.astype(jnp.float32))

            index = pieces[back]
            own_left = piece(left, index, size, 1)
            part_weight, part_moment = outer_mix(
                mean(piece(weight, index, size), far_part(e, which)),
                mean(piece(moment, index, size), far_part(e, which + 1)),
                mean(
                    as_delta(own_left, right, scale),
                    as_delta(far_left[e - 1], far_right[e - 1], scale),
                ),
            )
            new_weight = lax.dynamic_update_slice_in_dim(new_weight, part_weight, index * size, 0)
            new_moment = lax.dynamic_update_slice_in_dim(new_moment, part_moment, index * size, 0)
        return new_weight[None, None], new_moment[None, None]

    new_weight_b, new_moment_b = finish(
        weight_out, moment_b[0, 0], hidden, upstream, 2, far_hidden, far_up,
        scale_out, pieces_out, size_out,
    )
    new_weight_a, new_moment_a = finish(
        weight_in, moment_a[0, 0], normed, grad_pre, 0, far_normed, far_pre,
        scale_in, pieces_in, size_in,
    )
    return (new_weight_a, new_weight_b, new_moment_a, new_moment_b)


def solution(mesh):
    placed = (
        P("replica", None, None, "shard"),
        P("replica", None, None, "shard"),
        P("replica", "section", None, "shard"),
        P("replica", "section", "shard", None),
        P("replica", "section", None, "shard"),
        P("replica", "section", "shard", None),
        P(),
        P(),
    )
    return jax.shard_map(
        per_device,
        mesh=mesh,
        in_specs=placed,
        out_specs=(
            P("replica", "section", None, "shard"),
            P("replica", "section", "shard", None),
            P("replica", "section", None, "shard"),
            P("replica", "section", "shard", None),
        ),
        check_vma=False,
    )
```

```python
import functools
import math

import jax
import jax.numpy as jnp
from jax import lax
from jax.experimental import pallas as pl
from jax.experimental.pallas import tpu as pltpu
from jax.sharding import PartitionSpec as P

epsilon = 1e-05
inner_rate = 0.5
momentum_decay = 0.9
outer_rate = 0.7

axes = ("replica", "section", "shard")
contract_rows = (((0,), (0,)), ((), ()))
contract_last = (((1,), (1,)), ((), ()))


def dot(left, right, dims=(((1,), (0,)), ((), ()))):
    return lax.dot_general(left, right, dims, preferred_element_type=jnp.float32)


def outer_mix(weight, moment, delta):
    new_moment = momentum_decay * moment + delta
    new_weight = weight - outer_rate * (momentum_decay * new_moment + delta)
    return new_weight.astype(jnp.bfloat16), new_moment.astype(jnp.bfloat16)


def pack_kernel(size, starts, *refs):
    sources, (packed, buffer, read_sems, write_sems) = refs[:-4], refs[-4:]
    rows = pl.ds(pl.multiple_of(starts[0], size), size)
    reads, writes = [], []
    for k, source in enumerate(sources):
        there = pl.ds(k * size, size)
        reads.append(
            pltpu.make_async_copy(source.at[rows], buffer.at[there], read_sems.at[k])
        )
        writes.append(
            pltpu.make_async_copy(buffer.at[there], packed.at[there], write_sems.at[k])
        )
    for copy in reads:
        copy.start()
    for read, write in zip(reads, writes):
        read.wait()
        write.start()
    for copy in writes:
        copy.wait()


def pack(arrays, start, size):
    shape = (len(arrays) * size, arrays[0].shape[1])
    anywhere = pl.BlockSpec(memory_space=pl.ANY)
    return pl.pallas_call(
        functools.partial(pack_kernel, size),
        out_shape=jax.ShapeDtypeStruct(shape, arrays[0].dtype),
        in_specs=[pl.BlockSpec(memory_space=pltpu.SMEM)] + [anywhere] * len(arrays),
        out_specs=anywhere,
        scratch_shapes=[
            pltpu.VMEM(shape, arrays[0].dtype),
            pltpu.SemaphoreType.DMA((len(arrays),)),
            pltpu.SemaphoreType.DMA((len(arrays),)),
        ],
        compiler_params=pltpu.CompilerParams(vmem_limit_bytes=32 * 1024 * 1024),
        cost_estimate=pl.CostEstimate(
            flops=0, bytes_accessed=4 * shape[0] * shape[1], transcendentals=0
        ),
    )(start.reshape(1), *arrays)


class Sizes:
    def __init__(self, sections, row_count, width, local_hidden, panel, hidden_total, blocks):
        self.sections, self.row_count = sections, row_count
        self.width, self.local_hidden, self.panel = width, local_hidden, panel
        self.blocks = blocks
        self.block_rows = row_count // blocks
        self.panels_in = local_hidden // panel
        self.panels_out = width // panel
        self.scale_in = 1.0 / math.sqrt(width)
        self.scale_out = 1.0 / math.sqrt(hidden_total)


def kept_place(sz, step, forward):
    return (step if forward else sz.sections + step) * sz.row_count


def chain_kernel(sz, step, forward, counts, *refs):
    refs = list(refs)

    def take(count):
        taken = refs[:count]
        del refs[:count]
        return taken

    first = forward and step == 0
    parts = 1 if first else 2
    (table,) = take(1)
    received, edges, sources = take(counts[0]), take(counts[1]), take(2 * parts)
    take(0 if first else 2)
    sends = take(counts[2])
    kept, state = take(2)
    weights_in, weights_out, landing, rows, up, out, slope, wide_store = take(8)
    weight_sems, block_sems, edge_sems, send_sems, state_sems = take(5)
    panel, width, hidden_size = sz.panel, sz.width, sz.local_hidden
    links = sz.sections - 1
    whole = pl.ds(0, sz.row_count)

    def weight_copy(d, which):
        weights = (weights_in, weights_out)[which]
        return pltpu.make_async_copy(
            sources[2 * d + which], weights.at[d], weight_sems.at[d, which]
        )

    def place(line, e):
        return pl.ds(pl.multiple_of(table[line, e], sz.block_rows), sz.block_rows)

    def state_part(k, columns):
        return state.at[pl.ds(k * sz.row_count, sz.row_count), pl.ds(0, columns)]

    fresh_hbm = kept.at[pl.ds(kept_place(sz, step, forward), sz.row_count)]
    rows_hbm, slope_hbm = state_part(0, width), state_part(1, 2 * hidden_size)

    @pl.when(table[links + 1, step] == 1)
    def _():
        sequence = [
            (d, which if forward else 1 - which) for d in range(parts) for which in range(2)
        ]
        arrive = links if forward else step
        first_copies = []
        for i, source in enumerate(received):
            e, a = divmod(i, 2)
            rows_there = whole if len(received) == 2 else place(arrive, e)
            first_copies.append(
                pltpu.make_async_copy(source, landing.at[a, rows_there], block_sems.at[i])
            )
        for d in range(2 * len(edges)):
            column = pl.ds(pl.multiple_of(table[links + 2, d], panel), panel)
            source = edges[d // 2].at[pl.ds((d % 2) * sz.row_count, sz.row_count)]
            first_copies.append(
                pltpu.make_async_copy(source, out.at[:, column], edge_sems.at[d])
            )
        if not forward:
            first_copies.append(pltpu.make_async_copy(rows_hbm, wide_store, state_sems.at[0]))
            slope_copy = pltpu.make_async_copy(slope_hbm, slope, state_sems.at[1])
        for copy in first_copies:
            copy.start()
        for i, item in enumerate(sequence):
            weight_copy(*item).start()
            if i == 0 and not forward:
                slope_copy.start()

        def arrived(item):
            weight_copy(*item).wait()

        for copy in first_copies:
            copy.wait()
        if received:
            total = landing[0].astype(jnp.float32) + landing[1].astype(jnp.float32)
            total = total.astype(jnp.bfloat16)
        if forward:
            rows[...] = total if received else out[...]
        elif edges:
            goal = out[...].astype(jnp.float32)
            up[...] = (total.astype(jnp.float32) - goal).astype(jnp.bfloat16)
        else:
            up[...] = total
        fresh = rows if forward else up
        store_copies = [pltpu.make_async_copy(fresh, fresh_hbm, state_sems.at[2])]
        if forward:
            wide = rows[...].astype(jnp.float32)
            wide_store[...] = wide
            store_copies.append(pltpu.make_async_copy(wide_store, rows_hbm, state_sems.at[0]))
        else:
            wide = wide_store[...]
        inverse_rms = lax.rsqrt(jnp.mean(wide * wide, axis=1, keepdims=True) + epsilon)
        leads = table[links + 2, 4] == 1
        if forward:
            normed = (wide * inverse_rms).astype(jnp.bfloat16)
            total = [jnp.zeros((sz.row_count, panel), jnp.float32) for _ in range(sz.panels_out)]
            for d in range(parts):
                arrived((d, 0))
                hidden = []
                for p in range(sz.panels_in):
                    weight = weights_in[d, :, p * panel : (p + 1) * panel]
                    preact = dot(normed, weight) * sz.scale_in
                    gate = jax.nn.sigmoid(preact)
                    hidden.append((preact * gate).astype(jnp.bfloat16))
                    column = d * hidden_size + p * panel
                    slope[:, column : column + panel] = gate * (1.0 + preact * (1.0 - gate))
                hidden = jnp.concatenate(hidden, axis=1)
                arrived((d, 1))
                for n in range(sz.panels_out):
                    weight = weights_out[d, :, n * panel : (n + 1) * panel]
                    total[n] = total[n] + dot(hidden, weight)
            total = jnp.concatenate(total, axis=1) * sz.scale_out
            out[...] = (total + jnp.where(leads, wide, 0.0)).astype(jnp.bfloat16)
            store_copies.append(pltpu.make_async_copy(slope, slope_hbm, state_sems.at[1]))
        else:
            up_turned = up[...].T
            total = jnp.zeros((width, sz.row_count), jnp.float32)
            for d in range(parts):
                arrived((d, 1))
                grad_hidden = dot(weights_out[d], up_turned)
                if d == 0:
                    slope_copy.wait()
                local_slope = slope[:, d * hidden_size : (d + 1) * hidden_size].T
                grad_pre = (grad_hidden * sz.scale_out * local_slope).astype(jnp.bfloat16)
                arrived((d, 0))
                total = total + dot(weights_in[d], grad_pre)
            total = total.T * sz.scale_in
            exact = wide * inverse_rms
            along = jnp.mean(total * exact, axis=1, keepdims=True)
            own = jnp.where(leads, up[...].astype(jnp.float32), 0.0)
            out[...] = (own + inverse_rms * (total - exact * along)).astype(jnp.bfloat16)
        leave = step if forward else links
        send_copies = []
        for e, target in enumerate(sends):
            rows_here = whole if len(sends) == 1 else place(leave, e)
            send_copies.append(
                pltpu.make_async_copy(out.at[rows_here], target, send_sems.at[e])
            )
        for copy in send_copies + store_copies:
            copy.start()
        for copy in send_copies + store_copies:
            copy.wait()


def chain_step(sz, step, forward, table, received, edges, weights, stores):
    first = forward and step == 0
    count = 1 if forward and step in (0, sz.sections - 1) else sz.blocks
    anywhere = pl.BlockSpec(memory_space=pl.ANY)
    operands = [table, *received, *edges, *(weights[:2] if first else [*weights, *stores])]
    block = jax.ShapeDtypeStruct((sz.row_count // count, sz.width), jnp.bfloat16)
    shapes = [block] * count + [
        jax.ShapeDtypeStruct((144 * sz.row_count, sz.width), jnp.bfloat16),
        jax.ShapeDtypeStruct((48 * sz.row_count, 2 * sz.local_hidden), jnp.float32),
    ]
    in_specs = [pl.BlockSpec(memory_space=pltpu.SMEM)] + [anywhere] * (len(operands) - 1)
    whole = (sz.row_count, sz.width)
    results = pl.pallas_call(
        functools.partial(
            chain_kernel, sz, step, forward, (len(received), len(edges), count)
        ),
        out_shape=shapes,
        in_specs=in_specs,
        out_specs=[anywhere] * len(shapes),
        input_output_aliases=(
            {} if first else {len(operands) - 2: count, len(operands) - 1: count + 1}
        ),
        scratch_shapes=[
            pltpu.VMEM((2, sz.width, sz.local_hidden), jnp.bfloat16),
            pltpu.VMEM((2, sz.local_hidden, sz.width), jnp.bfloat16),
            pltpu.VMEM((2,) + whole, jnp.bfloat16),
            pltpu.VMEM(whole, jnp.bfloat16),
            pltpu.VMEM(whole, jnp.bfloat16),
            pltpu.VMEM(whole, jnp.bfloat16),
            pltpu.VMEM((sz.row_count, 2 * sz.local_hidden), jnp.float32),
            pltpu.VMEM(whole, jnp.float32),
            pltpu.SemaphoreType.DMA((2, 2)),
            pltpu.SemaphoreType.DMA((max(1, len(received)),)),
            pltpu.SemaphoreType.DMA((4,)),
            pltpu.SemaphoreType.DMA((count,)),
            pltpu.SemaphoreType.DMA((3,)),
        ],
        compiler_params=pltpu.CompilerParams(vmem_limit_bytes=32 * 1024 * 1024),
        cost_estimate=pl.CostEstimate(
            flops=8 * sz.row_count * sz.width * sz.local_hidden,
            bytes_accessed=8 * sz.width * sz.local_hidden,
            transcendentals=0,
        ),
    )(*operands)
    return list(results[:count]), list(results[count:])


def share_kernel(sz, whole, *refs):
    if whole:
        known, source, normed_ref, hidden_ref, slope, weights, sem = refs
    else:
        known, slope, source, grad_pre, weights, sem = refs
    panel = sz.panel
    copy = pltpu.make_async_copy(source, weights, sem)
    copy.start()
    if whole:
        wide = known[...].astype(jnp.float32)
        inverse_rms = lax.rsqrt(jnp.mean(wide * wide, axis=1, keepdims=True) + epsilon)
        normed = (wide * inverse_rms).astype(jnp.bfloat16)
        normed_ref[...] = normed
        copy.wait()
        for p in range(sz.panels_in):
            here = slice(p * panel, (p + 1) * panel)
            preact = dot(normed, weights[:, here]) * sz.scale_in
            gate = jax.nn.sigmoid(preact)
            hidden_ref[:, here] = (preact * gate).astype(jnp.bfloat16)
            slope[:, here] = gate * (1.0 + preact * (1.0 - gate))
    else:
        copy.wait()
        grad_hidden = dot(known[...], weights[...], contract_last)
        grad_pre[...] = (grad_hidden * sz.scale_out * slope[...]).astype(jnp.bfloat16)


def share_call(sz, operands, weight):
    whole = len(operands) == 1
    rows_count, hidden_size = sz.row_count, sz.local_hidden
    narrow = jax.ShapeDtypeStruct((rows_count, hidden_size), jnp.bfloat16)
    shapes = [narrow]
    if whole:
        shapes = [
            jax.ShapeDtypeStruct((rows_count, sz.width), jnp.bfloat16),
            narrow,
            jax.ShapeDtypeStruct((rows_count, hidden_size), jnp.float32),
        ]
    inside = pl.BlockSpec(memory_space=pltpu.VMEM)
    return pl.pallas_call(
        functools.partial(share_kernel, sz, whole),
        out_shape=shapes,
        in_specs=[inside] * len(operands) + [pl.BlockSpec(memory_space=pl.ANY)],
        out_specs=[inside] * len(shapes),
        scratch_shapes=[
            pltpu.VMEM(weight.shape, jnp.bfloat16),
            pltpu.SemaphoreType.DMA,
        ],
        compiler_params=pltpu.CompilerParams(vmem_limit_bytes=32 * 1024 * 1024),
        cost_estimate=pl.CostEstimate(
            flops=2 * rows_count * sz.width * hidden_size,
            bytes_accessed=2 * sz.width * hidden_size,
            transcendentals=0,
        ),
    )(*operands, weight)


def per_device(inputs, targets, weight_a, weight_b, moment_a, moment_b, routes, partners):
    replicas = lax.axis_size("replica")
    sections = lax.axis_size("section")
    shards = lax.axis_size("shard")
    replica_id = lax.axis_index("replica")
    section_id = lax.axis_index("section")
    shard_id = lax.axis_index("shard")
    row_count = inputs.shape[2]
    panel = inputs.shape[3]
    width = weight_a.shape[2]
    local_hidden = weight_a.shape[3]
    assert inputs.shape[1] == 1 and shards == 4
    assert local_hidden % panel == 0 and sections > 2
    hidden_total = local_hidden * shards
    scale_in = 1.0 / math.sqrt(width)
    scale_out = 1.0 / math.sqrt(hidden_total)
    weight_in = weight_a[0, 0]
    weight_out = weight_b[0, 0]
    block_rows = row_count // replicas
    links = sections - 1
    in_kernel = block_rows % 16 == 0
    blocks = replicas if in_kernel else 1
    sz = Sizes(sections, row_count, width, local_hidden, panel, hidden_total, blocks)

    def flat(replica, section, shard):
        return (replica * sections + section) * shards + shard

    def turn(section):
        return (section ^ (section >> 1)) & 1

    def holders(section):
        return [j for j in range(shards) if (j & 1) != turn(section)]

    def move(array, sources, target):
        pairs = [
            (flat(r, s, j), flat(*target(r, s, j)))
            for r in range(replicas)
            for s, j in sources
        ]
        return lax.ppermute(array, axes, pairs)

    def holder_sources(active):
        return [(s, j) for s in active for j in holders(s)]

    def to_holders(array, offset, active):
        sources = [(s, j ^ offset) for s, j in holder_sources(active)]
        return move(array, sources, lambda r, s, j: (r, s, j ^ offset))

    def from_holders(array, offset, active):
        return move(array, holder_sources(active), lambda r, s, j: (r, s, j ^ offset))

    def between_holders(array, offset, other_half, section, step):
        shift = turn(section) ^ turn(section + step) ^ (2 * other_half)
        return move(
            array,
            holder_sources([section]),
            lambda r, s, j: ((r + offset) % replicas, s + step, j ^ shift),
        )

    def across_replicas(array, offset, active):
        return move(
            array,
            [(s, j) for s in active for j in range(shards)],
            lambda r, s, j: ((r + offset) % replicas, s, j),
        )

    every = range(sections)
    others = range(1, replicas)
    is_holder = (shard_id & 1) != turn(section_id)

    edge = jnp.where(section_id == 0, inputs[0, 0], targets[0, 0])
    ends = [(s, j) for s in (0, links) for j in range(shards)]

    def at_ends(array, offset):
        return move(array, ends, lambda r, s, j: (r, s, j ^ offset))

    pair = jnp.concatenate([edge, at_ends(edge, 1)])
    edges = [pair, at_ends(pair, 2)]
    rest = range(1, sections)
    near_in = to_holders(weight_in, 1, rest)
    near_in, next_out = lax.optimization_barrier((near_in, weight_out))
    near = [near_in, to_holders(next_out, 1, rest)]

    tables = lax.dynamic_index_in_dim(partners, section_id, 0, keepdims=False)

    def piece_of(table, offset):
        wanted = (replica_id + offset) % replicas
        return jnp.argmax(table[:, replica_id] == wanted).astype(jnp.int32)

    pieces_in = [piece_of(tables[0], e) for e in range(replicas)]
    pieces_out = [piece_of(tables[1], e) for e in range(replicas)]
    size_in = width // replicas
    size_out = local_hidden // replicas

    def piece(array, index, size, axis=0):
        return lax.dynamic_slice_in_dim(array, index * size, size, axis)

    def exchange(arrays, active):
        return [across_replicas(array, e, active) for e, array in zip(others, arrays)]

    packed_in = [
        pack([weight_in, moment_a[0, 0]], pieces_in[e] * size_in, size_in) for e in others
    ]
    packed_out = [
        pack([weight_out, moment_b[0, 0]], pieces_out[e] * size_out, size_out) for e in others
    ]
    early = range(sections // 2, sections)
    late = range(sections // 2)
    far_states_in = exchange(packed_in, every)

    offsets = jnp.arange(replicas, dtype=jnp.int32)
    there = (replica_id + offsets) % replicas
    back = (replica_id - offsets) % replicas
    own_routes = routes[0, :, replica_id, :]
    slots = jnp.sum(
        (own_routes[:, None, :] == there[None, :, None]).astype(jnp.int32)
        * offsets[None, None, :],
        axis=2,
    )
    columns = max(replicas, sections, shards + 1)
    steps = jnp.arange(sections)
    ours = ((is_holder | (steps == 0)) & (section_id == steps)).astype(jnp.int32)
    features = (shard_id ^ jnp.arange(shards, dtype=jnp.int32)) * panel
    leads = (is_holder & ((shard_id & 2) == 0)).astype(jnp.int32)
    features = jnp.append(features, leads)

    def line(values):
        return jnp.pad(values, ((0, 0), (0, columns - values.shape[1])))

    starts = jnp.concatenate([slots, back[None]]) * block_rows
    if not in_kernel:
        starts = jnp.zeros_like(starts)
    table = jnp.concatenate([line(starts), line(ours[None]), line(features[None])])
    table = table.astype(jnp.int32)

    def send_blocks(sends, arrived, left, section, step):
        sign = step
        if in_kernel:
            return [
                between_holders(sends[e], sign * e, a, section, step)
                for e in range(replicas)
                for a in range(2)
            ]
        parts = sends[0].reshape(replicas, block_rows, width)
        moved = [jnp.zeros_like(parts), jnp.zeros_like(parts)]
        for e in range(replicas):
            chosen = lax.dynamic_index_in_dim(parts, left[e], 0, keepdims=False)
            for a in range(2):
                got = between_holders(chosen, sign * e, a, section, step)
                moved[a] = lax.dynamic_update_index_in_dim(moved[a], got, arrived[e], 0)
        return [one.reshape(row_count, width) for one in moved]

    def kept_of(stores, steps, forward):
        places = [kept_place(sz, step, forward) for step in steps]
        result = stores[0][places[0] : places[0] + row_count]
        for step, place in zip(steps[1:], places[1:]):
            result = jnp.where(section_id == step, stores[0][place : place + row_count], result)
        return result

    row_parts = []

    def spread_rows(received, rows, active):
        received, rows, row_parts[:] = lax.optimization_barrier(
            (received, rows, row_parts)
        )
        row_parts.append(from_holders(rows, 1, active))
        return received

    def bundle(normed, hidden, e):
        parts = [
            piece(normed, pieces_in[e], size_in, 1), piece(hidden, pieces_out[e], size_out, 1)
        ]
        return jnp.concatenate(parts, axis=1)

    weights = [weight_in, weight_out, *near]
    received, stores = [], []
    for step in every:
        sends, stores = chain_step(
            sz, step, True, table, received, edges if step == 0 else [], weights, stores
        )
        if step in (len(late) - 1, links):
            rows = kept_of(stores, range(step + 1), True)
        if step == 0:
            total = sends[0].astype(jnp.float32)
            total = total + at_ends(sends[0], 1).astype(jnp.float32)
            sends = [total.astype(jnp.bfloat16)]
            if in_kernel:
                sends = [piece(sends[0], slots[0, e], block_rows) for e in range(replicas)]
        if step < links:
            received = send_blocks(sends, back, slots[step], step, 1)
            if step == 0:
                received, far_states_in, packed_out = lax.optimization_barrier(
                    (received, far_states_in, packed_out)
                )
                far_states_out = exchange(packed_out, early)
        else:
            received = [sends[0], at_ends(sends[0], 2)]
            row_parts.append(from_holders(rows, 1, early))
            own_rows = jnp.where(is_holder, rows, sum(row_parts[1:], row_parts[0]))
            received, *shares = lax.optimization_barrier(
                (received, *share_call(sz, [own_rows], weight_in))
            )
            normed, hidden, slope = shares
            bundles = exchange([bundle(normed, hidden, e) for e in others], every)
        if step == len(late) - 1:
            received = spread_rows(received, rows, late)
        if step == len(late) - 1:
            received, packed_out = lax.optimization_barrier((received, packed_out))
            far_late = exchange(packed_out, late)
        if step == len(late):
            received, far_states_out = lax.optimization_barrier((received, far_states_out))

    for step in reversed(range(1, sections)):
        sends, stores = chain_step(
            sz, step, False, table, received, edges if step == links else [], weights, stores
        )
        received = send_blocks(sends, slots[step - 1], back, step, -1)
        if step == len(late):
            received, far_late, bundles = lax.optimization_barrier(
                (received, far_late, bundles)
            )

    far_normed = [one[:, :size_in] for one in bundles]
    far_hidden = [one[:, size_in:] for one in bundles]

    halves = []
    for a in range(2):
        half = received[a]
        if in_kernel:
            half = jnp.zeros((row_count, width), jnp.bfloat16)
            for e in range(replicas):
                half = lax.dynamic_update_slice_in_dim(
                    half, received[2 * e + a], slots[0, e] * block_rows, 0
                )
        halves.append(half.astype(jnp.float32))
    first_up = (halves[0] + halves[1]).astype(jnp.bfloat16)
    upstream = jnp.where(section_id == 0, first_up, kept_of(stores, rest, False))
    upstream = jnp.where(is_holder, upstream, from_holders(upstream, 1, every))
    far_up = exchange([upstream] * len(others), every)
    (grad_pre,) = share_call(sz, [upstream, slope], weight_out)
    far_pre = exchange([grad_pre] * len(others), every)
    far_states_out = [
        jnp.where(section_id < len(late), one, two)
        for one, two in zip(far_late, far_states_out)
    ]
    far_states = {0: far_states_in, 2: far_states_out}

    def far_part(e, which):
        size = size_out if which & 2 else size_in
        both = far_states[which & 2][e - 1]
        return both[size:] if which & 1 else both[:size]

    def as_delta(left, right, scale):
        return (inner_rate * (dot(left, right, contract_rows) * scale)).astype(jnp.bfloat16)

    def finish(weight, moment, left, right, which, far_left, far_right, scale, pieces, size):
        new_weight, new_moment = outer_mix(
            weight.astype(jnp.float32),
            moment.astype(jnp.float32),
            as_delta(left, right, scale).astype(jnp.float32),
        )
        for e in others:
            back = replicas - e

            def mean(own_array, far_array):
                return 0.5 * (own_array.astype(jnp.float32) + far_array.astype(jnp.float32))

            index = pieces[back]
            own_left = piece(left, index, size, 1)
            part_weight, part_moment = outer_mix(
                mean(piece(weight, index, size), far_part(e, which)),
                mean(piece(moment, index, size), far_part(e, which + 1)),
                mean(
                    as_delta(own_left, right, scale),
                    as_delta(far_left[e - 1], far_right[e - 1], scale),
                ),
            )
            new_weight = lax.dynamic_update_slice_in_dim(new_weight, part_weight, index * size, 0)
            new_moment = lax.dynamic_update_slice_in_dim(new_moment, part_moment, index * size, 0)
        return new_weight[None, None], new_moment[None, None]

    new_weight_b, new_moment_b = finish(
        weight_out, moment_b[0, 0], hidden, upstream, 2, far_hidden, far_up,
        scale_out, pieces_out, size_out,
    )
    new_weight_a, new_moment_a = finish(
        weight_in, moment_a[0, 0], normed, grad_pre, 0, far_normed, far_pre,
        scale_in, pieces_in, size_in,
    )
    return (new_weight_a, new_weight_b, new_moment_a, new_moment_b)


def solution(mesh):
    placed = (
        P("replica", None, None, "shard"),
        P("replica", None, None, "shard"),
        P("replica", "section", None, "shard"),
        P("replica", "section", "shard", None),
        P("replica", "section", None, "shard"),
        P("replica", "section", "shard", None),
        P(),
        P(),
    )
    return jax.shard_map(
        per_device,
        mesh=mesh,
        in_specs=placed,
        out_specs=(
            P("replica", "section", None, "shard"),
            P("replica", "section", "shard", None),
            P("replica", "section", None, "shard"),
            P("replica", "section", "shard", None),
        ),
        check_vma=False,
    )
```

```python
import functools
import math

import jax
import jax.numpy as jnp
from jax import lax
from jax.experimental import pallas as pl
from jax.experimental.pallas import tpu as pltpu
from jax.sharding import PartitionSpec as P

epsilon = 1e-05
inner_rate = 0.5
momentum_decay = 0.9
outer_rate = 0.7

axes = ("replica", "section", "shard")
contract_rows = (((0,), (0,)), ((), ()))
contract_last = (((1,), (1,)), ((), ()))


def dot(left, right, dims=(((1,), (0,)), ((), ()))):
    return lax.dot_general(left, right, dims, preferred_element_type=jnp.float32)


def outer_mix(weight, moment, delta):
    new_moment = momentum_decay * moment + delta
    new_weight = weight - outer_rate * (momentum_decay * new_moment + delta)
    return new_weight.astype(jnp.bfloat16), new_moment.astype(jnp.bfloat16)


def pack_kernel(size, starts, *refs):
    sources, (packed, buffer, read_sems, write_sems) = refs[:-4], refs[-4:]
    rows = pl.ds(pl.multiple_of(starts[0], size), size)
    reads, writes = [], []
    for k, source in enumerate(sources):
        there = pl.ds(k * size, size)
        reads.append(
            pltpu.make_async_copy(source.at[rows], buffer.at[there], read_sems.at[k])
        )
        writes.append(
            pltpu.make_async_copy(buffer.at[there], packed.at[there], write_sems.at[k])
        )
    for copy in reads:
        copy.start()
    for read, write in zip(reads, writes):
        read.wait()
        write.start()
    for copy in writes:
        copy.wait()


def pack(arrays, start, size):
    shape = (len(arrays) * size, arrays[0].shape[1])
    anywhere = pl.BlockSpec(memory_space=pl.ANY)
    return pl.pallas_call(
        functools.partial(pack_kernel, size),
        out_shape=jax.ShapeDtypeStruct(shape, arrays[0].dtype),
        in_specs=[pl.BlockSpec(memory_space=pltpu.SMEM)] + [anywhere] * len(arrays),
        out_specs=anywhere,
        scratch_shapes=[
            pltpu.VMEM(shape, arrays[0].dtype),
            pltpu.SemaphoreType.DMA((len(arrays),)),
            pltpu.SemaphoreType.DMA((len(arrays),)),
        ],
        compiler_params=pltpu.CompilerParams(vmem_limit_bytes=32 * 1024 * 1024),
        cost_estimate=pl.CostEstimate(
            flops=0, bytes_accessed=4 * shape[0] * shape[1], transcendentals=0
        ),
    )(start.reshape(1), *arrays)


class Sizes:
    def __init__(self, sections, row_count, width, local_hidden, panel, hidden_total, blocks):
        self.sections, self.row_count = sections, row_count
        self.width, self.local_hidden, self.panel = width, local_hidden, panel
        self.blocks = blocks
        self.block_rows = row_count // blocks
        self.panels_in = local_hidden // panel
        self.panels_out = width // panel
        self.scale_in = 1.0 / math.sqrt(width)
        self.scale_out = 1.0 / math.sqrt(hidden_total)


def kept_place(sz, step, forward):
    return (step if forward else sz.sections + step) * sz.row_count


def chain_kernel(sz, step, forward, counts, *refs):
    refs = list(refs)

    def take(count):
        taken = refs[:count]
        del refs[:count]
        return taken

    first = forward and step == 0
    parts = 1 if first else 2
    (table,) = take(1)
    received, edges, sources = take(counts[0]), take(counts[1]), take(2 * parts)
    take(0 if first else 2)
    sends = take(counts[2])
    kept, state = take(2)
    weights_in, weights_out, landing, rows, up, out, slope, wide_store = take(8)
    weight_sems, block_sems, edge_sems, send_sems, state_sems = take(5)
    panel, width, hidden_size = sz.panel, sz.width, sz.local_hidden
    links = sz.sections - 1
    whole = pl.ds(0, sz.row_count)

    def weight_copy(d, which):
        weights = (weights_in, weights_out)[which]
        return pltpu.make_async_copy(
            sources[2 * d + which], weights.at[d], weight_sems.at[d, which]
        )

    def place(line, e):
        return pl.ds(pl.multiple_of(table[line, e], sz.block_rows), sz.block_rows)

    def state_part(k, columns):
        return state.at[pl.ds(k * sz.row_count, sz.row_count), pl.ds(0, columns)]

    fresh_hbm = kept.at[pl.ds(kept_place(sz, step, forward), sz.row_count)]
    rows_hbm, slope_hbm = state_part(0, width), state_part(1, 2 * hidden_size)

    @pl.when(table[links + 1, step] == 1)
    def _():
        sequence = [
            (d, which if forward else 1 - which) for d in range(parts) for which in range(2)
        ]
        arrive = links if forward else step
        first_copies = []
        for i, source in enumerate(received):
            e, a = divmod(i, 2)
            rows_there = whole if len(received) == 2 else place(arrive, e)
            first_copies.append(
                pltpu.make_async_copy(source, landing.at[a, rows_there], block_sems.at[i])
            )
        for d in range(2 * len(edges)):
            column = pl.ds(pl.multiple_of(table[links + 2, d], panel), panel)
            source = edges[d // 2].at[pl.ds((d % 2) * sz.row_count, sz.row_count)]
            first_copies.append(
                pltpu.make_async_copy(source, out.at[:, column], edge_sems.at[d])
            )
        if not forward:
            first_copies.append(pltpu.make_async_copy(rows_hbm, wide_store, state_sems.at[0]))
            slope_copy = pltpu.make_async_copy(slope_hbm, slope, state_sems.at[1])
        for copy in first_copies:
            copy.start()
        for i, item in enumerate(sequence):
            weight_copy(*item).start()
            if i == 0 and not forward:
                slope_copy.start()

        def arrived(item):
            weight_copy(*item).wait()

        for copy in first_copies:
            copy.wait()
        if received:
            total = landing[0].astype(jnp.float32) + landing[1].astype(jnp.float32)
            total = total.astype(jnp.bfloat16)
        if forward:
            rows[...] = total if received else out[...]
        elif edges:
            goal = out[...].astype(jnp.float32)
            up[...] = (total.astype(jnp.float32) - goal).astype(jnp.bfloat16)
        else:
            up[...] = total
        fresh = rows if forward else up
        store_copies = [pltpu.make_async_copy(fresh, fresh_hbm, state_sems.at[2])]
        if forward:
            wide = rows[...].astype(jnp.float32)
            wide_store[...] = wide
            store_copies.append(pltpu.make_async_copy(wide_store, rows_hbm, state_sems.at[0]))
        else:
            wide = wide_store[...]
        inverse_rms = lax.rsqrt(jnp.mean(wide * wide, axis=1, keepdims=True) + epsilon)
        leads = table[links + 2, 4] == 1
        if forward:
            normed = (wide * inverse_rms).astype(jnp.bfloat16)
            total = [jnp.zeros((sz.row_count, panel), jnp.float32) for _ in range(sz.panels_out)]
            for d in range(parts):
                arrived((d, 0))
                hidden = []
                for p in range(sz.panels_in):
                    weight = weights_in[d, :, p * panel : (p + 1) * panel]
                    preact = dot(normed, weight) * sz.scale_in
                    gate = jax.nn.sigmoid(preact)
                    hidden.append((preact * gate).astype(jnp.bfloat16))
                    column = d * hidden_size + p * panel
                    slope[:, column : column + panel] = gate * (1.0 + preact * (1.0 - gate))
                hidden = jnp.concatenate(hidden, axis=1)
                arrived((d, 1))
                for n in range(sz.panels_out):
                    weight = weights_out[d, :, n * panel : (n + 1) * panel]
                    total[n] = total[n] + dot(hidden, weight)
            total = jnp.concatenate(total, axis=1) * sz.scale_out
            out[...] = (total + jnp.where(leads, wide, 0.0)).astype(jnp.bfloat16)
            store_copies.append(pltpu.make_async_copy(slope, slope_hbm, state_sems.at[1]))
        else:
            up_turned = up[...].T
            total = jnp.zeros((width, sz.row_count), jnp.float32)
            for d in range(parts):
                arrived((d, 1))
                grad_hidden = dot(weights_out[d], up_turned)
                if d == 0:
                    slope_copy.wait()
                local_slope = slope[:, d * hidden_size : (d + 1) * hidden_size].T
                grad_pre = (grad_hidden * sz.scale_out * local_slope).astype(jnp.bfloat16)
                arrived((d, 0))
                total = total + dot(weights_in[d], grad_pre)
            total = total.T * sz.scale_in
            exact = wide * inverse_rms
            along = jnp.mean(total * exact, axis=1, keepdims=True)
            own = jnp.where(leads, up[...].astype(jnp.float32), 0.0)
            out[...] = (own + inverse_rms * (total - exact * along)).astype(jnp.bfloat16)
        leave = step if forward else links
        send_copies = []
        for e, target in enumerate(sends):
            rows_here = whole if len(sends) == 1 else place(leave, e)
            send_copies.append(
                pltpu.make_async_copy(out.at[rows_here], target, send_sems.at[e])
            )
        for copy in send_copies + store_copies:
            copy.start()
        for copy in send_copies + store_copies:
            copy.wait()


def chain_step(sz, step, forward, table, received, edges, weights, stores):
    first = forward and step == 0
    count = 1 if forward and step in (0, sz.sections - 1) else sz.blocks
    anywhere = pl.BlockSpec(memory_space=pl.ANY)
    operands = [table, *received, *edges, *(weights[:2] if first else [*weights, *stores])]
    block = jax.ShapeDtypeStruct((sz.row_count // count, sz.width), jnp.bfloat16)
    shapes = [block] * count + [
        jax.ShapeDtypeStruct((144 * sz.row_count, sz.width), jnp.bfloat16),
        jax.ShapeDtypeStruct((48 * sz.row_count, 2 * sz.local_hidden), jnp.float32),
    ]
    in_specs = [pl.BlockSpec(memory_space=pltpu.SMEM)] + [anywhere] * (len(operands) - 1)
    whole = (sz.row_count, sz.width)
    results = pl.pallas_call(
        functools.partial(
            chain_kernel, sz, step, forward, (len(received), len(edges), count)
        ),
        out_shape=shapes,
        in_specs=in_specs,
        out_specs=[anywhere] * len(shapes),
        input_output_aliases=(
            {} if first else {len(operands) - 2: count, len(operands) - 1: count + 1}
        ),
        scratch_shapes=[
            pltpu.VMEM((2, sz.width, sz.local_hidden), jnp.bfloat16),
            pltpu.VMEM((2, sz.local_hidden, sz.width), jnp.bfloat16),
            pltpu.VMEM((2,) + whole, jnp.bfloat16),
            pltpu.VMEM(whole, jnp.bfloat16),
            pltpu.VMEM(whole, jnp.bfloat16),
            pltpu.VMEM(whole, jnp.bfloat16),
            pltpu.VMEM((sz.row_count, 2 * sz.local_hidden), jnp.float32),
            pltpu.VMEM(whole, jnp.float32),
            pltpu.SemaphoreType.DMA((2, 2)),
            pltpu.SemaphoreType.DMA((max(1, len(received)),)),
            pltpu.SemaphoreType.DMA((4,)),
            pltpu.SemaphoreType.DMA((count,)),
            pltpu.SemaphoreType.DMA((3,)),
        ],
        compiler_params=pltpu.CompilerParams(vmem_limit_bytes=32 * 1024 * 1024),
        cost_estimate=pl.CostEstimate(
            flops=8 * sz.row_count * sz.width * sz.local_hidden,
            bytes_accessed=8 * sz.width * sz.local_hidden,
            transcendentals=0,
        ),
    )(*operands)
    return list(results[:count]), list(results[count:])


def share_kernel(sz, whole, *refs):
    if whole:
        known, source, normed_ref, hidden_ref, slope, weights, sem = refs
    else:
        known, slope, source, grad_pre, weights, sem = refs
    panel = sz.panel
    copy = pltpu.make_async_copy(source, weights, sem)
    copy.start()
    if whole:
        wide = known[...].astype(jnp.float32)
        inverse_rms = lax.rsqrt(jnp.mean(wide * wide, axis=1, keepdims=True) + epsilon)
        normed = (wide * inverse_rms).astype(jnp.bfloat16)
        normed_ref[...] = normed
        copy.wait()
        for p in range(sz.panels_in):
            here = slice(p * panel, (p + 1) * panel)
            preact = dot(normed, weights[:, here]) * sz.scale_in
            gate = jax.nn.sigmoid(preact)
            hidden_ref[:, here] = (preact * gate).astype(jnp.bfloat16)
            slope[:, here] = gate * (1.0 + preact * (1.0 - gate))
    else:
        copy.wait()
        grad_hidden = dot(known[...], weights[...], contract_last)
        grad_pre[...] = (grad_hidden * sz.scale_out * slope[...]).astype(jnp.bfloat16)


def share_call(sz, operands, weight):
    whole = len(operands) == 1
    rows_count, hidden_size = sz.row_count, sz.local_hidden
    narrow = jax.ShapeDtypeStruct((rows_count, hidden_size), jnp.bfloat16)
    shapes = [narrow]
    if whole:
        shapes = [
            jax.ShapeDtypeStruct((rows_count, sz.width), jnp.bfloat16),
            narrow,
            jax.ShapeDtypeStruct((rows_count, hidden_size), jnp.float32),
        ]
    inside = pl.BlockSpec(memory_space=pltpu.VMEM)
    return pl.pallas_call(
        functools.partial(share_kernel, sz, whole),
        out_shape=shapes,
        in_specs=[inside] * len(operands) + [pl.BlockSpec(memory_space=pl.ANY)],
        out_specs=[inside] * len(shapes),
        scratch_shapes=[
            pltpu.VMEM(weight.shape, jnp.bfloat16),
            pltpu.SemaphoreType.DMA,
        ],
        compiler_params=pltpu.CompilerParams(vmem_limit_bytes=32 * 1024 * 1024),
        cost_estimate=pl.CostEstimate(
            flops=2 * rows_count * sz.width * hidden_size,
            bytes_accessed=2 * sz.width * hidden_size,
            transcendentals=0,
        ),
    )(*operands, weight)


def per_device(inputs, targets, weight_a, weight_b, moment_a, moment_b, routes, partners):
    replicas = lax.axis_size("replica")
    sections = lax.axis_size("section")
    shards = lax.axis_size("shard")
    replica_id = lax.axis_index("replica")
    section_id = lax.axis_index("section")
    shard_id = lax.axis_index("shard")
    row_count = inputs.shape[2]
    panel = inputs.shape[3]
    width = weight_a.shape[2]
    local_hidden = weight_a.shape[3]
    assert inputs.shape[1] == 1 and shards == 4
    assert local_hidden % panel == 0 and sections > 2
    hidden_total = local_hidden * shards
    scale_in = 1.0 / math.sqrt(width)
    scale_out = 1.0 / math.sqrt(hidden_total)
    weight_in = weight_a[0, 0]
    weight_out = weight_b[0, 0]
    block_rows = row_count // replicas
    links = sections - 1
    in_kernel = block_rows % 16 == 0
    blocks = replicas if in_kernel else 1
    sz = Sizes(sections, row_count, width, local_hidden, panel, hidden_total, blocks)

    def flat(replica, section, shard):
        return (replica * sections + section) * shards + shard

    def turn(section):
        return (section ^ (section >> 1)) & 1

    def holders(section):
        return [j for j in range(shards) if (j & 1) != turn(section)]

    def move(array, sources, target):
        pairs = [
            (flat(r, s, j), flat(*target(r, s, j)))
            for r in range(replicas)
            for s, j in sources
        ]
        return lax.ppermute(array, axes, pairs)

    def holder_sources(active):
        return [(s, j) for s in active for j in holders(s)]

    def to_holders(array, offset, active):
        sources = [(s, j ^ offset) for s, j in holder_sources(active)]
        return move(array, sources, lambda r, s, j: (r, s, j ^ offset))

    def from_holders(array, offset, active):
        return move(array, holder_sources(active), lambda r, s, j: (r, s, j ^ offset))

    def between_holders(array, offset, other_half, section, step):
        shift = turn(section) ^ turn(section + step) ^ (2 * other_half)
        return move(
            array,
            holder_sources([section]),
            lambda r, s, j: ((r + offset) % replicas, s + step, j ^ shift),
        )

    def across_replicas(array, offset, active):
        return move(
            array,
            [(s, j) for s in active for j in range(shards)],
            lambda r, s, j: ((r + offset) % replicas, s, j),
        )

    every = range(sections)
    others = range(1, replicas)
    is_holder = (shard_id & 1) != turn(section_id)

    edge = jnp.where(section_id == 0, inputs[0, 0], targets[0, 0])
    ends = [(s, j) for s in (0, links) for j in range(shards)]

    def at_ends(array, offset):
        return move(array, ends, lambda r, s, j: (r, s, j ^ offset))

    pair = jnp.concatenate([edge, at_ends(edge, 1)])
    pair, packed_weight = lax.optimization_barrier((pair, weight_in))
    edges = [pair, at_ends(pair, 2)]
    rest = range(1, sections)
    near_in = to_holders(weight_in, 1, rest)
    near_in, next_out = lax.optimization_barrier((near_in, weight_out))
    near = [near_in, to_holders(next_out, 1, rest)]

    tables = lax.dynamic_index_in_dim(partners, section_id, 0, keepdims=False)

    def piece_of(table, offset):
        wanted = (replica_id + offset) % replicas
        return jnp.argmax(table[:, replica_id] == wanted).astype(jnp.int32)

    pieces_in = [piece_of(tables[0], e) for e in range(replicas)]
    pieces_out = [piece_of(tables[1], e) for e in range(replicas)]
    size_in = width // replicas
    size_out = local_hidden // replicas

    def piece(array, index, size, axis=0):
        return lax.dynamic_slice_in_dim(array, index * size, size, axis)

    def exchange(arrays, active):
        return [across_replicas(array, e, active) for e, array in zip(others, arrays)]

    packed_in = [
        pack([packed_weight, moment_a[0, 0]], pieces_in[e] * size_in, size_in) for e in others
    ]
    packed_out = [
        pack([weight_out, moment_b[0, 0]], pieces_out[e] * size_out, size_out) for e in others
    ]
    early = range(sections // 2, sections)
    late = range(sections // 2)
    far_states_in = exchange(packed_in, every)

    offsets = jnp.arange(replicas, dtype=jnp.int32)
    there = (replica_id + offsets) % replicas
    back = (replica_id - offsets) % replicas
    own_routes = routes[0, :, replica_id, :]
    slots = jnp.sum(
        (own_routes[:, None, :] == there[None, :, None]).astype(jnp.int32)
        * offsets[None, None, :],
        axis=2,
    )
    columns = max(replicas, sections, shards + 1)
    steps = jnp.arange(sections)
    ours = ((is_holder | (steps == 0)) & (section_id == steps)).astype(jnp.int32)
    features = (shard_id ^ jnp.arange(shards, dtype=jnp.int32)) * panel
    leads = (is_holder & ((shard_id & 2) == 0)).astype(jnp.int32)
    features = jnp.append(features, leads)

    def line(values):
        return jnp.pad(values, ((0, 0), (0, columns - values.shape[1])))

    starts = jnp.concatenate([slots, back[None]]) * block_rows
    if not in_kernel:
        starts = jnp.zeros_like(starts)
    table = jnp.concatenate([line(starts), line(ours[None]), line(features[None])])
    table = table.astype(jnp.int32)

    def send_blocks(sends, arrived, left, section, step):
        sign = step
        if in_kernel:
            return [
                between_holders(sends[e], sign * e, a, section, step)
                for e in range(replicas)
                for a in range(2)
            ]
        parts = sends[0].reshape(replicas, block_rows, width)
        moved = [jnp.zeros_like(parts), jnp.zeros_like(parts)]
        for e in range(replicas):
            chosen = lax.dynamic_index_in_dim(parts, left[e], 0, keepdims=False)
            for a in range(2):
                got = between_holders(chosen, sign * e, a, section, step)
                moved[a] = lax.dynamic_update_index_in_dim(moved[a], got, arrived[e], 0)
        return [one.reshape(row_count, width) for one in moved]

    def kept_of(stores, steps, forward):
        places = [kept_place(sz, step, forward) for step in steps]
        result = stores[0][places[0] : places[0] + row_count]
        for step, place in zip(steps[1:], places[1:]):
            result = jnp.where(section_id == step, stores[0][place : place + row_count], result)
        return result

    row_parts = []

    def spread_rows(received, rows, active):
        received, rows, row_parts[:] = lax.optimization_barrier(
            (received, rows, row_parts)
        )
        row_parts.append(from_holders(rows, 1, active))
        return received

    def bundle(normed, hidden, e):
        parts = [
            piece(normed, pieces_in[e], size_in, 1), piece(hidden, pieces_out[e], size_out, 1)
        ]
        return jnp.concatenate(parts, axis=1)

    weights = [weight_in, weight_out, *near]
    received, stores = [], []
    for step in every:
        sends, stores = chain_step(
            sz, step, True, table, received, edges if step == 0 else [], weights, stores
        )
        if step in (len(late) - 1, links):
            rows = kept_of(stores, range(step + 1), True)
        if step == 0:
            total = sends[0].astype(jnp.float32)
            total = total + at_ends(sends[0], 1).astype(jnp.float32)
            sends = [total.astype(jnp.bfloat16)]
            if in_kernel:
                sends = [piece(sends[0], slots[0, e], block_rows) for e in range(replicas)]
        if step < links:
            received = send_blocks(sends, back, slots[step], step, 1)
            if step == 0:
                received, far_states_in, packed_out = lax.optimization_barrier(
                    (received, far_states_in, packed_out)
                )
                far_states_out = exchange(packed_out, early)
        else:
            received = [sends[0], at_ends(sends[0], 2)]
            row_parts.append(from_holders(rows, 1, early))
            own_rows = jnp.where(is_holder, rows, sum(row_parts[1:], row_parts[0]))
            received, *shares = lax.optimization_barrier(
                (received, *share_call(sz, [own_rows], weight_in))
            )
            normed, hidden, slope = shares
            bundles = exchange([bundle(normed, hidden, e) for e in others], every)
        if step == len(late) - 1:
            received = spread_rows(received, rows, late)
        if step == len(late) - 1:
            received, packed_out = lax.optimization_barrier((received, packed_out))
            far_late = exchange(packed_out, late)
        if step == len(late):
            received, far_states_out = lax.optimization_barrier((received, far_states_out))

    for step in reversed(range(1, sections)):
        sends, stores = chain_step(
            sz, step, False, table, received, edges if step == links else [], weights, stores
        )
        received = send_blocks(sends, slots[step - 1], back, step, -1)
        if step == len(late):
            received, far_late, bundles = lax.optimization_barrier(
                (received, far_late, bundles)
            )

    far_normed = [one[:, :size_in] for one in bundles]
    far_hidden = [one[:, size_in:] for one in bundles]

    halves = []
    for a in range(2):
        half = received[a]
        if in_kernel:
            half = jnp.zeros((row_count, width), jnp.bfloat16)
            for e in range(replicas):
                half = lax.dynamic_update_slice_in_dim(
                    half, received[2 * e + a], slots[0, e] * block_rows, 0
                )
        halves.append(half.astype(jnp.float32))
    first_up = (halves[0] + halves[1]).astype(jnp.bfloat16)
    upstream = jnp.where(section_id == 0, first_up, kept_of(stores, rest, False))
    upstream = jnp.where(is_holder, upstream, from_holders(upstream, 1, every))
    far_up = exchange([upstream] * len(others), every)
    (grad_pre,) = share_call(sz, [upstream, slope], weight_out)
    far_pre = exchange([grad_pre] * len(others), every)
    far_up, upstream, grad_pre = lax.optimization_barrier((far_up, upstream, grad_pre))
    far_states_out = [
        jnp.where(section_id < len(late), one, two)
        for one, two in zip(far_late, far_states_out)
    ]
    far_states = {0: far_states_in, 2: far_states_out}

    def far_part(e, which):
        size = size_out if which & 2 else size_in
        both = far_states[which & 2][e - 1]
        return both[size:] if which & 1 else both[:size]

    def as_delta(left, right, scale):
        return (inner_rate * (dot(left, right, contract_rows) * scale)).astype(jnp.bfloat16)

    def finish(weight, moment, left, right, which, far_left, far_right, scale, pieces, size):
        new_weight, new_moment = outer_mix(
            weight.astype(jnp.float32),
            moment.astype(jnp.float32),
            as_delta(left, right, scale).astype(jnp.float32),
        )
        for e in others:
            back = replicas - e

            def mean(own_array, far_array):
                return 0.5 * (own_array.astype(jnp.float32) + far_array.astype(jnp.float32))

            index = pieces[back]
            own_left = piece(left, index, size, 1)
            part_weight, part_moment = outer_mix(
                mean(piece(weight, index, size), far_part(e, which)),
                mean(piece(moment, index, size), far_part(e, which + 1)),
                mean(
                    as_delta(own_left, right, scale),
                    as_delta(far_left[e - 1], far_right[e - 1], scale),
                ),
            )
            new_weight = lax.dynamic_update_slice_in_dim(new_weight, part_weight, index * size, 0)
            new_moment = lax.dynamic_update_slice_in_dim(new_moment, part_moment, index * size, 0)
        return new_weight[None, None], new_moment[None, None]

    new_weight_b, new_moment_b = finish(
        weight_out, moment_b[0, 0], hidden, upstream, 2, far_hidden, far_up,
        scale_out, pieces_out, size_out,
    )
    new_weight_a, new_moment_a = finish(
        weight_in, moment_a[0, 0], normed, grad_pre, 0, far_normed, far_pre,
        scale_in, pieces_in, size_in,
    )
    return (new_weight_a, new_weight_b, new_moment_a, new_moment_b)


def solution(mesh):
    placed = (
        P("replica", None, None, "shard"),
        P("replica", None, None, "shard"),
        P("replica", "section", None, "shard"),
        P("replica", "section", "shard", None),
        P("replica", "section", None, "shard"),
        P("replica", "section", "shard", None),
        P(),
        P(),
    )
    return jax.shard_map(
        per_device,
        mesh=mesh,
        in_specs=placed,
        out_specs=(
            P("replica", "section", None, "shard"),
            P("replica", "section", "shard", None),
            P("replica", "section", None, "shard"),
            P("replica", "section", "shard", None),
        ),
        check_vma=False,
    )
```

```python
import functools
import math

import jax
import jax.numpy as jnp
from jax import lax
from jax.experimental import pallas as pl
from jax.experimental.pallas import tpu as pltpu
from jax.sharding import PartitionSpec as P

epsilon = 1e-05
inner_rate = 0.5
momentum_decay = 0.9
outer_rate = 0.7

axes = ("replica", "section", "shard")
contract_rows = (((0,), (0,)), ((), ()))
contract_last = (((1,), (1,)), ((), ()))


def dot(left, right, dims=(((1,), (0,)), ((), ()))):
    return lax.dot_general(left, right, dims, preferred_element_type=jnp.float32)


def outer_mix(weight, moment, delta):
    new_moment = momentum_decay * moment + delta
    new_weight = weight - outer_rate * (momentum_decay * new_moment + delta)
    return new_weight.astype(jnp.bfloat16), new_moment.astype(jnp.bfloat16)


def pack_kernel(size, starts, *refs):
    sources, (packed, buffer, read_sems, write_sems) = refs[:-4], refs[-4:]
    rows = pl.ds(pl.multiple_of(starts[0], size), size)
    reads, writes = [], []
    for k, source in enumerate(sources):
        there = pl.ds(k * size, size)
        reads.append(
            pltpu.make_async_copy(source.at[rows], buffer.at[there], read_sems.at[k])
        )
        writes.append(
            pltpu.make_async_copy(buffer.at[there], packed.at[there], write_sems.at[k])
        )
    for copy in reads:
        copy.start()
    for read, write in zip(reads, writes):
        read.wait()
        write.start()
    for copy in writes:
        copy.wait()


def pack(arrays, start, size):
    shape = (len(arrays) * size, arrays[0].shape[1])
    anywhere = pl.BlockSpec(memory_space=pl.ANY)
    return pl.pallas_call(
        functools.partial(pack_kernel, size),
        out_shape=jax.ShapeDtypeStruct(shape, arrays[0].dtype),
        in_specs=[pl.BlockSpec(memory_space=pltpu.SMEM)] + [anywhere] * len(arrays),
        out_specs=anywhere,
        scratch_shapes=[
            pltpu.VMEM(shape, arrays[0].dtype),
            pltpu.SemaphoreType.DMA((len(arrays),)),
            pltpu.SemaphoreType.DMA((len(arrays),)),
        ],
        compiler_params=pltpu.CompilerParams(vmem_limit_bytes=32 * 1024 * 1024),
        cost_estimate=pl.CostEstimate(
            flops=0, bytes_accessed=4 * shape[0] * shape[1], transcendentals=0
        ),
    )(start.reshape(1), *arrays)


class Sizes:
    def __init__(self, sections, row_count, width, local_hidden, panel, hidden_total, blocks):
        self.sections, self.row_count = sections, row_count
        self.width, self.local_hidden, self.panel = width, local_hidden, panel
        self.blocks = blocks
        self.block_rows = row_count // blocks
        self.panels_in = local_hidden // panel
        self.panels_out = width // panel
        self.scale_in = 1.0 / math.sqrt(width)
        self.scale_out = 1.0 / math.sqrt(hidden_total)


def kept_place(sz, step, forward):
    return (step if forward else sz.sections + step) * sz.row_count


def chain_kernel(sz, step, forward, counts, *refs):
    refs = list(refs)

    def take(count):
        taken = refs[:count]
        del refs[:count]
        return taken

    first = forward and step == 0
    parts = 1 if first else 2
    (table,) = take(1)
    received, edges, sources = take(counts[0]), take(counts[1]), take(2 * parts)
    take(0 if first else 2)
    sends = take(counts[2])
    kept, state = take(2)
    weights_in, weights_out, landing, rows, up, out, slope, wide_store = take(8)
    weight_sems, block_sems, edge_sems, send_sems, state_sems = take(5)
    panel, width, hidden_size = sz.panel, sz.width, sz.local_hidden
    links = sz.sections - 1
    whole = pl.ds(0, sz.row_count)

    def weight_copy(d, which):
        weights = (weights_in, weights_out)[which]
        return pltpu.make_async_copy(
            sources[2 * d + which], weights.at[d], weight_sems.at[d, which]
        )

    def place(line, e):
        return pl.ds(pl.multiple_of(table[line, e], sz.block_rows), sz.block_rows)

    def state_part(k, columns):
        return state.at[pl.ds(k * sz.row_count, sz.row_count), pl.ds(0, columns)]

    fresh_hbm = kept.at[pl.ds(kept_place(sz, step, forward), sz.row_count)]
    rows_hbm, slope_hbm = state_part(0, width), state_part(1, 2 * hidden_size)

    @pl.when(table[links + 1, step] == 1)
    def _():
        sequence = [
            (d, which if forward else 1 - which) for d in range(parts) for which in range(2)
        ]
        arrive = links if forward else step
        first_copies = []
        for i, source in enumerate(received):
            e, a = divmod(i, 2)
            rows_there = whole if len(received) == 2 else place(arrive, e)
            first_copies.append(
                pltpu.make_async_copy(source, landing.at[a, rows_there], block_sems.at[i])
            )
        for d in range(2 * len(edges)):
            column = pl.ds(pl.multiple_of(table[links + 2, d], panel), panel)
            source = edges[d // 2].at[pl.ds((d % 2) * sz.row_count, sz.row_count)]
            first_copies.append(
                pltpu.make_async_copy(source, out.at[:, column], edge_sems.at[d])
            )
        if not forward:
            first_copies.append(pltpu.make_async_copy(rows_hbm, wide_store, state_sems.at[0]))
            slope_copy = pltpu.make_async_copy(slope_hbm, slope, state_sems.at[1])
        for copy in first_copies:
            copy.start()
        for i, item in enumerate(sequence):
            weight_copy(*item).start()
            if i == 0 and not forward:
                slope_copy.start()

        def arrived(item):
            weight_copy(*item).wait()

        for copy in first_copies:
            copy.wait()
        if received:
            total = landing[0].astype(jnp.float32) + landing[1].astype(jnp.float32)
            total = total.astype(jnp.bfloat16)
        if forward:
            rows[...] = total if received else out[...]
        elif edges:
            goal = out[...].astype(jnp.float32)
            up[...] = (total.astype(jnp.float32) - goal).astype(jnp.bfloat16)
        else:
            up[...] = total
        fresh = rows if forward else up
        store_copies = [pltpu.make_async_copy(fresh, fresh_hbm, state_sems.at[2])]
        if forward:
            wide = rows[...].astype(jnp.float32)
            wide_store[...] = wide
            store_copies.append(pltpu.make_async_copy(wide_store, rows_hbm, state_sems.at[0]))
        else:
            wide = wide_store[...]
        inverse_rms = lax.rsqrt(jnp.mean(wide * wide, axis=1, keepdims=True) + epsilon)
        leads = table[links + 2, 4] == 1
        if forward:
            normed = (wide * inverse_rms).astype(jnp.bfloat16)
            total = [jnp.zeros((sz.row_count, panel), jnp.float32) for _ in range(sz.panels_out)]
            for d in range(parts):
                arrived((d, 0))
                hidden = []
                for p in range(sz.panels_in):
                    weight = weights_in[d, :, p * panel : (p + 1) * panel]
                    preact = dot(normed, weight) * sz.scale_in
                    gate = jax.nn.sigmoid(preact)
                    hidden.append((preact * gate).astype(jnp.bfloat16))
                    column = d * hidden_size + p * panel
                    slope[:, column : column + panel] = gate * (1.0 + preact * (1.0 - gate))
                hidden = jnp.concatenate(hidden, axis=1)
                arrived((d, 1))
                for n in range(sz.panels_out):
                    weight = weights_out[d, :, n * panel : (n + 1) * panel]
                    total[n] = total[n] + dot(hidden, weight)
            total = jnp.concatenate(total, axis=1) * sz.scale_out
            out[...] = (total + jnp.where(leads, wide, 0.0)).astype(jnp.bfloat16)
            store_copies.append(pltpu.make_async_copy(slope, slope_hbm, state_sems.at[1]))
        else:
            up_turned = up[...].T
            total = jnp.zeros((width, sz.row_count), jnp.float32)
            for d in range(parts):
                arrived((d, 1))
                grad_hidden = dot(weights_out[d], up_turned)
                if d == 0:
                    slope_copy.wait()
                local_slope = slope[:, d * hidden_size : (d + 1) * hidden_size].T
                grad_pre = (grad_hidden * sz.scale_out * local_slope).astype(jnp.bfloat16)
                arrived((d, 0))
                total = total + dot(weights_in[d], grad_pre)
            total = total.T * sz.scale_in
            exact = wide * inverse_rms
            along = jnp.mean(total * exact, axis=1, keepdims=True)
            own = jnp.where(leads, up[...].astype(jnp.float32), 0.0)
            out[...] = (own + inverse_rms * (total - exact * along)).astype(jnp.bfloat16)
        leave = step if forward else links
        send_copies = []
        for e, target in enumerate(sends):
            rows_here = whole if len(sends) == 1 else place(leave, e)
            send_copies.append(
                pltpu.make_async_copy(out.at[rows_here], target, send_sems.at[e])
            )
        for copy in send_copies + store_copies:
            copy.start()
        for copy in send_copies + store_copies:
            copy.wait()


def chain_step(sz, step, forward, table, received, edges, weights, stores):
    first = forward and step == 0
    count = 1 if forward and step in (0, sz.sections - 1) else sz.blocks
    anywhere = pl.BlockSpec(memory_space=pl.ANY)
    operands = [table, *received, *edges, *(weights[:2] if first else [*weights, *stores])]
    block = jax.ShapeDtypeStruct((sz.row_count // count, sz.width), jnp.bfloat16)
    shapes = [block] * count + [
        jax.ShapeDtypeStruct((144 * sz.row_count, sz.width), jnp.bfloat16),
        jax.ShapeDtypeStruct((48 * sz.row_count, 2 * sz.local_hidden), jnp.float32),
    ]
    in_specs = [pl.BlockSpec(memory_space=pltpu.SMEM)] + [anywhere] * (len(operands) - 1)
    whole = (sz.row_count, sz.width)
    results = pl.pallas_call(
        functools.partial(
            chain_kernel, sz, step, forward, (len(received), len(edges), count)
        ),
        out_shape=shapes,
        in_specs=in_specs,
        out_specs=[anywhere] * len(shapes),
        input_output_aliases=(
            {} if first else {len(operands) - 2: count, len(operands) - 1: count + 1}
        ),
        scratch_shapes=[
            pltpu.VMEM((2, sz.width, sz.local_hidden), jnp.bfloat16),
            pltpu.VMEM((2, sz.local_hidden, sz.width), jnp.bfloat16),
            pltpu.VMEM((2,) + whole, jnp.bfloat16),
            pltpu.VMEM(whole, jnp.bfloat16),
            pltpu.VMEM(whole, jnp.bfloat16),
            pltpu.VMEM(whole, jnp.bfloat16),
            pltpu.VMEM((sz.row_count, 2 * sz.local_hidden), jnp.float32),
            pltpu.VMEM(whole, jnp.float32),
            pltpu.SemaphoreType.DMA((2, 2)),
            pltpu.SemaphoreType.DMA((max(1, len(received)),)),
            pltpu.SemaphoreType.DMA((4,)),
            pltpu.SemaphoreType.DMA((count,)),
            pltpu.SemaphoreType.DMA((3,)),
        ],
        compiler_params=pltpu.CompilerParams(vmem_limit_bytes=32 * 1024 * 1024),
        cost_estimate=pl.CostEstimate(
            flops=8 * sz.row_count * sz.width * sz.local_hidden,
            bytes_accessed=8 * sz.width * sz.local_hidden,
            transcendentals=0,
        ),
    )(*operands)
    return list(results[:count]), list(results[count:])


def share_kernel(sz, whole, *refs):
    if whole:
        known, source, normed_ref, hidden_ref, slope, weights, sem = refs
    else:
        known, slope, source, grad_pre, weights, sem = refs
    panel = sz.panel
    copy = pltpu.make_async_copy(source, weights, sem)
    copy.start()
    if whole:
        wide = known[...].astype(jnp.float32)
        inverse_rms = lax.rsqrt(jnp.mean(wide * wide, axis=1, keepdims=True) + epsilon)
        normed = (wide * inverse_rms).astype(jnp.bfloat16)
        normed_ref[...] = normed
        copy.wait()
        for p in range(sz.panels_in):
            here = slice(p * panel, (p + 1) * panel)
            preact = dot(normed, weights[:, here]) * sz.scale_in
            gate = jax.nn.sigmoid(preact)
            hidden_ref[:, here] = (preact * gate).astype(jnp.bfloat16)
            slope[:, here] = gate * (1.0 + preact * (1.0 - gate))
    else:
        copy.wait()
        grad_hidden = dot(known[...], weights[...], contract_last)
        grad_pre[...] = (grad_hidden * sz.scale_out * slope[...]).astype(jnp.bfloat16)


def share_call(sz, operands, weight):
    whole = len(operands) == 1
    rows_count, hidden_size = sz.row_count, sz.local_hidden
    narrow = jax.ShapeDtypeStruct((rows_count, hidden_size), jnp.bfloat16)
    shapes = [narrow]
    if whole:
        shapes = [
            jax.ShapeDtypeStruct((rows_count, sz.width), jnp.bfloat16),
            narrow,
            jax.ShapeDtypeStruct((rows_count, hidden_size), jnp.float32),
        ]
    inside = pl.BlockSpec(memory_space=pltpu.VMEM)
    return pl.pallas_call(
        functools.partial(share_kernel, sz, whole),
        out_shape=shapes,
        in_specs=[inside] * len(operands) + [pl.BlockSpec(memory_space=pl.ANY)],
        out_specs=[inside] * len(shapes),
        scratch_shapes=[
            pltpu.VMEM(weight.shape, jnp.bfloat16),
            pltpu.SemaphoreType.DMA,
        ],
        compiler_params=pltpu.CompilerParams(vmem_limit_bytes=32 * 1024 * 1024),
        cost_estimate=pl.CostEstimate(
            flops=2 * rows_count * sz.width * hidden_size,
            bytes_accessed=2 * sz.width * hidden_size,
            transcendentals=0,
        ),
    )(*operands, weight)


def per_device(inputs, targets, weight_a, weight_b, moment_a, moment_b, routes, partners):
    replicas = lax.axis_size("replica")
    sections = lax.axis_size("section")
    shards = lax.axis_size("shard")
    replica_id = lax.axis_index("replica")
    section_id = lax.axis_index("section")
    shard_id = lax.axis_index("shard")
    row_count = inputs.shape[2]
    panel = inputs.shape[3]
    width = weight_a.shape[2]
    local_hidden = weight_a.shape[3]
    assert inputs.shape[1] == 1 and shards == 4
    assert local_hidden % panel == 0 and sections > 2
    hidden_total = local_hidden * shards
    scale_in = 1.0 / math.sqrt(width)
    scale_out = 1.0 / math.sqrt(hidden_total)
    weight_in = weight_a[0, 0]
    weight_out = weight_b[0, 0]
    block_rows = row_count // replicas
    links = sections - 1
    in_kernel = block_rows % 16 == 0
    blocks = replicas if in_kernel else 1
    sz = Sizes(sections, row_count, width, local_hidden, panel, hidden_total, blocks)

    def flat(replica, section, shard):
        return (replica * sections + section) * shards + shard

    def turn(section):
        return (section ^ (section >> 1)) & 1

    def holders(section):
        return [j for j in range(shards) if (j & 1) != turn(section)]

    def move(array, sources, target):
        pairs = [
            (flat(r, s, j), flat(*target(r, s, j)))
            for r in range(replicas)
            for s, j in sources
        ]
        return lax.ppermute(array, axes, pairs)

    def holder_sources(active):
        return [(s, j) for s in active for j in holders(s)]

    def to_holders(array, offset, active):
        sources = [(s, j ^ offset) for s, j in holder_sources(active)]
        return move(array, sources, lambda r, s, j: (r, s, j ^ offset))

    def from_holders(array, offset, active):
        return move(array, holder_sources(active), lambda r, s, j: (r, s, j ^ offset))

    def between_holders(array, offset, other_half, section, step):
        shift = turn(section) ^ turn(section + step) ^ (2 * other_half)
        return move(
            array,
            holder_sources([section]),
            lambda r, s, j: ((r + offset) % replicas, s + step, j ^ shift),
        )

    def across_replicas(array, offset, active):
        return move(
            array,
            [(s, j) for s in active for j in range(shards)],
            lambda r, s, j: ((r + offset) % replicas, s, j),
        )

    every = range(sections)
    others = range(1, replicas)
    is_holder = (shard_id & 1) != turn(section_id)

    edge = jnp.where(section_id == 0, inputs[0, 0], targets[0, 0])
    ends = [(s, j) for s in (0, links) for j in range(shards)]

    def at_ends(array, offset):
        return move(array, ends, lambda r, s, j: (r, s, j ^ offset))

    pair = jnp.concatenate([edge, at_ends(edge, 1)])
    pair, packed_weight = lax.optimization_barrier((pair, weight_in))
    edges = [pair, at_ends(pair, 2)]
    rest = range(1, sections)
    near_in = to_holders(weight_in, 1, rest)
    near_in, next_out = lax.optimization_barrier((near_in, weight_out))
    near = [near_in, to_holders(next_out, 1, rest)]

    tables = lax.dynamic_index_in_dim(partners, section_id, 0, keepdims=False)

    def piece_of(table, offset):
        wanted = (replica_id + offset) % replicas
        return jnp.argmax(table[:, replica_id] == wanted).astype(jnp.int32)

    pieces_in = [piece_of(tables[0], e) for e in range(replicas)]
    pieces_out = [piece_of(tables[1], e) for e in range(replicas)]
    size_in = width // replicas
    size_out = local_hidden // replicas

    def piece(array, index, size, axis=0):
        return lax.dynamic_slice_in_dim(array, index * size, size, axis)

    def exchange(arrays, active):
        return [across_replicas(array, e, active) for e, array in zip(others, arrays)]

    packed_in = [
        pack([packed_weight, moment_a[0, 0]], pieces_in[e] * size_in, size_in) for e in others
    ]
    packed_out = [
        pack([weight_out, moment_b[0, 0]], pieces_out[e] * size_out, size_out) for e in others
    ]
    early = range(sections // 2, sections)
    late = range(sections // 2)
    far_states_in = exchange(packed_in, every)

    offsets = jnp.arange(replicas, dtype=jnp.int32)
    there = (replica_id + offsets) % replicas
    back = (replica_id - offsets) % replicas
    own_routes = routes[0, :, replica_id, :]
    slots = jnp.sum(
        (own_routes[:, None, :] == there[None, :, None]).astype(jnp.int32)
        * offsets[None, None, :],
        axis=2,
    )
    columns = max(replicas, sections, shards + 1)
    steps = jnp.arange(sections)
    ours = ((is_holder | (steps == 0)) & (section_id == steps)).astype(jnp.int32)
    features = (shard_id ^ jnp.arange(shards, dtype=jnp.int32)) * panel
    leads = (is_holder & ((shard_id & 2) == 0)).astype(jnp.int32)
    features = jnp.append(features, leads)

    def line(values):
        return jnp.pad(values, ((0, 0), (0, columns - values.shape[1])))

    starts = jnp.concatenate([slots, back[None]]) * block_rows
    if not in_kernel:
        starts = jnp.zeros_like(starts)
    table = jnp.concatenate([line(starts), line(ours[None]), line(features[None])])
    table = table.astype(jnp.int32)

    def send_blocks(sends, arrived, left, section, step):
        sign = step
        if in_kernel:
            return [
                between_holders(sends[e], sign * e, a, section, step)
                for e in range(replicas)
                for a in range(2)
            ]
        parts = sends[0].reshape(replicas, block_rows, width)
        moved = [jnp.zeros_like(parts), jnp.zeros_like(parts)]
        for e in range(replicas):
            chosen = lax.dynamic_index_in_dim(parts, left[e], 0, keepdims=False)
            for a in range(2):
                got = between_holders(chosen, sign * e, a, section, step)
                moved[a] = lax.dynamic_update_index_in_dim(moved[a], got, arrived[e], 0)
        return [one.reshape(row_count, width) for one in moved]

    def kept_of(stores, steps, forward):
        places = [kept_place(sz, step, forward) for step in steps]
        result = stores[0][places[0] : places[0] + row_count]
        for step, place in zip(steps[1:], places[1:]):
            result = jnp.where(section_id == step, stores[0][place : place + row_count], result)
        return result

    row_parts = []

    def spread_rows(received, rows, active):
        received, rows, row_parts[:] = lax.optimization_barrier(
            (received, rows, row_parts)
        )
        row_parts.append(from_holders(rows, 1, active))
        return received

    def bundle(normed, hidden, e):
        parts = [
            piece(normed, pieces_in[e], size_in, 1), piece(hidden, pieces_out[e], size_out, 1)
        ]
        return jnp.concatenate(parts, axis=1)

    weights = [weight_in, weight_out, *near]
    received, stores = [], []
    for step in every:
        sends, stores = chain_step(
            sz, step, True, table, received, edges if step == 0 else [], weights, stores
        )
        if step == len(late) - 1:
            rows = kept_of(stores, late, True)
        if step == links:
            rows = kept_of(stores, early, True)
            late_rows = kept_of(stores, late, True)
        if step == 0:
            total = sends[0].astype(jnp.float32)
            total = total + at_ends(sends[0], 1).astype(jnp.float32)
            sends = [total.astype(jnp.bfloat16)]
            if in_kernel:
                sends = [piece(sends[0], slots[0, e], block_rows) for e in range(replicas)]
        if step < links:
            received = send_blocks(sends, back, slots[step], step, 1)
            if step == 0:
                received, far_states_in, packed_out = lax.optimization_barrier(
                    (received, far_states_in, packed_out)
                )
                far_states_out = exchange(packed_out, early)
        else:
            received = [sends[0], at_ends(sends[0], 2)]
            row_parts.append(from_holders(rows, 1, early))
            own_rows = jnp.where(section_id < len(late), late_rows, rows)
            own_rows = jnp.where(is_holder, own_rows, sum(row_parts[1:], row_parts[0]))
            received, *shares = lax.optimization_barrier(
                (received, *share_call(sz, [own_rows], weight_in))
            )
            normed, hidden, slope = shares
            bundles = exchange([bundle(normed, hidden, e) for e in others], every)
        if step == len(late) - 1:
            received = spread_rows(received, rows, late)
        if step == len(late) - 1:
            received, packed_out = lax.optimization_barrier((received, packed_out))
            far_late = exchange(packed_out, late)
        if step == len(late):
            received, far_states_out = lax.optimization_barrier((received, far_states_out))

    for step in reversed(range(1, sections)):
        sends, stores = chain_step(
            sz, step, False, table, received, edges if step == links else [], weights, stores
        )
        received = send_blocks(sends, slots[step - 1], back, step, -1)
        if step == len(late):
            received, far_late, bundles = lax.optimization_barrier(
                (received, far_late, bundles)
            )

    far_normed = [one[:, :size_in] for one in bundles]
    far_hidden = [one[:, size_in:] for one in bundles]

    halves = []
    for a in range(2):
        half = received[a]
        if in_kernel:
            half = jnp.zeros((row_count, width), jnp.bfloat16)
            for e in range(replicas):
                half = lax.dynamic_update_slice_in_dim(
                    half, received[2 * e + a], slots[0, e] * block_rows, 0
                )
        halves.append(half.astype(jnp.float32))
    first_up = (halves[0] + halves[1]).astype(jnp.bfloat16)
    upstream = jnp.where(section_id == 0, first_up, kept_of(stores, rest, False))
    upstream = jnp.where(is_holder, upstream, from_holders(upstream, 1, every))
    far_up = exchange([upstream] * len(others), every)
    (grad_pre,) = share_call(sz, [upstream, slope], weight_out)
    far_pre = exchange([grad_pre] * len(others), every)
    upstream, grad_pre = lax.optimization_barrier((upstream, grad_pre))
    far_states_out = [
        jnp.where(section_id < len(late), one, two)
        for one, two in zip(far_late, far_states_out)
    ]
    far_states = {0: far_states_in, 2: far_states_out}

    def far_part(e, which):
        size = size_out if which & 2 else size_in
        both = far_states[which & 2][e - 1]
        return both[size:] if which & 1 else both[:size]

    def as_delta(left, right, scale):
        return (inner_rate * (dot(left, right, contract_rows) * scale)).astype(jnp.bfloat16)

    def finish(weight, moment, left, right, which, far_left, far_right, scale, pieces, size):
        new_weight, new_moment = outer_mix(
            weight.astype(jnp.float32),
            moment.astype(jnp.float32),
            as_delta(left, right, scale).astype(jnp.float32),
        )
        for e in others:
            back = replicas - e

            def mean(own_array, far_array):
                return 0.5 * (own_array.astype(jnp.float32) + far_array.astype(jnp.float32))

            index = pieces[back]
            own_left = piece(left, index, size, 1)
            part_weight, part_moment = outer_mix(
                mean(piece(weight, index, size), far_part(e, which)),
                mean(piece(moment, index, size), far_part(e, which + 1)),
                mean(
                    as_delta(own_left, right, scale),
                    as_delta(far_left[e - 1], far_right[e - 1], scale),
                ),
            )
            new_weight = lax.dynamic_update_slice_in_dim(new_weight, part_weight, index * size, 0)
            new_moment = lax.dynamic_update_slice_in_dim(new_moment, part_moment, index * size, 0)
        return new_weight[None, None], new_moment[None, None]

    new_weight_b, new_moment_b = finish(
        weight_out, moment_b[0, 0], hidden, upstream, 2, far_hidden, far_up,
        scale_out, pieces_out, size_out,
    )
    new_weight_a, new_moment_a = finish(
        weight_in, moment_a[0, 0], normed, grad_pre, 0, far_normed, far_pre,
        scale_in, pieces_in, size_in,
    )
    return (new_weight_a, new_weight_b, new_moment_a, new_moment_b)


def solution(mesh):
    placed = (
        P("replica", None, None, "shard"),
        P("replica", None, None, "shard"),
        P("replica", "section", None, "shard"),
        P("replica", "section", "shard", None),
        P("replica", "section", None, "shard"),
        P("replica", "section", "shard", None),
        P(),
        P(),
    )
    return jax.shard_map(
        per_device,
        mesh=mesh,
        in_specs=placed,
        out_specs=(
            P("replica", "section", None, "shard"),
            P("replica", "section", "shard", None),
            P("replica", "section", None, "shard"),
            P("replica", "section", "shard", None),
        ),
        check_vma=False,
    )
```

```python
import functools
import math

import jax
import jax.numpy as jnp
from jax import lax
from jax.experimental import pallas as pl
from jax.experimental.pallas import tpu as pltpu
from jax.sharding import PartitionSpec as P

epsilon = 1e-05
inner_rate = 0.5
momentum_decay = 0.9
outer_rate = 0.7

axes = ("replica", "section", "shard")
contract_rows = (((0,), (0,)), ((), ()))
contract_last = (((1,), (1,)), ((), ()))


def dot(left, right, dims=(((1,), (0,)), ((), ()))):
    return lax.dot_general(left, right, dims, preferred_element_type=jnp.float32)


def outer_mix(weight, moment, delta):
    new_moment = momentum_decay * moment + delta
    new_weight = weight - outer_rate * (momentum_decay * new_moment + delta)
    return new_weight.astype(jnp.bfloat16), new_moment.astype(jnp.bfloat16)


def pack_kernel(size, starts, *refs):
    sources, (packed, buffer, read_sems, write_sems) = refs[:-4], refs[-4:]
    rows = pl.ds(pl.multiple_of(starts[0], size), size)
    reads, writes = [], []
    for k, source in enumerate(sources):
        there = pl.ds(k * size, size)
        reads.append(
            pltpu.make_async_copy(source.at[rows], buffer.at[there], read_sems.at[k])
        )
        writes.append(
            pltpu.make_async_copy(buffer.at[there], packed.at[there], write_sems.at[k])
        )
    for copy in reads:
        copy.start()
    for read, write in zip(reads, writes):
        read.wait()
        write.start()
    for copy in writes:
        copy.wait()


def pack(arrays, start, size):
    shape = (len(arrays) * size, arrays[0].shape[1])
    anywhere = pl.BlockSpec(memory_space=pl.ANY)
    return pl.pallas_call(
        functools.partial(pack_kernel, size),
        out_shape=jax.ShapeDtypeStruct(shape, arrays[0].dtype),
        in_specs=[pl.BlockSpec(memory_space=pltpu.SMEM)] + [anywhere] * len(arrays),
        out_specs=anywhere,
        scratch_shapes=[
            pltpu.VMEM(shape, arrays[0].dtype),
            pltpu.SemaphoreType.DMA((len(arrays),)),
            pltpu.SemaphoreType.DMA((len(arrays),)),
        ],
        compiler_params=pltpu.CompilerParams(vmem_limit_bytes=32 * 1024 * 1024),
        cost_estimate=pl.CostEstimate(
            flops=0, bytes_accessed=4 * shape[0] * shape[1], transcendentals=0
        ),
    )(start.reshape(1), *arrays)


class Sizes:
    def __init__(self, sections, row_count, width, local_hidden, panel, hidden_total, blocks):
        self.sections, self.row_count = sections, row_count
        self.width, self.local_hidden, self.panel = width, local_hidden, panel
        self.blocks = blocks
        self.block_rows = row_count // blocks
        self.panels_in = local_hidden // panel
        self.panels_out = width // panel
        self.scale_in = 1.0 / math.sqrt(width)
        self.scale_out = 1.0 / math.sqrt(hidden_total)


def kept_place(sz, step, forward):
    return (step if forward else sz.sections + step) * sz.row_count


def chain_kernel(sz, step, forward, counts, *refs):
    refs = list(refs)

    def take(count):
        taken = refs[:count]
        del refs[:count]
        return taken

    first = forward and step == 0
    parts = 1 if first else 2
    (table,) = take(1)
    received, edges, sources = take(counts[0]), take(counts[1]), take(2 * parts)
    take(0 if first else 2)
    sends = take(counts[2])
    kept, state = take(2)
    weights_in, weights_out, landing, rows, up, out, slope, wide_store = take(8)
    weight_sems, block_sems, edge_sems, send_sems, state_sems = take(5)
    panel, width, hidden_size = sz.panel, sz.width, sz.local_hidden
    links = sz.sections - 1
    whole = pl.ds(0, sz.row_count)

    def weight_copy(d, which):
        weights = (weights_in, weights_out)[which]
        return pltpu.make_async_copy(
            sources[2 * d + which], weights.at[d], weight_sems.at[d, which]
        )

    def place(line, e):
        return pl.ds(pl.multiple_of(table[line, e], sz.block_rows), sz.block_rows)

    def state_part(k, columns):
        return state.at[pl.ds(k * sz.row_count, sz.row_count), pl.ds(0, columns)]

    fresh_hbm = kept.at[pl.ds(kept_place(sz, step, forward), sz.row_count)]
    rows_hbm, slope_hbm = state_part(0, width), state_part(1, 2 * hidden_size)

    @pl.when(table[links + 1, step] == 1)
    def _():
        sequence = [
            (d, which if forward else 1 - which) for d in range(parts) for which in range(2)
        ]
        arrive = links if forward else step
        first_copies = []
        for i, source in enumerate(received):
            e, a = divmod(i, 2)
            rows_there = whole if len(received) == 2 else place(arrive, e)
            first_copies.append(
                pltpu.make_async_copy(source, landing.at[a, rows_there], block_sems.at[i])
            )
        for d in range(2 * len(edges)):
            column = pl.ds(pl.multiple_of(table[links + 2, d], panel), panel)
            source = edges[d // 2].at[pl.ds((d % 2) * sz.row_count, sz.row_count)]
            first_copies.append(
                pltpu.make_async_copy(source, out.at[:, column], edge_sems.at[d])
            )
        if not forward:
            first_copies.append(pltpu.make_async_copy(rows_hbm, wide_store, state_sems.at[0]))
            slope_copy = pltpu.make_async_copy(slope_hbm, slope, state_sems.at[1])
        for copy in first_copies:
            copy.start()
        for i, item in enumerate(sequence):
            weight_copy(*item).start()
            if i == 0 and not forward:
                slope_copy.start()

        def arrived(item):
            weight_copy(*item).wait()

        for copy in first_copies:
            copy.wait()
        if received:
            total = landing[0].astype(jnp.float32) + landing[1].astype(jnp.float32)
            total = total.astype(jnp.bfloat16)
        if forward:
            rows[...] = total if received else out[...]
        elif edges:
            goal = out[...].astype(jnp.float32)
            up[...] = (total.astype(jnp.float32) - goal).astype(jnp.bfloat16)
        else:
            up[...] = total
        fresh = rows if forward else up
        store_copies = [pltpu.make_async_copy(fresh, fresh_hbm, state_sems.at[2])]
        if forward:
            wide = rows[...].astype(jnp.float32)
            wide_store[...] = wide
            store_copies.append(pltpu.make_async_copy(wide_store, rows_hbm, state_sems.at[0]))
        else:
            wide = wide_store[...]
        inverse_rms = lax.rsqrt(jnp.mean(wide * wide, axis=1, keepdims=True) + epsilon)
        leads = table[links + 2, 4] == 1
        if forward:
            normed = (wide * inverse_rms).astype(jnp.bfloat16)
            total = [jnp.zeros((sz.row_count, panel), jnp.float32) for _ in range(sz.panels_out)]
            for d in range(parts):
                arrived((d, 0))
                hidden = []
                for p in range(sz.panels_in):
                    weight = weights_in[d, :, p * panel : (p + 1) * panel]
                    preact = dot(normed, weight) * sz.scale_in
                    gate = jax.nn.sigmoid(preact)
                    hidden.append((preact * gate).astype(jnp.bfloat16))
                    column = d * hidden_size + p * panel
                    slope[:, column : column + panel] = gate * (1.0 + preact * (1.0 - gate))
                hidden = jnp.concatenate(hidden, axis=1)
                arrived((d, 1))
                for n in range(sz.panels_out):
                    weight = weights_out[d, :, n * panel : (n + 1) * panel]
                    total[n] = total[n] + dot(hidden, weight)
            total = jnp.concatenate(total, axis=1) * sz.scale_out
            out[...] = (total + jnp.where(leads, wide, 0.0)).astype(jnp.bfloat16)
            store_copies.append(pltpu.make_async_copy(slope, slope_hbm, state_sems.at[1]))
        else:
            up_turned = up[...].T
            total = jnp.zeros((width, sz.row_count), jnp.float32)
            for d in range(parts):
                arrived((d, 1))
                grad_hidden = dot(weights_out[d], up_turned)
                if d == 0:
                    slope_copy.wait()
                local_slope = slope[:, d * hidden_size : (d + 1) * hidden_size].T
                grad_pre = (grad_hidden * sz.scale_out * local_slope).astype(jnp.bfloat16)
                arrived((d, 0))
                total = total + dot(weights_in[d], grad_pre)
            total = total.T * sz.scale_in
            exact = wide * inverse_rms
            along = jnp.mean(total * exact, axis=1, keepdims=True)
            own = jnp.where(leads, up[...].astype(jnp.float32), 0.0)
            out[...] = (own + inverse_rms * (total - exact * along)).astype(jnp.bfloat16)
        leave = step if forward else links
        send_copies = []
        for e, target in enumerate(sends):
            rows_here = whole if len(sends) == 1 else place(leave, e)
            send_copies.append(
                pltpu.make_async_copy(out.at[rows_here], target, send_sems.at[e])
            )
        for copy in send_copies + store_copies:
            copy.start()
        for copy in send_copies + store_copies:
            copy.wait()


def chain_step(sz, step, forward, table, received, edges, weights, stores):
    first = forward and step == 0
    count = 1 if forward and step in (0, sz.sections - 1) else sz.blocks
    anywhere = pl.BlockSpec(memory_space=pl.ANY)
    operands = [table, *received, *edges, *(weights[:2] if first else [*weights, *stores])]
    block = jax.ShapeDtypeStruct((sz.row_count // count, sz.width), jnp.bfloat16)
    shapes = [block] * count + [
        jax.ShapeDtypeStruct((144 * sz.row_count, sz.width), jnp.bfloat16),
        jax.ShapeDtypeStruct((48 * sz.row_count, 2 * sz.local_hidden), jnp.float32),
    ]
    in_specs = [pl.BlockSpec(memory_space=pltpu.SMEM)] + [anywhere] * (len(operands) - 1)
    whole = (sz.row_count, sz.width)
    results = pl.pallas_call(
        functools.partial(
            chain_kernel, sz, step, forward, (len(received), len(edges), count)
        ),
        out_shape=shapes,
        in_specs=in_specs,
        out_specs=[anywhere] * len(shapes),
        input_output_aliases=(
            {} if first else {len(operands) - 2: count, len(operands) - 1: count + 1}
        ),
        scratch_shapes=[
            pltpu.VMEM((2, sz.width, sz.local_hidden), jnp.bfloat16),
            pltpu.VMEM((2, sz.local_hidden, sz.width), jnp.bfloat16),
            pltpu.VMEM((2,) + whole, jnp.bfloat16),
            pltpu.VMEM(whole, jnp.bfloat16),
            pltpu.VMEM(whole, jnp.bfloat16),
            pltpu.VMEM(whole, jnp.bfloat16),
            pltpu.VMEM((sz.row_count, 2 * sz.local_hidden), jnp.float32),
            pltpu.VMEM(whole, jnp.float32),
            pltpu.SemaphoreType.DMA((2, 2)),
            pltpu.SemaphoreType.DMA((max(1, len(received)),)),
            pltpu.SemaphoreType.DMA((4,)),
            pltpu.SemaphoreType.DMA((count,)),
            pltpu.SemaphoreType.DMA((3,)),
        ],
        compiler_params=pltpu.CompilerParams(vmem_limit_bytes=32 * 1024 * 1024),
        cost_estimate=pl.CostEstimate(
            flops=8 * sz.row_count * sz.width * sz.local_hidden,
            bytes_accessed=8 * sz.width * sz.local_hidden,
            transcendentals=0,
        ),
    )(*operands)
    return list(results[:count]), list(results[count:])


def share_kernel(sz, whole, *refs):
    if whole:
        known, source, normed_ref, hidden_ref, slope, weights, sem = refs
    else:
        known, slope, source, grad_pre, weights, sem = refs
    panel = sz.panel
    copy = pltpu.make_async_copy(source, weights, sem)
    copy.start()
    if whole:
        wide = known[...].astype(jnp.float32)
        inverse_rms = lax.rsqrt(jnp.mean(wide * wide, axis=1, keepdims=True) + epsilon)
        normed = (wide * inverse_rms).astype(jnp.bfloat16)
        normed_ref[...] = normed
        copy.wait()
        for p in range(sz.panels_in):
            here = slice(p * panel, (p + 1) * panel)
            preact = dot(normed, weights[:, here]) * sz.scale_in
            gate = jax.nn.sigmoid(preact)
            hidden_ref[:, here] = (preact * gate).astype(jnp.bfloat16)
            slope[:, here] = gate * (1.0 + preact * (1.0 - gate))
    else:
        copy.wait()
        grad_hidden = dot(known[...], weights[...], contract_last)
        grad_pre[...] = (grad_hidden * sz.scale_out * slope[...]).astype(jnp.bfloat16)


def share_call(sz, operands, weight):
    whole = len(operands) == 1
    rows_count, hidden_size = sz.row_count, sz.local_hidden
    narrow = jax.ShapeDtypeStruct((rows_count, hidden_size), jnp.bfloat16)
    shapes = [narrow]
    if whole:
        shapes = [
            jax.ShapeDtypeStruct((rows_count, sz.width), jnp.bfloat16),
            narrow,
            jax.ShapeDtypeStruct((rows_count, hidden_size), jnp.float32),
        ]
    inside = pl.BlockSpec(memory_space=pltpu.VMEM)
    return pl.pallas_call(
        functools.partial(share_kernel, sz, whole),
        out_shape=shapes,
        in_specs=[inside] * len(operands) + [pl.BlockSpec(memory_space=pl.ANY)],
        out_specs=[inside] * len(shapes),
        scratch_shapes=[
            pltpu.VMEM(weight.shape, jnp.bfloat16),
            pltpu.SemaphoreType.DMA,
        ],
        compiler_params=pltpu.CompilerParams(vmem_limit_bytes=32 * 1024 * 1024),
        cost_estimate=pl.CostEstimate(
            flops=2 * rows_count * sz.width * hidden_size,
            bytes_accessed=2 * sz.width * hidden_size,
            transcendentals=0,
        ),
    )(*operands, weight)


def per_device(inputs, targets, weight_a, weight_b, moment_a, moment_b, routes, partners):
    replicas = lax.axis_size("replica")
    sections = lax.axis_size("section")
    shards = lax.axis_size("shard")
    replica_id = lax.axis_index("replica")
    section_id = lax.axis_index("section")
    shard_id = lax.axis_index("shard")
    row_count = inputs.shape[2]
    panel = inputs.shape[3]
    width = weight_a.shape[2]
    local_hidden = weight_a.shape[3]
    assert inputs.shape[1] == 1 and shards == 4
    assert local_hidden % panel == 0 and sections > 2
    hidden_total = local_hidden * shards
    scale_in = 1.0 / math.sqrt(width)
    scale_out = 1.0 / math.sqrt(hidden_total)
    weight_in = weight_a[0, 0]
    weight_out = weight_b[0, 0]
    block_rows = row_count // replicas
    links = sections - 1
    in_kernel = block_rows % 16 == 0
    blocks = replicas if in_kernel else 1
    sz = Sizes(sections, row_count, width, local_hidden, panel, hidden_total, blocks)

    def flat(replica, section, shard):
        return (replica * sections + section) * shards + shard

    def turn(section):
        return (section ^ (section >> 1)) & 1

    def holders(section):
        return [j for j in range(shards) if (j & 1) != turn(section)]

    def move(array, sources, target):
        pairs = [
            (flat(r, s, j), flat(*target(r, s, j)))
            for r in range(replicas)
            for s, j in sources
        ]
        return lax.ppermute(array, axes, pairs)

    def holder_sources(active):
        return [(s, j) for s in active for j in holders(s)]

    def to_holders(array, offset, active):
        sources = [(s, j ^ offset) for s, j in holder_sources(active)]
        return move(array, sources, lambda r, s, j: (r, s, j ^ offset))

    def from_holders(array, offset, active):
        return move(array, holder_sources(active), lambda r, s, j: (r, s, j ^ offset))

    def between_holders(array, offset, other_half, section, step):
        shift = turn(section) ^ turn(section + step) ^ (2 * other_half)
        return move(
            array,
            holder_sources([section]),
            lambda r, s, j: ((r + offset) % replicas, s + step, j ^ shift),
        )

    def across_replicas(array, offset, active):
        return move(
            array,
            [(s, j) for s in active for j in range(shards)],
            lambda r, s, j: ((r + offset) % replicas, s, j),
        )

    every = range(sections)
    others = range(1, replicas)
    is_holder = (shard_id & 1) != turn(section_id)

    edge = jnp.where(section_id == 0, inputs[0, 0], targets[0, 0])
    ends = [(s, j) for s in (0, links) for j in range(shards)]

    def at_ends(array, offset):
        return move(array, ends, lambda r, s, j: (r, s, j ^ offset))

    pair = jnp.concatenate([edge, at_ends(edge, 1)])
    second, packed_weight = lax.optimization_barrier((at_ends(pair, 2), weight_in))
    edges = [pair, second]
    rest = range(1, sections)
    near_in = to_holders(weight_in, 1, rest)
    near_in, next_out = lax.optimization_barrier((near_in, weight_out))
    near = [near_in, to_holders(next_out, 1, rest)]

    tables = lax.dynamic_index_in_dim(partners, section_id, 0, keepdims=False)

    def piece_of(table, offset):
        wanted = (replica_id + offset) % replicas
        return jnp.argmax(table[:, replica_id] == wanted).astype(jnp.int32)

    pieces_in = [piece_of(tables[0], e) for e in range(replicas)]
    pieces_out = [piece_of(tables[1], e) for e in range(replicas)]
    size_in = width // replicas
    size_out = local_hidden // replicas

    def piece(array, index, size, axis=0):
        return lax.dynamic_slice_in_dim(array, index * size, size, axis)

    def exchange(arrays, active):
        return [across_replicas(array, e, active) for e, array in zip(others, arrays)]

    packed_in = [
        pack([packed_weight, moment_a[0, 0]], pieces_in[e] * size_in, size_in) for e in others
    ]
    packed_out = [
        pack([weight_out, moment_b[0, 0]], pieces_out[e] * size_out, size_out) for e in others
    ]
    early = range(sections // 2, sections)
    late = range(sections // 2)
    far_states_in = exchange(packed_in, every)

    offsets = jnp.arange(replicas, dtype=jnp.int32)
    there = (replica_id + offsets) % replicas
    back = (replica_id - offsets) % replicas
    own_routes = routes[0, :, replica_id, :]
    slots = jnp.sum(
        (own_routes[:, None, :] == there[None, :, None]).astype(jnp.int32)
        * offsets[None, None, :],
        axis=2,
    )
    columns = max(replicas, sections, shards + 1)
    steps = jnp.arange(sections)
    ours = ((is_holder | (steps == 0)) & (section_id == steps)).astype(jnp.int32)
    features = (shard_id ^ jnp.arange(shards, dtype=jnp.int32)) * panel
    leads = (is_holder & ((shard_id & 2) == 0)).astype(jnp.int32)
    features = jnp.append(features, leads)

    def line(values):
        return jnp.pad(values, ((0, 0), (0, columns - values.shape[1])))

    starts = jnp.concatenate([slots, back[None]]) * block_rows
    if not in_kernel:
        starts = jnp.zeros_like(starts)
    table = jnp.concatenate([line(starts), line(ours[None]), line(features[None])])
    table = table.astype(jnp.int32)

    def send_blocks(sends, arrived, left, section, step):
        sign = step
        if in_kernel:
            return [
                between_holders(sends[e], sign * e, a, section, step)
                for e in range(replicas)
                for a in range(2)
            ]
        parts = sends[0].reshape(replicas, block_rows, width)
        moved = [jnp.zeros_like(parts), jnp.zeros_like(parts)]
        for e in range(replicas):
            chosen = lax.dynamic_index_in_dim(parts, left[e], 0, keepdims=False)
            for a in range(2):
                got = between_holders(chosen, sign * e, a, section, step)
                moved[a] = lax.dynamic_update_index_in_dim(moved[a], got, arrived[e], 0)
        return [one.reshape(row_count, width) for one in moved]

    def kept_of(stores, steps, forward):
        places = [kept_place(sz, step, forward) for step in steps]
        result = stores[0][places[0] : places[0] + row_count]
        for step, place in zip(steps[1:], places[1:]):
            result = jnp.where(section_id == step, stores[0][place : place + row_count], result)
        return result

    row_parts = []

    def spread_rows(received, rows, active):
        received, rows, row_parts[:] = lax.optimization_barrier(
            (received, rows, row_parts)
        )
        row_parts.append(from_holders(rows, 1, active))
        return received

    def bundle(normed, hidden, e):
        parts = [
            piece(normed, pieces_in[e], size_in, 1), piece(hidden, pieces_out[e], size_out, 1)
        ]
        return jnp.concatenate(parts, axis=1)

    weights = [weight_in, weight_out, *near]
    received, stores = [], []
    for step in every:
        sends, stores = chain_step(
            sz, step, True, table, received, edges if step == 0 else [], weights, stores
        )
        if step in (len(late) - 1, links):
            rows = kept_of(stores, range(step + 1), True)
        if step == 1:
            sends, far_states_in, packed_out = lax.optimization_barrier(
                (sends, far_states_in, packed_out)
            )
            far_states_out = exchange(packed_out, early)
        if step == 0:
            total = sends[0].astype(jnp.float32)
            total = total + at_ends(sends[0], 1).astype(jnp.float32)
            sends = [total.astype(jnp.bfloat16)]
            if in_kernel:
                sends = [piece(sends[0], slots[0, e], block_rows) for e in range(replicas)]
        if step < links:
            received = send_blocks(sends, back, slots[step], step, 1)
        else:
            received = [sends[0], at_ends(sends[0], 2)]
            row_parts.append(from_holders(rows, 1, early))
            own_rows = jnp.where(is_holder, rows, sum(row_parts[1:], row_parts[0]))
            received, *shares = lax.optimization_barrier(
                (received, *share_call(sz, [own_rows], weight_in))
            )
            normed, hidden, slope = shares
            bundles = exchange([bundle(normed, hidden, e) for e in others], every)
        if step == len(late) - 1:
            received = spread_rows(received, rows, late)
        if step == len(late) - 1:
            received, packed_out = lax.optimization_barrier((received, packed_out))
            far_late = exchange(packed_out, late)
        if step == len(late):
            received, far_states_out = lax.optimization_barrier((received, far_states_out))

    for step in reversed(range(1, sections)):
        sends, stores = chain_step(
            sz, step, False, table, received, edges if step == links else [], weights, stores
        )
        received = send_blocks(sends, slots[step - 1], back, step, -1)
        if step == len(late):
            received, far_late, bundles = lax.optimization_barrier(
                (received, far_late, bundles)
            )

    far_normed = [one[:, :size_in] for one in bundles]
    far_hidden = [one[:, size_in:] for one in bundles]

    halves = []
    for a in range(2):
        half = received[a]
        if in_kernel:
            half = jnp.zeros((row_count, width), jnp.bfloat16)
            for e in range(replicas):
                half = lax.dynamic_update_slice_in_dim(
                    half, received[2 * e + a], slots[0, e] * block_rows, 0
                )
        halves.append(half.astype(jnp.float32))
    first_up = (halves[0] + halves[1]).astype(jnp.bfloat16)
    upstream = jnp.where(section_id == 0, first_up, kept_of(stores, rest, False))
    upstream = jnp.where(is_holder, upstream, from_holders(upstream, 1, every))
    far_up = exchange([upstream] * len(others), every)
    (grad_pre,) = share_call(sz, [upstream, slope], weight_out)
    far_pre = exchange([grad_pre] * len(others), every)
    far_up, upstream, grad_pre = lax.optimization_barrier((far_up, upstream, grad_pre))
    far_states_out = [
        jnp.where(section_id < len(late), one, two)
        for one, two in zip(far_late, far_states_out)
    ]
    far_states = {0: far_states_in, 2: far_states_out}

    def far_part(e, which):
        size = size_out if which & 2 else size_in
        both = far_states[which & 2][e - 1]
        return both[size:] if which & 1 else both[:size]

    def as_delta(left, right, scale):
        return (inner_rate * (dot(left, right, contract_rows) * scale)).astype(jnp.bfloat16)

    def finish(weight, moment, left, right, which, far_left, far_right, scale, pieces, size):
        new_weight, new_moment = outer_mix(
            weight.astype(jnp.float32),
            moment.astype(jnp.float32),
            as_delta(left, right, scale).astype(jnp.float32),
        )
        for e in others:
            back = replicas - e

            def mean(own_array, far_array):
                return 0.5 * (own_array.astype(jnp.float32) + far_array.astype(jnp.float32))

            index = pieces[back]
            own_left = piece(left, index, size, 1)
            part_weight, part_moment = outer_mix(
                mean(piece(weight, index, size), far_part(e, which)),
                mean(piece(moment, index, size), far_part(e, which + 1)),
                mean(
                    as_delta(own_left, right, scale),
                    as_delta(far_left[e - 1], far_right[e - 1], scale),
                ),
            )
            new_weight = lax.dynamic_update_slice_in_dim(new_weight, part_weight, index * size, 0)
            new_moment = lax.dynamic_update_slice_in_dim(new_moment, part_moment, index * size, 0)
        return new_weight[None, None], new_moment[None, None]

    new_weight_b, new_moment_b = finish(
        weight_out, moment_b[0, 0], hidden, upstream, 2, far_hidden, far_up,
        scale_out, pieces_out, size_out,
    )
    new_weight_a, new_moment_a = finish(
        weight_in, moment_a[0, 0], normed, grad_pre, 0, far_normed, far_pre,
        scale_in, pieces_in, size_in,
    )
    return (new_weight_a, new_weight_b, new_moment_a, new_moment_b)


def solution(mesh):
    placed = (
        P("replica", None, None, "shard"),
        P("replica", None, None, "shard"),
        P("replica", "section", None, "shard"),
        P("replica", "section", "shard", None),
        P("replica", "section", None, "shard"),
        P("replica", "section", "shard", None),
        P(),
        P(),
    )
    return jax.shard_map(
        per_device,
        mesh=mesh,
        in_specs=placed,
        out_specs=(
            P("replica", "section", None, "shard"),
            P("replica", "section", "shard", None),
            P("replica", "section", None, "shard"),
            P("replica", "section", "shard", None),
        ),
        check_vma=False,
    )
```
